32 devices in a mesh: dp: 8 (over z, x), fsdp: 4 (over y, core).
Axes of the slice: x: 2, y: 2, z: 4, core: 2. Of those that a mesh axis runs over, the one named last changes fastest.
Arguments:
- counts: bfloat16 [8192, 13500], P(('dp', 'fsdp')), may hold values from 0 to 8
- library: float32 [8192], P(('dp', 'fsdp')), may hold values from 1000 to 100000
- coords: int32 [2, 8192], P(None, ('dp', 'fsdp')), may hold values from 0 to 2047
- lengths: int32 [8, 1], P('dp'), may hold values from 768 to 1024, as said below
- cotangent: bfloat16 [8192, 13500], P(('dp', 'fsdp')), may hold values from -6 to 6
- w_enc: bfloat16 [13500, 1024], P(None, ('dp', 'fsdp')), may hold values from -0.0546875 to 0.0546875
- w_qkv: bfloat16 [1024, 3072], P(('dp', 'fsdp')), may hold values from -0.25 to 0.25
- w_out: bfloat16 [1024, 1024], P(('dp', 'fsdp')), may hold values from -1 to 1
- gain_one: bfloat16 [1024], P(('dp', 'fsdp')), may hold values from 0.5 to 1.5
- shift_one: bfloat16 [1024], P(('dp', 'fsdp')), may hold values from -3 to 3
- w_up: bfloat16 [1024, 4096], P(('dp', 'fsdp')), may hold values from -0.1875 to 0.1875
- w_down: bfloat16 [4096, 1024], P(('dp', 'fsdp')), may hold values from -0.09375 to 0.09375
- gain_two: bfloat16 [1024], P(('dp', 'fsdp')), may hold values from 0.5 to 1.5
- shift_two: bfloat16 [1024], P(('dp', 'fsdp')), may hold values from -3 to 3
- w_dec: bfloat16 [13500, 1024], P(None, ('dp', 'fsdp')), may hold values from -0.1875 to 0.1875
Outputs:
- logits: bfloat16 [8192, 13500], P(('dp', 'fsdp'))
- counts_grad: float32 [8192, 13500], P(('dp', 'fsdp'))
- grad_enc: float32 [13500, 1024], P(None, ('dp', 'fsdp'))
- grad_qkv: float32 [1024, 3072], P(('dp', 'fsdp'))
- grad_out: float32 [1024, 1024], P(('dp', 'fsdp'))
- grad_gain_one: float32 [1024], P(('dp', 'fsdp'))
- grad_shift_one: float32 [1024], P(('dp', 'fsdp'))
- grad_up: float32 [1024, 4096], P(('dp', 'fsdp'))
- grad_down: float32 [4096, 1024], P(('dp', 'fsdp'))
- grad_gain_two: float32 [1024], P(('dp', 'fsdp'))
- grad_shift_two: float32 [1024], P(('dp', 'fsdp'))
- grad_dec: float32 [13500, 1024], P(None, ('dp', 'fsdp'))
The draws below stay inside these ranges and needn't reach their ends.
Inputs may be any that keep to these rules, and one draw needn't show every extreme that they name: `lengths`: each group holds 1 slide starting at its first slot; the slots after it are padding. In every draw some group has no padding.
All inputs are finite; a program needn't handle non-finite values.
Results may differ from the reference program's by a relative error of at most 0.012.
Values may be sent and summed in bfloat16 or wider, within the bound.
A program may use at most 576 MiB of HBM per device.

```python
import math
import jax
import jax.numpy as jnp
from jax import lax

G = 13500
D = 1024
FF = 4096
HEADS = 16
TOK_DEV = 256
SLIDES = 1
TOKENS = 8192
N_DP = 8
N_FSDP = 4


def draw_lengths(key, part):
    key = jax.random.fold_in(key, 7)
    key_len, key_full = jax.random.split(key, 2)
    group_slots = TOK_DEV * N_FSDP
    shortest = 3 * group_slots // 4
    drawn = jax.random.randint(key_len, (N_DP, SLIDES), shortest, group_slots + 1)
    full = jax.random.randint(key_full, (), 0, N_DP)
    chosen = (jnp.arange(N_DP) == full)[:, None]
    return jnp.where(chosen, group_slots, drawn).astype(jnp.int32)


def plant(values, own_key, least, high):
    longest = values.shape.index(max(values.shape))
    spots = []
    for shift in (0, 1):
        where = [jax.random.randint(jax.random.fold_in(own_key, axis), (), 0, length) for axis, length in enumerate(values.shape)]
        where[longest] = (where[longest] + shift) % values.shape[longest]
        spots.append(tuple(where))
    return values.at[spots[0]].set(least).at[spots[1]].set(high)


def steps_of(stream_key, extent, cuts, low, high):
    level = 1.0
    for position, shards_of in cuts:
        draws = jax.random.uniform(jax.random.fold_in(jax.random.fold_in(stream_key, 6), position), (shards_of,), jnp.float32, low / len(cuts), high / len(cuts))
        level = level * jnp.repeat(jnp.exp(draws), extent[position] // shards_of).reshape((-1,) + (1,) * (len(extent) - 1 - position))
    return level


def normal_values(stream_key, shape, deviation, limit, shards=(), kind=jnp.bfloat16):
    loudness = steps_of(stream_key, shape, shards, -0.22, 0.18) if shards else 1.0
    values = jax.random.normal(stream_key, shape, jnp.float32) * deviation * loudness
    return jnp.minimum(jnp.maximum(values, -limit), limit).astype(kind)


def setup_inputs(seed: int = 0) -> dict:
    splits = jax.random.split(jax.random.key(seed), 16)
    return {
        "counts": jnp.clip(8.0 * jax.random.uniform(splits[0], (TOKENS, G), jnp.float32) ** steps_of(splits[0], (TOKENS, G), ((0, 32),), -0.2, 0.2), 0.0, 8.0).astype(jnp.bfloat16),
        "library": jnp.clip(jnp.exp(math.log(100000.0) - 4.6051702 * jax.random.uniform(splits[1], (TOKENS,), jnp.float32) ** steps_of(splits[1], (TOKENS,), ((0, 32),), -0.2, 0.2)), 1000.0, 100000.0),
        "coords": plant(jax.random.randint(splits[2], (2, TOKENS), 0, 2048), jax.random.fold_in(splits[2], 1), 0, 2047).astype(jnp.int32),
        "lengths": draw_lengths(jax.random.fold_in(splits[15], 71), 0),
        "cotangent": normal_values(splits[4], (TOKENS, G), 1.0, 6.0, ((0, 32),)),
        "w_enc": normal_values(splits[5], (G, D), G ** -0.5, 0.0546875, ((1, 32),)),
        "w_qkv": normal_values(splits[6], (D, 3 * D), (D // 2) ** -0.5, 0.25, ((0, 32),)),
        "w_out": normal_values(splits[7], (D, D), (D // 32) ** -0.5, 1.0, ((0, 32),)),
        "gain_one": jnp.clip(1.0 + 0.1 * jax.random.normal(splits[8], (D,), jnp.float32), 0.5, 1.5).astype(jnp.bfloat16),
        "shift_one": normal_values(splits[9], (D,), 0.5, 3.0, ((0, 32),)),
        "w_up": normal_values(splits[10], (D, FF), D ** -0.5, 0.1875, ((0, 32),)),
        "w_down": normal_values(splits[11], (FF, D), FF ** -0.5, 0.09375, ((0, 32),)),
        "gain_two": jnp.clip(1.0 + 0.1 * jax.random.normal(splits[12], (D,), jnp.float32), 0.5, 1.5).astype(jnp.bfloat16),
        "shift_two": normal_values(splits[13], (D,), 0.5, 3.0, ((0, 32),)),
        "w_dec": normal_values(splits[14], (G, D), D ** -0.5, 0.1875, ((1, 32),)),
    }


HIGH = lax.Precision.HIGHEST
eps = 1e-05

@jax.custom_vjp
def low(v):
    return lax.optimization_barrier(v.astype(jnp.bfloat16)).astype(jnp.float32)

@jax.custom_vjp
def low_back(v):
    return v

def low_keep(v):
    return (low(v), None)

def low_pass(kept, grad):
    return (grad,)

def back_keep(v):
    return (v, None)

def back_low(kept, grad):
    return (low(grad),)
low.defvjp(low_keep, low_pass)
low_back.defvjp(back_keep, back_low)

def matmul(left, right):
    return jnp.dot(left, right, precision=HIGH)

def layer_norm(value, gain, shift):
    mean = lax.optimization_barrier(jnp.mean(value, axis=1, keepdims=True))
    centred = value - mean
    variance = lax.optimization_barrier(jnp.mean(centred * centred, axis=1, keepdims=True))
    return centred * lax.rsqrt(variance + eps) * gain + shift

def positions(coords, width):
    quarter = width // 4
    freqs = 0.05 * jnp.exp(-jnp.arange(quarter, dtype=jnp.float32) * (math.log(10000.0) / quarter))
    along_x = coords[0].astype(jnp.float32)[:, None] * freqs[None, :]
    along_y = coords[1].astype(jnp.float32)[:, None] * freqs[None, :]
    return jnp.concatenate([jnp.sin(along_x), jnp.cos(along_x), jnp.sin(along_y), jnp.cos(along_y)], axis=1)

def segments(lengths_row, slots):
    ends = jnp.cumsum(lengths_row)
    place = jnp.arange(slots, dtype=jnp.int32)
    return lax.optimization_barrier(jnp.sum((place[:, None] >= ends[None, :]).astype(jnp.int32), axis=1)).astype(jnp.int32)

def layer(params, counts, scale, pe, seg):
    w_enc, w_qkv, w_out, gain_one, shift_one, w_up, w_down, gain_two, shift_two, w_dec = params
    xb = low(jnp.log1p(counts * scale[:, None]))
    h0 = low_back(matmul(xb, w_enc)) + pe
    a1 = low(layer_norm(h0, gain_one, shift_one))
    qkv = low_back(low(matmul(a1, w_qkv)))
    rows = qkv.shape[0]
    width = D // HEADS
    query = qkv[:, :D].reshape(rows, HEADS, width)
    keys = qkv[:, D:2 * D].reshape(rows, HEADS, width)
    values = qkv[:, 2 * D:].reshape(rows, HEADS, width)
    raw = jnp.einsum('qhd,khd->hqk', query, keys, precision=HIGH) * width ** (-0.5)
    same = (seg[:, None] == seg[None, :])[None]
    scores = jnp.where(same, low_back(raw), -1000000000.0)
    top = lax.optimization_barrier(jnp.max(scores, axis=-1, keepdims=True))
    expo = jnp.exp(scores - top)
    probs = low(expo / lax.optimization_barrier(jnp.sum(expo, axis=-1, keepdims=True)))
    attended = jnp.einsum('hqk,khd->qhd', probs, values, precision=HIGH).reshape(rows, D)
    attended = low_back(low(attended))
    h1 = h0 + low_back(matmul(attended, w_out))
    a2 = low(layer_norm(h1, gain_two, shift_two))
    hidden = low_back(matmul(a2, w_up))
    act = low(jax.nn.gelu(hidden, approximate=False))
    h2 = h1 + low_back(matmul(act, w_down))
    return matmul(low(h2), w_dec.T)

def reference(counts, library, coords, lengths, cotangent, w_enc, w_qkv, w_out, gain_one, shift_one, w_up, w_down, gain_two, shift_two, w_dec):
    groups = N_DP
    slots = TOK_DEV * N_FSDP
    counts_all = counts.astype(jnp.float32).reshape(groups, slots, G)
    scale = (10000.0 / library).reshape(groups, slots)
    pe = positions(coords, D).reshape(groups, slots, D)
    seg = jax.vmap(lambda row: segments(row, slots))(lengths)
    params = tuple((w.astype(jnp.float32) for w in (w_enc, w_qkv, w_out, gain_one, shift_one, w_up, w_down, gain_two, shift_two, w_dec)))
    step = jax.checkpoint(layer)

    def forward(weights, inputs):
        return lax.map(lambda item: step(weights, item[0], item[1], item[2], item[3]), (inputs, scale, pe, seg))
    logits, pull = jax.vjp(forward, params, counts_all)
    grads, counts_grad = pull(cotangent.astype(jnp.float32).reshape(groups, slots, G))
    return (logits.reshape(TOKENS, G).astype(jnp.bfloat16), counts_grad.reshape(TOKENS, G), grads[0], grads[1], grads[2], grads[3], grads[4], grads[5], grads[6], grads[7], grads[8], grads[9])
```

```python
import math

import jax
import jax.numpy as jnp
from jax import lax
from jax.sharding import Mesh
from jax.sharding import PartitionSpec as P

HEADS = 16


eps = 1e-05


def layer_norm(value, gain, shift):
    mean = jnp.mean(value, axis=1, keepdims=True)
    centred = value - mean
    variance = jnp.mean(centred * centred, axis=1, keepdims=True)
    return centred * lax.rsqrt(variance + eps) * gain + shift


def positions(coords, width):
    quarter = width // 4
    freqs = 0.05 * jnp.exp(-jnp.arange(quarter, dtype=jnp.float32) * (math.log(10000.0) / quarter))
    along_x = coords[0].astype(jnp.float32)[:, None] * freqs[None, :]
    along_y = coords[1].astype(jnp.float32)[:, None] * freqs[None, :]
    return jnp.concatenate(
        [jnp.sin(along_x), jnp.cos(along_x), jnp.sin(along_y), jnp.cos(along_y)], axis=1
    )


def contract_rows(left, right):
    return lax.dot_general(
        left, right, (((0,), (0,)), ((), ())), preferred_element_type=jnp.float32
    )


def contract_cols(left, right):
    return lax.dot_general(
        left, right, (((1,), (1,)), ((), ())), preferred_element_type=jnp.float32
    )


def matmul(left, right):
    return jnp.dot(left, right, preferred_element_type=jnp.float32)


def swap(value, axis):
    return lax.ppermute(value, axis, [(0, 1), (1, 0)])


def by_owner(value, axis):
    n_h = lax.axis_size("h")
    at = value.shape
    block = at[axis] // (8 * n_h)
    split = value.reshape(at[:axis] + (n_h, 2, 2, 2, block) + at[axis + 1 :])
    order = list(range(axis)) + [axis + 3, axis + 1, axis + 2, axis, axis + 4]
    order += list(range(axis + 5, split.ndim))
    return split.transpose(order).reshape(at)


def from_owner(value, axis):
    n_h = lax.axis_size("h")
    at = value.shape
    block = at[axis] // (8 * n_h)
    split = value.reshape(at[:axis] + (2, 2, 2, n_h, block) + at[axis + 1 :])
    order = list(range(axis)) + [axis + 3, axis + 1, axis + 2, axis, axis + 4]
    order += list(range(axis + 5, split.ndim))
    return split.transpose(order).reshape(at)


def relative(value, axis):
    eighth = value.shape[axis] // 8
    mine = lax.axis_index("c") * 4 + lax.axis_index("x") * 2 + lax.axis_index("y")
    parts = [
        lax.dynamic_slice_in_dim(value, (mine ^ part) * eighth, eighth, axis) for part in range(8)
    ]
    return jnp.concatenate(parts, axis=axis)


def gather_parts(shard, first, second):
    own = lax.all_gather(shard, "h", axis=0, tiled=True)
    one = swap(own, first)
    two = swap(own, second)
    both = swap(one, second)
    four = [own, two, one, both] if first == "x" else [own, one, two, both]
    return four + [swap(part, "c") for part in four]


def gather_rows(shard, first, second):
    return jnp.concatenate(gather_parts(shard, first, second), axis=0)


def gather_columns(shard):
    cut = -(-shard.shape[1] // 256) * 128
    left = gather_parts(shard[:, :cut], "x", "y")
    right = gather_parts(shard[:, cut:], "y", "x")
    return jnp.concatenate(
        [jnp.concatenate([a, b], axis=1) for a, b in zip(left, right)], axis=0
    )


def scatter_rows(part, first, second):
    half = part.shape[0] // 2
    other = swap(part[half:], "c")
    part = part[:half].astype(jnp.float32) + other.astype(jnp.float32)
    part = part.astype(jnp.bfloat16).reshape((2, 2, half // 4, -1))
    if first == "x":
        part = part[0].astype(jnp.float32) + swap(part[1], "x").astype(jnp.float32)
    else:
        part = part[:, 0].astype(jnp.float32) + swap(part[:, 1], "y").astype(jnp.float32)
    part = part.astype(jnp.bfloat16)
    part = part[0].astype(jnp.float32) + swap(part[1], second).astype(jnp.float32)
    part = part.astype(jnp.bfloat16)
    return lax.psum_scatter(part, "h", scatter_dimension=0, tiled=True).astype(jnp.float32)


def scatter_columns(left, right):
    cut = -(-right.shape[1] // 256) * 128
    left = relative(left, 1)
    one = contract_rows(left, right[:, :cut]).astype(jnp.bfloat16)
    two = contract_rows(left, right[:, cut:]).astype(jnp.bfloat16)
    return jnp.concatenate(
        [scatter_rows(one, "x", "y"), scatter_rows(two, "y", "x")], axis=1
    ).T


def gather_group(mine):
    at_y, at_c = lax.axis_index("y"), lax.axis_index("c")
    pair = jnp.stack([mine, swap(mine, "y")])
    both = jnp.stack([pair, swap(pair, "c")])
    order = [
        lax.dynamic_index_in_dim(
            lax.dynamic_index_in_dim(both, at_c ^ c, 0, False), at_y ^ y, 0, False
        )
        for y in range(2)
        for c in range(2)
    ]
    return jnp.concatenate(order, axis=0)


def scatter_group(rows_all):
    at_y, at_c = lax.axis_index("y"), lax.axis_index("c")
    part = rows_all.astype(jnp.bfloat16).reshape((2, 2, rows_all.shape[0] // 4, -1))
    keep = lax.dynamic_index_in_dim(part, at_c, 1, False).astype(jnp.float32)
    send = lax.dynamic_index_in_dim(part, 1 - at_c, 1, False)
    part = (keep + swap(send, "c").astype(jnp.float32)).astype(jnp.bfloat16)
    keep = lax.dynamic_index_in_dim(part, at_y, 0, False).astype(jnp.float32)
    send = lax.dynamic_index_in_dim(part, 1 - at_y, 0, False)
    return keep + swap(send, "y").astype(jnp.float32)


def on_device(
    counts,
    library,
    coords,
    lengths,
    cotangent,
    w_enc,
    w_qkv,
    w_out,
    gain_one,
    shift_one,
    w_up,
    w_down,
    gain_two,
    shift_two,
    w_dec,
):
    rows = counts.shape[0]
    width = w_qkv.shape[1] // 3
    heads = HEADS
    head_width = width // heads
    att_scale = head_width ** (-0.5)
    group_size = 4
    slots = rows * group_size
    scale = 10000.0 / library
    counts_f = counts.astype(jnp.float32)
    xb = jnp.log1p(counts_f * scale[:, None]).astype(jnp.bfloat16)
    pe = by_owner(positions(coords, width), 1)
    ends = jnp.cumsum(lengths[0])
    place = jnp.arange(slots, dtype=jnp.int32)
    seg_all = jnp.sum((place[:, None] >= ends[None, :]).astype(jnp.int32), axis=1)
    seg_mine = lax.dynamic_slice_in_dim(seg_all, (lax.axis_index("y") * 2 + lax.axis_index("c")) * rows, rows)
    same = (seg_mine[:, None] == seg_all[None, :])[None]
    enc_all = gather_columns(w_enc.T)
    vectors = jnp.stack([gain_one, shift_one, gain_two, shift_two], axis=1)
    vectors = jnp.pad(vectors, ((0, 0), (0, 124)))
    qkv_all = gather_rows(jnp.concatenate([w_qkv, vectors], axis=1), "x", "y")
    out_all = gather_rows(by_owner(w_out, 1), "y", "x")
    up_all = gather_rows(by_owner(w_up, 1), "y", "x")
    down_all = gather_rows(by_owner(w_down, 1), "x", "y")
    dec_all = gather_columns(w_dec.T)
    vectors = relative(qkv_all[:, 3 * width :].astype(jnp.float32), 0).T
    qkv_all = qkv_all[:, : 3 * width]
    g1f, b1f, g2f, b2f = vectors[0], vectors[1], vectors[2], vectors[3]
    h0 = relative(contract_cols(xb, enc_all), 1) + pe
    a1 = layer_norm(h0, g1f, b1f).astype(jnp.bfloat16)
    a1_rel = relative(a1, 1)
    qkv = matmul(a1_rel, qkv_all).astype(jnp.bfloat16)
    query = qkv[:, :width].reshape(rows, heads, head_width)
    kv_all = gather_group(qkv[:, width:])
    keys = kv_all[:, :width].reshape(slots, heads, head_width)
    values = kv_all[:, width:].reshape(slots, heads, head_width)

    def scores_of():
        raw = (
            jnp.einsum("qhd,khd->hqk", query, keys, preferred_element_type=jnp.float32) * att_scale
        )
        return jnp.where(same, raw, -1000000000.0)

    scores = scores_of()
    top = jnp.max(scores, axis=-1, keepdims=True)
    expo = jnp.exp(scores - top)
    total = jnp.sum(expo, axis=-1, keepdims=True)
    log_total = top + jnp.log(total)
    probs_b = (expo / total).astype(jnp.bfloat16)
    attended = jnp.einsum("hqk,khd->qhd", probs_b, values, preferred_element_type=jnp.float32)
    attended_b = attended.reshape(rows, width).astype(jnp.bfloat16)
    attended_rel = relative(by_owner(attended_b, 1), 1)
    h1 = h0 + matmul(attended_rel, out_all)
    a2 = layer_norm(h1, g2f, b2f).astype(jnp.bfloat16)
    a2_rel = relative(a2, 1)
    hidden = matmul(a2_rel, up_all)
    act = jax.nn.gelu(hidden, approximate=False).astype(jnp.bfloat16)
    act_rel = relative(act, 1)
    h2 = h1 + matmul(act_rel, down_all)
    hb = h2.astype(jnp.bfloat16)
    logits = matmul(relative(hb, 1), dec_all).astype(jnp.bfloat16)
    grad_dec = scatter_columns(hb, cotangent)
    dh2 = relative(contract_cols(cotangent, dec_all), 1)
    dfb = dh2.astype(jnp.bfloat16)
    grad_down = contract_rows(act_rel, dfb)
    d_act = relative(contract_cols(dfb, down_all), 1)
    slope = jax.vjp(lambda v: jax.nn.gelu(v, approximate=False), hidden)[1](d_act)[0]
    d_hidden = slope.astype(jnp.bfloat16)
    grad_up = contract_rows(a2_rel, d_hidden)
    da2 = relative(contract_cols(d_hidden, up_all), 1)
    norm_pull = jax.vjp(layer_norm, h1, g2f, b2f)[1]
    dh1_norm, grad_gain_two, grad_shift_two = norm_pull(da2)
    dh1 = dh2 + dh1_norm
    grad_down = from_owner(scatter_rows(grad_down.astype(jnp.bfloat16), "x", "y"), 1)
    grad_up = from_owner(scatter_rows(grad_up.astype(jnp.bfloat16), "y", "x"), 1)
    dab = dh1.astype(jnp.bfloat16)
    grad_out = contract_rows(attended_rel, dab)
    d_attended = relative(contract_cols(dab, out_all).astype(jnp.bfloat16), 1)
    d_attended = from_owner(d_attended, 1).reshape(rows, heads, head_width)
    probs = jnp.exp(scores_of() - log_total)
    probs_b = probs.astype(jnp.bfloat16)
    d_probs = jnp.einsum("qhd,khd->hqk", d_attended, values, preferred_element_type=jnp.float32)
    inner = jnp.sum(probs * d_probs, axis=-1, keepdims=True)
    d_scores = (probs * (d_probs - inner)).astype(jnp.bfloat16)
    d_query = (
        jnp.einsum("hqk,khd->qhd", d_scores, keys, preferred_element_type=jnp.float32) * att_scale
    )
    d_keys = (
        jnp.einsum("hqk,qhd->khd", d_scores, query, preferred_element_type=jnp.float32) * att_scale
    )
    d_values = jnp.einsum("hqk,qhd->khd", probs_b, d_attended, preferred_element_type=jnp.float32)
    d_kv = jnp.concatenate([d_keys.reshape(slots, width), d_values.reshape(slots, width)], axis=1)
    d_kv = scatter_group(d_kv)
    d_qkv = jnp.concatenate([d_query.reshape(rows, width), d_kv], axis=1).astype(jnp.bfloat16)
    grad_qkv = contract_rows(a1_rel, d_qkv)
    da1 = relative(contract_cols(d_qkv, qkv_all), 1)
    first_pull = jax.vjp(layer_norm, h0, g1f, b1f)[1]
    dh0_norm, grad_gain_one, grad_shift_one = first_pull(da1)
    grad_vectors = jnp.stack([grad_gain_one, grad_shift_one, grad_gain_two, grad_shift_two], axis=1)
    grad_vectors = jnp.pad(relative(grad_vectors, 0), ((0, 0), (0, 124)))
    grad_qkv = jnp.concatenate([grad_qkv, grad_vectors], axis=1).astype(jnp.bfloat16)
    grad_out = from_owner(scatter_rows(grad_out.astype(jnp.bfloat16), "y", "x"), 1)
    grad_qkv = scatter_rows(grad_qkv, "x", "y")
    grad_gain_one, grad_shift_one, grad_gain_two, grad_shift_two = (
        grad_qkv[:, 3 * width + k] for k in range(4)
    )
    grad_qkv = grad_qkv[:, : 3 * width]
    dh0b = (dh1 + dh0_norm).astype(jnp.bfloat16)

    grad_enc = scatter_columns(dh0b, xb)
    d_xb = matmul(relative(dh0b, 1), enc_all)
    counts_grad = d_xb * scale[:, None] / (1.0 + counts_f * scale[:, None])
    return (
        logits,
        counts_grad,
        grad_enc,
        grad_qkv,
        grad_out,
        grad_gain_one,
        grad_shift_one,
        grad_up,
        grad_down,
        grad_gain_two,
        grad_shift_two,
        grad_dec,
    )


ALL = ("h", "x", "y", "c")


def solution(mesh):
    n_dp, n_fsdp = mesh.shape["dp"], mesh.shape["fsdp"]
    mesh = Mesh(mesh.devices.reshape((n_dp // 2, 2, 2, n_fsdp // 2)), ALL)
    placed = (
        P(ALL, None),
        P(ALL),
        P(None, ALL),
        P(("h", "x"), None),
        P(ALL, None),
        P(None, ALL),
        P(ALL, None),
        P(ALL, None),
        P(ALL),
        P(ALL),
        P(ALL, None),
        P(ALL, None),
        P(ALL),
        P(ALL),
        P(None, ALL),
    )
    return jax.shard_map(
        on_device,
        mesh=mesh,
        in_specs=placed,
        out_specs=(
            P(ALL, None),
            P(ALL, None),
            P(None, ALL),
            P(ALL, None),
            P(ALL, None),
            P(ALL),
            P(ALL),
            P(ALL, None),
            P(ALL, None),
            P(ALL),
            P(ALL),
            P(None, ALL),
        ),
        check_vma=False,
    )
```

```python
import math

import jax
import jax.numpy as jnp
from jax import lax
from jax.sharding import Mesh
from jax.sharding import PartitionSpec as P

HEADS = 16


eps = 1e-05


def layer_norm(value, gain, shift):
    mean = jnp.mean(value, axis=1, keepdims=True)
    centred = value - mean
    variance = jnp.mean(centred * centred, axis=1, keepdims=True)
    return centred * lax.rsqrt(variance + eps) * gain + shift


def positions(coords, width):
    quarter = width // 4
    freqs = 0.05 * jnp.exp(-jnp.arange(quarter, dtype=jnp.float32) * (math.log(10000.0) / quarter))
    along_x = coords[0].astype(jnp.float32)[:, None] * freqs[None, :]
    along_y = coords[1].astype(jnp.float32)[:, None] * freqs[None, :]
    return jnp.concatenate(
        [jnp.sin(along_x), jnp.cos(along_x), jnp.sin(along_y), jnp.cos(along_y)], axis=1
    )


def contract_rows(left, right):
    return lax.dot_general(
        left, right, (((0,), (0,)), ((), ())), preferred_element_type=jnp.float32
    )


def contract_cols(left, right):
    return lax.dot_general(
        left, right, (((1,), (1,)), ((), ())), preferred_element_type=jnp.float32
    )


def matmul(left, right):
    return jnp.dot(left, right, preferred_element_type=jnp.float32)


def swap(value, axis):
    return lax.ppermute(value, axis, [(0, 1), (1, 0)])


def by_owner(value, axis):
    n_h = lax.axis_size("h")
    at = value.shape
    block = at[axis] // (8 * n_h)
    split = value.reshape(at[:axis] + (n_h, 2, 2, 2, block) + at[axis + 1 :])
    order = list(range(axis)) + [axis + 3, axis + 1, axis + 2, axis, axis + 4]
    order += list(range(axis + 5, split.ndim))
    return split.transpose(order).reshape(at)


def from_owner(value, axis):
    n_h = lax.axis_size("h")
    at = value.shape
    block = at[axis] // (8 * n_h)
    split = value.reshape(at[:axis] + (2, 2, 2, n_h, block) + at[axis + 1 :])
    order = list(range(axis)) + [axis + 3, axis + 1, axis + 2, axis, axis + 4]
    order += list(range(axis + 5, split.ndim))
    return split.transpose(order).reshape(at)


def relative(value, axis):
    eighth = value.shape[axis] // 8
    mine = lax.axis_index("c") * 4 + lax.axis_index("x") * 2 + lax.axis_index("y")
    parts = [
        lax.dynamic_slice_in_dim(value, (mine ^ part) * eighth, eighth, axis) for part in range(8)
    ]
    return jnp.concatenate(parts, axis=axis)


def gather_parts(shard, first, second):
    own = lax.all_gather(shard, "h", axis=0, tiled=True)
    one = swap(own, first)
    two = swap(own, second)
    both = swap(one, second)
    four = [own, two, one, both] if first == "x" else [own, one, two, both]
    return four + [swap(part, "c") for part in four]


def gather_rows(shard, first, second):
    return jnp.concatenate(gather_parts(shard, first, second), axis=0)


def gather_columns(shard):
    cut = -(-shard.shape[1] // 256) * 128
    left = gather_parts(shard[:, :cut], "x", "y")
    right = gather_parts(shard[:, cut:], "y", "x")
    return jnp.concatenate(
        [jnp.concatenate([a, b], axis=1) for a, b in zip(left, right)], axis=0
    )


def with_other_core(value):
    return jnp.concatenate([value, swap(value, "c")], axis=0)


def own_half(left):
    half = left.shape[1] // 2
    return jnp.concatenate([left[:, :half], swap(left[:, half:], "c")], axis=0)


def sum_over_h(part):
    n_h = lax.axis_size("h")
    rows = part.shape[0] // n_h
    at = lax.axis_index("h")
    total = lax.dynamic_slice_in_dim(part, at * rows, rows, 0).astype(jnp.float32)
    for step in range(1, n_h):
        send = lax.dynamic_slice_in_dim(part, lax.rem(at + step, n_h) * rows, rows, 0)
        ring = [(i, (i + step) % n_h) for i in range(n_h)]
        total = total + lax.ppermute(send, "h", ring).astype(jnp.float32)
    return total


def scatter(left, right, first, second):
    w = left.shape[1] // 4
    near, by_y, by_x, far = (left[:, k * w : (k + 1) * w] for k in range(4))
    one, two = (by_x, by_y) if first == "x" else (by_y, by_x)
    got_far = swap(contract_rows(far, right).astype(jnp.bfloat16), first).astype(jnp.float32)
    got_one = swap(contract_rows(one, right).astype(jnp.bfloat16), first).astype(jnp.float32)
    got_two = swap((contract_rows(two, right) + got_far).astype(jnp.bfloat16), second)
    part = contract_rows(near, right) + got_one + got_two.astype(jnp.float32)
    return sum_over_h(part.astype(jnp.bfloat16))


def scatter_columns(left, right):
    cut = -(-right.shape[1] // 256) * 128
    return jnp.concatenate(
        [scatter(left, right[:, :cut], "x", "y"), scatter(left, right[:, cut:], "y", "x")], axis=1
    ).T


def scatter_vectors(part):
    half = part.shape[0] // 2
    part = part[:half] + swap(part[half:].astype(jnp.bfloat16), "c").astype(jnp.float32)
    part = part[: half // 2] + swap(part[half // 2 :].astype(jnp.bfloat16), "x").astype(jnp.float32)
    half = half // 2
    part = part[: half // 2] + swap(part[half // 2 :].astype(jnp.bfloat16), "y").astype(jnp.float32)
    return sum_over_h(part.astype(jnp.bfloat16))


def gather_group(mine):
    at_y, at_c = lax.axis_index("y"), lax.axis_index("c")
    pair = jnp.stack([mine, swap(mine, "y")])
    both = jnp.stack([pair, swap(pair, "c")])
    order = [
        lax.dynamic_index_in_dim(
            lax.dynamic_index_in_dim(both, at_c ^ c, 0, False), at_y ^ y, 0, False
        )
        for y in range(2)
        for c in range(2)
    ]
    return jnp.concatenate(order, axis=0)


def scatter_group(rows_all):
    at_y, at_c = lax.axis_index("y"), lax.axis_index("c")
    part = rows_all.astype(jnp.bfloat16).reshape((2, 2, rows_all.shape[0] // 4, -1))
    keep = lax.dynamic_index_in_dim(part, at_c, 1, False).astype(jnp.float32)
    send = lax.dynamic_index_in_dim(part, 1 - at_c, 1, False)
    part = (keep + swap(send, "c").astype(jnp.float32)).astype(jnp.bfloat16)
    keep = lax.dynamic_index_in_dim(part, at_y, 0, False).astype(jnp.float32)
    send = lax.dynamic_index_in_dim(part, 1 - at_y, 0, False)
    return keep + swap(send, "y").astype(jnp.float32)


def on_device(
    counts,
    library,
    coords,
    lengths,
    cotangent,
    w_enc,
    w_qkv,
    w_out,
    gain_one,
    shift_one,
    w_up,
    w_down,
    gain_two,
    shift_two,
    w_dec,
):
    rows = counts.shape[0]
    width = w_qkv.shape[1] // 3
    heads = HEADS
    head_width = width // heads
    att_scale = head_width ** (-0.5)
    group_size = 4
    slots = rows * group_size
    scale = 10000.0 / library
    counts_f = counts.astype(jnp.float32)
    xb = jnp.log1p(counts_f * scale[:, None]).astype(jnp.bfloat16)
    pe = by_owner(positions(coords, width), 1)
    ends = jnp.cumsum(lengths[0])
    place = jnp.arange(slots, dtype=jnp.int32)
    seg_all = jnp.sum((place[:, None] >= ends[None, :]).astype(jnp.int32), axis=1)
    seg_mine = lax.dynamic_slice_in_dim(seg_all, (lax.axis_index("y") * 2 + lax.axis_index("c")) * rows, rows)
    same = (seg_mine[:, None] == seg_all[None, :])[None]
    enc_all = gather_columns(w_enc.T)
    vectors = jnp.stack([gain_one, shift_one, gain_two, shift_two], axis=1)
    vectors = jnp.pad(vectors, ((0, 0), (0, 124)))
    qkv_all = gather_rows(jnp.concatenate([w_qkv, vectors], axis=1), "x", "y")
    out_all = gather_rows(by_owner(w_out, 1), "y", "x")
    up_all = gather_rows(by_owner(w_up, 1), "y", "x")
    down_all = gather_rows(by_owner(w_down, 1), "x", "y")
    dec_all = gather_columns(w_dec.T)
    vectors = relative(qkv_all[:, 3 * width :].astype(jnp.float32), 0).T
    qkv_all = qkv_all[:, : 3 * width]
    g1f, b1f, g2f, b2f = vectors[0], vectors[1], vectors[2], vectors[3]
    h0 = relative(contract_cols(xb, enc_all), 1) + pe
    a1 = layer_norm(h0, g1f, b1f).astype(jnp.bfloat16)
    a1_rel = relative(a1, 1)
    qkv = matmul(a1_rel, qkv_all).astype(jnp.bfloat16)
    query = qkv[:, :width].reshape(rows, heads, head_width)
    kv_all = gather_group(qkv[:, width:])
    keys = kv_all[:, :width].reshape(slots, heads, head_width)
    values = kv_all[:, width:].reshape(slots, heads, head_width)

    def scores_of():
        raw = (
            jnp.einsum("qhd,khd->hqk", query, keys, preferred_element_type=jnp.float32) * att_scale
        )
        return jnp.where(same, raw, -1000000000.0)

    scores = scores_of()
    top = jnp.max(scores, axis=-1, keepdims=True)
    expo = jnp.exp(scores - top)
    total = jnp.sum(expo, axis=-1, keepdims=True)
    log_total = top + jnp.log(total)
    probs_b = (expo / total).astype(jnp.bfloat16)
    attended = jnp.einsum("hqk,khd->qhd", probs_b, values, preferred_element_type=jnp.float32)
    attended_b = attended.reshape(rows, width).astype(jnp.bfloat16)
    attended_rel = relative(by_owner(attended_b, 1), 1)
    h1 = h0 + matmul(attended_rel, out_all)
    a2 = layer_norm(h1, g2f, b2f).astype(jnp.bfloat16)
    a2_rel = relative(a2, 1)
    hidden = matmul(a2_rel, up_all)
    act = jax.nn.gelu(hidden, approximate=False).astype(jnp.bfloat16)
    act_rel = relative(act, 1)
    h2 = h1 + matmul(act_rel, down_all)
    hb_rel = relative(h2.astype(jnp.bfloat16), 1)
    logits = matmul(hb_rel, dec_all).astype(jnp.bfloat16)
    grad_dec = scatter_columns(own_half(hb_rel), with_other_core(cotangent))
    dh2 = relative(contract_cols(cotangent, dec_all), 1)
    dfb = dh2.astype(jnp.bfloat16)
    grad_down = scatter(own_half(act_rel), with_other_core(dfb), "x", "y")
    d_act = relative(contract_cols(dfb, down_all), 1)
    slope = jax.vjp(lambda v: jax.nn.gelu(v, approximate=False), hidden)[1](d_act)[0]
    d_hidden = slope.astype(jnp.bfloat16)
    grad_up = scatter(own_half(a2_rel), with_other_core(d_hidden), "y", "x")
    da2 = relative(contract_cols(d_hidden, up_all), 1)
    norm_pull = jax.vjp(layer_norm, h1, g2f, b2f)[1]
    dh1_norm, grad_gain_two, grad_shift_two = norm_pull(da2)
    dh1 = dh2 + dh1_norm
    grad_down = from_owner(grad_down, 1)
    grad_up = from_owner(grad_up, 1)
    dab = dh1.astype(jnp.bfloat16)
    grad_out = from_owner(scatter(own_half(attended_rel), with_other_core(dab), "y", "x"), 1)
    d_attended = relative(contract_cols(dab, out_all).astype(jnp.bfloat16), 1)
    d_attended = from_owner(d_attended, 1).reshape(rows, heads, head_width)
    probs = jnp.exp(scores_of() - log_total)
    probs_b = probs.astype(jnp.bfloat16)
    d_probs = jnp.einsum("qhd,khd->hqk", d_attended, values, preferred_element_type=jnp.float32)
    inner = jnp.sum(probs * d_probs, axis=-1, keepdims=True)
    d_scores = (probs * (d_probs - inner)).astype(jnp.bfloat16)
    d_query = (
        jnp.einsum("hqk,khd->qhd", d_scores, keys, preferred_element_type=jnp.float32) * att_scale
    )
    d_keys = (
        jnp.einsum("hqk,qhd->khd", d_scores, query, preferred_element_type=jnp.float32) * att_scale
    )
    d_values = jnp.einsum("hqk,qhd->khd", probs_b, d_attended, preferred_element_type=jnp.float32)
    d_kv = jnp.concatenate([d_keys.reshape(slots, width), d_values.reshape(slots, width)], axis=1)
    d_kv = scatter_group(d_kv)
    d_qkv = jnp.concatenate([d_query.reshape(rows, width), d_kv], axis=1).astype(jnp.bfloat16)
    grad_qkv = scatter(own_half(a1_rel), with_other_core(d_qkv), "x", "y")
    da1 = relative(contract_cols(d_qkv, qkv_all), 1)
    first_pull = jax.vjp(layer_norm, h0, g1f, b1f)[1]
    dh0_norm, grad_gain_one, grad_shift_one = first_pull(da1)
    grad_vectors = jnp.stack([grad_gain_one, grad_shift_one, grad_gain_two, grad_shift_two], axis=1)
    grad_vectors = scatter_vectors(relative(grad_vectors, 0))
    grad_gain_one, grad_shift_one, grad_gain_two, grad_shift_two = (
        grad_vectors[:, k] for k in range(4)
    )
    dh0b = (dh1 + dh0_norm).astype(jnp.bfloat16)

    dh0b_rel = relative(dh0b, 1)
    grad_enc = scatter_columns(own_half(dh0b_rel), with_other_core(xb))
    d_xb = matmul(dh0b_rel, enc_all)
    counts_grad = d_xb * scale[:, None] / (1.0 + counts_f * scale[:, None])
    return (
        logits,
        counts_grad,
        grad_enc,
        grad_qkv,
        grad_out,
        grad_gain_one,
        grad_shift_one,
        grad_up,
        grad_down,
        grad_gain_two,
        grad_shift_two,
        grad_dec,
    )


ALL = ("h", "x", "y", "c")


def solution(mesh):
    n_dp, n_fsdp = mesh.shape["dp"], mesh.shape["fsdp"]
    mesh = Mesh(mesh.devices.reshape((n_dp // 2, 2, 2, n_fsdp // 2)), ALL)
    placed = (
        P(ALL, None),
        P(ALL),
        P(None, ALL),
        P(("h", "x"), None),
        P(ALL, None),
        P(None, ALL),
        P(ALL, None),
        P(ALL, None),
        P(ALL),
        P(ALL),
        P(ALL, None),
        P(ALL, None),
        P(ALL),
        P(ALL),
        P(None, ALL),
    )
    return jax.shard_map(
        on_device,
        mesh=mesh,
        in_specs=placed,
        out_specs=(
            P(ALL, None),
            P(ALL, None),
            P(None, ALL),
            P(ALL, None),
            P(ALL, None),
            P(ALL),
            P(ALL),
            P(ALL, None),
            P(ALL, None),
            P(ALL),
            P(ALL),
            P(None, ALL),
        ),
        check_vma=False,
    )
```

```python
import functools
import math

import jax
import jax.numpy as jnp
from jax import lax
from jax.experimental import pallas as pl
from jax.experimental.pallas import tpu as pltpu
from jax.sharding import Mesh
from jax.sharding import PartitionSpec as P

HEADS = 16
MESH = pl.DeviceIdType.MESH
RING = 8


eps = 1e-05


def layer_norm(value, gain, shift):
    mean = jnp.mean(value, axis=1, keepdims=True)
    centred = value - mean
    variance = jnp.mean(centred * centred, axis=1, keepdims=True)
    return centred * lax.rsqrt(variance + eps) * gain + shift


def positions(coords, width):
    quarter = width // 4
    freqs = 0.05 * jnp.exp(-jnp.arange(quarter, dtype=jnp.float32) * (math.log(10000.0) / quarter))
    along_x = coords[0].astype(jnp.float32)[:, None] * freqs[None, :]
    along_y = coords[1].astype(jnp.float32)[:, None] * freqs[None, :]
    return jnp.concatenate(
        [jnp.sin(along_x), jnp.cos(along_x), jnp.sin(along_y), jnp.cos(along_y)], axis=1
    )


def contract_rows(left, right):
    return lax.dot_general(
        left, right, (((0,), (0,)), ((), ())), preferred_element_type=jnp.float32
    )


def contract_cols(left, right):
    return lax.dot_general(
        left, right, (((1,), (1,)), ((), ())), preferred_element_type=jnp.float32
    )


def matmul(left, right):
    return jnp.dot(left, right, preferred_element_type=jnp.float32)


def swap(value, axis):
    return lax.ppermute(value, axis, [(0, 1), (1, 0)])


def by_owner(value, axis):
    n_h = lax.axis_size("h")
    at = value.shape
    block = at[axis] // (8 * n_h)
    split = value.reshape(at[:axis] + (n_h, 2, 2, 2, block) + at[axis + 1 :])
    order = list(range(axis)) + [axis + 3, axis + 1, axis + 2, axis, axis + 4]
    order += list(range(axis + 5, split.ndim))
    return split.transpose(order).reshape(at)


def from_owner(value, axis):
    n_h = lax.axis_size("h")
    at = value.shape
    block = at[axis] // (8 * n_h)
    split = value.reshape(at[:axis] + (2, 2, 2, n_h, block) + at[axis + 1 :])
    order = list(range(axis)) + [axis + 3, axis + 1, axis + 2, axis, axis + 4]
    order += list(range(axis + 5, split.ndim))
    return split.transpose(order).reshape(at)


def relative(value, axis):
    eighth = value.shape[axis] // 8
    mine = lax.axis_index("c") * 4 + lax.axis_index("x") * 2 + lax.axis_index("y")
    parts = [
        lax.dynamic_slice_in_dim(value, (mine ^ part) * eighth, eighth, axis) for part in range(8)
    ]
    return jnp.concatenate(parts, axis=axis)


def greet(peers):
    barrier = pltpu.get_barrier_semaphore()
    for peer in peers:
        pl.semaphore_signal(barrier, inc=1, device_id=peer, device_id_type=MESH)
    pl.semaphore_wait(barrier, len(peers))


def gather_kernel(n_h, jobs, n_arrays, n_full, *refs):
    shards, wholes = refs[:n_arrays], refs[n_arrays : 2 * n_arrays]
    own_sem, h_send, h_recv, send, recv = refs[2 * n_arrays :]
    h, x, y, c = (lax.axis_index(name) for name in ("h", "x", "y", "c"))
    h = 0 if n_h == 1 else h
    to_x, to_y, to_c = {"x": 1 - x}, {"y": 1 - y}, {"c": 1 - c}
    greet([{"h": lax.rem(h + d, n_h)} for d in range(1, n_h)] + [to_x, to_y, to_c])

    def rows_of(job, at):
        array, low, high, _ = job
        rows = shards[array].shape[0]
        place = (pl.ds(at * rows, rows), pl.ds(low, high - low))
        return wholes[array].at[(c, x, y, *place) if array < n_full else place]

    def h_copy(j, d):
        array, low, high, _ = jobs[j]
        return pltpu.make_async_remote_copy(
            src_ref=shards[array].at[:, pl.ds(low, high - low)],
            dst_ref=rows_of(jobs[j], h),
            send_sem=h_send.at[j, d - 1],
            recv_sem=h_recv.at[j, d - 1],
            device_id={"h": lax.rem(h + d, n_h)},
            device_id_type=MESH,
        )

    def own_copy(j):
        array, low, high, _ = jobs[j]
        return pltpu.make_async_copy(
            shards[array].at[:, pl.ds(low, high - low)], rows_of(jobs[j], h), own_sem.at[j]
        )

    def block_copy(j, k, block, to, columns):
        view = wholes[jobs[j][0]].at[(*block, slice(None), pl.ds(columns[0], columns[1] - columns[0]))]
        return pltpu.make_async_remote_copy(
            src_ref=view,
            dst_ref=view,
            send_sem=send.at[j, k],
            recv_sem=recv.at[j, k],
            device_id=to,
            device_id_type=MESH,
        )

    own, by_x, by_y, far = (c, x, y), (c, 1 - x, y), (c, x, 1 - y), (c, 1 - x, 1 - y)

    def copy(j, k):
        _, low, high, middle = jobs[j]
        block, to, columns = [
            (own, to_x, (low, high)),
            (own, to_y, (low, high)),
            (own, to_c, (low, high)),
            (by_x, to_y, (low, middle)),
            (by_y, to_x, (middle, high)),
            (by_x, to_c, (low, high)),
            (by_y, to_c, (low, high)),
            (far, to_c, (low, high)),
        ][k]
        return block_copy(j, k, block, to, columns)

    def start_h(j):
        own_copy(j).start()
        for d in range(1, n_h):
            h_copy(j, d).start()

    n = sum(array < n_full for array, *_ in jobs)
    ahead = 2
    for j in range(ahead):
        start_h(j)
    for step in range(n + 2):
        if step < n:
            own_copy(step).wait()
            for d in range(1, n_h):
                h_copy(step, d).wait_recv()
            for k in (0, 1, 2):
                copy(step, k).start()
            if step + ahead < len(jobs):
                start_h(step + ahead)
        if 0 <= step - 1 < n:
            for k in (0, 1):
                copy(step - 1, k).wait_recv()
            for k in (3, 4, 5, 6):
                copy(step - 1, k).start()
        if 0 <= step - 2 < n:
            for k in (3, 4):
                copy(step - 2, k).wait_recv()
            copy(step - 2, 7).start()
    for j in range(n + ahead, len(jobs)):
        start_h(j)
    for j in range(n, len(jobs)):
        own_copy(j).wait()
        for d in range(1, n_h):
            h_copy(j, d).wait_recv()
    for j in range(len(jobs)):
        for d in range(1, n_h):
            h_copy(j, d).wait_send()
    for j in range(n):
        for k in range(8):
            copy(j, k).wait_send()
        for k in (2, 5, 6, 7):
            copy(j, k).wait_recv()


def gather_all(shards, n_full, cuts, order, collective_id):
    n_h = lax.axis_size("h")
    if any(shard.shape[0] % 16 for shard in shards):
        shards = [lax.all_gather(s, "h", axis=0, tiled=True) for s in shards]
        n_h = 1
    jobs = []
    for array, piece in order:
        low, high = cuts[array][piece], cuts[array][piece + 1]
        jobs.append((array, low, high, low + (high - low) // 256 * 128))
    n, others, dma = len(jobs), max(n_h - 1, 1), pltpu.SemaphoreType.DMA
    shapes = [(n_h * s.shape[0], s.shape[1]) for s in shards]
    return pl.pallas_call(
        functools.partial(gather_kernel, n_h, jobs, len(shards), n_full),
        out_shape=[
            jax.ShapeDtypeStruct((2, 2, 2) + shape if k < n_full else shape, jnp.bfloat16)
            for k, shape in enumerate(shapes)
        ],
        in_specs=[pl.BlockSpec(memory_space=pl.ANY)] * len(shards),
        out_specs=[pl.BlockSpec(memory_space=pl.ANY)] * len(shards),
        scratch_shapes=[dma((n,)), dma((n, others)), dma((n, others)), dma((n, 8)), dma((n, 8))],
        compiler_params=pltpu.CompilerParams(collective_id=collective_id, has_side_effects=True),
    )(*shards)


def scatter_kernel(n_h, n, n_first, run, lefts, rights, more, out, right_buf, own, s1, r1, s2, r2, s3, r3,
                   load_sem, send1, recv1, send2, recv2, send3, recv3):
    h, x, y = (lax.axis_index(name) for name in ("h", "x", "y"))
    to_x, to_y = {"x": 1 - x}, {"y": 1 - y}
    w = s3.shape[1]
    rows = w // n_h
    f32, b16 = jnp.float32, jnp.bfloat16
    greet([{"h": lax.rem(h + d, n_h)} for d in range(1, n_h)] + [to_x, to_y])

    def load(i, source, k):
        slot = lax.rem(i, 3)
        return pltpu.make_async_copy(source.at[k], right_buf.at[slot], load_sem.at[slot])

    def start_load(i):
        @pl.when(i < n_first)
        def _():
            load(i, rights, i).start()

        @pl.when((i >= n_first) & (i < n))
        def _():
            load(i, more, i - n_first).start()

    def hop(i, source, target, send_sem, recv_sem, to):
        slot = lax.rem(i, RING)
        return pltpu.make_async_remote_copy(
            src_ref=source.at[slot], dst_ref=target.at[i], send_sem=send_sem.at[slot],
            recv_sem=recv_sem.at[i], device_id=to, device_id_type=MESH,
        )

    def first(i, odd):
        return hop(i, s1, r1, send1, recv1, to_y if odd else to_x)

    def second(i, odd):
        return hop(i, s2, r2, send2, recv2, to_x if odd else to_y)

    def third(i, d):
        to = lax.rem(h + d, n_h)
        slot = lax.rem(i, RING)
        return pltpu.make_async_remote_copy(
            src_ref=s3.at[slot, pl.ds(to * rows, rows)], dst_ref=r3.at[i, d - 1],
            send_sem=send3.at[slot, d - 1], recv_sem=recv3.at[i, d - 1],
            device_id={"h": to}, device_id_type=MESH,
        )

    def multiply(i, odd):
        slot = lax.rem(i, RING)
        load(i, rights, 0).wait()
        pair = i // 2
        left = lefts[pair - (pair + 1024 - run) // 1024 * (pair - run)]
        right = right_buf[lax.rem(i, 3)]
        start_load(i + 2)

        @pl.when(i >= RING)
        def _():
            first(i - RING, odd).wait_send()

        part = lax.dot_general(left, right, (((1,), (1,)), ((), ())), preferred_element_type=f32)
        own[slot, :w] = part[:w]
        if odd:
            own[slot, w:] = part[2 * w : 3 * w]
            s1[slot, :w] = part[w : 2 * w].astype(b16)
            s1[slot, w:] = part[3 * w :].astype(b16)
        else:
            own[slot, w:] = part[w : 2 * w]
            s1[slot] = part[2 * w :].astype(b16)
        first(i, odd).start()

    def pass_on(i, odd):
        slot = lax.rem(i, RING)
        first(i, odd).wait_recv()

        @pl.when(i >= RING)
        def _():
            second(i - RING, odd).wait_send()

        s2[slot] = (own[slot, w:] + r1[i, w:].astype(f32)).astype(b16)
        second(i, odd).start()

    def keep(i, odd):
        slot = lax.rem(i, RING)
        second(i, odd).wait_recv()
        part = own[slot, :w] + r1[i, :w].astype(f32) + r2[i].astype(f32)
        if n_h == 1:
            out[i] = part.astype(b16)
            return

        @pl.when(i >= RING)
        def _():
            for d in range(1, n_h):
                third(i - RING, d).wait_send()

        s3[slot] = part.astype(b16)
        for d in range(1, n_h):
            third(i, d).start()

    def finish(i, odd):
        if n_h == 1:
            return
        total = s3[lax.rem(i, RING), pl.ds(h * rows, rows)].astype(f32)
        for d in range(1, n_h):
            third(i, d).wait_recv()
            total = total + r3[i, d - 1].astype(f32)
        out[i] = total

    start_load(jnp.int32(0))
    start_load(jnp.int32(1))
    pairs = (n + 1) // 2

    def step(p, carry):
        for lag, stage in enumerate((multiply, pass_on, keep, finish)):
            for odd in (0, 1):
                i = 2 * (p - lag) + odd

                @pl.when((i >= 0) & (i < n))
                def _(stage=stage, i=i, odd=odd):
                    stage(i, odd)

        return carry

    lax.fori_loop(0, pairs + 3, step, 0)
    for i in range(max(n - RING, 0), n):
        first(i, i % 2).wait_send()
        second(i, i % 2).wait_send()
        for d in range(1, n_h):
            third(i, d).wait_send()


def scatter_all(lefts, rights, more, collective_id):
    n_first, m, cells = rights.shape
    n = n_first + more.shape[0]
    w = lefts.shape[1] // 4
    n_h = lax.axis_size("h")
    rows = w // n_h
    inner_h = n_h if rows % 16 == 0 else 1
    dma, bf16 = pltpu.SemaphoreType.DMA, jnp.bfloat16
    vmem, hbm = pl.BlockSpec(memory_space=pltpu.VMEM), pl.BlockSpec(memory_space=pl.ANY)
    others = max(inner_h - 1, 1)
    part = pl.pallas_call(
        functools.partial(scatter_kernel, inner_h, n, n_first, lefts.shape[0] - 1),
        out_shape=(
            jax.ShapeDtypeStruct((n, rows, m), jnp.float32)
            if inner_h > 1
            else jax.ShapeDtypeStruct((n, w, m), bf16)
        ),
        in_specs=[vmem, hbm, hbm],
        out_specs=vmem,
        scratch_shapes=[
            pltpu.VMEM((3, m, cells), bf16),
            pltpu.VMEM((RING, 2 * w, m), jnp.float32),
            pltpu.VMEM((RING, 2 * w, m), bf16),
            pltpu.VMEM((n, 2 * w, m), bf16),
            pltpu.VMEM((RING, w, m), bf16),
            pltpu.VMEM((n, w, m), bf16),
            pltpu.VMEM((RING, w, m), bf16),
            pltpu.VMEM((n, others, w // inner_h, m), bf16),
            dma((3,)),
            dma((RING,)),
            dma((n,)),
            dma((RING,)),
            dma((n,)),
            dma((RING, others)),
            dma((n, others)),
        ],
        compiler_params=pltpu.CompilerParams(
            collective_id=collective_id, has_side_effects=True, vmem_limit_bytes=60 * 2**20
        ),
    )(lefts, rights, more)
    if inner_h > 1:
        return part
    return lax.psum_scatter(part, "h", scatter_dimension=1, tiled=True).astype(jnp.float32)


def gather_dec(own):
    by_x, by_y = swap(own, "x"), swap(own, "y")
    middle = own.shape[1] // 256 * 128
    far = [swap(by_x[:, :middle], "y"), swap(by_y[:, middle:], "x")]
    four = [own, by_y, by_x, jnp.concatenate(far, axis=1)]
    return jnp.concatenate(four + [swap(part, "c") for part in four], axis=0)


def with_other_core(value):
    return jnp.concatenate([value, swap(value, "c")], axis=0)


def own_half(left):
    half = left.shape[1] // 2
    return jnp.concatenate([left[:, :half], swap(left[:, half:], "c")], axis=0)


def sum_over_h(part):
    n_h = lax.axis_size("h")
    rows = part.shape[0] // n_h
    at = lax.axis_index("h")
    total = lax.dynamic_slice_in_dim(part, at * rows, rows, 0).astype(jnp.float32)
    for step in range(1, n_h):
        send = lax.dynamic_slice_in_dim(part, lax.rem(at + step, n_h) * rows, rows, 0)
        ring = [(i, (i + step) % n_h) for i in range(n_h)]
        total = total + lax.ppermute(send, "h", ring).astype(jnp.float32)
    return total


def scatter(left, right, first, second):
    w = left.shape[1] // 4
    near, by_y, by_x, far = (left[:, k * w : (k + 1) * w] for k in range(4))
    one, two = (by_x, by_y) if first == "x" else (by_y, by_x)
    got_far = swap(contract_rows(far, right).astype(jnp.bfloat16), first).astype(jnp.float32)
    got_one = swap(contract_rows(one, right).astype(jnp.bfloat16), first).astype(jnp.float32)
    got_two = swap((contract_rows(two, right) + got_far).astype(jnp.bfloat16), second)
    part = contract_rows(near, right) + got_one + got_two.astype(jnp.float32)
    return sum_over_h(part.astype(jnp.bfloat16))


def scatter_columns(left, right):
    cut = -(-right.shape[1] // 256) * 128
    return jnp.concatenate(
        [scatter(left, right[:, :cut], "x", "y"), scatter(left, right[:, cut:], "y", "x")], axis=1
    ).T


def scatter_vectors(part):
    half = part.shape[0] // 2
    part = part[:half] + swap(part[half:].astype(jnp.bfloat16), "c").astype(jnp.float32)
    part = part[: half // 2] + swap(part[half // 2 :].astype(jnp.bfloat16), "x").astype(jnp.float32)
    half = half // 2
    part = part[: half // 2] + swap(part[half // 2 :].astype(jnp.bfloat16), "y").astype(jnp.float32)
    return sum_over_h(part.astype(jnp.bfloat16))


def gather_group(mine):
    at_y, at_c = lax.axis_index("y"), lax.axis_index("c")
    pair = jnp.stack([mine, swap(mine, "y")])
    both = jnp.stack([pair, swap(pair, "c")])
    order = [
        lax.dynamic_index_in_dim(
            lax.dynamic_index_in_dim(both, at_c ^ c, 0, False), at_y ^ y, 0, False
        )
        for y in range(2)
        for c in range(2)
    ]
    return jnp.concatenate(order, axis=0)


def scatter_group(rows_all):
    at_y, at_c = lax.axis_index("y"), lax.axis_index("c")
    part = rows_all.astype(jnp.bfloat16).reshape((2, 2, rows_all.shape[0] // 4, -1))
    keep = lax.dynamic_index_in_dim(part, at_c, 1, False).astype(jnp.float32)
    send = lax.dynamic_index_in_dim(part, 1 - at_c, 1, False)
    part = (keep + swap(send, "c").astype(jnp.float32)).astype(jnp.bfloat16)
    keep = lax.dynamic_index_in_dim(part, at_y, 0, False).astype(jnp.float32)
    send = lax.dynamic_index_in_dim(part, 1 - at_y, 0, False)
    return keep + swap(send, "y").astype(jnp.float32)


def in_chunks(right):
    n = -(-right.shape[0] // 512) * 512
    return jnp.pad(right, ((0, n - right.shape[0]), (0, 0))).reshape(n // 512, 512, -1)


def left_of(left, pieces):
    left = own_half(relative(left, 1)).T
    n_h = lax.axis_size("h")
    left = left.reshape(4, n_h, pieces, -1, left.shape[1])
    return left.transpose(2, 0, 1, 3, 4).reshape(pieces, -1, left.shape[-1])


def right_of(right):
    return in_chunks(with_other_core(right).T)


def on_device(
    counts,
    library,
    coords,
    lengths,
    cotangent,
    w_enc,
    w_qkv,
    w_out,
    gain_one,
    shift_one,
    w_up,
    w_down,
    gain_two,
    shift_two,
    w_dec,
):
    rows = counts.shape[0]
    width = w_qkv.shape[1] // 3
    heads = HEADS
    head_width = width // heads
    att_scale = head_width ** (-0.5)
    group_size = 4
    slots = rows * group_size
    scale = 10000.0 / library
    genes = counts.shape[1]
    padded = -(-genes // 128) * 128
    counts_f = counts.astype(jnp.float32)
    xb = jnp.pad(counts.T, ((0, padded - genes), (0, 0))).astype(jnp.float32)
    xb = jnp.log1p(xb * scale[None, :]).astype(jnp.bfloat16)
    xb_both = in_chunks(jnp.concatenate([xb, swap(xb, "c")], axis=1))
    pe = by_owner(positions(coords, width), 1)
    ends = jnp.cumsum(lengths[0])
    place = jnp.arange(slots, dtype=jnp.int32)
    seg_all = jnp.sum((place[:, None] >= ends[None, :]).astype(jnp.int32), axis=1)
    seg_mine = lax.dynamic_slice_in_dim(seg_all, (lax.axis_index("y") * 2 + lax.axis_index("c")) * rows, rows)
    same = (seg_mine[:, None] == seg_all[None, :])[None]
    vectors = jnp.stack([gain_one, shift_one, gain_two, shift_two], axis=1)
    vectors = jnp.pad(vectors, ((0, 0), (0, 124)))
    pad = ((0, 0), (0, padded - genes))
    quarter = -(-padded // 512) * 128
    gene_cuts = [0, quarter, 2 * quarter, 3 * quarter, padded]
    shards = [
        jnp.pad(w_enc.T, pad),
        jnp.concatenate([w_qkv, vectors], axis=1),
        by_owner(w_out, 1),
        by_owner(w_up, 1),
        by_owner(w_down, 1),
        jnp.pad(w_dec.T, pad),
    ]
    cuts = [gene_cuts, [0, width // 2 * 3, 3 * width + 128], [0, width]]
    cuts += [[0, 2 * width, 4 * width], [0, width // 2, width], [0, padded]]
    order = [(0, 0), (0, 1), (0, 2), (0, 3), (1, 0), (1, 1), (2, 0), (3, 0), (3, 1), (4, 0), (4, 1), (5, 0)]
    gathered = gather_all(shards, 5, cuts, order, 0)
    enc_all, qkv_all, out_all, up_all, down_all = (
        w.reshape(-1, w.shape[-1]) for w in gathered[:5]
    )
    dec_all = gather_dec(gathered[5])
    vectors = qkv_all[:, 3 * width :].astype(jnp.float32).T
    qkv_all = qkv_all[:, : 3 * width]
    g1f, b1f, g2f, b2f = vectors[0], vectors[1], vectors[2], vectors[3]
    h0 = contract_cols(xb.T, enc_all) + pe
    a1 = layer_norm(h0, g1f, b1f).astype(jnp.bfloat16)
    qkv = matmul(a1, qkv_all).astype(jnp.bfloat16)
    query = qkv[:, :width].reshape(rows, heads, head_width)
    kv_all = gather_group(qkv[:, width:])
    keys = kv_all[:, :width].reshape(slots, heads, head_width)
    values = kv_all[:, width:].reshape(slots, heads, head_width)

    def scores_of():
        raw = (
            jnp.einsum("qhd,khd->hqk", query, keys, preferred_element_type=jnp.float32) * att_scale
        )
        return jnp.where(same, raw, -1000000000.0)

    scores = scores_of()
    top = jnp.max(scores, axis=-1, keepdims=True)
    expo = jnp.exp(scores - top)
    total = jnp.sum(expo, axis=-1, keepdims=True)
    log_total = top + jnp.log(total)
    probs_b = (expo / total).astype(jnp.bfloat16)
    attended = jnp.einsum("hqk,khd->qhd", probs_b, values, preferred_element_type=jnp.float32)
    attended_b = attended.reshape(rows, width).astype(jnp.bfloat16)
    attended_b = by_owner(attended_b, 1)
    h1 = h0 + matmul(attended_b, out_all)
    a2 = layer_norm(h1, g2f, b2f).astype(jnp.bfloat16)
    hidden = matmul(a2, up_all)
    act = jax.nn.gelu(hidden, approximate=False).astype(jnp.bfloat16)
    h2 = h1 + matmul(act, down_all)
    hb_rel = relative(h2.astype(jnp.bfloat16), 1)
    logits = matmul(hb_rel, dec_all).astype(jnp.bfloat16)[:, :genes]
    grad_dec = scatter_columns(own_half(hb_rel), with_other_core(cotangent))
    dh2 = relative(contract_cols(jnp.pad(cotangent, pad), dec_all), 1)
    dfb = dh2.astype(jnp.bfloat16)
    d_act = contract_cols(dfb, down_all)
    slope = jax.vjp(lambda v: jax.nn.gelu(v, approximate=False), hidden)[1](d_act)[0]
    d_hidden = slope.astype(jnp.bfloat16)
    da2 = contract_cols(d_hidden, up_all)
    norm_pull = jax.vjp(layer_norm, h1, g2f, b2f)[1]
    dh1_norm, grad_gain_two, grad_shift_two = norm_pull(da2)
    dh1 = dh2 + dh1_norm
    dab = dh1.astype(jnp.bfloat16)
    d_attended = contract_cols(dab, out_all).astype(jnp.bfloat16)
    d_attended = from_owner(d_attended, 1).reshape(rows, heads, head_width)
    probs = jnp.exp(scores_of() - log_total)
    probs_b = probs.astype(jnp.bfloat16)
    d_probs = jnp.einsum("qhd,khd->hqk", d_attended, values, preferred_element_type=jnp.float32)
    inner = jnp.sum(probs * d_probs, axis=-1, keepdims=True)
    d_scores = (probs * (d_probs - inner)).astype(jnp.bfloat16)
    d_query = (
        jnp.einsum("hqk,khd->qhd", d_scores, keys, preferred_element_type=jnp.float32) * att_scale
    )
    d_keys = (
        jnp.einsum("hqk,qhd->khd", d_scores, query, preferred_element_type=jnp.float32) * att_scale
    )
    d_values = jnp.einsum("hqk,qhd->khd", probs_b, d_attended, preferred_element_type=jnp.float32)
    d_kv = jnp.concatenate([d_keys.reshape(slots, width), d_values.reshape(slots, width)], axis=1)
    d_kv = scatter_group(d_kv)
    d_qkv = jnp.concatenate([d_query.reshape(rows, width), d_kv], axis=1).astype(jnp.bfloat16)
    da1 = contract_cols(d_qkv, qkv_all)
    first_pull = jax.vjp(layer_norm, h0, g1f, b1f)[1]
    dh0_norm, grad_gain_one, grad_shift_one = first_pull(da1)
    grad_vectors = jnp.stack([grad_gain_one, grad_shift_one, grad_gain_two, grad_shift_two], axis=1)
    grad_vectors = scatter_vectors(relative(grad_vectors, 0))
    grad_gain_one, grad_shift_one, grad_gain_two, grad_shift_two = (
        grad_vectors[:, k] for k in range(4)
    )
    dh0b = (dh1 + dh0_norm).astype(jnp.bfloat16)

    lefts = [left_of(a1, 1)] * 3 + [left_of(attended_b, 1)] + [left_of(a2, 1)] * 4
    lefts += [left_of(act, act.shape[1] // width), left_of(dh0b, 1)]
    rights = [right_of(d_qkv), right_of(dab), right_of(d_hidden)] + [right_of(dfb)] * 4
    grads = scatter_all(
        jnp.concatenate(lefts, axis=0), jnp.concatenate(rights, axis=0), xb_both, 1
    )
    own_rows, m = grads.shape[1:]
    ends = [0]
    for columns in (3 * width, width, 4 * width, 4 * width):
        ends.append(ends[-1] + columns // m)
    grad_qkv, grad_out, grad_up, grad_down, grad_enc = (
        grads[low:high] for low, high in zip(ends, ends[1:] + [grads.shape[0]])
    )
    grad_qkv, grad_out, grad_up, grad_enc = (
        g.transpose(1, 0, 2).reshape(own_rows, -1) for g in (grad_qkv, grad_out, grad_up, grad_enc)
    )
    grad_down = grad_down.reshape(4, -1, own_rows, m).transpose(0, 2, 1, 3).reshape(4 * own_rows, -1)
    grad_out, grad_up, grad_down = (from_owner(g, 1) for g in (grad_out, grad_up, grad_down))
    grad_enc = grad_enc[:, :genes].T
    d_xb = matmul(dh0b, enc_all)[:, :genes]
    counts_grad = d_xb * scale[:, None] / (1.0 + counts_f * scale[:, None])
    return (
        logits,
        counts_grad,
        grad_enc,
        grad_qkv,
        grad_out,
        grad_gain_one,
        grad_shift_one,
        grad_up,
        grad_down,
        grad_gain_two,
        grad_shift_two,
        grad_dec,
    )


ALL = ("h", "x", "y", "c")


def solution(mesh):
    n_dp, n_fsdp = mesh.shape["dp"], mesh.shape["fsdp"]
    mesh = Mesh(mesh.devices.reshape((n_dp // 2, 2, 2, n_fsdp // 2)), ALL)
    placed = (
        P(ALL, None),
        P(ALL),
        P(None, ALL),
        P(("h", "x"), None),
        P(ALL, None),
        P(None, ALL),
        P(ALL, None),
        P(ALL, None),
        P(ALL),
        P(ALL),
        P(ALL, None),
        P(ALL, None),
        P(ALL),
        P(ALL),
        P(None, ALL),
    )
    return jax.shard_map(
        on_device,
        mesh=mesh,
        in_specs=placed,
        out_specs=(
            P(ALL, None),
            P(ALL, None),
            P(None, ALL),
            P(ALL, None),
            P(ALL, None),
            P(ALL),
            P(ALL),
            P(ALL, None),
            P(ALL, None),
            P(ALL),
            P(ALL),
            P(None, ALL),
        ),
        check_vma=False,
    )
```

```python
import functools
import math

import jax
import jax.numpy as jnp
from jax import lax
from jax.experimental import pallas as pl
from jax.experimental.pallas import tpu as pltpu
from jax.sharding import Mesh
from jax.sharding import PartitionSpec as P

HEADS = 16
MESH = pl.DeviceIdType.MESH
RING = 8
CHUNK = 256


eps = 1e-05


def layer_norm(value, gain, shift):
    mean = jnp.mean(value, axis=1, keepdims=True)
    centred = value - mean
    variance = jnp.mean(centred * centred, axis=1, keepdims=True)
    return centred * lax.rsqrt(variance + eps) * gain + shift


def positions(coords, width):
    quarter = width // 4
    freqs = 0.05 * jnp.exp(-jnp.arange(quarter, dtype=jnp.float32) * (math.log(10000.0) / quarter))
    along_x = coords[0].astype(jnp.float32)[:, None] * freqs[None, :]
    along_y = coords[1].astype(jnp.float32)[:, None] * freqs[None, :]
    return jnp.concatenate(
        [jnp.sin(along_x), jnp.cos(along_x), jnp.sin(along_y), jnp.cos(along_y)], axis=1
    )


def contract_rows(left, right):
    return lax.dot_general(
        left, right, (((0,), (0,)), ((), ())), preferred_element_type=jnp.float32
    )


def contract_cols(left, right):
    return lax.dot_general(
        left, right, (((1,), (1,)), ((), ())), preferred_element_type=jnp.float32
    )


def matmul(left, right):
    return jnp.dot(left, right, preferred_element_type=jnp.float32)


def swap(value, axis):
    return lax.ppermute(value, axis, [(0, 1), (1, 0)])


def by_owner(value, axis):
    n_h = lax.axis_size("h")
    at = value.shape
    block = at[axis] // (8 * n_h)
    split = value.reshape(at[:axis] + (n_h, 2, 2, 2, block) + at[axis + 1 :])
    order = list(range(axis)) + [axis + 3, axis + 1, axis + 2, axis, axis + 4]
    order += list(range(axis + 5, split.ndim))
    return split.transpose(order).reshape(at)


def from_owner(value, axis):
    n_h = lax.axis_size("h")
    at = value.shape
    block = at[axis] // (8 * n_h)
    split = value.reshape(at[:axis] + (2, 2, 2, n_h, block) + at[axis + 1 :])
    order = list(range(axis)) + [axis + 3, axis + 1, axis + 2, axis, axis + 4]
    order += list(range(axis + 5, split.ndim))
    return split.transpose(order).reshape(at)


def relative(value, axis):
    eighth = value.shape[axis] // 8
    mine = lax.axis_index("c") * 4 + lax.axis_index("x") * 2 + lax.axis_index("y")
    parts = [
        lax.dynamic_slice_in_dim(value, (mine ^ part) * eighth, eighth, axis) for part in range(8)
    ]
    return jnp.concatenate(parts, axis=axis)


def greet(peers):
    barrier = pltpu.get_barrier_semaphore()
    for peer in peers:
        pl.semaphore_signal(barrier, inc=1, device_id=peer, device_id_type=MESH)
    pl.semaphore_wait(barrier, len(peers))


def gather_kernel(n_h, jobs, n_arrays, n_full, *refs):
    shards, wholes = refs[:n_arrays], refs[n_arrays : 2 * n_arrays]
    own_sem, h_send, h_recv, send, recv = refs[2 * n_arrays :]
    h, x, y, c = (lax.axis_index(name) for name in ("h", "x", "y", "c"))
    h = 0 if n_h == 1 else h
    to_x, to_y, to_c = {"x": 1 - x}, {"y": 1 - y}, {"c": 1 - c}
    greet([{"h": lax.rem(h + d, n_h)} for d in range(1, n_h)] + [to_x, to_y, to_c])

    def rows_of(job, at):
        array, low, high, _ = job
        rows = shards[array].shape[0]
        place = (pl.ds(at * rows, rows), pl.ds(low, high - low))
        return wholes[array].at[(c, x, y, *place) if array < n_full else place]

    def h_copy(j, d):
        array, low, high, _ = jobs[j]
        return pltpu.make_async_remote_copy(
            src_ref=shards[array].at[:, pl.ds(low, high - low)],
            dst_ref=rows_of(jobs[j], h),
            send_sem=h_send.at[j, d - 1],
            recv_sem=h_recv.at[j, d - 1],
            device_id={"h": lax.rem(h + d, n_h)},
            device_id_type=MESH,
        )

    def own_copy(j):
        array, low, high, _ = jobs[j]
        return pltpu.make_async_copy(
            shards[array].at[:, pl.ds(low, high - low)], rows_of(jobs[j], h), own_sem.at[j]
        )

    def block_copy(j, k, block, to, columns):
        view = wholes[jobs[j][0]].at[(*block, slice(None), pl.ds(columns[0], columns[1] - columns[0]))]
        return pltpu.make_async_remote_copy(
            src_ref=view,
            dst_ref=view,
            send_sem=send.at[j, k],
            recv_sem=recv.at[j, k],
            device_id=to,
            device_id_type=MESH,
        )

    own, by_x, by_y, far = (c, x, y), (c, 1 - x, y), (c, x, 1 - y), (c, 1 - x, 1 - y)

    def copy(j, k):
        _, low, high, middle = jobs[j]
        block, to, columns = [
            (own, to_x, (low, high)),
            (own, to_y, (low, high)),
            (own, to_c, (low, high)),
            (by_x, to_y, (low, middle)),
            (by_y, to_x, (middle, high)),
            (by_x, to_c, (low, high)),
            (by_y, to_c, (low, high)),
            (far, to_c, (low, high)),
        ][k]
        return block_copy(j, k, block, to, columns)

    def start_h(j):
        own_copy(j).start()
        for d in range(1, n_h):
            h_copy(j, d).start()

    n = sum(array < n_full for array, *_ in jobs)
    ahead = 2
    for j in range(ahead):
        start_h(j)
    for step in range(n + 2):
        if step < n:
            own_copy(step).wait()
            for d in range(1, n_h):
                h_copy(step, d).wait_recv()
            for k in (0, 1, 2):
                copy(step, k).start()
            if step + ahead < len(jobs):
                start_h(step + ahead)
        if 0 <= step - 1 < n:
            for k in (0, 1):
                copy(step - 1, k).wait_recv()
            for k in (3, 4, 5, 6):
                copy(step - 1, k).start()
        if 0 <= step - 2 < n:
            for k in (3, 4):
                copy(step - 2, k).wait_recv()
            copy(step - 2, 7).start()
    for j in range(n + ahead, len(jobs)):
        start_h(j)
    for j in range(n, len(jobs)):
        own_copy(j).wait()
        for d in range(1, n_h):
            h_copy(j, d).wait_recv()
    for j in range(len(jobs)):
        for d in range(1, n_h):
            h_copy(j, d).wait_send()
    for j in range(n):
        for k in range(8):
            copy(j, k).wait_send()
        for k in (2, 5, 6, 7):
            copy(j, k).wait_recv()


def gather_all(shards, n_full, cuts, order, collective_id):
    n_h = lax.axis_size("h")
    if any(shard.shape[0] % 16 for shard in shards):
        shards = [lax.all_gather(s, "h", axis=0, tiled=True) for s in shards]
        n_h = 1
    jobs = []
    for array, piece in order:
        low, high = cuts[array][piece], cuts[array][piece + 1]
        jobs.append((array, low, high, low + (high - low) // 256 * 128))
    n, others, dma = len(jobs), max(n_h - 1, 1), pltpu.SemaphoreType.DMA
    shapes = [(n_h * s.shape[0], s.shape[1]) for s in shards]
    return pl.pallas_call(
        functools.partial(gather_kernel, n_h, jobs, len(shards), n_full),
        out_shape=[
            jax.ShapeDtypeStruct((2, 2, 2) + shape if k < n_full else shape, jnp.bfloat16)
            for k, shape in enumerate(shapes)
        ],
        in_specs=[pl.BlockSpec(memory_space=pl.ANY)] * len(shards),
        out_specs=[pl.BlockSpec(memory_space=pl.ANY)] * len(shards),
        scratch_shapes=[dma((n,)), dma((n, others)), dma((n, others)), dma((n, 8)), dma((n, 8))],
        compiler_params=pltpu.CompilerParams(collective_id=collective_id, has_side_effects=True),
    )(*shards)


def scatter_kernel(n_h, sections, run, n_weights, with_sum, *refs):
    lefts, vector = refs[:2]
    n_sections = len(sections)
    rights = refs[2 : 2 + 2 * n_sections]
    weights = refs[2 + 2 * n_sections : 2 + 2 * n_sections + n_weights]
    rest = refs[2 + 2 * n_sections + n_weights :]
    out, product = rest[:2]
    total_out = rest[2] if with_sum else None
    (right_buf, weight_buf, product_buf, own, s1, r1, s2, r2, s3, r3, load_sem, weight_sem, product_sem,
     send1, recv1, send2, recv2, send3, recv3) = rest[3 if with_sum else 2 :]
    h, x, y = (lax.axis_index(name) for name in ("h", "x", "y"))
    to_x, to_y = {"x": 1 - x}, {"y": 1 - y}
    w = s3.shape[1]
    rows = w // n_h
    f32, b16 = jnp.float32, jnp.bfloat16
    cells = vector.shape[0]
    starts = [sum(sections[:k]) for k in range(n_sections)]
    n = sum(sections)
    begin = starts[-1]
    greet([{"h": lax.rem(h + d, n_h)} for d in range(1, n_h)] + [to_x, to_y])

    def chunk_of(k):
        return pl.ds(pl.multiple_of(k * CHUNK, CHUNK), CHUNK)

    def loads(i, section, k):
        slot = lax.rem(i, 3)
        return [
            pltpu.make_async_copy(
                rights[2 * section + half].at[chunk_of(k)],
                right_buf.at[slot, :, pl.ds(half * cells, cells)],
                load_sem.at[slot, half],
            )
            for half in (0, 1)
        ]

    def weight_loads(k):
        slot = lax.rem(k, 3)
        size = weights[0].shape[0]
        return [
            pltpu.make_async_copy(
                weight.at[:, chunk_of(k)],
                weight_buf.at[slot, pl.ds(part * size, size)],
                weight_sem.at[slot, part],
            )
            for part, weight in enumerate(weights)
        ]

    def start_loads(i):
        for section, (start, count) in enumerate(zip(starts, sections)):

            @pl.when((i >= start) & (i < start + count))
            def _(section=section, start=start):
                for copy in loads(i, section, i - start):
                    copy.start()
                if section == n_sections - 1:
                    for copy in weight_loads(i - start):
                        copy.start()

    def product_store(k):
        slot = lax.rem(k, 2)
        return pltpu.make_async_copy(product_buf.at[slot], product.at[chunk_of(k)], product_sem.at[slot])

    def hop(i, source, target, send_sem, recv_sem, to):
        slot = lax.rem(i, RING)
        return pltpu.make_async_remote_copy(
            src_ref=source.at[slot], dst_ref=target.at[i], send_sem=send_sem.at[slot],
            recv_sem=recv_sem.at[i], device_id=to, device_id_type=MESH,
        )

    def first(i, odd):
        return hop(i, s1, r1, send1, recv1, to_y if odd else to_x)

    def second(i, odd):
        return hop(i, s2, r2, send2, recv2, to_x if odd else to_y)

    def third(i, d):
        to = lax.rem(h + d, n_h)
        slot = lax.rem(i, RING)
        return pltpu.make_async_remote_copy(
            src_ref=s3.at[slot, pl.ds(to * rows, rows)], dst_ref=r3.at[i, d - 1],
            send_sem=send3.at[slot, d - 1], recv_sem=recv3.at[i, d - 1],
            device_id={"h": to}, device_id_type=MESH,
        )

    def multiply(i, odd):
        slot = lax.rem(i, RING)
        for copy in loads(i, 0, 0):
            copy.wait()
        two = i // 4
        left = lefts[two - (two + 1024 - run) // 1024 * (two - run)]
        right = right_buf.at[lax.rem(i, 3)]

        @pl.when(i >= RING)
        def _():
            first(i - RING, odd).wait_send()

        part = lax.dot_general(left, right[...], (((1,), (1,)), ((), ())), preferred_element_type=f32)
        own[slot, :w] = part[:w]
        if odd:
            own[slot, w:] = part[2 * w : 3 * w]
            s1[slot, :w] = part[w : 2 * w].astype(b16)
            s1[slot, w:] = part[3 * w :].astype(b16)
        else:
            own[slot, w:] = part[w : 2 * w]
            s1[slot] = part[2 * w :].astype(b16)
        first(i, odd).start()

        def beside(k):
            for copy in weight_loads(k):
                copy.wait()
            weight = weight_buf[lax.rem(k, 3)]

            @pl.when(k >= 2)
            def _():
                product_store(k - 2).wait()

            value = jnp.dot(vector[...], weight, preferred_element_type=f32)
            product_buf[lax.rem(k, 2)] = value.T.astype(product_buf.dtype)
            product_store(k).start()
            if with_sum:
                term = jnp.dot(weight, right[:, :cells], preferred_element_type=f32)

                @pl.when(k == 0)
                def _():
                    total_out[...] = term

                @pl.when(k > 0)
                def _():
                    total_out[...] += term

        if begin == 0:
            beside(i)
        else:

            @pl.when(i >= begin)
            def _():
                beside(i - begin)

        start_loads(i + 2)

    def pass_on(i, odd):
        slot = lax.rem(i, RING)
        first(i, odd).wait_recv()

        @pl.when(i >= RING)
        def _():
            second(i - RING, odd).wait_send()

        s2[slot] = (own[slot, w:] + r1[i, w:].astype(f32)).astype(b16)
        second(i, odd).start()

    def keep(i, odd):
        slot = lax.rem(i, RING)
        second(i, odd).wait_recv()
        part = own[slot, :w] + r1[i, :w].astype(f32) + r2[i].astype(f32)
        if n_h == 1:
            out[i] = part.astype(b16)
            return

        @pl.when(i >= RING)
        def _():
            for d in range(1, n_h):
                third(i - RING, d).wait_send()

        s3[slot] = part.astype(b16)
        for d in range(1, n_h):
            third(i, d).start()

    def finish(i, odd):
        if n_h == 1:
            return
        total = s3[lax.rem(i, RING), pl.ds(h * rows, rows)].astype(f32)
        for d in range(1, n_h):
            third(i, d).wait_recv()
            total = total + r3[i, d - 1].astype(f32)
        out[i] = total

    start_loads(jnp.int32(0))
    start_loads(jnp.int32(1))
    pairs = (n + 1) // 2

    def step(p, carry):
        for lag, stage in enumerate((multiply, pass_on, keep, finish)):
            for odd in (0, 1):
                i = 2 * (p - lag) + odd

                @pl.when((i >= 0) & (i < n))
                def _(stage=stage, i=i, odd=odd):
                    stage(i, odd)

        return carry

    lax.fori_loop(0, pairs + 3, step, 0)
    for i in range(max(n - RING, 0), n):
        first(i, i % 2).wait_send()
        second(i, i % 2).wait_send()
        for d in range(1, n_h):
            third(i, d).wait_send()
    for k in range(max(sections[-1] - 2, 0), sections[-1]):
        product_store(k).wait()


def scatter_all(lefts, rights, vector, weights, product_type, with_sum, collective_id):
    sections = [own.shape[0] // CHUNK for own, _ in rights]
    n, cells = sum(sections), vector.shape[0]
    features = vector.shape[1]
    w = lefts.shape[1] // 4
    n_h = lax.axis_size("h")
    rows = w // n_h
    inner_h = n_h if rows % 16 == 0 else 1
    dma, bf16, f32 = pltpu.SemaphoreType.DMA, jnp.bfloat16, jnp.float32
    vmem, hbm = pl.BlockSpec(memory_space=pltpu.VMEM), pl.BlockSpec(memory_space=pl.ANY)
    others = max(inner_h - 1, 1)
    part_shape = jax.ShapeDtypeStruct((n, rows, CHUNK), f32)
    if inner_h == 1:
        part_shape = jax.ShapeDtypeStruct((n, w, CHUNK), bf16)
    out_shape = [part_shape, jax.ShapeDtypeStruct((sections[-1] * CHUNK, cells), product_type)]
    out_specs = [vmem, hbm]
    if with_sum:
        out_shape.append(jax.ShapeDtypeStruct((features, cells), f32))
        out_specs.append(vmem)
    part, *more = pl.pallas_call(
        functools.partial(
            scatter_kernel, inner_h, sections, lefts.shape[0] - 1, len(weights), with_sum
        ),
        out_shape=out_shape,
        in_specs=[vmem, vmem] + [hbm] * (2 * len(rights) + len(weights)),
        out_specs=out_specs,
        scratch_shapes=[
            pltpu.VMEM((3, CHUNK, 2 * cells), bf16),
            pltpu.VMEM((3, features, CHUNK), bf16),
            pltpu.VMEM((2, CHUNK, cells), product_type),
            pltpu.VMEM((RING, 2 * w, CHUNK), f32),
            pltpu.VMEM((RING, 2 * w, CHUNK), bf16),
            pltpu.VMEM((n, 2 * w, CHUNK), bf16),
            pltpu.VMEM((RING, w, CHUNK), bf16),
            pltpu.VMEM((n, w, CHUNK), bf16),
            pltpu.VMEM((RING, w, CHUNK), bf16),
            pltpu.VMEM((n, others, w // inner_h, CHUNK), bf16),
            dma((3, 2)),
            dma((3, len(weights))),
            dma((2,)),
            dma((RING,)),
            dma((n,)),
            dma((RING,)),
            dma((n,)),
            dma((RING, others)),
            dma((n, others)),
        ],
        compiler_params=pltpu.CompilerParams(
            collective_id=collective_id, has_side_effects=True, vmem_limit_bytes=60 * 2**20
        ),
    )(lefts, vector, *(half for pair in rights for half in pair), *weights)
    if inner_h == 1:
        part = lax.psum_scatter(part, "h", scatter_dimension=1, tiled=True).astype(f32)
    return part, *more


def gather_dec(own, after):
    by_x = swap(own, "x")
    by_y = swap(lax.optimization_barrier((own, after))[0], "y")
    middle = own.shape[1] // 256 * 128
    far = [swap(by_x[:, :middle], "y"), swap(by_y[:, middle:], "x")]
    four = [own, by_y, by_x, jnp.concatenate(far, axis=1)]
    return four + [swap(part, "c") for part in four]


def own_half(left):
    half = left.shape[1] // 2
    return jnp.concatenate([left[:, :half], swap(left[:, half:], "c")], axis=0)


def sum_over_h(part):
    n_h = lax.axis_size("h")
    rows = part.shape[0] // n_h
    at = lax.axis_index("h")
    total = lax.dynamic_slice_in_dim(part, at * rows, rows, 0).astype(jnp.float32)
    for step in range(1, n_h):
        send = lax.dynamic_slice_in_dim(part, lax.rem(at + step, n_h) * rows, rows, 0)
        ring = [(i, (i + step) % n_h) for i in range(n_h)]
        total = total + lax.ppermute(send, "h", ring).astype(jnp.float32)
    return total


def scatter_vectors(part):
    half = part.shape[0] // 2
    part = part[:half] + swap(part[half:].astype(jnp.bfloat16), "c").astype(jnp.float32)
    part = part[: half // 2] + swap(part[half // 2 :].astype(jnp.bfloat16), "x").astype(jnp.float32)
    half = half // 2
    part = part[: half // 2] + swap(part[half // 2 :].astype(jnp.bfloat16), "y").astype(jnp.float32)
    return sum_over_h(part.astype(jnp.bfloat16))


def gather_group(mine):
    at_y, at_c = lax.axis_index("y"), lax.axis_index("c")
    by_y = swap(mine, "y")
    pair = jnp.stack([mine, by_y])
    both = jnp.stack([pair, swap(pair, "c")])
    order = [
        lax.dynamic_index_in_dim(
            lax.dynamic_index_in_dim(both, at_c ^ c, 0, False), at_y ^ y, 0, False
        )
        for y in range(2)
        for c in range(2)
    ]
    return jnp.concatenate(order, axis=0), by_y


def scatter_group(rows_all):
    at_y, at_c = lax.axis_index("y"), lax.axis_index("c")
    part = rows_all.astype(jnp.bfloat16).reshape((2, 2, rows_all.shape[0] // 4, -1))
    keep = lax.dynamic_index_in_dim(part, at_c, 1, False).astype(jnp.float32)
    send = lax.dynamic_index_in_dim(part, 1 - at_c, 1, False)
    part = (keep + swap(send, "c").astype(jnp.float32)).astype(jnp.bfloat16)
    keep = lax.dynamic_index_in_dim(part, at_y, 0, False).astype(jnp.float32)
    send = lax.dynamic_index_in_dim(part, 1 - at_y, 0, False)
    return keep + swap(send, "y").astype(jnp.float32)


def left_of(left, pieces):
    left = own_half(relative(left, 1)).T
    n_h = lax.axis_size("h")
    left = left.reshape(4, n_h, pieces, -1, left.shape[1])
    return left.transpose(2, 0, 1, 3, 4).reshape(pieces, -1, left.shape[-1])


def both_cores(right):
    return right, swap(right, "c")


def columns_of(chunks):
    return chunks.transpose(1, 0, 2).reshape(chunks.shape[1], -1)


def on_device(
    counts,
    library,
    coords,
    lengths,
    cotangent,
    w_enc,
    w_qkv,
    w_out,
    gain_one,
    shift_one,
    w_up,
    w_down,
    gain_two,
    shift_two,
    w_dec,
):
    rows = counts.shape[0]
    width = w_qkv.shape[1] // 3
    heads = HEADS
    head_width = width // heads
    att_scale = head_width ** (-0.5)
    group_size = 4
    slots = rows * group_size
    scale = 10000.0 / library
    genes = counts.shape[1]
    padded = -(-genes // 128) * 128
    counts_f = counts.astype(jnp.float32)
    xb = jnp.pad(counts.T, ((0, padded - genes), (0, 0))).astype(jnp.float32)
    xb = jnp.log1p(xb * scale[None, :]).astype(jnp.bfloat16)
    xb_pair = both_cores(xb)
    cot = jnp.pad(cotangent.T, ((0, padded - genes), (0, 0)))
    cot_pair = both_cores(cot)
    pe = by_owner(positions(coords, width), 1)
    ends = jnp.cumsum(lengths[0])
    place = jnp.arange(slots, dtype=jnp.int32)
    seg_all = jnp.sum((place[:, None] >= ends[None, :]).astype(jnp.int32), axis=1)
    seg_mine = lax.dynamic_slice_in_dim(seg_all, (lax.axis_index("y") * 2 + lax.axis_index("c")) * rows, rows)
    same = (seg_mine[:, None] == seg_all[None, :])[None]
    vectors = jnp.stack([gain_one, shift_one, gain_two, shift_two], axis=1)
    vectors = jnp.pad(vectors, ((0, 0), (0, 124)))
    pad = ((0, 0), (0, padded - genes))
    quarter = -(-padded // 512) * 128
    gene_cuts = [0, quarter, 2 * quarter, 3 * quarter, padded]
    shards = [
        jnp.pad(w_enc.T, pad),
        jnp.concatenate([w_qkv, vectors], axis=1),
        by_owner(w_out, 1),
        by_owner(w_up, 1),
        by_owner(w_down, 1),
        jnp.pad(w_dec.T, pad),
    ]
    cuts = [gene_cuts, [0, width // 2 * 3, 3 * width + 128], [0, width]]
    cuts += [[0, 2 * width, 4 * width], [0, width // 2, width], [0, padded]]
    order = [(0, 0), (0, 1), (0, 2), (0, 3), (1, 0), (1, 1), (2, 0), (3, 0), (3, 1), (4, 0), (4, 1), (5, 0)]
    gathered = gather_all(shards, 5, cuts, order, 0)
    enc_all, qkv_all, out_all, up_all, down_all = (
        w.reshape(-1, w.shape[-1]) for w in gathered[:5]
    )
    vectors = qkv_all[:, 3 * width :].astype(jnp.float32).T
    qkv_all = qkv_all[:, : 3 * width]
    g1f, b1f, g2f, b2f = vectors[0], vectors[1], vectors[2], vectors[3]
    h0 = contract_cols(xb.T, enc_all) + pe
    a1 = layer_norm(h0, g1f, b1f).astype(jnp.bfloat16)
    qkv = matmul(a1, qkv_all).astype(jnp.bfloat16)
    query = qkv[:, :width].reshape(rows, heads, head_width)
    kv_all, arrived = gather_group(qkv[:, width:])
    dec_parts = gather_dec(gathered[5], arrived)
    keys = kv_all[:, :width].reshape(slots, heads, head_width)
    values = kv_all[:, width:].reshape(slots, heads, head_width)

    def scores_of():
        raw = (
            jnp.einsum("qhd,khd->hqk", query, keys, preferred_element_type=jnp.float32) * att_scale
        )
        return jnp.where(same, raw, -1000000000.0)

    scores = scores_of()
    top = jnp.max(scores, axis=-1, keepdims=True)
    expo = jnp.exp(scores - top)
    total = jnp.sum(expo, axis=-1, keepdims=True)
    log_total = top + jnp.log(total)
    probs_b = (expo / total).astype(jnp.bfloat16)
    attended = jnp.einsum("hqk,khd->qhd", probs_b, values, preferred_element_type=jnp.float32)
    attended_b = attended.reshape(rows, width).astype(jnp.bfloat16)
    attended_b = by_owner(attended_b, 1)
    h1 = h0 + matmul(attended_b, out_all)
    a2 = layer_norm(h1, g2f, b2f).astype(jnp.bfloat16)
    hidden = matmul(a2, up_all)
    act = jax.nn.gelu(hidden, approximate=False).astype(jnp.bfloat16)
    h2 = h1 + matmul(act, down_all)
    hb = h2.astype(jnp.bfloat16)
    grad_dec, logits, dh2 = scatter_all(
        left_of(hb, 1), [cot_pair], relative(hb, 1), dec_parts, jnp.bfloat16, True, 1
    )
    own_rows = grad_dec.shape[1]
    grad_dec = columns_of(grad_dec)[:, :genes].T
    logits = logits[:genes].T
    dh2 = relative(dh2, 0).T
    dfb = dh2.astype(jnp.bfloat16)
    d_act = contract_cols(dfb, down_all)
    slope = jax.vjp(lambda v: jax.nn.gelu(v, approximate=False), hidden)[1](d_act)[0]
    d_hidden = slope.astype(jnp.bfloat16)
    da2 = contract_cols(d_hidden, up_all)
    norm_pull = jax.vjp(layer_norm, h1, g2f, b2f)[1]
    dh1_norm, grad_gain_two, grad_shift_two = norm_pull(da2)
    dh1 = dh2 + dh1_norm
    dab = dh1.astype(jnp.bfloat16)
    d_attended = contract_cols(dab, out_all).astype(jnp.bfloat16)
    d_attended = from_owner(d_attended, 1).reshape(rows, heads, head_width)
    probs = jnp.exp(scores_of() - log_total)
    probs_b = probs.astype(jnp.bfloat16)
    d_probs = jnp.einsum("qhd,khd->hqk", d_attended, values, preferred_element_type=jnp.float32)
    inner = jnp.sum(probs * d_probs, axis=-1, keepdims=True)
    d_scores = (probs * (d_probs - inner)).astype(jnp.bfloat16)
    d_query = (
        jnp.einsum("hqk,khd->qhd", d_scores, keys, preferred_element_type=jnp.float32) * att_scale
    )
    d_keys = (
        jnp.einsum("hqk,qhd->khd", d_scores, query, preferred_element_type=jnp.float32) * att_scale
    )
    d_values = jnp.einsum("hqk,qhd->khd", probs_b, d_attended, preferred_element_type=jnp.float32)
    d_kv = jnp.concatenate([d_keys.reshape(slots, width), d_values.reshape(slots, width)], axis=1)
    d_kv = scatter_group(d_kv)
    d_qkv = jnp.concatenate([d_query.reshape(rows, width), d_kv], axis=1).astype(jnp.bfloat16)
    da1 = contract_cols(d_qkv, qkv_all)
    first_pull = jax.vjp(layer_norm, h0, g1f, b1f)[1]
    dh0_norm, grad_gain_one, grad_shift_one = first_pull(da1)
    grad_vectors = jnp.stack([grad_gain_one, grad_shift_one, grad_gain_two, grad_shift_two], axis=1)
    grad_vectors = scatter_vectors(relative(grad_vectors, 0))
    grad_gain_one, grad_shift_one, grad_gain_two, grad_shift_two = (
        grad_vectors[:, k] for k in range(4)
    )
    dh0b = (dh1 + dh0_norm).astype(jnp.bfloat16)

    lefts = [left_of(a2, 1)] * 4 + [left_of(act, act.shape[1] // width)]
    lefts += [left_of(attended_b, 1)] + [left_of(a1, 1)] * 3 + [left_of(dh0b, 1)]
    rights = [d_hidden.T] + [dfb.T] * 4 + [dab.T]
    grads, d_xb = scatter_all(
        jnp.concatenate(lefts, axis=0),
        [both_cores(jnp.concatenate(rights, axis=0)), both_cores(d_qkv.T), xb_pair],
        dh0b,
        [enc_all],
        jnp.float32,
        False,
        2,
    )
    ends = [0]
    for columns in (4 * width, 4 * width, width, 3 * width):
        ends.append(ends[-1] + columns // CHUNK)
    grad_up, grad_down, grad_out, grad_qkv, grad_enc = (
        grads[low:high] for low, high in zip(ends, ends[1:] + [grads.shape[0]])
    )
    grad_up, grad_out, grad_qkv, grad_enc = (
        columns_of(g) for g in (grad_up, grad_out, grad_qkv, grad_enc)
    )
    grad_down = grad_down.reshape(4, -1, own_rows, CHUNK).transpose(0, 2, 1, 3)
    grad_down = grad_down.reshape(4 * own_rows, -1)
    grad_out, grad_up, grad_down = (from_owner(g, 1) for g in (grad_out, grad_up, grad_down))
    grad_enc = grad_enc[:, :genes].T
    d_xb = d_xb[:genes].T
    counts_grad = d_xb * scale[:, None] / (1.0 + counts_f * scale[:, None])
    return (
        logits,
        counts_grad,
        grad_enc,
        grad_qkv,
        grad_out,
        grad_gain_one,
        grad_shift_one,
        grad_up,
        grad_down,
        grad_gain_two,
        grad_shift_two,
        grad_dec,
    )


ALL = ("h", "x", "y", "c")


def solution(mesh):
    n_dp, n_fsdp = mesh.shape["dp"], mesh.shape["fsdp"]
    mesh = Mesh(mesh.devices.reshape((n_dp // 2, 2, 2, n_fsdp // 2)), ALL)
    placed = (
        P(ALL, None),
        P(ALL),
        P(None, ALL),
        P(("h", "x"), None),
        P(ALL, None),
        P(None, ALL),
        P(ALL, None),
        P(ALL, None),
        P(ALL),
        P(ALL),
        P(ALL, None),
        P(ALL, None),
        P(ALL),
        P(ALL),
        P(None, ALL),
    )
    return jax.shard_map(
        on_device,
        mesh=mesh,
        in_specs=placed,
        out_specs=(
            P(ALL, None),
            P(ALL, None),
            P(None, ALL),
            P(ALL, None),
            P(ALL, None),
            P(ALL),
            P(ALL),
            P(ALL, None),
            P(ALL, None),
            P(ALL),
            P(ALL),
            P(None, ALL),
        ),
        check_vma=False,
    )
```

```python
import functools
import math

import jax
import jax.numpy as jnp
from jax import lax
from jax.experimental import pallas as pl
from jax.experimental.pallas import tpu as pltpu
from jax.sharding import Mesh
from jax.sharding import PartitionSpec as P

HEADS = 16
MESH = pl.DeviceIdType.MESH
RING = 8
CHUNK = 256


eps = 1e-05


def layer_norm(value, gain, shift):
    mean = jnp.mean(value, axis=1, keepdims=True)
    centred = value - mean
    variance = jnp.mean(centred * centred, axis=1, keepdims=True)
    return centred * lax.rsqrt(variance + eps) * gain + shift


def positions(coords, width):
    quarter = width // 4
    freqs = 0.05 * jnp.exp(-jnp.arange(quarter, dtype=jnp.float32) * (math.log(10000.0) / quarter))
    along_x = coords[0].astype(jnp.float32)[:, None] * freqs[None, :]
    along_y = coords[1].astype(jnp.float32)[:, None] * freqs[None, :]
    return jnp.concatenate(
        [jnp.sin(along_x), jnp.cos(along_x), jnp.sin(along_y), jnp.cos(along_y)], axis=1
    )


def contract_rows(left, right):
    return lax.dot_general(
        left, right, (((0,), (0,)), ((), ())), preferred_element_type=jnp.float32
    )


def contract_cols(left, right):
    return lax.dot_general(
        left, right, (((1,), (1,)), ((), ())), preferred_element_type=jnp.float32
    )


def matmul(left, right):
    return jnp.dot(left, right, preferred_element_type=jnp.float32)


def swap(value, axis):
    return lax.ppermute(value, axis, [(0, 1), (1, 0)])


def by_owner(value, axis):
    n_h = lax.axis_size("h")
    at = value.shape
    block = at[axis] // (8 * n_h)
    split = value.reshape(at[:axis] + (n_h, 2, 2, 2, block) + at[axis + 1 :])
    order = list(range(axis)) + [axis + 3, axis + 1, axis + 2, axis, axis + 4]
    order += list(range(axis + 5, split.ndim))
    return split.transpose(order).reshape(at)


def from_owner(value, axis):
    n_h = lax.axis_size("h")
    at = value.shape
    block = at[axis] // (8 * n_h)
    split = value.reshape(at[:axis] + (2, 2, 2, n_h, block) + at[axis + 1 :])
    order = list(range(axis)) + [axis + 3, axis + 1, axis + 2, axis, axis + 4]
    order += list(range(axis + 5, split.ndim))
    return split.transpose(order).reshape(at)


def relative(value, axis):
    eighth = value.shape[axis] // 8
    mine = lax.axis_index("c") * 4 + lax.axis_index("x") * 2 + lax.axis_index("y")
    parts = [
        lax.dynamic_slice_in_dim(value, (mine ^ part) * eighth, eighth, axis) for part in range(8)
    ]
    return jnp.concatenate(parts, axis=axis)


def greet(peers):
    barrier = pltpu.get_barrier_semaphore()
    for peer in peers:
        pl.semaphore_signal(barrier, inc=1, device_id=peer, device_id_type=MESH)
    pl.semaphore_wait(barrier, len(peers))


def gather_kernel(n_h, jobs, n_arrays, n_full, *refs):
    shards, wholes = refs[:n_arrays], refs[n_arrays : 2 * n_arrays]
    own_sem, h_send, h_recv, send, recv = refs[2 * n_arrays :]
    h, x, y, c = (lax.axis_index(name) for name in ("h", "x", "y", "c"))
    h = 0 if n_h == 1 else h
    to_x, to_y, to_c = {"x": 1 - x}, {"y": 1 - y}, {"c": 1 - c}
    greet([{"h": lax.rem(h + d, n_h)} for d in range(1, n_h)] + [to_x, to_y, to_c])

    def rows_of(job, at):
        array, low, high, _ = job
        rows = shards[array].shape[0]
        place = (pl.ds(at * rows, rows), pl.ds(low, high - low))
        return wholes[array].at[(c, x, y, *place) if array < n_full else place]

    def h_copy(j, d):
        array, low, high, _ = jobs[j]
        return pltpu.make_async_remote_copy(
            src_ref=shards[array].at[:, pl.ds(low, high - low)],
            dst_ref=rows_of(jobs[j], h),
            send_sem=h_send.at[j, d - 1],
            recv_sem=h_recv.at[j, d - 1],
            device_id={"h": lax.rem(h + d, n_h)},
            device_id_type=MESH,
        )

    def own_copy(j):
        array, low, high, _ = jobs[j]
        return pltpu.make_async_copy(
            shards[array].at[:, pl.ds(low, high - low)], rows_of(jobs[j], h), own_sem.at[j]
        )

    def block_copy(j, k, block, to, columns):
        view = wholes[jobs[j][0]].at[(*block, slice(None), pl.ds(columns[0], columns[1] - columns[0]))]
        return pltpu.make_async_remote_copy(
            src_ref=view,
            dst_ref=view,
            send_sem=send.at[j, k],
            recv_sem=recv.at[j, k],
            device_id=to,
            device_id_type=MESH,
        )

    own, by_x, by_y, far = (c, x, y), (c, 1 - x, y), (c, x, 1 - y), (c, 1 - x, 1 - y)

    def copy(j, k):
        _, low, high, middle = jobs[j]
        block, to, columns = [
            (own, to_x, (low, high)),
            (own, to_y, (low, high)),
            (own, to_c, (low, high)),
            (by_x, to_y, (low, middle)),
            (by_y, to_x, (middle, high)),
            (by_x, to_c, (low, high)),
            (by_y, to_c, (low, high)),
            (far, to_c, (low, high)),
        ][k]
        return block_copy(j, k, block, to, columns)

    def start_h(j):
        own_copy(j).start()
        for d in range(1, n_h):
            h_copy(j, d).start()

    n = sum(array < n_full for array, *_ in jobs)
    ahead = 2
    for j in range(ahead):
        start_h(j)
    for step in range(n + 2):
        if step < n:
            own_copy(step).wait()
            for d in range(1, n_h):
                h_copy(step, d).wait_recv()
            for k in (0, 1, 2):
                copy(step, k).start()
            if step + ahead < len(jobs):
                start_h(step + ahead)
        if 0 <= step - 1 < n:
            for k in (0, 1):
                copy(step - 1, k).wait_recv()
            for k in (3, 4, 5, 6):
                copy(step - 1, k).start()
        if 0 <= step - 2 < n:
            for k in (3, 4):
                copy(step - 2, k).wait_recv()
            copy(step - 2, 7).start()
    for j in range(n + ahead, len(jobs)):
        start_h(j)
    for j in range(n, len(jobs)):
        own_copy(j).wait()
        for d in range(1, n_h):
            h_copy(j, d).wait_recv()
    for j in range(len(jobs)):
        for d in range(1, n_h):
            h_copy(j, d).wait_send()
    for j in range(n):
        for k in range(8):
            copy(j, k).wait_send()
        for k in (2, 5, 6, 7):
            copy(j, k).wait_recv()


def gather_all(shards, n_full, cuts, order, collective_id):
    n_h = lax.axis_size("h")
    if any(shard.shape[0] % 16 for shard in shards):
        shards = [lax.all_gather(s, "h", axis=0, tiled=True) for s in shards]
        n_h = 1
    jobs = []
    for array, piece in order:
        low, high = cuts[array][piece], cuts[array][piece + 1]
        jobs.append((array, low, high, low + (high - low) // 256 * 128))
    n, others, dma = len(jobs), max(n_h - 1, 1), pltpu.SemaphoreType.DMA
    shapes = [(n_h * s.shape[0], s.shape[1]) for s in shards]
    return pl.pallas_call(
        functools.partial(gather_kernel, n_h, jobs, len(shards), n_full),
        out_shape=[
            jax.ShapeDtypeStruct((2, 2, 2) + shape if k < n_full else shape, jnp.bfloat16)
            for k, shape in enumerate(shapes)
        ],
        in_specs=[pl.BlockSpec(memory_space=pl.ANY)] * len(shards),
        out_specs=[pl.BlockSpec(memory_space=pl.ANY)] * len(shards),
        scratch_shapes=[dma((n,)), dma((n, others)), dma((n, others)), dma((n, 8)), dma((n, 8))],
        compiler_params=pltpu.CompilerParams(collective_id=collective_id, has_side_effects=True),
    )(*shards)


def scatter_kernel(n_h, sections, left_starts, n_weights, with_sum, *refs):
    lefts, vector = refs[:2]
    n_sections = len(sections)
    rights = refs[2 : 2 + 2 * n_sections]
    weights = refs[2 + 2 * n_sections : 2 + 2 * n_sections + n_weights]
    rest = refs[2 + 2 * n_sections + n_weights :]
    out, product = rest[:2]
    total_out = rest[2] if with_sum else None
    (right_buf, weight_buf, product_buf, own, s1, r1, s2, r2, s3, r3, load_sem, weight_sem, product_sem,
     send1, recv1, send2, recv2, send3, recv3) = rest[3 if with_sum else 2 :]
    h, x, y = (lax.axis_index(name) for name in ("h", "x", "y"))
    to_x, to_y = {"x": 1 - x}, {"y": 1 - y}
    w = s3.shape[1]
    rows = w // n_h
    f32, b16 = jnp.float32, jnp.bfloat16
    cells = vector.shape[0]
    starts = [sum(sections[:k]) for k in range(n_sections)]
    n = sum(sections)
    begin = starts[-1]
    greet([{"h": lax.rem(h + d, n_h)} for d in range(1, n_h)] + [to_x, to_y])

    def chunk_of(k):
        return pl.ds(pl.multiple_of(k * CHUNK, CHUNK), CHUNK)

    def loads(i, section, k):
        slot = lax.rem(i, 3)
        return [
            pltpu.make_async_copy(
                rights[2 * section + half].at[chunk_of(k)],
                right_buf.at[slot, :, pl.ds(half * cells, cells)],
                load_sem.at[slot, half],
            )
            for half in (0, 1)
        ]

    def weight_loads(k):
        slot = lax.rem(k, 3)
        size = weights[0].shape[0]
        return [
            pltpu.make_async_copy(
                weight.at[:, chunk_of(k)],
                weight_buf.at[slot, pl.ds(part * size, size)],
                weight_sem.at[slot, part],
            )
            for part, weight in enumerate(weights)
        ]

    def start_loads(i):
        for section, (start, count) in enumerate(zip(starts, sections)):

            @pl.when((i >= start) & (i < start + count))
            def _(section=section, start=start):
                for copy in loads(i, section, i - start):
                    copy.start()
                if section == n_sections - 1:
                    for copy in weight_loads(i - start):
                        copy.start()

    def product_store(k):
        slot = lax.rem(k, 2)
        return pltpu.make_async_copy(product_buf.at[slot], product.at[chunk_of(k)], product_sem.at[slot])

    def hop(i, source, target, send_sem, recv_sem, to):
        slot = lax.rem(i, RING)
        return pltpu.make_async_remote_copy(
            src_ref=source.at[slot], dst_ref=target.at[i], send_sem=send_sem.at[slot],
            recv_sem=recv_sem.at[i], device_id=to, device_id_type=MESH,
        )

    def first(i, odd):
        return hop(i, s1, r1, send1, recv1, to_y if odd else to_x)

    def second(i, odd):
        return hop(i, s2, r2, send2, recv2, to_x if odd else to_y)

    def third(i, d):
        to = lax.rem(h + d, n_h)
        slot = lax.rem(i, RING)
        return pltpu.make_async_remote_copy(
            src_ref=s3.at[slot, pl.ds(to * rows, rows)], dst_ref=r3.at[i, d - 1],
            send_sem=send3.at[slot, d - 1], recv_sem=recv3.at[i, d - 1],
            device_id={"h": to}, device_id_type=MESH,
        )

    def multiply(i, odd):
        slot = lax.rem(i, RING)
        for copy in loads(i, 0, 0):
            copy.wait()
        left = lefts[sum((i + 1024 - start) // 1024 for start in left_starts[1:]) if left_starts[1:] else 0]
        right = right_buf.at[lax.rem(i, 3)]

        @pl.when(i >= RING)
        def _():
            first(i - RING, odd).wait_send()

        part = lax.dot_general(left, right[...], (((1,), (1,)), ((), ())), preferred_element_type=f32)
        own[slot, :w] = part[:w]
        if odd:
            own[slot, w:] = part[2 * w : 3 * w]
            s1[slot, :w] = part[w : 2 * w].astype(b16)
            s1[slot, w:] = part[3 * w :].astype(b16)
        else:
            own[slot, w:] = part[w : 2 * w]
            s1[slot] = part[2 * w :].astype(b16)
        first(i, odd).start()

        def beside(k):
            for copy in weight_loads(k):
                copy.wait()
            weight = weight_buf[lax.rem(k, 3)]

            @pl.when(k >= 2)
            def _():
                product_store(k - 2).wait()

            value = jnp.dot(vector[...], weight, preferred_element_type=f32)
            product_buf[lax.rem(k, 2)] = value.T.astype(product_buf.dtype)
            product_store(k).start()
            if with_sum:
                term = jnp.dot(weight, right[:, :cells], preferred_element_type=f32)

                @pl.when(k == 0)
                def _():
                    total_out[...] = term

                @pl.when(k > 0)
                def _():
                    total_out[...] += term

        if begin == 0:
            beside(i)
        else:

            @pl.when(i >= begin)
            def _():
                beside(i - begin)

        start_loads(i + 2)

    def pass_on(i, odd):
        slot = lax.rem(i, RING)
        first(i, odd).wait_recv()

        @pl.when(i >= RING)
        def _():
            second(i - RING, odd).wait_send()

        s2[slot] = (own[slot, w:] + r1[i, w:].astype(f32)).astype(b16)
        second(i, odd).start()

    def keep(i, odd):
        slot = lax.rem(i, RING)
        second(i, odd).wait_recv()
        part = own[slot, :w] + r1[i, :w].astype(f32) + r2[i].astype(f32)
        if n_h == 1:
            out[i] = part.astype(b16)
            return

        @pl.when(i >= RING)
        def _():
            for d in range(1, n_h):
                third(i - RING, d).wait_send()

        s3[slot] = part.astype(b16)
        for d in range(1, n_h):
            third(i, d).start()

    def finish(i, odd):
        if n_h == 1:
            return
        total = s3[lax.rem(i, RING), pl.ds(h * rows, rows)].astype(f32)
        for d in range(1, n_h):
            third(i, d).wait_recv()
            total = total + r3[i, d - 1].astype(f32)
        out[i] = total

    start_loads(jnp.int32(0))
    start_loads(jnp.int32(1))
    pairs = (n + 1) // 2

    def step(p, carry):
        for lag, stage in enumerate((multiply, pass_on, keep, finish)):
            for odd in (0, 1):
                i = 2 * (p - lag) + odd

                @pl.when((i >= 0) & (i < n))
                def _(stage=stage, i=i, odd=odd):
                    stage(i, odd)

        return carry

    lax.fori_loop(0, pairs + 3, step, 0)
    for i in range(max(n - RING, 0), n):
        first(i, i % 2).wait_send()
        second(i, i % 2).wait_send()
        for d in range(1, n_h):
            third(i, d).wait_send()
    for k in range(max(sections[-1] - 2, 0), sections[-1]):
        product_store(k).wait()


def scatter_all(lefts, left_starts, rights, vector, weights, product_type, with_sum, collective_id):
    sections = [own.shape[0] // CHUNK for own, _ in rights]
    n, cells = sum(sections), vector.shape[0]
    features = vector.shape[1]
    w = lefts.shape[1] // 4
    n_h = lax.axis_size("h")
    rows = w // n_h
    inner_h = n_h if rows % 16 == 0 else 1
    dma, bf16, f32 = pltpu.SemaphoreType.DMA, jnp.bfloat16, jnp.float32
    vmem, hbm = pl.BlockSpec(memory_space=pltpu.VMEM), pl.BlockSpec(memory_space=pl.ANY)
    others = max(inner_h - 1, 1)
    part_shape = jax.ShapeDtypeStruct((n, rows, CHUNK), f32)
    if inner_h == 1:
        part_shape = jax.ShapeDtypeStruct((n, w, CHUNK), bf16)
    out_shape = [part_shape, jax.ShapeDtypeStruct((sections[-1] * CHUNK, cells), product_type)]
    out_specs = [vmem, hbm]
    if with_sum:
        out_shape.append(jax.ShapeDtypeStruct((features, cells), f32))
        out_specs.append(vmem)
    part, *more = pl.pallas_call(
        functools.partial(
            scatter_kernel, inner_h, sections, left_starts, len(weights), with_sum
        ),
        out_shape=out_shape,
        in_specs=[vmem, vmem] + [hbm] * (2 * len(rights) + len(weights)),
        out_specs=out_specs,
        scratch_shapes=[
            pltpu.VMEM((3, CHUNK, 2 * cells), bf16),
            pltpu.VMEM((3, features, CHUNK), bf16),
            pltpu.VMEM((2, CHUNK, cells), product_type),
            pltpu.VMEM((RING, 2 * w, CHUNK), f32),
            pltpu.VMEM((RING, 2 * w, CHUNK), bf16),
            pltpu.VMEM((n, 2 * w, CHUNK), bf16),
            pltpu.VMEM((RING, w, CHUNK), bf16),
            pltpu.VMEM((n, w, CHUNK), bf16),
            pltpu.VMEM((RING, w, CHUNK), bf16),
            pltpu.VMEM((n, others, w // inner_h, CHUNK), bf16),
            dma((3, 2)),
            dma((3, len(weights))),
            dma((2,)),
            dma((RING,)),
            dma((n,)),
            dma((RING,)),
            dma((n,)),
            dma((RING, others)),
            dma((n, others)),
        ],
        compiler_params=pltpu.CompilerParams(
            collective_id=collective_id, has_side_effects=True, vmem_limit_bytes=60 * 2**20
        ),
    )(lefts, vector, *(half for pair in rights for half in pair), *weights)
    if inner_h == 1:
        part = lax.psum_scatter(part, "h", scatter_dimension=1, tiled=True).astype(f32)
    return part, *more


def after(value, first):
    return lax.optimization_barrier((value, first))


def own_half(left):
    half = left.shape[1] // 2
    return jnp.concatenate([left[:, :half], swap(left[:, half:], "c")], axis=0)


def gather_group(mine):
    at_y, at_c = lax.axis_index("y"), lax.axis_index("c")
    by_y = swap(mine, "y")
    pair = jnp.stack([mine, by_y])
    both = jnp.stack([pair, swap(pair, "c")])
    order = [
        lax.dynamic_index_in_dim(
            lax.dynamic_index_in_dim(both, at_c ^ c, 0, False), at_y ^ y, 0, False
        )
        for y in range(2)
        for c in range(2)
    ]
    return jnp.concatenate(order, axis=0), by_y


def scatter_group(rows_all):
    at_y, at_c = lax.axis_index("y"), lax.axis_index("c")
    part = rows_all.astype(jnp.bfloat16).reshape((2, 2, rows_all.shape[0] // 4, -1))
    keep = lax.dynamic_index_in_dim(part, at_c, 1, False).astype(jnp.float32)
    send = lax.dynamic_index_in_dim(part, 1 - at_c, 1, False)
    part = (keep + swap(send, "c").astype(jnp.float32)).astype(jnp.bfloat16)
    keep = lax.dynamic_index_in_dim(part, at_y, 0, False).astype(jnp.float32)
    send = lax.dynamic_index_in_dim(part, 1 - at_y, 0, False)
    return keep + swap(send, "y").astype(jnp.float32)


def left_of(left, pieces):
    left = own_half(relative(left, 1)).T
    n_h = lax.axis_size("h")
    left = left.reshape(4, n_h, pieces, -1, left.shape[1])
    return left.transpose(2, 0, 1, 3, 4).reshape(pieces, -1, left.shape[-1])


def both_cores(right):
    return right, swap(right, "c")


def columns_of(chunks):
    return chunks.transpose(1, 0, 2).reshape(chunks.shape[1], -1)


def on_device(
    counts,
    library,
    coords,
    lengths,
    cotangent,
    w_enc,
    w_qkv,
    w_out,
    gain_one,
    shift_one,
    w_up,
    w_down,
    gain_two,
    shift_two,
    w_dec,
):
    rows = counts.shape[0]
    width = w_qkv.shape[1] // 3
    heads = HEADS
    head_width = width // heads
    att_scale = head_width ** (-0.5)
    group_size = 4
    slots = rows * group_size
    scale = 10000.0 / library
    genes = counts.shape[1]
    padded = -(-genes // 128) * 128
    counts_f = counts.astype(jnp.float32)
    xb = jnp.pad(counts.T, ((0, padded - genes), (0, 0))).astype(jnp.float32)
    xb = jnp.log1p(xb * scale[None, :]).astype(jnp.bfloat16)
    xb_pair = both_cores(xb)
    cot = jnp.pad(cotangent.T, ((0, padded - genes), (0, 0)))
    cot_pair = both_cores(cot)
    pe = by_owner(positions(coords, width), 1)
    ends = jnp.cumsum(lengths[0])
    place = jnp.arange(slots, dtype=jnp.int32)
    seg_all = jnp.sum((place[:, None] >= ends[None, :]).astype(jnp.int32), axis=1)
    seg_mine = lax.dynamic_slice_in_dim(seg_all, (lax.axis_index("y") * 2 + lax.axis_index("c")) * rows, rows)
    same = (seg_mine[:, None] == seg_all[None, :])[None]
    vectors = jnp.stack([gain_one, shift_one, gain_two, shift_two], axis=1)
    vectors = jnp.pad(vectors, ((0, 0), (0, 124)))
    pad = ((0, 0), (0, padded - genes))
    quarter = -(-padded // 512) * 128
    gene_cuts = [0, quarter, 2 * quarter, 3 * quarter, padded]
    shards = [
        jnp.pad(w_enc.T, pad),
        jnp.concatenate([w_qkv, vectors], axis=1),
        by_owner(w_out, 1),
        by_owner(w_up, 1),
        by_owner(w_down, 1),
        jnp.pad(w_dec.T, pad),
    ]
    cuts = [gene_cuts, [0, width // 2 * 3, 3 * width + 128], [0, width]]
    cuts += [[0, 2 * width, 4 * width], [0, width // 2, width], [0, padded]]
    order = [(0, 0), (0, 1), (0, 2), (0, 3), (1, 0), (1, 1), (2, 0), (3, 0), (3, 1), (4, 0), (4, 1), (5, 0)]
    gathered = gather_all(shards, 5, cuts, order, 0)
    enc_all, qkv_all, out_all, up_all, down_all = (
        w.reshape(-1, w.shape[-1]) for w in gathered[:5]
    )
    vectors = qkv_all[:, 3 * width :].astype(jnp.float32).T
    qkv_all = qkv_all[:, : 3 * width]
    g1f, b1f, g2f, b2f = vectors[0], vectors[1], vectors[2], vectors[3]
    h0 = contract_cols(xb.T, enc_all) + pe
    a1 = layer_norm(h0, g1f, b1f).astype(jnp.bfloat16)
    qkv = matmul(a1, qkv_all).astype(jnp.bfloat16)
    query = qkv[:, :width].reshape(rows, heads, head_width)
    kv_all, arrived = gather_group(qkv[:, width:])
    dec_own = gathered[5]
    middle = dec_own.shape[1] // 256 * 128
    query, by_x = after(query, swap(dec_own, "x"))
    by_y = swap(after(dec_own, arrived)[0], "y")
    far_left = swap(by_x[:, :middle], "y")
    keys = kv_all[:, :width].reshape(slots, heads, head_width)
    values = kv_all[:, width:].reshape(slots, heads, head_width)

    def scores_of():
        raw = (
            jnp.einsum("qhd,khd->hqk", query, keys, preferred_element_type=jnp.float32) * att_scale
        )
        return jnp.where(same, raw, -1000000000.0)

    scores = scores_of()
    top = jnp.max(scores, axis=-1, keepdims=True)
    expo = jnp.exp(scores - top)
    total = jnp.sum(expo, axis=-1, keepdims=True)
    log_total = top + jnp.log(total)
    probs_b = (expo / total).astype(jnp.bfloat16)
    attended = jnp.einsum("hqk,khd->qhd", probs_b, values, preferred_element_type=jnp.float32)
    attended_b = attended.reshape(rows, width).astype(jnp.bfloat16)
    attended_b, by_y = after(by_owner(attended_b, 1), by_y)
    far_right = swap(by_y[:, middle:], "x")
    h1 = h0 + matmul(attended_b, out_all)
    a2 = layer_norm(h1, g2f, b2f).astype(jnp.bfloat16)
    hidden = matmul(a2, up_all)
    act = jax.nn.gelu(hidden, approximate=False).astype(jnp.bfloat16)
    act, far = after(act, (far_left, far_right))
    dec_parts = [dec_own, by_y, by_x, jnp.concatenate(far, axis=1)]
    dec_parts += [swap(part, "c") for part in dec_parts]
    h2 = h1 + matmul(act, down_all)
    hb = h2.astype(jnp.bfloat16)
    grad_dec, logits, dh2 = scatter_all(
        left_of(hb, 1), [0], [cot_pair], relative(hb, 1), dec_parts, jnp.bfloat16, True, 1
    )
    own_rows = grad_dec.shape[1]
    grad_dec = columns_of(grad_dec)[:, :genes].T
    logits = logits[:genes].T
    dh2 = relative(dh2, 0).T
    dfb = dh2.astype(jnp.bfloat16)
    d_act = contract_cols(dfb, down_all)
    slope = jax.vjp(lambda v: jax.nn.gelu(v, approximate=False), hidden)[1](d_act)[0]
    d_hidden = slope.astype(jnp.bfloat16)
    da2 = contract_cols(d_hidden, up_all)
    norm_pull = jax.vjp(layer_norm, h1, g2f, b2f)[1]
    dh1_norm, grad_gain_two, grad_shift_two = norm_pull(da2)
    dh1 = dh2 + dh1_norm
    dab = dh1.astype(jnp.bfloat16)
    d_attended = contract_cols(dab, out_all).astype(jnp.bfloat16)
    d_attended = from_owner(d_attended, 1).reshape(rows, heads, head_width)
    probs = jnp.exp(scores_of() - log_total)
    probs_b = probs.astype(jnp.bfloat16)
    d_probs = jnp.einsum("qhd,khd->hqk", d_attended, values, preferred_element_type=jnp.float32)
    inner = jnp.sum(probs * d_probs, axis=-1, keepdims=True)
    d_scores = (probs * (d_probs - inner)).astype(jnp.bfloat16)
    d_query = (
        jnp.einsum("hqk,khd->qhd", d_scores, keys, preferred_element_type=jnp.float32) * att_scale
    )
    d_keys = (
        jnp.einsum("hqk,qhd->khd", d_scores, query, preferred_element_type=jnp.float32) * att_scale
    )
    d_values = jnp.einsum("hqk,qhd->khd", probs_b, d_attended, preferred_element_type=jnp.float32)
    d_kv = jnp.concatenate([d_keys.reshape(slots, width), d_values.reshape(slots, width)], axis=1)
    d_kv = scatter_group(d_kv)
    d_qkv = jnp.concatenate([d_query.reshape(rows, width), d_kv], axis=1).astype(jnp.bfloat16)
    da1 = contract_cols(d_qkv, qkv_all)
    first_pull = jax.vjp(layer_norm, h0, g1f, b1f)[1]
    dh0_norm, grad_gain_one, grad_shift_one = first_pull(da1)
    vectors_b = jnp.stack([grad_gain_one, grad_shift_one, grad_gain_two, grad_shift_two])
    vectors_b = jnp.pad(vectors_b, ((0, rows - 4), (0, 0))).astype(jnp.bfloat16)
    unit = jnp.eye(rows, dtype=jnp.bfloat16)
    dh0b = (dh1 + dh0_norm).astype(jnp.bfloat16)

    lefts = [left_of(a2, 1), left_of(act, act.shape[1] // width), left_of(attended_b, 1)]
    lefts += [left_of(a1, 1), left_of(vectors_b, 1), left_of(dh0b, 1)]
    pieces = (4 * width,) + (width,) * 5 + (3 * width, rows)
    left_starts = [sum(pieces[:k]) // CHUNK for k in range(len(pieces) + 1)]
    rights = [d_hidden.T] + [dfb.T] * 4 + [dab.T]
    grads, d_xb = scatter_all(
        jnp.concatenate(lefts, axis=0),
        left_starts,
        [both_cores(jnp.concatenate(rights, axis=0)), both_cores(d_qkv.T), (unit, unit), xb_pair],
        dh0b,
        [enc_all],
        jnp.float32,
        False,
        2,
    )
    ends = [0]
    for columns in (4 * width, 4 * width, width, 3 * width, rows):
        ends.append(ends[-1] + columns // CHUNK)
    grad_up, grad_down, grad_out, grad_qkv, grad_vectors, grad_enc = (
        grads[low:high] for low, high in zip(ends, ends[1:] + [grads.shape[0]])
    )
    grad_up, grad_out, grad_qkv, grad_enc = (
        columns_of(g) for g in (grad_up, grad_out, grad_qkv, grad_enc)
    )
    grad_gain_one, grad_shift_one, grad_gain_two, grad_shift_two = (
        grad_vectors[0, :, k] for k in range(4)
    )
    grad_down = grad_down.reshape(4, -1, own_rows, CHUNK).transpose(0, 2, 1, 3)
    grad_down = grad_down.reshape(4 * own_rows, -1)
    grad_out, grad_up, grad_down = (from_owner(g, 1) for g in (grad_out, grad_up, grad_down))
    grad_enc = grad_enc[:, :genes].T
    d_xb = d_xb[:genes].T
    counts_grad = d_xb * scale[:, None] / (1.0 + counts_f * scale[:, None])
    return (
        logits,
        counts_grad,
        grad_enc,
        grad_qkv,
        grad_out,
        grad_gain_one,
        grad_shift_one,
        grad_up,
        grad_down,
        grad_gain_two,
        grad_shift_two,
        grad_dec,
    )


ALL = ("h", "x", "y", "c")


def solution(mesh):
    n_dp, n_fsdp = mesh.shape["dp"], mesh.shape["fsdp"]
    mesh = Mesh(mesh.devices.reshape((n_dp // 2, 2, 2, n_fsdp // 2)), ALL)
    placed = (
        P(ALL, None),
        P(ALL),
        P(None, ALL),
        P(("h", "x"), None),
        P(ALL, None),
        P(None, ALL),
        P(ALL, None),
        P(ALL, None),
        P(ALL),
        P(ALL),
        P(ALL, None),
        P(ALL, None),
        P(ALL),
        P(ALL),
        P(None, ALL),
    )
    return jax.shard_map(
        on_device,
        mesh=mesh,
        in_specs=placed,
        out_specs=(
            P(ALL, None),
            P(ALL, None),
            P(None, ALL),
            P(ALL, None),
            P(ALL, None),
            P(ALL),
            P(ALL),
            P(ALL, None),
            P(ALL, None),
            P(ALL),
            P(ALL),
            P(None, ALL),
        ),
        check_vma=False,
    )
```

```python
import functools
import math

import jax
import jax.numpy as jnp
from jax import lax
from jax.experimental import pallas as pl
from jax.experimental.pallas import tpu as pltpu
from jax.sharding import Mesh
from jax.sharding import PartitionSpec as P

HEADS = 16
MESH = pl.DeviceIdType.MESH
RING = 8
CHUNK = 256


eps = 1e-05


def layer_norm(value, gain, shift):
    mean = jnp.mean(value, axis=1, keepdims=True)
    centred = value - mean
    variance = jnp.mean(centred * centred, axis=1, keepdims=True)
    return centred * lax.rsqrt(variance + eps) * gain + shift


def positions(coords, width):
    quarter = width // 4
    freqs = 0.05 * jnp.exp(-jnp.arange(quarter, dtype=jnp.float32) * (math.log(10000.0) / quarter))
    along_x = coords[0].astype(jnp.float32)[:, None] * freqs[None, :]
    along_y = coords[1].astype(jnp.float32)[:, None] * freqs[None, :]
    return jnp.concatenate(
        [jnp.sin(along_x), jnp.cos(along_x), jnp.sin(along_y), jnp.cos(along_y)], axis=1
    )


def contract_rows(left, right):
    return lax.dot_general(
        left, right, (((0,), (0,)), ((), ())), preferred_element_type=jnp.float32
    )


def contract_cols(left, right):
    return lax.dot_general(
        left, right, (((1,), (1,)), ((), ())), preferred_element_type=jnp.float32
    )


def matmul(left, right):
    return jnp.dot(left, right, preferred_element_type=jnp.float32)


def swap(value, axis):
    return lax.ppermute(value, axis, [(0, 1), (1, 0)])


def by_owner(value, axis):
    n_h = lax.axis_size("h")
    at = value.shape
    block = at[axis] // (8 * n_h)
    split = value.reshape(at[:axis] + (n_h, 2, 2, 2, block) + at[axis + 1 :])
    order = list(range(axis)) + [axis + 3, axis + 1, axis + 2, axis, axis + 4]
    order += list(range(axis + 5, split.ndim))
    return split.transpose(order).reshape(at)


def from_owner(value, axis):
    n_h = lax.axis_size("h")
    at = value.shape
    block = at[axis] // (8 * n_h)
    split = value.reshape(at[:axis] + (2, 2, 2, n_h, block) + at[axis + 1 :])
    order = list(range(axis)) + [axis + 3, axis + 1, axis + 2, axis, axis + 4]
    order += list(range(axis + 5, split.ndim))
    return split.transpose(order).reshape(at)


def relative(value, axis):
    eighth = value.shape[axis] // 8
    mine = lax.axis_index("c") * 4 + lax.axis_index("x") * 2 + lax.axis_index("y")
    parts = [
        lax.dynamic_slice_in_dim(value, (mine ^ part) * eighth, eighth, axis) for part in range(8)
    ]
    return jnp.concatenate(parts, axis=axis)


def greet(peers):
    barrier = pltpu.get_barrier_semaphore()
    for peer in peers:
        pl.semaphore_signal(barrier, inc=1, device_id=peer, device_id_type=MESH)
    pl.semaphore_wait(barrier, len(peers))


def gather_kernel(n_h, jobs, n_full, shards, wholes, sems, between):
    own_sem, h_send, h_recv, send, recv = sems
    h, x, y, c = (lax.axis_index(name) for name in ("h", "x", "y", "c"))
    h = 0 if n_h == 1 else h
    to_x, to_y, to_c = {"x": 1 - x}, {"y": 1 - y}, {"c": 1 - c}
    greet([{"h": lax.rem(h + d, n_h)} for d in range(1, n_h)] + [to_x, to_y, to_c])

    def rows_of(job, at):
        array, low, high, _ = job
        rows = shards[array].shape[0]
        place = (pl.ds(at * rows, rows), pl.ds(low, high - low))
        return wholes[array].at[(c, x, y, *place) if array < n_full else place]

    def h_copy(j, d):
        array, low, high, _ = jobs[j]
        return pltpu.make_async_remote_copy(
            src_ref=shards[array].at[:, pl.ds(low, high - low)],
            dst_ref=rows_of(jobs[j], h),
            send_sem=h_send.at[j, d - 1],
            recv_sem=h_recv.at[j, d - 1],
            device_id={"h": lax.rem(h + d, n_h)},
            device_id_type=MESH,
        )

    def own_copy(j):
        array, low, high, _ = jobs[j]
        return pltpu.make_async_copy(
            shards[array].at[:, pl.ds(low, high - low)], rows_of(jobs[j], h), own_sem.at[j]
        )

    def block_copy(j, k, block, to, columns):
        view = wholes[jobs[j][0]].at[(*block, slice(None), pl.ds(columns[0], columns[1] - columns[0]))]
        return pltpu.make_async_remote_copy(
            src_ref=view,
            dst_ref=view,
            send_sem=send.at[j, k],
            recv_sem=recv.at[j, k],
            device_id=to,
            device_id_type=MESH,
        )

    own, by_x, by_y, far = (c, x, y), (c, 1 - x, y), (c, x, 1 - y), (c, 1 - x, 1 - y)

    def copy(j, k):
        _, low, high, middle = jobs[j]
        block, to, columns = [
            (own, to_x, (low, high)),
            (own, to_y, (low, high)),
            (own, to_c, (low, high)),
            (by_x, to_y, (low, middle)),
            (by_y, to_x, (middle, high)),
            (by_x, to_c, (low, high)),
            (by_y, to_c, (low, high)),
            (far, to_c, (low, high)),
        ][k]
        return block_copy(j, k, block, to, columns)

    def start_h(j):
        own_copy(j).start()
        for d in range(1, n_h):
            h_copy(j, d).start()

    whole = set()

    def landed(j):
        if j not in whole:
            whole.add(j)
            for k in (2, 5, 6, 7):
                copy(j, k).wait_recv()

    n = sum(array < n_full for array, *_ in jobs)
    ahead = 2
    for j in range(ahead):
        start_h(j)
    for step in range(n + 2):
        if step < n:
            own_copy(step).wait()
            for d in range(1, n_h):
                h_copy(step, d).wait_recv()
            for k in (0, 1, 2):
                copy(step, k).start()
            if step + ahead < len(jobs):
                start_h(step + ahead)
        if 0 <= step - 1 < n:
            for k in (0, 1):
                copy(step - 1, k).wait_recv()
            for k in (3, 4, 5, 6):
                copy(step - 1, k).start()
        if 0 <= step - 2 < n:
            for k in (3, 4):
                copy(step - 2, k).wait_recv()
            copy(step - 2, 7).start()
        between(step, landed)
    for j in range(n + ahead, len(jobs)):
        start_h(j)
    for j in range(n, len(jobs)):
        own_copy(j).wait()
        for d in range(1, n_h):
            h_copy(j, d).wait_recv()
    for j in range(len(jobs)):
        for d in range(1, n_h):
            h_copy(j, d).wait_send()
    for j in range(n):
        for k in range(8):
            copy(j, k).wait_send()
        landed(j)


def front_kernel(n_h, jobs, n_arrays, n_full, *refs):
    shards, (counts, tail, scale, pe) = refs[:n_arrays], refs[n_arrays : n_arrays + 4]
    rest = refs[n_arrays + 4 :]
    wholes, (xb, h0, a1, query, pairs) = rest[:n_arrays], rest[n_arrays : n_arrays + 5]
    (count_buf, enc_buf, xb_buf, total, qkv_buf, mine, count_sem, enc_sem, xb_sem, qkv_sem, kv_sem,
     kv_send, kv_recv, *sems) = rest[n_arrays + 5 :]
    y, c = lax.axis_index("y"), lax.axis_index("c")
    f32, b16 = jnp.float32, jnp.bfloat16
    width = h0.shape[1]
    n_chunks = xb.shape[0] // CHUNK
    by_chunk = lambda k: pl.ds(pl.multiple_of(k * CHUNK, CHUNK), CHUNK)

    def loads(k, last):
        slot = lax.rem(k, 2)
        source = tail if last else counts.at[by_chunk(k)]
        return (
            pltpu.make_async_copy(source, count_buf.at[slot], count_sem.at[slot]),
            pltpu.make_async_copy(
                wholes[0].at[:, :, :, :, by_chunk(k)], enc_buf.at[slot], enc_sem.at[slot]
            ),
        )

    def store(k):
        slot = lax.rem(k, 2)
        return pltpu.make_async_copy(xb_buf.at[slot], xb.at[by_chunk(k)], xb_sem.at[slot])

    def encode(k, first, last, low, high):
        slot = lax.rem(k, 2)
        for copy in loads(k, last):
            copy.wait()
        if not last:

            @pl.when(k + 1 < (high - 1 if high == n_chunks else high))
            def _():
                for copy in loads(k + 1, False):
                    copy.start()

        @pl.when(k >= low + 2)
        def _():
            store(k - 2).wait()

        value = jnp.log1p(count_buf[slot].astype(f32) * scale[...]).astype(b16)
        xb_buf[slot] = value
        store(k).start()
        term = jnp.dot(enc_buf[slot].reshape(width, CHUNK), value, preferred_element_type=f32)
        if first:

            @pl.when(k == 0)
            def _():
                total[...] = pe[...] + term

            @pl.when(k > 0)
            def _():
                total[...] += term

        else:
            total[...] += term

    def encode_job(low, high):
        low, high = low // CHUNK, high // CHUNK
        stop = high - 1 if high == n_chunks else high
        for copy in loads(jnp.int32(low), False):
            copy.start()

        def body(k, carry):
            encode(k, low == 0, False, low, high)
            return carry

        lax.fori_loop(low, stop, body, 0)
        if stop < high:
            for copy in loads(jnp.int32(stop), True):
                copy.start()
            encode(jnp.int32(stop), False, True, low, high)
        for k in range(max(low, high - 2), high):
            store(jnp.int32(k)).wait()

    def fetch_qkv():
        return pltpu.make_async_copy(wholes[1], qkv_buf, qkv_sem.at[0])

    def project():
        fetch_qkv().wait()
        vectors = qkv_buf[:, :, :, :, 3 * width :].reshape(width, 128).astype(f32)
        value = total[...]
        centred = value - jnp.mean(value, axis=0, keepdims=True)
        variance = jnp.mean(centred * centred, axis=0, keepdims=True)
        normed = centred * lax.rsqrt(variance + eps) * vectors[:, 0:1] + vectors[:, 1:2]
        h0[...] = value.T
        a1[...] = normed.T.astype(b16)

        def tile(k):
            weight = qkv_buf[:, :, :, :, by_chunk(k)].reshape(width, CHUNK)
            return jnp.dot(a1[...], weight, preferred_element_type=f32).astype(b16)

        def keys(k, carry):
            mine[:, by_chunk(k)] = tile(k + width // CHUNK)
            return carry

        lax.fori_loop(0, 2 * width // CHUNK, keys, 0)
        kv_own().start()
        kv_copy(0).start()

        def queries(k, carry):
            query[:, by_chunk(k)] = tile(k)
            return carry

        lax.fori_loop(0, width // CHUNK, queries, 0)

    def kv_own():
        return pltpu.make_async_copy(mine, pairs.at[0, 0], kv_sem.at[0])

    def kv_copy(k):
        return pltpu.make_async_remote_copy(
            src_ref=(mine, pairs.at[0])[k],
            dst_ref=(pairs.at[0, 1], pairs.at[1])[k],
            send_sem=kv_send.at[k],
            recv_sem=kv_recv.at[k],
            device_id=({"y": 1 - y}, {"c": 1 - c})[k],
            device_id_type=MESH,
        )

    arrays = [array for array, *_ in jobs]
    enc_jobs = [j for j, array in enumerate(arrays) if array == 0]
    qkv_jobs = [j for j, array in enumerate(arrays) if array == 1]
    at = max(qkv_jobs) + 3

    def between(step, landed):
        if step - 3 in enc_jobs:
            landed(step - 3)
            encode_job(*jobs[step - 3][1:3])
        if step == at:
            for j in qkv_jobs:
                landed(j)
            fetch_qkv().start()
            project()
        if step == at + 2:
            kv_own().wait()
            kv_copy(0).wait_recv()
            kv_copy(1).start()

    gather_kernel(n_h, jobs, n_full, shards, wholes, sems, between)
    kv_copy(0).wait_send()
    kv_copy(1).wait()


def gather_all(shards, n_full, cuts, order, counts, scale, pe, collective_id):
    n_h = lax.axis_size("h")
    if any(shard.shape[0] % 16 for shard in shards):
        shards = [lax.all_gather(s, "h", axis=0, tiled=True) for s in shards]
        n_h = 1
    jobs = []
    for array, piece in order:
        low, high = cuts[array][piece], cuts[array][piece + 1]
        jobs.append((array, low, high, low + (high - low) // 256 * 128))
    n, others, dma = len(jobs), max(n_h - 1, 1), pltpu.SemaphoreType.DMA
    shapes = [(n_h * s.shape[0], s.shape[1]) for s in shards]
    (genes, cells), width, padded = counts.shape, pe.shape[0], shards[0].shape[1]
    tail = counts[genes // CHUNK * CHUNK :]
    tail = jnp.pad(tail, ((0, CHUNK - tail.shape[0]), (0, 0)))
    bf16, f32 = jnp.bfloat16, jnp.float32
    vmem, hbm = pl.BlockSpec(memory_space=pltpu.VMEM), pl.BlockSpec(memory_space=pl.ANY)
    out = pl.pallas_call(
        functools.partial(front_kernel, n_h, jobs, len(shards), n_full),
        out_shape=[
            jax.ShapeDtypeStruct((2, 2, 2) + shape if k < n_full else shape, bf16)
            for k, shape in enumerate(shapes)
        ]
        + [
            jax.ShapeDtypeStruct((padded, cells), bf16),
            jax.ShapeDtypeStruct((cells, width), f32),
            jax.ShapeDtypeStruct((cells, width), bf16),
            jax.ShapeDtypeStruct((cells, width), bf16),
            jax.ShapeDtypeStruct((2, 2, cells, 2 * width), bf16),
        ],
        in_specs=[hbm] * (len(shards) + 2) + [vmem] * 2,
        out_specs=[hbm] * (len(shards) + 1) + [vmem] * 3 + [hbm],
        scratch_shapes=[
            pltpu.VMEM((2, CHUNK, cells), bf16),
            pltpu.VMEM((2, 2, 2, 2, width // 8, CHUNK), bf16),
            pltpu.VMEM((2, CHUNK, cells), bf16),
            pltpu.VMEM((width, cells), f32),
            pltpu.VMEM((2, 2, 2, width // 8, shards[1].shape[1]), bf16),
            pltpu.VMEM((cells, 2 * width), bf16),
            dma((2,)),
            dma((2,)),
            dma((2,)),
            dma((1,)),
            dma((1,)),
            dma((2,)),
            dma((2,)),
            dma((n,)),
            dma((n, others)),
            dma((n, others)),
            dma((n, 8)),
            dma((n, 8)),
        ],
        compiler_params=pltpu.CompilerParams(
            collective_id=collective_id, has_side_effects=True, vmem_limit_bytes=60 * 2**20
        ),
    )(*shards, counts, tail, scale, pe)
    return out[: len(shards)], *out[len(shards) :]


def scatter_kernel(n_h, sections, left_starts, n_weights, with_sum, *refs):
    lefts, vector = refs[:2]
    n_sections = len(sections)
    rights = refs[2 : 2 + 2 * n_sections]
    weights = refs[2 + 2 * n_sections : 2 + 2 * n_sections + n_weights]
    rest = refs[2 + 2 * n_sections + n_weights :]
    out, product = rest[:2]
    total_out = rest[2] if with_sum else None
    (right_buf, weight_buf, product_buf, own, s1, r1, s2, r2, s3, r3, load_sem, weight_sem, product_sem,
     send1, recv1, send2, recv2, send3, recv3) = rest[3 if with_sum else 2 :]
    h, x, y = (lax.axis_index(name) for name in ("h", "x", "y"))
    to_x, to_y = {"x": 1 - x}, {"y": 1 - y}
    w = s3.shape[1]
    rows = w // n_h
    f32, b16 = jnp.float32, jnp.bfloat16
    cells = vector.shape[0]
    starts = [sum(sections[:k]) for k in range(n_sections)]
    n = sum(sections)
    begin = starts[-1]
    greet([{"h": lax.rem(h + d, n_h)} for d in range(1, n_h)] + [to_x, to_y])

    def chunk_of(k):
        return pl.ds(pl.multiple_of(k * CHUNK, CHUNK), CHUNK)

    def loads(i, section, k):
        slot = lax.rem(i, 3)
        return [
            pltpu.make_async_copy(
                rights[2 * section + half].at[chunk_of(k)],
                right_buf.at[slot, :, pl.ds(half * cells, cells)],
                load_sem.at[slot, half],
            )
            for half in (0, 1)
        ]

    def weight_loads(k):
        slot = lax.rem(k, 3)
        size = weights[0].shape[0]
        return [
            pltpu.make_async_copy(
                weight.at[:, chunk_of(k)],
                weight_buf.at[slot, pl.ds(part * size, size)],
                weight_sem.at[slot, part],
            )
            for part, weight in enumerate(weights)
        ]

    def start_loads(i):
        for section, (start, count) in enumerate(zip(starts, sections)):

            @pl.when((i >= start) & (i < start + count))
            def _(section=section, start=start):
                for copy in loads(i, section, i - start):
                    copy.start()
                if section == n_sections - 1:
                    for copy in weight_loads(i - start):
                        copy.start()

    def product_store(k):
        slot = lax.rem(k, 2)
        return pltpu.make_async_copy(product_buf.at[slot], product.at[chunk_of(k)], product_sem.at[slot])

    def hop(i, source, target, send_sem, recv_sem, to):
        slot = lax.rem(i, RING)
        return pltpu.make_async_remote_copy(
            src_ref=source.at[slot], dst_ref=target.at[i], send_sem=send_sem.at[slot],
            recv_sem=recv_sem.at[i], device_id=to, device_id_type=MESH,
        )

    def first(i, odd):
        return hop(i, s1, r1, send1, recv1, to_y if odd else to_x)

    def second(i, odd):
        return hop(i, s2, r2, send2, recv2, to_x if odd else to_y)

    def third(i, d):
        to = lax.rem(h + d, n_h)
        slot = lax.rem(i, RING)
        return pltpu.make_async_remote_copy(
            src_ref=s3.at[slot, pl.ds(to * rows, rows)], dst_ref=r3.at[i, d - 1],
            send_sem=send3.at[slot, d - 1], recv_sem=recv3.at[i, d - 1],
            device_id={"h": to}, device_id_type=MESH,
        )

    def multiply(i, odd):
        slot = lax.rem(i, RING)
        for copy in loads(i, 0, 0):
            copy.wait()
        left = lefts[sum((i + 1024 - start) // 1024 for start in left_starts[1:]) if left_starts[1:] else 0]
        right = right_buf.at[lax.rem(i, 3)]

        @pl.when(i >= RING)
        def _():
            first(i - RING, odd).wait_send()

        part = lax.dot_general(left, right[...], (((1,), (1,)), ((), ())), preferred_element_type=f32)
        own[slot, :w] = part[:w]
        if odd:
            own[slot, w:] = part[2 * w : 3 * w]
            s1[slot, :w] = part[w : 2 * w].astype(b16)
            s1[slot, w:] = part[3 * w :].astype(b16)
        else:
            own[slot, w:] = part[w : 2 * w]
            s1[slot] = part[2 * w :].astype(b16)
        first(i, odd).start()

        def beside(k):
            for copy in weight_loads(k):
                copy.wait()
            weight = weight_buf[lax.rem(k, 3)]

            @pl.when(k >= 2)
            def _():
                product_store(k - 2).wait()

            value = jnp.dot(vector[...], weight, preferred_element_type=f32)
            product_buf[lax.rem(k, 2)] = value.T.astype(product_buf.dtype)
            product_store(k).start()
            if with_sum:
                term = jnp.dot(weight, right[:, :cells], preferred_element_type=f32)

                @pl.when(k == 0)
                def _():
                    total_out[...] = term

                @pl.when(k > 0)
                def _():
                    total_out[...] += term

        if begin == 0:
            beside(i)
        else:

            @pl.when(i >= begin)
            def _():
                beside(i - begin)

        start_loads(i + 2)

    def pass_on(i, odd):
        slot = lax.rem(i, RING)
        first(i, odd).wait_recv()

        @pl.when(i >= RING)
        def _():
            second(i - RING, odd).wait_send()

        s2[slot] = (own[slot, w:] + r1[i, w:].astype(f32)).astype(b16)
        second(i, odd).start()

    def keep(i, odd):
        slot = lax.rem(i, RING)
        second(i, odd).wait_recv()
        part = own[slot, :w] + r1[i, :w].astype(f32) + r2[i].astype(f32)
        if n_h == 1:
            out[i] = part.astype(b16)
            return

        @pl.when(i >= RING)
        def _():
            for d in range(1, n_h):
                third(i - RING, d).wait_send()

        s3[slot] = part.astype(b16)
        for d in range(1, n_h):
            third(i, d).start()

    def finish(i, odd):
        if n_h == 1:
            return
        total = s3[lax.rem(i, RING), pl.ds(h * rows, rows)].astype(f32)
        for d in range(1, n_h):
            third(i, d).wait_recv()
            total = total + r3[i, d - 1].astype(f32)
        out[i] = total

    start_loads(jnp.int32(0))
    start_loads(jnp.int32(1))
    pairs = (n + 1) // 2

    def step(p, carry):
        for lag, stage in enumerate((multiply, pass_on, keep, finish)):
            for odd in (0, 1):
                i = 2 * (p - lag) + odd

                @pl.when((i >= 0) & (i < n))
                def _(stage=stage, i=i, odd=odd):
                    stage(i, odd)

        return carry

    lax.fori_loop(0, pairs + 3, step, 0)
    for i in range(max(n - RING, 0), n):
        first(i, i % 2).wait_send()
        second(i, i % 2).wait_send()
        for d in range(1, n_h):
            third(i, d).wait_send()
    for k in range(max(sections[-1] - 2, 0), sections[-1]):
        product_store(k).wait()


def scatter_all(lefts, left_starts, rights, vector, weights, product_type, with_sum, collective_id):
    sections = [own.shape[0] // CHUNK for own, _ in rights]
    n, cells = sum(sections), vector.shape[0]
    features = vector.shape[1]
    w = lefts.shape[1] // 4
    n_h = lax.axis_size("h")
    rows = w // n_h
    inner_h = n_h if rows % 16 == 0 else 1
    dma, bf16, f32 = pltpu.SemaphoreType.DMA, jnp.bfloat16, jnp.float32
    vmem, hbm = pl.BlockSpec(memory_space=pltpu.VMEM), pl.BlockSpec(memory_space=pl.ANY)
    others = max(inner_h - 1, 1)
    part_shape = jax.ShapeDtypeStruct((n, rows, CHUNK), f32)
    if inner_h == 1:
        part_shape = jax.ShapeDtypeStruct((n, w, CHUNK), bf16)
    out_shape = [part_shape, jax.ShapeDtypeStruct((sections[-1] * CHUNK, cells), product_type)]
    out_specs = [vmem, hbm]
    if with_sum:
        out_shape.append(jax.ShapeDtypeStruct((features, cells), f32))
        out_specs.append(vmem)
    part, *more = pl.pallas_call(
        functools.partial(
            scatter_kernel, inner_h, sections, left_starts, len(weights), with_sum
        ),
        out_shape=out_shape,
        in_specs=[vmem, vmem] + [hbm] * (2 * len(rights) + len(weights)),
        out_specs=out_specs,
        scratch_shapes=[
            pltpu.VMEM((3, CHUNK, 2 * cells), bf16),
            pltpu.VMEM((3, features, CHUNK), bf16),
            pltpu.VMEM((2, CHUNK, cells), product_type),
            pltpu.VMEM((RING, 2 * w, CHUNK), f32),
            pltpu.VMEM((RING, 2 * w, CHUNK), bf16),
            pltpu.VMEM((n, 2 * w, CHUNK), bf16),
            pltpu.VMEM((RING, w, CHUNK), bf16),
            pltpu.VMEM((n, w, CHUNK), bf16),
            pltpu.VMEM((RING, w, CHUNK), bf16),
            pltpu.VMEM((n, others, w // inner_h, CHUNK), bf16),
            dma((3, 2)),
            dma((3, len(weights))),
            dma((2,)),
            dma((RING,)),
            dma((n,)),
            dma((RING,)),
            dma((n,)),
            dma((RING, others)),
            dma((n, others)),
        ],
        compiler_params=pltpu.CompilerParams(
            collective_id=collective_id, has_side_effects=True, vmem_limit_bytes=60 * 2**20
        ),
    )(lefts, vector, *(half for pair in rights for half in pair), *weights)
    if inner_h == 1:
        part = lax.psum_scatter(part, "h", scatter_dimension=1, tiled=True).astype(f32)
    return part, *more


def own_half(left):
    half = left.shape[1] // 2
    return jnp.concatenate([left[:, :half], swap(left[:, half:], "c")], axis=0)


def scatter_group(rows_all):
    part = rows_all.astype(jnp.bfloat16).reshape((2, 2, rows_all.shape[0] // 4, -1))
    got = swap(part[1], "c").astype(jnp.float32)
    part = (part[0].astype(jnp.float32) + got).astype(jnp.bfloat16)
    return part[0].astype(jnp.float32) + swap(part[1], "y").astype(jnp.float32)


def left_of(left, pieces):
    left = own_half(relative(left, 1)).T
    n_h = lax.axis_size("h")
    left = left.reshape(4, n_h, pieces, -1, left.shape[1])
    return left.transpose(2, 0, 1, 3, 4).reshape(pieces, -1, left.shape[-1])


def both_cores(right):
    return right, swap(right, "c")


def columns_of(chunks):
    return chunks.transpose(1, 0, 2).reshape(chunks.shape[1], -1)


def on_device(
    counts,
    library,
    coords,
    lengths,
    cotangent,
    w_enc,
    w_qkv,
    w_out,
    gain_one,
    shift_one,
    w_up,
    w_down,
    gain_two,
    shift_two,
    w_dec,
):
    rows = counts.shape[0]
    width = w_qkv.shape[1] // 3
    heads = HEADS
    head_width = width // heads
    att_scale = head_width ** (-0.5)
    group_size = 4
    slots = rows * group_size
    scale = 10000.0 / library
    genes = counts.shape[1]
    padded = -(-genes // CHUNK) * CHUNK
    counts_f = counts.astype(jnp.float32)
    cot = jnp.pad(cotangent.T, ((0, padded - genes), (0, 0)))
    cot_pair = both_cores(cot)
    pe = by_owner(positions(coords, width), 1)
    ends = jnp.cumsum(lengths[0])
    group = [
        (lax.axis_index("y") ^ by_y) * 2 + (lax.axis_index("c") ^ by_c)
        for by_c in range(2)
        for by_y in range(2)
    ]
    place = jnp.concatenate([at * rows + jnp.arange(rows, dtype=jnp.int32) for at in group])
    seg_all = jnp.sum((place[:, None] >= ends[None, :]).astype(jnp.int32), axis=1)
    same = (seg_all[:rows, None] == seg_all[None, :])[None]
    vectors = jnp.stack([gain_one, shift_one, gain_two, shift_two], axis=1)
    vectors = jnp.pad(vectors, ((0, 0), (0, 124)))
    pad = ((0, 0), (0, padded - genes))
    quarter = padded // CHUNK // 4 * CHUNK
    gene_cuts = [0, quarter, 2 * quarter, 3 * quarter, padded]
    shards = [
        jnp.pad(w_enc.T, pad),
        jnp.concatenate([w_qkv, vectors], axis=1),
        by_owner(w_out, 1),
        by_owner(w_up, 1),
        by_owner(w_down, 1),
        jnp.pad(w_dec.T, pad),
    ]
    cuts = [gene_cuts, [0, width // 2 * 3, 3 * width + 128], [0, width]]
    cuts += [[0, 2 * width, 4 * width], [0, width // 2, width], [0, padded]]
    order = [(0, 0), (0, 1), (0, 2), (0, 3), (1, 0), (1, 1), (2, 0), (3, 0), (3, 1), (4, 0), (4, 1), (5, 0)]
    gathered, xb, h0, a1, query, kv_all = gather_all(
        shards, 5, cuts, order, counts.T, scale[None, :], pe.T, 0
    )
    xb_pair = both_cores(xb)
    enc_all, qkv_all, out_all, up_all, down_all = (
        w.reshape(-1, w.shape[-1]) for w in gathered[:5]
    )
    vectors = qkv_all[:, 3 * width :].astype(jnp.float32).T
    qkv_all = qkv_all[:, : 3 * width]
    g1f, b1f, g2f, b2f = vectors[0], vectors[1], vectors[2], vectors[3]
    query = query.reshape(rows, heads, head_width)
    kv_all = kv_all.reshape(slots, -1)
    dec_own = gathered[5]
    middle = dec_own.shape[1] // 256 * 128
    by_x, by_y = swap(dec_own, "x"), swap(dec_own, "y")
    far = (swap(by_x[:, :middle], "y"), swap(by_y[:, middle:], "x"))
    dec_parts = [dec_own, by_y, by_x, jnp.concatenate(far, axis=1)]
    dec_parts += [swap(part, "c") for part in dec_parts]
    keys = kv_all[:, :width].reshape(slots, heads, head_width)
    values = kv_all[:, width:].reshape(slots, heads, head_width)

    def scores_of():
        raw = (
            jnp.einsum("qhd,khd->hqk", query, keys, preferred_element_type=jnp.float32) * att_scale
        )
        return jnp.where(same, raw, -1000000000.0)

    scores = scores_of()
    top = jnp.max(scores, axis=-1, keepdims=True)
    expo = jnp.exp(scores - top)
    total = jnp.sum(expo, axis=-1, keepdims=True)
    log_total = top + jnp.log(total)
    probs_b = (expo / total).astype(jnp.bfloat16)
    attended = jnp.einsum("hqk,khd->qhd", probs_b, values, preferred_element_type=jnp.float32)
    attended_b = attended.reshape(rows, width).astype(jnp.bfloat16)
    attended_b = by_owner(attended_b, 1)
    h1 = h0 + matmul(attended_b, out_all)
    a2 = layer_norm(h1, g2f, b2f).astype(jnp.bfloat16)
    hidden = matmul(a2, up_all)
    act = jax.nn.gelu(hidden, approximate=False).astype(jnp.bfloat16)
    h2 = h1 + matmul(act, down_all)
    hb = h2.astype(jnp.bfloat16)
    grad_dec, logits, dh2 = scatter_all(
        left_of(hb, 1), [0], [cot_pair], relative(hb, 1), dec_parts, jnp.bfloat16, True, 1
    )
    own_rows = grad_dec.shape[1]
    grad_dec = columns_of(grad_dec)[:, :genes].T
    logits = logits[:genes].T
    dh2 = relative(dh2, 0).T
    dfb = dh2.astype(jnp.bfloat16)
    d_act = contract_cols(dfb, down_all)
    slope = jax.vjp(lambda v: jax.nn.gelu(v, approximate=False), hidden)[1](d_act)[0]
    d_hidden = slope.astype(jnp.bfloat16)
    da2 = contract_cols(d_hidden, up_all)
    norm_pull = jax.vjp(layer_norm, h1, g2f, b2f)[1]
    dh1_norm, grad_gain_two, grad_shift_two = norm_pull(da2)
    dh1 = dh2 + dh1_norm
    dab = dh1.astype(jnp.bfloat16)
    d_attended = contract_cols(dab, out_all).astype(jnp.bfloat16)
    d_attended = from_owner(d_attended, 1).reshape(rows, heads, head_width)
    probs = jnp.exp(scores_of() - log_total)
    probs_b = probs.astype(jnp.bfloat16)
    d_probs = jnp.einsum("qhd,khd->hqk", d_attended, values, preferred_element_type=jnp.float32)
    inner = jnp.sum(probs * d_probs, axis=-1, keepdims=True)
    d_scores = (probs * (d_probs - inner)).astype(jnp.bfloat16)
    d_query = (
        jnp.einsum("hqk,khd->qhd", d_scores, keys, preferred_element_type=jnp.float32) * att_scale
    )
    d_keys = (
        jnp.einsum("hqk,qhd->khd", d_scores, query, preferred_element_type=jnp.float32) * att_scale
    )
    d_values = jnp.einsum("hqk,qhd->khd", probs_b, d_attended, preferred_element_type=jnp.float32)
    d_kv = jnp.concatenate([d_keys.reshape(slots, width), d_values.reshape(slots, width)], axis=1)
    d_kv = scatter_group(d_kv)
    d_qkv = jnp.concatenate([d_query.reshape(rows, width), d_kv], axis=1).astype(jnp.bfloat16)
    da1 = contract_cols(d_qkv, qkv_all)
    first_pull = jax.vjp(layer_norm, h0, g1f, b1f)[1]
    dh0_norm, grad_gain_one, grad_shift_one = first_pull(da1)
    vectors_b = jnp.stack([grad_gain_one, grad_shift_one, grad_gain_two, grad_shift_two])
    vectors_b = jnp.pad(vectors_b, ((0, rows - 4), (0, 0))).astype(jnp.bfloat16)
    unit = jnp.eye(rows, dtype=jnp.bfloat16)
    dh0b = (dh1 + dh0_norm).astype(jnp.bfloat16)

    lefts = [left_of(a2, 1), left_of(act, act.shape[1] // width), left_of(attended_b, 1)]
    lefts += [left_of(a1, 1), left_of(vectors_b, 1), left_of(dh0b, 1)]
    pieces = (4 * width,) + (width,) * 5 + (3 * width, rows)
    left_starts = [sum(pieces[:k]) // CHUNK for k in range(len(pieces) + 1)]
    rights = [d_hidden.T] + [dfb.T] * 4 + [dab.T]
    grads, d_xb = scatter_all(
        jnp.concatenate(lefts, axis=0),
        left_starts,
        [both_cores(jnp.concatenate(rights, axis=0)), both_cores(d_qkv.T), (unit, unit), xb_pair],
        dh0b,
        [enc_all],
        jnp.float32,
        False,
        2,
    )
    ends = [0]
    for columns in (4 * width, 4 * width, width, 3 * width, rows):
        ends.append(ends[-1] + columns // CHUNK)
    grad_up, grad_down, grad_out, grad_qkv, grad_vectors, grad_enc = (
        grads[low:high] for low, high in zip(ends, ends[1:] + [grads.shape[0]])
    )
    grad_up, grad_out, grad_qkv, grad_enc = (
        columns_of(g) for g in (grad_up, grad_out, grad_qkv, grad_enc)
    )
    grad_gain_one, grad_shift_one, grad_gain_two, grad_shift_two = (
        grad_vectors[0, :, k] for k in range(4)
    )
    grad_down = grad_down.reshape(4, -1, own_rows, CHUNK).transpose(0, 2, 1, 3)
    grad_down = grad_down.reshape(4 * own_rows, -1)
    grad_out, grad_up, grad_down = (from_owner(g, 1) for g in (grad_out, grad_up, grad_down))
    grad_enc = grad_enc[:, :genes].T
    d_xb = d_xb[:genes].T
    counts_grad = d_xb * scale[:, None] / (1.0 + counts_f * scale[:, None])
    return (
        logits,
        counts_grad,
        grad_enc,
        grad_qkv,
        grad_out,
        grad_gain_one,
        grad_shift_one,
        grad_up,
        grad_down,
        grad_gain_two,
        grad_shift_two,
        grad_dec,
    )


ALL = ("h", "x", "y", "c")


def solution(mesh):
    n_dp, n_fsdp = mesh.shape["dp"], mesh.shape["fsdp"]
    mesh = Mesh(mesh.devices.reshape((n_dp // 2, 2, 2, n_fsdp // 2)), ALL)
    placed = (
        P(ALL, None),
        P(ALL),
        P(None, ALL),
        P(("h", "x"), None),
        P(ALL, None),
        P(None, ALL),
        P(ALL, None),
        P(ALL, None),
        P(ALL),
        P(ALL),
        P(ALL, None),
        P(ALL, None),
        P(ALL),
        P(ALL),
        P(None, ALL),
    )
    return jax.shard_map(
        on_device,
        mesh=mesh,
        in_specs=placed,
        out_specs=(
            P(ALL, None),
            P(ALL, None),
            P(None, ALL),
            P(ALL, None),
            P(ALL, None),
            P(ALL),
            P(ALL),
            P(ALL, None),
            P(ALL, None),
            P(ALL),
            P(ALL),
            P(None, ALL),
        ),
        check_vma=False,
    )
```

```python
import functools
import math

import jax
import jax.numpy as jnp
from jax import lax
from jax.experimental import pallas as pl
from jax.experimental.pallas import tpu as pltpu
from jax.sharding import Mesh
from jax.sharding import PartitionSpec as P

HEADS = 16
MESH = pl.DeviceIdType.MESH
RING = 8
CHUNK = 256


eps = 1e-05


def layer_norm(value, gain, shift):
    mean = jnp.mean(value, axis=1, keepdims=True)
    centred = value - mean
    variance = jnp.mean(centred * centred, axis=1, keepdims=True)
    return centred * lax.rsqrt(variance + eps) * gain + shift


def positions(coords, width):
    quarter = width // 4
    freqs = 0.05 * jnp.exp(-jnp.arange(quarter, dtype=jnp.float32) * (math.log(10000.0) / quarter))
    along_x = coords[0].astype(jnp.float32)[:, None] * freqs[None, :]
    along_y = coords[1].astype(jnp.float32)[:, None] * freqs[None, :]
    return jnp.concatenate(
        [jnp.sin(along_x), jnp.cos(along_x), jnp.sin(along_y), jnp.cos(along_y)], axis=1
    )


def contract_rows(left, right):
    return lax.dot_general(
        left, right, (((0,), (0,)), ((), ())), preferred_element_type=jnp.float32
    )


def contract_cols(left, right):
    return lax.dot_general(
        left, right, (((1,), (1,)), ((), ())), preferred_element_type=jnp.float32
    )


def matmul(left, right):
    return jnp.dot(left, right, preferred_element_type=jnp.float32)


def swap(value, axis):
    return lax.ppermute(value, axis, [(0, 1), (1, 0)])


def by_owner(value, axis):
    n_h = lax.axis_size("h")
    at = value.shape
    block = at[axis] // (8 * n_h)
    split = value.reshape(at[:axis] + (n_h, 2, 2, 2, block) + at[axis + 1 :])
    order = list(range(axis)) + [axis + 3, axis + 1, axis + 2, axis, axis + 4]
    order += list(range(axis + 5, split.ndim))
    return split.transpose(order).reshape(at)


def from_owner(value, axis):
    n_h = lax.axis_size("h")
    at = value.shape
    block = at[axis] // (8 * n_h)
    split = value.reshape(at[:axis] + (2, 2, 2, n_h, block) + at[axis + 1 :])
    order = list(range(axis)) + [axis + 3, axis + 1, axis + 2, axis, axis + 4]
    order += list(range(axis + 5, split.ndim))
    return split.transpose(order).reshape(at)


def relative(value, axis):
    eighth = value.shape[axis] // 8
    mine = lax.axis_index("c") * 4 + lax.axis_index("x") * 2 + lax.axis_index("y")
    parts = [
        lax.dynamic_slice_in_dim(value, (mine ^ part) * eighth, eighth, axis) for part in range(8)
    ]
    return jnp.concatenate(parts, axis=axis)


def greet(peers):
    barrier = pltpu.get_barrier_semaphore()
    for peer in peers:
        pl.semaphore_signal(barrier, inc=1, device_id=peer, device_id_type=MESH)
    pl.semaphore_wait(barrier, len(peers))


def gather_kernel(n_h, jobs, n_full, shards, wholes, sems, between):
    own_sem, h_send, h_recv, send, recv = sems
    h, x, y, c = (lax.axis_index(name) for name in ("h", "x", "y", "c"))
    h = 0 if n_h == 1 else h
    to_x, to_y, to_c = {"x": 1 - x}, {"y": 1 - y}, {"c": 1 - c}
    greet([{"h": lax.rem(h + d, n_h)} for d in range(1, n_h)] + [to_x, to_y, to_c])

    def rows_of(job, at):
        array, low, high, _ = job
        rows = shards[array].shape[0]
        place = (pl.ds(at * rows, rows), pl.ds(low, high - low))
        return wholes[array].at[(c, x, y, *place) if array < n_full else place]

    def h_copy(j, d):
        array, low, high, _ = jobs[j]
        return pltpu.make_async_remote_copy(
            src_ref=shards[array].at[:, pl.ds(low, high - low)],
            dst_ref=rows_of(jobs[j], h),
            send_sem=h_send.at[j, d - 1],
            recv_sem=h_recv.at[j, d - 1],
            device_id={"h": lax.rem(h + d, n_h)},
            device_id_type=MESH,
        )

    def own_copy(j):
        array, low, high, _ = jobs[j]
        return pltpu.make_async_copy(
            shards[array].at[:, pl.ds(low, high - low)], rows_of(jobs[j], h), own_sem.at[j]
        )

    def block_copy(j, k, block, to, columns):
        view = wholes[jobs[j][0]].at[(*block, slice(None), pl.ds(columns[0], columns[1] - columns[0]))]
        return pltpu.make_async_remote_copy(
            src_ref=view,
            dst_ref=view,
            send_sem=send.at[j, k],
            recv_sem=recv.at[j, k],
            device_id=to,
            device_id_type=MESH,
        )

    own, by_x, by_y, far = (c, x, y), (c, 1 - x, y), (c, x, 1 - y), (c, 1 - x, 1 - y)

    def copy(j, k):
        _, low, high, middle = jobs[j]
        block, to, columns = [
            (own, to_x, (low, high)),
            (own, to_y, (low, high)),
            (own, to_c, (low, high)),
            (by_x, to_y, (low, middle)),
            (by_y, to_x, (middle, high)),
            (by_x, to_c, (low, high)),
            (by_y, to_c, (low, high)),
            (far, to_c, (low, high)),
        ][k]
        return block_copy(j, k, block, to, columns)

    def start_h(j):
        own_copy(j).start()
        for d in range(1, n_h):
            h_copy(j, d).start()

    whole = set()

    def landed(j):
        if j not in whole:
            whole.add(j)
            for k in (2, 5, 6, 7):
                copy(j, k).wait_recv()

    n = sum(array < n_full for array, *_ in jobs)
    ahead = 2
    for j in range(ahead):
        start_h(j)
    for step in range(n + 2):
        if step < n:
            own_copy(step).wait()
            for d in range(1, n_h):
                h_copy(step, d).wait_recv()
            for k in (0, 1, 2):
                copy(step, k).start()
            if step + ahead < len(jobs):
                start_h(step + ahead)
        if 0 <= step - 1 < n:
            for k in (0, 1):
                copy(step - 1, k).wait_recv()
            for k in (3, 4, 5, 6):
                copy(step - 1, k).start()
        if 0 <= step - 2 < n:
            for k in (3, 4):
                copy(step - 2, k).wait_recv()
            copy(step - 2, 7).start()
        between(step, landed)
    for j in range(n + ahead, len(jobs)):
        start_h(j)
    for j in range(n, len(jobs)):
        own_copy(j).wait()
        for d in range(1, n_h):
            h_copy(j, d).wait_recv()
    for j in range(len(jobs)):
        for d in range(1, n_h):
            h_copy(j, d).wait_send()
    for j in range(n):
        for k in range(8):
            copy(j, k).wait_send()
        landed(j)


def front_kernel(n_h, jobs, n_arrays, n_full, *refs):
    shards, (counts, tail, scale, pe) = refs[:n_arrays], refs[n_arrays : n_arrays + 4]
    rest = refs[n_arrays + 4 :]
    wholes, (xb, h0, a1, query, pairs) = rest[:n_arrays], rest[n_arrays : n_arrays + 5]
    (count_buf, enc_buf, xb_buf, total, qkv_buf, mine, count_sem, enc_sem, xb_sem, qkv_sem, kv_sem,
     kv_send, kv_recv, *sems) = rest[n_arrays + 5 :]
    y, c = lax.axis_index("y"), lax.axis_index("c")
    f32, b16 = jnp.float32, jnp.bfloat16
    width = h0.shape[1]
    n_chunks = xb.shape[0] // CHUNK
    by_chunk = lambda k: pl.ds(pl.multiple_of(k * CHUNK, CHUNK), CHUNK)

    def loads(k, last):
        slot = lax.rem(k, 2)
        source = tail if last else counts.at[by_chunk(k)]
        return (
            pltpu.make_async_copy(source, count_buf.at[slot], count_sem.at[slot]),
            pltpu.make_async_copy(
                wholes[0].at[:, :, :, :, by_chunk(k)], enc_buf.at[slot], enc_sem.at[slot]
            ),
        )

    def store(k):
        slot = lax.rem(k, 2)
        return pltpu.make_async_copy(xb_buf.at[slot], xb.at[by_chunk(k)], xb_sem.at[slot])

    def encode(k, first, last, low, high):
        slot = lax.rem(k, 2)
        for copy in loads(k, last):
            copy.wait()
        if not last:

            @pl.when(k + 1 < (high - 1 if high == n_chunks else high))
            def _():
                for copy in loads(k + 1, False):
                    copy.start()

        @pl.when(k >= low + 2)
        def _():
            store(k - 2).wait()

        value = jnp.log1p(count_buf[slot].astype(f32) * scale[...]).astype(b16)
        xb_buf[slot] = value
        store(k).start()
        term = jnp.dot(enc_buf[slot].reshape(width, CHUNK), value, preferred_element_type=f32)
        if first:

            @pl.when(k == 0)
            def _():
                total[...] = pe[...] + term

            @pl.when(k > 0)
            def _():
                total[...] += term

        else:
            total[...] += term

    def encode_job(low, high):
        low, high = low // CHUNK, high // CHUNK
        stop = high - 1 if high == n_chunks else high
        for copy in loads(jnp.int32(low), False):
            copy.start()

        def body(k, carry):
            encode(k, low == 0, False, low, high)
            return carry

        lax.fori_loop(low, stop, body, 0)
        if stop < high:
            for copy in loads(jnp.int32(stop), True):
                copy.start()
            encode(jnp.int32(stop), False, True, low, high)
        for k in range(max(low, high - 2), high):
            store(jnp.int32(k)).wait()

    def fetch_qkv():
        return pltpu.make_async_copy(wholes[1], qkv_buf, qkv_sem.at[0])

    def project():
        fetch_qkv().wait()
        vectors = qkv_buf[:, :, :, :, 3 * width :].reshape(width, 128).astype(f32)
        value = total[...]
        centred = value - jnp.mean(value, axis=0, keepdims=True)
        variance = jnp.mean(centred * centred, axis=0, keepdims=True)
        normed = centred * lax.rsqrt(variance + eps) * vectors[:, 0:1] + vectors[:, 1:2]
        h0[...] = value.T
        a1[...] = normed.T.astype(b16)

        def tile(k):
            weight = qkv_buf[:, :, :, :, by_chunk(k)].reshape(width, CHUNK)
            return jnp.dot(a1[...], weight, preferred_element_type=f32).astype(b16)

        def keys(k, carry):
            mine[:, by_chunk(k)] = tile(k + width // CHUNK)
            return carry

        lax.fori_loop(0, 2 * width // CHUNK, keys, 0)
        kv_own().start()
        kv_copy(0).start()

        def queries(k, carry):
            query[:, by_chunk(k)] = tile(k)
            return carry

        lax.fori_loop(0, width // CHUNK, queries, 0)

    def kv_own():
        return pltpu.make_async_copy(mine, pairs.at[0, 0], kv_sem.at[0])

    def kv_copy(k):
        return pltpu.make_async_remote_copy(
            src_ref=(mine, pairs.at[0])[k],
            dst_ref=(pairs.at[0, 1], pairs.at[1])[k],
            send_sem=kv_send.at[k],
            recv_sem=kv_recv.at[k],
            device_id=({"y": 1 - y}, {"c": 1 - c})[k],
            device_id_type=MESH,
        )

    arrays = [array for array, *_ in jobs]
    enc_jobs = [j for j, array in enumerate(arrays) if array == 0]
    qkv_jobs = [j for j, array in enumerate(arrays) if array == 1]
    at = max(qkv_jobs) + 3

    def between(step, landed):
        if step - 3 in enc_jobs:
            landed(step - 3)
            encode_job(*jobs[step - 3][1:3])
        if step == at:
            for j in qkv_jobs:
                landed(j)
            fetch_qkv().start()
            project()
        if step == at + 2:
            kv_own().wait()
            kv_copy(0).wait_recv()
            kv_copy(1).start()

    gather_kernel(n_h, jobs, n_full, shards, wholes, sems, between)
    kv_copy(0).wait_send()
    kv_copy(1).wait()


def gather_all(shards, n_full, cuts, order, counts, scale, pe, collective_id):
    n_h = lax.axis_size("h")
    if any(shard.shape[0] % 16 for shard in shards):
        shards = [lax.all_gather(s, "h", axis=0, tiled=True) for s in shards]
        n_h = 1
    jobs = []
    for array, piece in order:
        low, high = cuts[array][piece], cuts[array][piece + 1]
        jobs.append((array, low, high, low + (high - low) // 256 * 128))
    n, others, dma = len(jobs), max(n_h - 1, 1), pltpu.SemaphoreType.DMA
    shapes = [(n_h * s.shape[0], s.shape[1]) for s in shards]
    (genes, cells), width, padded = counts.shape, pe.shape[0], shards[0].shape[1]
    tail = counts[genes // CHUNK * CHUNK :]
    tail = jnp.pad(tail, ((0, CHUNK - tail.shape[0]), (0, 0)))
    bf16, f32 = jnp.bfloat16, jnp.float32
    vmem, hbm = pl.BlockSpec(memory_space=pltpu.VMEM), pl.BlockSpec(memory_space=pl.ANY)
    out = pl.pallas_call(
        functools.partial(front_kernel, n_h, jobs, len(shards), n_full),
        out_shape=[
            jax.ShapeDtypeStruct((2, 2, 2) + shape if k < n_full else shape, bf16)
            for k, shape in enumerate(shapes)
        ]
        + [
            jax.ShapeDtypeStruct((padded, cells), bf16),
            jax.ShapeDtypeStruct((cells, width), f32),
            jax.ShapeDtypeStruct((cells, width), bf16),
            jax.ShapeDtypeStruct((cells, width), bf16),
            jax.ShapeDtypeStruct((2, 2, cells, 2 * width), bf16),
        ],
        in_specs=[hbm] * (len(shards) + 2) + [vmem] * 2,
        out_specs=[hbm] * (len(shards) + 1) + [vmem] * 3 + [hbm],
        scratch_shapes=[
            pltpu.VMEM((2, CHUNK, cells), bf16),
            pltpu.VMEM((2, 2, 2, 2, width // 8, CHUNK), bf16),
            pltpu.VMEM((2, CHUNK, cells), bf16),
            pltpu.VMEM((width, cells), f32),
            pltpu.VMEM((2, 2, 2, width // 8, shards[1].shape[1]), bf16),
            pltpu.VMEM((cells, 2 * width), bf16),
            dma((2,)),
            dma((2,)),
            dma((2,)),
            dma((1,)),
            dma((1,)),
            dma((2,)),
            dma((2,)),
            dma((n,)),
            dma((n, others)),
            dma((n, others)),
            dma((n, 8)),
            dma((n, 8)),
        ],
        compiler_params=pltpu.CompilerParams(
            collective_id=collective_id, has_side_effects=True, vmem_limit_bytes=60 * 2**20
        ),
    )(*shards, counts, tail, scale, pe)
    return out[: len(shards)], *out[len(shards) :]


def scatter_kernel(n_h, sections, left_starts, lefts, rights, out, scratch, peers, prefetch, beside, after):
    (right_buf, own, s1, r1, s2, r2, s3, r3, load_sem, send1, recv1, send2, recv2, send3, recv3) = scratch
    h, x, y = (lax.axis_index(name) for name in ("h", "x", "y"))
    to_x, to_y = {"x": 1 - x}, {"y": 1 - y}
    w = s3.shape[1]
    rows = w // n_h
    f32, b16 = jnp.float32, jnp.bfloat16
    n_sections = len(sections)
    starts = [sum(sections[:k]) for k in range(n_sections)]
    n = sum(sections)
    cells = right_buf.shape[2] // 2
    greet([{"h": lax.rem(h + d, n_h)} for d in range(1, n_h)] + [to_x, to_y] + peers)

    def loads(i, section, k):
        slot = lax.rem(i, 3)
        return [
            pltpu.make_async_copy(
                rights[2 * section + half].at[chunk_of(k)],
                right_buf.at[slot, :, pl.ds(half * cells, cells)],
                load_sem.at[slot, half],
            )
            for half in (0, 1)
        ]

    def start_loads(i):
        for section, (start, count) in enumerate(zip(starts, sections)):

            @pl.when((i >= start) & (i < start + count))
            def _(section=section, start=start):
                for copy in loads(i, section, i - start):
                    copy.start()
                prefetch(section, i - start)

    def hop(i, source, target, send_sem, recv_sem, to):
        slot = lax.rem(i, RING)
        return pltpu.make_async_remote_copy(
            src_ref=source.at[slot], dst_ref=target.at[i], send_sem=send_sem.at[slot],
            recv_sem=recv_sem.at[i], device_id=to, device_id_type=MESH,
        )

    def first(i, odd):
        return hop(i, s1, r1, send1, recv1, to_y if odd else to_x)

    def second(i, odd):
        return hop(i, s2, r2, send2, recv2, to_x if odd else to_y)

    def third(i, d):
        to = lax.rem(h + d, n_h)
        slot = lax.rem(i, RING)
        return pltpu.make_async_remote_copy(
            src_ref=s3.at[slot, pl.ds(to * rows, rows)], dst_ref=r3.at[i, d - 1],
            send_sem=send3.at[slot, d - 1], recv_sem=recv3.at[i, d - 1],
            device_id={"h": to}, device_id_type=MESH,
        )

    def multiply(i, odd):
        slot = lax.rem(i, RING)
        for copy in loads(i, 0, 0):
            copy.wait()
        left = lefts[sum((i + 1024 - start) // 1024 for start in left_starts[1:]) if left_starts[1:] else 0]
        right = right_buf.at[lax.rem(i, 3)]

        @pl.when(i >= RING)
        def _():
            first(i - RING, odd).wait_send()

        part = lax.dot_general(left, right[...], (((1,), (1,)), ((), ())), preferred_element_type=f32)
        own[slot, :w] = part[:w]
        if odd:
            own[slot, w:] = part[2 * w : 3 * w]
            s1[slot, :w] = part[w : 2 * w].astype(b16)
            s1[slot, w:] = part[3 * w :].astype(b16)
        else:
            own[slot, w:] = part[w : 2 * w]
            s1[slot] = part[2 * w :].astype(b16)
        first(i, odd).start()

        beside(i, right, odd)
        start_loads(i + 2)

    def pass_on(i, odd):
        slot = lax.rem(i, RING)
        first(i, odd).wait_recv()

        @pl.when(i >= RING)
        def _():
            second(i - RING, odd).wait_send()

        s2[slot] = (own[slot, w:] + r1[i, w:].astype(f32)).astype(b16)
        second(i, odd).start()

    def keep(i, odd):
        slot = lax.rem(i, RING)
        second(i, odd).wait_recv()
        part = own[slot, :w] + r1[i, :w].astype(f32) + r2[i].astype(f32)
        if n_h == 1:
            out[i] = part.astype(b16)
            return

        @pl.when(i >= RING)
        def _():
            for d in range(1, n_h):
                third(i - RING, d).wait_send()

        s3[slot] = part.astype(b16)
        for d in range(1, n_h):
            third(i, d).start()

    def finish(i, odd):
        if n_h == 1:
            return
        total = s3[lax.rem(i, RING), pl.ds(h * rows, rows)].astype(f32)
        for d in range(1, n_h):
            third(i, d).wait_recv()
            total = total + r3[i, d - 1].astype(f32)
        out[i] = total

    start_loads(jnp.int32(0))
    start_loads(jnp.int32(1))
    pairs = (n + 1) // 2

    def step(p, carry):
        for lag, stage in enumerate((multiply, pass_on, keep, finish)):
            for odd in (0, 1):
                i = 2 * (p - lag) + odd

                @pl.when((i >= 0) & (i < n))
                def _(stage=stage, i=i, odd=odd):
                    stage(i, odd)

        after(p)
        return carry

    lax.fori_loop(0, pairs + 3, step, 0)
    for i in range(max(n - RING, 0), n):
        first(i, i % 2).wait_send()
        second(i, i % 2).wait_send()
        for d in range(1, n_h):
            third(i, d).wait_send()


def chunk_of(k):
    return pl.ds(pl.multiple_of(k * CHUNK, CHUNK), CHUNK)


def product_kernel(n_h, sections, left_starts, n_weights, with_sum, *refs):
    lefts, vector = refs[:2]
    n_rights = 2 * len(sections)
    rights, weights = refs[2 : 2 + n_rights], refs[2 + n_rights : 2 + n_rights + n_weights]
    rest = refs[2 + n_rights + n_weights :]
    out, product = rest[:2]
    total_out = rest[2] if with_sum else None
    weight_buf, product_buf, weight_sem, product_sem, *scratch = rest[3 if with_sum else 2 :]
    begin, count = sum(sections[:-1]), sections[-1]
    cells = vector.shape[0]

    def weight_loads(k):
        slot = lax.rem(k, 3)
        size = weights[0].shape[0]
        return [
            pltpu.make_async_copy(
                weight.at[:, chunk_of(k)],
                weight_buf.at[slot, pl.ds(part * size, size)],
                weight_sem.at[slot, part],
            )
            for part, weight in enumerate(weights)
        ]

    def product_store(k):
        slot = lax.rem(k, 2)
        return pltpu.make_async_copy(product_buf.at[slot], product.at[chunk_of(k)], product_sem.at[slot])

    def prefetch(section, k):
        if section == len(sections) - 1:
            for copy in weight_loads(k):
                copy.start()

    def multiply(k, right):
        for copy in weight_loads(k):
            copy.wait()
        weight = weight_buf[lax.rem(k, 3)]

        @pl.when(k >= 2)
        def _():
            product_store(k - 2).wait()

        value = jnp.dot(vector[...], weight, preferred_element_type=jnp.float32)
        product_buf[lax.rem(k, 2)] = value.T.astype(product_buf.dtype)
        product_store(k).start()
        if with_sum:
            term = jnp.dot(weight, right[:, :cells], preferred_element_type=jnp.float32)

            @pl.when(k == 0)
            def _():
                total_out[...] = term

            @pl.when(k > 0)
            def _():
                total_out[...] += term

    def beside(i, right, odd):
        if begin == 0:
            multiply(i, right)
        else:

            @pl.when(i >= begin)
            def _():
                multiply(i - begin, right)

    scatter_kernel(
        n_h, sections, left_starts, lefts, rights, out, scratch, [], prefetch, beside, lambda p: None
    )
    for k in range(max(count - 2, 0), count):
        product_store(k).wait()


def attention_kernel(n_h, sections, left_starts, scale, *refs):
    lefts, query, pairs, d_out, log_total, seg_keys, seg_mine = refs[:7]
    n_rights = 2 * len(sections)
    rights = refs[7 : 7 + n_rights]
    out, d_qkv, d_pairs, by_core, by_y, d_query, send, recv, *scratch = refs[7 + n_rights :]
    y, c = lax.axis_index("y"), lax.axis_index("c")
    f32, b16 = jnp.float32, jnp.bfloat16
    cells, width = query.shape
    slots = 4 * cells
    n_pairs, head = width // 128, 64
    into = (((1,), (1,)), ((), ()))

    def backward(j, half):
        lanes = pl.ds(pl.multiple_of(j * 128, 128), 128)
        value_lanes = pl.ds(pl.multiple_of(width + j * 128, 128), 128)
        side = slice(half * head, (half + 1) * head)
        keys = pairs[:, :, :, lanes].reshape(slots, 128)[:, side]
        values = pairs[:, :, :, value_lanes].reshape(slots, 128)[:, side]
        mine, above = query[:, lanes][:, side], d_out[:, lanes][:, side]
        scores = lax.dot_general(keys, mine, into, preferred_element_type=f32) * scale
        scores = jnp.where(seg_keys[...] == seg_mine[...], scores, -1000000000.0)
        probs = jnp.exp(scores - log_total[pl.ds(2 * j + half, 1), :])
        d_probs = lax.dot_general(values, above, into, preferred_element_type=f32)
        inner = jnp.sum(probs * d_probs, axis=0, keepdims=True)
        d_scores = (probs * (d_probs - inner)).astype(b16)
        d_keys = jnp.dot(d_scores, mine, preferred_element_type=f32) * scale
        d_values = jnp.dot(probs.astype(b16), above, preferred_element_type=f32)
        d_pairs[0, j, :, side] = d_keys.astype(b16)
        d_pairs[1, j, :, side] = d_values.astype(b16)
        turned = keys.astype(f32).T.astype(b16)
        d_query[side] = jnp.dot(turned, d_scores, preferred_element_type=f32) * scale
        if half:
            d_qkv[:, lanes] = d_query[...].T.astype(b16)

    def to_core():
        return pltpu.make_async_remote_copy(
            src_ref=d_pairs.at[:, :, pl.ds(2 * cells, 2 * cells)], dst_ref=by_core,
            send_sem=send.at[0], recv_sem=recv.at[0], device_id={"c": 1 - c}, device_id_type=MESH,
        )

    def to_y():
        return pltpu.make_async_remote_copy(
            src_ref=d_pairs.at[:, :, pl.ds(cells, cells)], dst_ref=by_y,
            send_sem=send.at[1], recv_sem=recv.at[1], device_id={"y": 1 - y}, device_id_type=MESH,
        )

    def beside(i, right, odd):
        @pl.when(i < 2 * n_pairs)
        def _():
            backward(i // 2, odd)

    def after(p):
        @pl.when(p == n_pairs)
        def _():
            to_core().start()

        @pl.when(p == n_pairs + 2)
        def _():
            to_core().wait_recv()

            def add(j, carry):
                for kind in (0, 1):
                    total = d_pairs[kind, j, : 2 * cells].astype(f32) + by_core[kind, j].astype(f32)
                    d_pairs[kind, j, : 2 * cells] = total.astype(b16)
                return carry

            lax.fori_loop(0, n_pairs, add, 0)
            to_y().start()

    scatter_kernel(
        n_h, sections, left_starts, lefts, rights, out, scratch, [{"c": 1 - c}],
        lambda section, k: None, beside, after,
    )
    to_y().wait_recv()

    def add(j, carry):
        for kind in (0, 1):
            lanes = pl.ds(pl.multiple_of((kind + 1) * width + j * 128, 128), 128)
            total = d_pairs[kind, j, :cells].astype(f32) + by_y[kind, j].astype(f32)
            d_qkv[:, lanes] = total.astype(b16)
        return carry

    lax.fori_loop(0, n_pairs, add, 0)
    to_core().wait_send()
    to_y().wait_send()


def scatter_call(kernel, lefts, rights, operands, more_operands, out_shapes, out_specs, scratch, collective_id):
    sections = [own.shape[0] // CHUNK for own, _ in rights]
    n, cells = sum(sections), rights[0][0].shape[1]
    w = lefts.shape[1] // 4
    n_h = lax.axis_size("h")
    rows = w // n_h
    inner_h = n_h if rows % 16 == 0 else 1
    dma, bf16, f32 = pltpu.SemaphoreType.DMA, jnp.bfloat16, jnp.float32
    vmem, hbm = pl.BlockSpec(memory_space=pltpu.VMEM), pl.BlockSpec(memory_space=pl.ANY)
    others = max(inner_h - 1, 1)
    part_shape = jax.ShapeDtypeStruct((n, rows, CHUNK), f32)
    if inner_h == 1:
        part_shape = jax.ShapeDtypeStruct((n, w, CHUNK), bf16)
    part, *more = pl.pallas_call(
        functools.partial(kernel, inner_h, sections),
        out_shape=[part_shape] + out_shapes,
        in_specs=[vmem] * (1 + len(operands)) + [hbm] * (2 * len(rights) + len(more_operands)),
        out_specs=[vmem] + out_specs,
        scratch_shapes=scratch
        + [
            pltpu.VMEM((3, CHUNK, 2 * cells), bf16),
            pltpu.VMEM((RING, 2 * w, CHUNK), f32),
            pltpu.VMEM((RING, 2 * w, CHUNK), bf16),
            pltpu.VMEM((n, 2 * w, CHUNK), bf16),
            pltpu.VMEM((RING, w, CHUNK), bf16),
            pltpu.VMEM((n, w, CHUNK), bf16),
            pltpu.VMEM((RING, w, CHUNK), bf16),
            pltpu.VMEM((n, others, w // inner_h, CHUNK), bf16),
            dma((3, 2)),
            dma((RING,)),
            dma((n,)),
            dma((RING,)),
            dma((n,)),
            dma((RING, others)),
            dma((n, others)),
        ],
        compiler_params=pltpu.CompilerParams(
            collective_id=collective_id, has_side_effects=True, vmem_limit_bytes=60 * 2**20
        ),
    )(lefts, *operands, *(half for pair in rights for half in pair), *more_operands)
    if inner_h == 1:
        part = lax.psum_scatter(part, "h", scatter_dimension=1, tiled=True).astype(f32)
    return part, *more


def scatter_product(lefts, left_starts, rights, vector, weights, product_type, with_sum, collective_id):
    (cells, features), columns = vector.shape, rights[-1][0].shape[0]
    dma = pltpu.SemaphoreType.DMA
    vmem, hbm = pl.BlockSpec(memory_space=pltpu.VMEM), pl.BlockSpec(memory_space=pl.ANY)

    def kernel(n_h, sections, *refs):
        product_kernel(n_h, sections, left_starts, len(weights), with_sum, *refs)

    return scatter_call(
        kernel,
        lefts,
        rights,
        [vector],
        weights,
        [jax.ShapeDtypeStruct((columns, cells), product_type)]
        + [jax.ShapeDtypeStruct((features, cells), jnp.float32)] * with_sum,
        [hbm] + [vmem] * with_sum,
        [
            pltpu.VMEM((3, features, CHUNK), jnp.bfloat16),
            pltpu.VMEM((2, CHUNK, cells), product_type),
            dma((3, len(weights))),
            dma((2,)),
        ],
        collective_id,
    )


def scatter_attention(lefts, left_starts, rights, query, pairs, d_out, log_total, seg, scale, collective_id):
    cells, width = query.shape
    bf16, vmem = jnp.bfloat16, pl.BlockSpec(memory_space=pltpu.VMEM)

    def kernel(n_h, sections, *refs):
        attention_kernel(n_h, sections, left_starts, scale, *refs)

    return scatter_call(
        kernel,
        lefts,
        rights,
        [query, pairs, d_out, log_total, seg[:, None], seg[None, :cells]],
        [],
        [jax.ShapeDtypeStruct((cells, 3 * width), bf16)],
        [vmem],
        [
            pltpu.VMEM((2, width // 128, 4 * cells, 128), bf16),
            pltpu.VMEM((2, width // 128, 2 * cells, 128), bf16),
            pltpu.VMEM((2, width // 128, cells, 128), bf16),
            pltpu.VMEM((128, cells), jnp.float32),
            pltpu.SemaphoreType.DMA((2,)),
            pltpu.SemaphoreType.DMA((2,)),
        ],
        collective_id,
    )


def own_half(left):
    half = left.shape[1] // 2
    return jnp.concatenate([left[:, :half], swap(left[:, half:], "c")], axis=0)


def left_of(left, pieces):
    left = own_half(relative(left, 1)).T
    n_h = lax.axis_size("h")
    left = left.reshape(4, n_h, pieces, -1, left.shape[1])
    return left.transpose(2, 0, 1, 3, 4).reshape(pieces, -1, left.shape[-1])


def both_cores(right):
    return right, swap(right, "c")


def columns_of(chunks):
    return chunks.transpose(1, 0, 2).reshape(chunks.shape[1], -1)


def on_device(
    counts,
    library,
    coords,
    lengths,
    cotangent,
    w_enc,
    w_qkv,
    w_out,
    gain_one,
    shift_one,
    w_up,
    w_down,
    gain_two,
    shift_two,
    w_dec,
):
    rows = counts.shape[0]
    width = w_qkv.shape[1] // 3
    heads = HEADS
    head_width = width // heads
    att_scale = head_width ** (-0.5)
    group_size = 4
    slots = rows * group_size
    scale = 10000.0 / library
    genes = counts.shape[1]
    padded = -(-genes // CHUNK) * CHUNK
    counts_f = counts.astype(jnp.float32)
    cot = jnp.pad(cotangent.T, ((0, padded - genes), (0, 0)))
    cot_pair = both_cores(cot)
    pe = by_owner(positions(coords, width), 1)
    ends = jnp.cumsum(lengths[0])
    group = [
        (lax.axis_index("y") ^ by_y) * 2 + (lax.axis_index("c") ^ by_c)
        for by_c in range(2)
        for by_y in range(2)
    ]
    place = jnp.concatenate([at * rows + jnp.arange(rows, dtype=jnp.int32) for at in group])
    seg_all = jnp.sum((place[:, None] >= ends[None, :]).astype(jnp.int32), axis=1)
    same = (seg_all[:rows, None] == seg_all[None, :])[None]
    vectors = jnp.stack([gain_one, shift_one, gain_two, shift_two], axis=1)
    vectors = jnp.pad(vectors, ((0, 0), (0, 124)))
    pad = ((0, 0), (0, padded - genes))
    quarter = padded // CHUNK // 4 * CHUNK
    gene_cuts = [0, quarter, 2 * quarter, 3 * quarter, padded]
    shards = [
        jnp.pad(w_enc.T, pad),
        jnp.concatenate([w_qkv, vectors], axis=1),
        by_owner(w_out, 1),
        by_owner(w_up, 1),
        by_owner(w_down, 1),
        jnp.pad(w_dec.T, pad),
    ]
    cuts = [gene_cuts, [0, width // 2 * 3, 3 * width + 128], [0, width]]
    cuts += [[0, 2 * width, 4 * width], [0, width // 2, width], [0, padded]]
    order = [(0, 0), (0, 1), (0, 2), (0, 3), (1, 0), (1, 1), (2, 0), (3, 0), (3, 1), (4, 0), (4, 1), (5, 0)]
    gathered, xb, h0, a1, query, kv_all = gather_all(
        shards, 5, cuts, order, counts.T, scale[None, :], pe.T, 0
    )
    xb_pair = both_cores(xb)
    enc_all, qkv_all, out_all, up_all, down_all = (
        w.reshape(-1, w.shape[-1]) for w in gathered[:5]
    )
    vectors = qkv_all[:, 3 * width :].astype(jnp.float32).T
    qkv_all = qkv_all[:, : 3 * width]
    g1f, b1f, g2f, b2f = vectors[0], vectors[1], vectors[2], vectors[3]
    kv_pairs, query_b = kv_all, query
    query = query.reshape(rows, heads, head_width)
    kv_all = kv_all.reshape(slots, -1)
    dec_own = gathered[5]
    middle = dec_own.shape[1] // 256 * 128
    by_x, by_y = swap(dec_own, "x"), swap(dec_own, "y")
    far = (swap(by_x[:, :middle], "y"), swap(by_y[:, middle:], "x"))
    dec_parts = [dec_own, by_y, by_x, jnp.concatenate(far, axis=1)]
    dec_parts += [swap(part, "c") for part in dec_parts]
    keys = kv_all[:, :width].reshape(slots, heads, head_width)
    values = kv_all[:, width:].reshape(slots, heads, head_width)

    def scores_of():
        raw = (
            jnp.einsum("qhd,khd->hqk", query, keys, preferred_element_type=jnp.float32) * att_scale
        )
        return jnp.where(same, raw, -1000000000.0)

    scores = scores_of()
    top = jnp.max(scores, axis=-1, keepdims=True)
    expo = jnp.exp(scores - top)
    total = jnp.sum(expo, axis=-1, keepdims=True)
    log_total = top + jnp.log(total)
    probs_b = (expo / total).astype(jnp.bfloat16)
    attended = jnp.einsum("hqk,khd->qhd", probs_b, values, preferred_element_type=jnp.float32)
    attended_b = attended.reshape(rows, width).astype(jnp.bfloat16)
    attended_b = by_owner(attended_b, 1)
    h1 = h0 + matmul(attended_b, out_all)
    a2 = layer_norm(h1, g2f, b2f).astype(jnp.bfloat16)
    hidden = matmul(a2, up_all)
    act = jax.nn.gelu(hidden, approximate=False).astype(jnp.bfloat16)
    h2 = h1 + matmul(act, down_all)
    hb = h2.astype(jnp.bfloat16)
    grad_dec, logits, dh2 = scatter_product(
        left_of(hb, 1), [0], [cot_pair], relative(hb, 1), dec_parts, jnp.bfloat16, True, 1
    )
    own_rows = grad_dec.shape[1]
    grad_dec = columns_of(grad_dec)[:, :genes].T
    logits = logits[:genes].T
    dh2 = relative(dh2, 0).T
    dfb = dh2.astype(jnp.bfloat16)
    d_act = contract_cols(dfb, down_all)
    slope = jax.vjp(lambda v: jax.nn.gelu(v, approximate=False), hidden)[1](d_act)[0]
    d_hidden = slope.astype(jnp.bfloat16)
    da2 = contract_cols(d_hidden, up_all)
    norm_pull = jax.vjp(layer_norm, h1, g2f, b2f)[1]
    dh1_norm, grad_gain_two, grad_shift_two = norm_pull(da2)
    dh1 = dh2 + dh1_norm
    dab = dh1.astype(jnp.bfloat16)
    d_attended = contract_cols(dab, out_all).astype(jnp.bfloat16)
    d_attended = from_owner(d_attended, 1)
    lefts = [left_of(a2, 1), left_of(act, act.shape[1] // width), left_of(attended_b, 1)]
    pieces = (4 * width,) + (width,) * 4
    rights = [d_hidden.T] + [dfb.T] * 4 + [dab.T]
    grads, d_qkv = scatter_attention(
        jnp.concatenate(lefts, axis=0),
        [sum(pieces[:k]) // CHUNK for k in range(len(pieces) + 1)],
        [both_cores(jnp.concatenate(rights, axis=0))],
        query_b,
        kv_pairs,
        d_attended,
        log_total[:, :, 0],
        seg_all,
        att_scale,
        2,
    )
    ends = [0]
    for columns in (4 * width, 4 * width, width):
        ends.append(ends[-1] + columns // CHUNK)
    grad_up, grad_down, grad_out = (grads[low:high] for low, high in zip(ends, ends[1:]))
    grad_up, grad_out = columns_of(grad_up), columns_of(grad_out)
    grad_down = grad_down.reshape(4, -1, own_rows, CHUNK).transpose(0, 2, 1, 3)
    grad_down = grad_down.reshape(4 * own_rows, -1)
    grad_out, grad_up, grad_down = (from_owner(g, 1) for g in (grad_out, grad_up, grad_down))
    da1 = contract_cols(d_qkv, qkv_all)
    first_pull = jax.vjp(layer_norm, h0, g1f, b1f)[1]
    dh0_norm, grad_gain_one, grad_shift_one = first_pull(da1)
    vectors_b = jnp.stack([grad_gain_one, grad_shift_one, grad_gain_two, grad_shift_two])
    vectors_b = jnp.pad(vectors_b, ((0, rows - 4), (0, 0))).astype(jnp.bfloat16)
    unit = jnp.eye(rows, dtype=jnp.bfloat16)
    dh0b = (dh1 + dh0_norm).astype(jnp.bfloat16)

    lefts = [left_of(a1, 1), left_of(vectors_b, 1), left_of(dh0b, 1)]
    grads, d_xb = scatter_product(
        jnp.concatenate(lefts, axis=0),
        [0, 3 * width // CHUNK, (3 * width + rows) // CHUNK],
        [both_cores(d_qkv.T), (unit, unit), xb_pair],
        dh0b,
        [enc_all],
        jnp.float32,
        False,
        3,
    )
    ends = [0]
    for columns in (3 * width, rows):
        ends.append(ends[-1] + columns // CHUNK)
    grad_qkv, grad_vectors, grad_enc = (
        grads[low:high] for low, high in zip(ends, ends[1:] + [grads.shape[0]])
    )
    grad_qkv, grad_enc = columns_of(grad_qkv), columns_of(grad_enc)
    grad_gain_one, grad_shift_one, grad_gain_two, grad_shift_two = (
        grad_vectors[0, :, k] for k in range(4)
    )
    grad_enc = grad_enc[:, :genes].T
    d_xb = d_xb[:genes].T
    counts_grad = d_xb * scale[:, None] / (1.0 + counts_f * scale[:, None])
    return (
        logits,
        counts_grad,
        grad_enc,
        grad_qkv,
        grad_out,
        grad_gain_one,
        grad_shift_one,
        grad_up,
        grad_down,
        grad_gain_two,
        grad_shift_two,
        grad_dec,
    )


ALL = ("h", "x", "y", "c")


def solution(mesh):
    n_dp, n_fsdp = mesh.shape["dp"], mesh.shape["fsdp"]
    mesh = Mesh(mesh.devices.reshape((n_dp // 2, 2, 2, n_fsdp // 2)), ALL)
    placed = (
        P(ALL, None),
        P(ALL),
        P(None, ALL),
        P(("h", "x"), None),
        P(ALL, None),
        P(None, ALL),
        P(ALL, None),
        P(ALL, None),
        P(ALL),
        P(ALL),
        P(ALL, None),
        P(ALL, None),
        P(ALL),
        P(ALL),
        P(None, ALL),
    )
    return jax.shard_map(
        on_device,
        mesh=mesh,
        in_specs=placed,
        out_specs=(
            P(ALL, None),
            P(ALL, None),
            P(None, ALL),
            P(ALL, None),
            P(ALL, None),
            P(ALL),
            P(ALL),
            P(ALL, None),
            P(ALL, None),
            P(ALL),
            P(ALL),
            P(None, ALL),
        ),
        check_vma=False,
    )
```

```python
import functools
import math

import jax
import jax.numpy as jnp
from jax import lax
from jax.experimental import pallas as pl
from jax.experimental.pallas import tpu as pltpu
from jax.sharding import Mesh
from jax.sharding import PartitionSpec as P

HEADS = 16
MESH = pl.DeviceIdType.MESH
RING = 8
CHUNK = 256


eps = 1e-05


def layer_norm(value, gain, shift):
    mean = jnp.mean(value, axis=1, keepdims=True)
    centred = value - mean
    variance = jnp.mean(centred * centred, axis=1, keepdims=True)
    return centred * lax.rsqrt(variance + eps) * gain + shift


def positions(coords, width):
    quarter = width // 4
    freqs = 0.05 * jnp.exp(-jnp.arange(quarter, dtype=jnp.float32) * (math.log(10000.0) / quarter))
    along_x = coords[0].astype(jnp.float32)[:, None] * freqs[None, :]
    along_y = coords[1].astype(jnp.float32)[:, None] * freqs[None, :]
    return jnp.concatenate(
        [jnp.sin(along_x), jnp.cos(along_x), jnp.sin(along_y), jnp.cos(along_y)], axis=1
    )


def contract_rows(left, right):
    return lax.dot_general(
        left, right, (((0,), (0,)), ((), ())), preferred_element_type=jnp.float32
    )


def contract_cols(left, right):
    return lax.dot_general(
        left, right, (((1,), (1,)), ((), ())), preferred_element_type=jnp.float32
    )


def matmul(left, right):
    return jnp.dot(left, right, preferred_element_type=jnp.float32)


def swap(value, axis):
    return lax.ppermute(value, axis, [(0, 1), (1, 0)])


def by_owner(value, axis):
    n_h = lax.axis_size("h")
    at = value.shape
    block = at[axis] // (8 * n_h)
    split = value.reshape(at[:axis] + (n_h, 2, 2, 2, block) + at[axis + 1 :])
    order = list(range(axis)) + [axis + 3, axis + 1, axis + 2, axis, axis + 4]
    order += list(range(axis + 5, split.ndim))
    return split.transpose(order).reshape(at)


def from_owner(value, axis):
    n_h = lax.axis_size("h")
    at = value.shape
    block = at[axis] // (8 * n_h)
    split = value.reshape(at[:axis] + (2, 2, 2, n_h, block) + at[axis + 1 :])
    order = list(range(axis)) + [axis + 3, axis + 1, axis + 2, axis, axis + 4]
    order += list(range(axis + 5, split.ndim))
    return split.transpose(order).reshape(at)


def relative(value, axis):
    eighth = value.shape[axis] // 8
    mine = lax.axis_index("c") * 4 + lax.axis_index("x") * 2 + lax.axis_index("y")
    parts = [
        lax.dynamic_slice_in_dim(value, (mine ^ part) * eighth, eighth, axis) for part in range(8)
    ]
    return jnp.concatenate(parts, axis=axis)


def greet(peers):
    barrier = pltpu.get_barrier_semaphore()
    for peer in peers:
        pl.semaphore_signal(barrier, inc=1, device_id=peer, device_id_type=MESH)
    pl.semaphore_wait(barrier, len(peers))


def gather_kernel(n_h, jobs, n_full, shards, wholes, sems, between):
    own_sem, h_send, h_recv, send, recv = sems
    h, x, y, c = (lax.axis_index(name) for name in ("h", "x", "y", "c"))
    h = 0 if n_h == 1 else h
    to_x, to_y, to_c = {"x": 1 - x}, {"y": 1 - y}, {"c": 1 - c}
    greet([{"h": lax.rem(h + d, n_h)} for d in range(1, n_h)] + [to_x, to_y, to_c])

    def rows_of(job, at):
        array, low, high, _ = job
        rows = shards[array].shape[0]
        place = (pl.ds(at * rows, rows), pl.ds(low, high - low))
        return wholes[array].at[(c, x, y, *place) if array < n_full else place]

    def h_copy(j, d):
        array, low, high, _ = jobs[j]
        return pltpu.make_async_remote_copy(
            src_ref=shards[array].at[:, pl.ds(low, high - low)],
            dst_ref=rows_of(jobs[j], h),
            send_sem=h_send.at[j, d - 1],
            recv_sem=h_recv.at[j, d - 1],
            device_id={"h": lax.rem(h + d, n_h)},
            device_id_type=MESH,
        )

    def own_copy(j):
        array, low, high, _ = jobs[j]
        return pltpu.make_async_copy(
            shards[array].at[:, pl.ds(low, high - low)], rows_of(jobs[j], h), own_sem.at[j]
        )

    def block_copy(j, k, block, to, columns):
        view = wholes[jobs[j][0]].at[(*block, slice(None), pl.ds(columns[0], columns[1] - columns[0]))]
        return pltpu.make_async_remote_copy(
            src_ref=view,
            dst_ref=view,
            send_sem=send.at[j, k],
            recv_sem=recv.at[j, k],
            device_id=to,
            device_id_type=MESH,
        )

    own, by_x, by_y, far = (c, x, y), (c, 1 - x, y), (c, x, 1 - y), (c, 1 - x, 1 - y)

    def copy(j, k):
        _, low, high, middle = jobs[j]
        block, to, columns = [
            (own, to_x, (low, high)),
            (own, to_y, (low, high)),
            (own, to_c, (low, high)),
            (by_x, to_y, (low, middle)),
            (by_y, to_x, (middle, high)),
            (by_x, to_c, (low, high)),
            (by_y, to_c, (low, high)),
            (far, to_c, (low, high)),
        ][k]
        return block_copy(j, k, block, to, columns)

    def start_h(j):
        own_copy(j).start()
        for d in range(1, n_h):
            h_copy(j, d).start()

    whole = set()

    def landed(j):
        if j not in whole:
            whole.add(j)
            for k in (2, 5, 6, 7):
                copy(j, k).wait_recv()

    n = sum(array < n_full for array, *_ in jobs)
    start_h(0)
    start_h(1)
    for step in range(n + 2):
        if step < n:
            own_copy(step).wait()
            for d in range(1, n_h):
                h_copy(step, d).wait_recv()
            for k in (0, 1, 2):
                copy(step, k).start()
            for j in (2, 3) if step == 0 else (step + 3,):
                if j < n:
                    start_h(j)
            if 0 < step and n + step - 1 < len(jobs):
                start_h(n + step - 1)
        if 0 <= step - 1 < n:
            for k in (0, 1):
                copy(step - 1, k).wait_recv()
            for k in (3, 4, 5, 6):
                copy(step - 1, k).start()
        if 0 <= step - 2 < n:
            for k in (3, 4):
                copy(step - 2, k).wait_recv()
            copy(step - 2, 7).start()
        between(step, landed)
    for j in range(n, len(jobs)):
        own_copy(j).wait()
        for d in range(1, n_h):
            h_copy(j, d).wait_recv()
    for j in range(len(jobs)):
        for d in range(1, n_h):
            h_copy(j, d).wait_send()
    for j in range(n):
        for k in range(8):
            copy(j, k).wait_send()
        landed(j)


def front_kernel(n_h, jobs, n_arrays, n_full, *refs):
    shards, (counts, tail, scale, pe) = refs[:n_arrays], refs[n_arrays : n_arrays + 4]
    rest = refs[n_arrays + 4 :]
    wholes, (xb, h0, a1, query, pairs) = rest[:n_arrays], rest[n_arrays : n_arrays + 5]
    (count_buf, enc_buf, xb_buf, total, qkv_buf, mine, count_sem, enc_sem, xb_sem, qkv_sem, kv_sem,
     kv_send, kv_recv, *sems) = rest[n_arrays + 5 :]
    y, c = lax.axis_index("y"), lax.axis_index("c")
    f32, b16 = jnp.float32, jnp.bfloat16
    width = h0.shape[1]
    n_chunks = xb.shape[0] // CHUNK
    by_chunk = lambda k: pl.ds(pl.multiple_of(k * CHUNK, CHUNK), CHUNK)

    def loads(k, last):
        slot = lax.rem(k, 2)
        source = tail if last else counts.at[by_chunk(k)]
        return (
            pltpu.make_async_copy(source, count_buf.at[slot], count_sem.at[slot]),
            pltpu.make_async_copy(
                wholes[0].at[:, :, :, :, by_chunk(k)], enc_buf.at[slot], enc_sem.at[slot]
            ),
        )

    def store(k):
        slot = lax.rem(k, 2)
        return pltpu.make_async_copy(xb_buf.at[slot], xb.at[by_chunk(k)], xb_sem.at[slot])

    def encode(k, first, last, low, high):
        slot = lax.rem(k, 2)
        for copy in loads(k, last):
            copy.wait()
        if not last:

            @pl.when(k + 1 < (high - 1 if high == n_chunks else high))
            def _():
                for copy in loads(k + 1, False):
                    copy.start()

        @pl.when(k >= low + 2)
        def _():
            store(k - 2).wait()

        value = jnp.log1p(count_buf[slot].astype(f32) * scale[...]).astype(b16)
        xb_buf[slot] = value
        store(k).start()
        term = jnp.dot(enc_buf[slot].reshape(width, CHUNK), value, preferred_element_type=f32)
        if first:

            @pl.when(k == 0)
            def _():
                total[...] = pe[...] + term

            @pl.when(k > 0)
            def _():
                total[...] += term

        else:
            total[...] += term

    def encode_job(low, high):
        low, high = low // CHUNK, high // CHUNK
        stop = high - 1 if high == n_chunks else high
        for copy in loads(jnp.int32(low), False):
            copy.start()

        def body(k, carry):
            encode(k, low == 0, False, low, high)
            return carry

        lax.fori_loop(low, stop, body, 0)
        if stop < high:
            for copy in loads(jnp.int32(stop), True):
                copy.start()
            encode(jnp.int32(stop), False, True, low, high)
        for k in range(max(low, high - 2), high):
            store(jnp.int32(k)).wait()

    def fetch_qkv():
        return pltpu.make_async_copy(wholes[1], qkv_buf, qkv_sem.at[0])

    def project():
        fetch_qkv().wait()
        vectors = qkv_buf[:, :, :, :, 3 * width :].reshape(width, 128).astype(f32)
        value = total[...]
        centred = value - jnp.mean(value, axis=0, keepdims=True)
        variance = jnp.mean(centred * centred, axis=0, keepdims=True)
        normed = centred * lax.rsqrt(variance + eps) * vectors[:, 0:1] + vectors[:, 1:2]
        h0[...] = value.T
        a1[...] = normed.T.astype(b16)

        def tile(k):
            weight = qkv_buf[:, :, :, :, by_chunk(k)].reshape(width, CHUNK)
            return jnp.dot(a1[...], weight, preferred_element_type=f32).astype(b16)

        def keys(k, carry):
            mine[:, by_chunk(k)] = tile(k + width // CHUNK)
            return carry

        lax.fori_loop(0, 2 * width // CHUNK, keys, 0)
        kv_own().start()
        kv_copy(0).start()

        def queries(k, carry):
            query[:, by_chunk(k)] = tile(k)
            return carry

        lax.fori_loop(0, width // CHUNK, queries, 0)

    def kv_own():
        return pltpu.make_async_copy(mine, pairs.at[0, 0], kv_sem.at[0])

    def kv_copy(k):
        return pltpu.make_async_remote_copy(
            src_ref=(mine, pairs.at[0])[k],
            dst_ref=(pairs.at[0, 1], pairs.at[1])[k],
            send_sem=kv_send.at[k],
            recv_sem=kv_recv.at[k],
            device_id=({"y": 1 - y}, {"c": 1 - c})[k],
            device_id_type=MESH,
        )

    arrays = [array for array, *_ in jobs]
    enc_jobs = [j for j, array in enumerate(arrays) if array == 0]
    qkv_jobs = [j for j, array in enumerate(arrays) if array == 1]
    at = max(qkv_jobs) + 3

    def between(step, landed):
        if step - 3 in enc_jobs:
            landed(step - 3)
            encode_job(*jobs[step - 3][1:3])
        if step == at:
            for j in qkv_jobs:
                landed(j)
            fetch_qkv().start()
            project()
        if step == at + 2:
            kv_own().wait()
            kv_copy(0).wait_recv()
            kv_copy(1).start()

    gather_kernel(n_h, jobs, n_full, shards, wholes, sems, between)
    kv_copy(0).wait_send()
    kv_copy(1).wait()


def gather_all(shards, n_full, cuts, order, counts, scale, pe, collective_id):
    n_h = lax.axis_size("h")
    if any(shard.shape[0] % 16 for shard in shards):
        shards = [lax.all_gather(s, "h", axis=0, tiled=True) for s in shards]
        n_h = 1
    jobs = []
    for array, piece in order:
        low, high = cuts[array][piece], cuts[array][piece + 1]
        jobs.append((array, low, high, low + (high - low) // 256 * 128))
    n, others, dma = len(jobs), max(n_h - 1, 1), pltpu.SemaphoreType.DMA
    shapes = [(n_h * s.shape[0], s.shape[1]) for s in shards]
    (genes, cells), width, padded = counts.shape, pe.shape[0], shards[0].shape[1]
    tail = counts[genes // CHUNK * CHUNK :]
    tail = jnp.pad(tail, ((0, CHUNK - tail.shape[0]), (0, 0)))
    bf16, f32 = jnp.bfloat16, jnp.float32
    vmem, hbm = pl.BlockSpec(memory_space=pltpu.VMEM), pl.BlockSpec(memory_space=pl.ANY)
    out = pl.pallas_call(
        functools.partial(front_kernel, n_h, jobs, len(shards), n_full),
        out_shape=[
            jax.ShapeDtypeStruct((2, 2, 2) + shape if k < n_full else shape, bf16)
            for k, shape in enumerate(shapes)
        ]
        + [
            jax.ShapeDtypeStruct((padded, cells), bf16),
            jax.ShapeDtypeStruct((cells, width), f32),
            jax.ShapeDtypeStruct((cells, width), bf16),
            jax.ShapeDtypeStruct((cells, width), bf16),
            jax.ShapeDtypeStruct((2, 2, cells, 2 * width), bf16),
        ],
        in_specs=[hbm] * (len(shards) + 2) + [vmem] * 2,
        out_specs=[hbm] * (len(shards) + 1) + [vmem] * 3 + [hbm],
        scratch_shapes=[
            pltpu.VMEM((2, CHUNK, cells), bf16),
            pltpu.VMEM((2, 2, 2, 2, width // 8, CHUNK), bf16),
            pltpu.VMEM((2, CHUNK, cells), bf16),
            pltpu.VMEM((width, cells), f32),
            pltpu.VMEM((2, 2, 2, width // 8, shards[1].shape[1]), bf16),
            pltpu.VMEM((cells, 2 * width), bf16),
            dma((2,)),
            dma((2,)),
            dma((2,)),
            dma((1,)),
            dma((1,)),
            dma((2,)),
            dma((2,)),
            dma((n,)),
            dma((n, others)),
            dma((n, others)),
            dma((n, 8)),
            dma((n, 8)),
        ],
        compiler_params=pltpu.CompilerParams(
            collective_id=collective_id, has_side_effects=True, vmem_limit_bytes=60 * 2**20
        ),
    )(*shards, counts, tail, scale, pe)
    return out[: len(shards)], *out[len(shards) :]


def scatter_kernel(n_h, sections, periods, left_starts, lefts, rights, out, scratch, peers, prefetch, beside, after):
    (right_buf, own, s1, r1, s2, r2, s3, r3, load_sem, send1, recv1, send2, recv2, send3, recv3) = scratch
    h, x, y = (lax.axis_index(name) for name in ("h", "x", "y"))
    to_x, to_y = {"x": 1 - x}, {"y": 1 - y}
    w = s3.shape[1]
    rows = w // n_h
    f32, b16 = jnp.float32, jnp.bfloat16
    n_sections = len(sections)
    starts = [sum(sections[:k]) for k in range(n_sections)]
    n = sum(sections)
    cells = right_buf.shape[2] // 2
    greet([{"h": lax.rem(h + d, n_h)} for d in range(1, n_h)] + [to_x, to_y] + peers)

    def loads(i, section, k):
        slot = lax.rem(i, 3)
        return [
            pltpu.make_async_copy(
                rights[2 * section + half].at[chunk_of(k)],
                right_buf.at[slot, :, pl.ds(half * cells, cells)],
                load_sem.at[slot, half],
            )
            for half in (0, 1)
        ]

    def start_loads(i):
        for section, (start, count) in enumerate(zip(starts, sections)):

            @pl.when((i >= start) & (i < start + count))
            def _(section=section, start=start):
                for copy in loads(i, section, lax.rem(i - start, periods[section])):
                    copy.start()
                prefetch(section, i - start)

    def hop(i, source, target, send_sem, recv_sem, to):
        slot = lax.rem(i, RING)
        return pltpu.make_async_remote_copy(
            src_ref=source.at[slot], dst_ref=target.at[i], send_sem=send_sem.at[slot],
            recv_sem=recv_sem.at[i], device_id=to, device_id_type=MESH,
        )

    def first(i, odd):
        return hop(i, s1, r1, send1, recv1, to_y if odd else to_x)

    def second(i, odd):
        return hop(i, s2, r2, send2, recv2, to_x if odd else to_y)

    def third(i, d):
        to = lax.rem(h + d, n_h)
        slot = lax.rem(i, RING)
        return pltpu.make_async_remote_copy(
            src_ref=s3.at[slot, pl.ds(to * rows, rows)], dst_ref=r3.at[i, d - 1],
            send_sem=send3.at[slot, d - 1], recv_sem=recv3.at[i, d - 1],
            device_id={"h": to}, device_id_type=MESH,
        )

    def multiply(i, odd):
        slot = lax.rem(i, RING)
        for copy in loads(i, 0, 0):
            copy.wait()
        left = lefts[sum((i + 1024 - start) // 1024 for start in left_starts[1:]) if left_starts[1:] else 0]
        right = right_buf.at[lax.rem(i, 3)]

        @pl.when(i >= RING)
        def _():
            first(i - RING, odd).wait_send()

        part = lax.dot_general(left, right[...], (((1,), (1,)), ((), ())), preferred_element_type=f32)
        own[slot, :w] = part[:w]
        if odd:
            own[slot, w:] = part[2 * w : 3 * w]
            s1[slot, :w] = part[w : 2 * w].astype(b16)
            s1[slot, w:] = part[3 * w :].astype(b16)
        else:
            own[slot, w:] = part[w : 2 * w]
            s1[slot] = part[2 * w :].astype(b16)
        first(i, odd).start()

        beside(i, right, odd)
        start_loads(i + 2)

    def pass_on(i, odd):
        slot = lax.rem(i, RING)
        first(i, odd).wait_recv()

        @pl.when(i >= RING)
        def _():
            second(i - RING, odd).wait_send()

        s2[slot] = (own[slot, w:] + r1[i, w:].astype(f32)).astype(b16)
        second(i, odd).start()

    def keep(i, odd):
        slot = lax.rem(i, RING)
        second(i, odd).wait_recv()
        part = own[slot, :w] + r1[i, :w].astype(f32) + r2[i].astype(f32)
        if n_h == 1:
            out[i] = part.astype(b16)
            return

        @pl.when(i >= RING)
        def _():
            for d in range(1, n_h):
                third(i - RING, d).wait_send()

        s3[slot] = part.astype(b16)
        for d in range(1, n_h):
            third(i, d).start()

    def finish(i, odd):
        if n_h == 1:
            return
        total = s3[lax.rem(i, RING), pl.ds(h * rows, rows)].astype(f32)
        for d in range(1, n_h):
            third(i, d).wait_recv()
            total = total + r3[i, d - 1].astype(f32)
        out[i] = total

    start_loads(jnp.int32(0))
    start_loads(jnp.int32(1))
    pairs = (n + 1) // 2

    def step(p, carry):
        for lag, stage in enumerate((multiply, pass_on, keep, finish)):
            for odd in (0, 1):
                i = 2 * (p - lag) + odd

                @pl.when((i >= 0) & (i < n))
                def _(stage=stage, i=i, odd=odd):
                    stage(i, odd)

        after(p)
        return carry

    lax.fori_loop(0, pairs + 3, step, 0)
    for i in range(max(n - RING, 0), n):
        first(i, i % 2).wait_send()
        second(i, i % 2).wait_send()
        for d in range(1, n_h):
            third(i, d).wait_send()


def chunk_of(k):
    return pl.ds(pl.multiple_of(k * CHUNK, CHUNK), CHUNK)


def product_kernel(n_h, sections, periods, left_starts, n_weights, with_sum, *refs):
    lefts, vector = refs[:2]
    n_rights = 2 * len(sections)
    rights, weights = refs[2 : 2 + n_rights], refs[2 + n_rights : 2 + n_rights + n_weights]
    rest = refs[2 + n_rights + n_weights :]
    out, product = rest[:2]
    total_out = rest[2] if with_sum else None
    weight_buf, product_buf, weight_sem, product_sem, *scratch = rest[3 if with_sum else 2 :]
    begin, count = sum(sections[:-1]), sections[-1]
    cells = vector.shape[0]

    def weight_loads(k):
        slot = lax.rem(k, 3)
        size = weights[0].shape[0]
        return [
            pltpu.make_async_copy(
                weight.at[:, chunk_of(k)],
                weight_buf.at[slot, pl.ds(part * size, size)],
                weight_sem.at[slot, part],
            )
            for part, weight in enumerate(weights)
        ]

    def product_store(k):
        slot = lax.rem(k, 2)
        return pltpu.make_async_copy(product_buf.at[slot], product.at[chunk_of(k)], product_sem.at[slot])

    def prefetch(section, k):
        if section == len(sections) - 1:
            for copy in weight_loads(k):
                copy.start()

    def multiply(k, right):
        for copy in weight_loads(k):
            copy.wait()
        weight = weight_buf[lax.rem(k, 3)]

        @pl.when(k >= 2)
        def _():
            product_store(k - 2).wait()

        value = jnp.dot(vector[...], weight, preferred_element_type=jnp.float32)
        product_buf[lax.rem(k, 2)] = value.T.astype(product_buf.dtype)
        product_store(k).start()
        if with_sum:
            term = jnp.dot(weight, right[:, :cells], preferred_element_type=jnp.float32)

            @pl.when(k == 0)
            def _():
                total_out[...] = term

            @pl.when(k > 0)
            def _():
                total_out[...] += term

    def beside(i, right, odd):
        if begin == 0:
            multiply(i, right)
        else:

            @pl.when(i >= begin)
            def _():
                multiply(i - begin, right)

    scatter_kernel(
        n_h, sections, periods, left_starts, lefts, rights, out, scratch, [], prefetch, beside, lambda p: None
    )
    for k in range(max(count - 2, 0), count):
        product_store(k).wait()


def attention_kernel(n_h, sections, periods, left_starts, scale, *refs):
    lefts, query, pairs, d_out, log_total, seg_keys, seg_mine = refs[:7]
    n_rights = 2 * len(sections)
    rights = refs[7 : 7 + n_rights]
    out, d_qkv, d_pairs, by_core, by_y, d_query, send, recv, *scratch = refs[7 + n_rights :]
    y, c = lax.axis_index("y"), lax.axis_index("c")
    f32, b16 = jnp.float32, jnp.bfloat16
    cells, width = query.shape
    slots = 4 * cells
    n_pairs, head = width // 128, 64
    into = (((1,), (1,)), ((), ()))

    def backward(j, half):
        lanes = pl.ds(pl.multiple_of(j * 128, 128), 128)
        value_lanes = pl.ds(pl.multiple_of(width + j * 128, 128), 128)
        side = slice(half * head, (half + 1) * head)
        keys = pairs[:, :, :, lanes].reshape(slots, 128)[:, side]
        values = pairs[:, :, :, value_lanes].reshape(slots, 128)[:, side]
        mine, above = query[:, lanes][:, side], d_out[:, lanes][:, side]
        scores = lax.dot_general(keys, mine, into, preferred_element_type=f32) * scale
        scores = jnp.where(seg_keys[...] == seg_mine[...], scores, -1000000000.0)
        probs = jnp.exp(scores - log_total[pl.ds(2 * j + half, 1), :])
        d_probs = lax.dot_general(values, above, into, preferred_element_type=f32)
        inner = jnp.sum(probs * d_probs, axis=0, keepdims=True)
        d_scores = (probs * (d_probs - inner)).astype(b16)
        d_keys = jnp.dot(d_scores, mine, preferred_element_type=f32) * scale
        d_values = jnp.dot(probs.astype(b16), above, preferred_element_type=f32)
        d_pairs[0, j, :, side] = d_keys.astype(b16)
        d_pairs[1, j, :, side] = d_values.astype(b16)
        turned = keys.astype(f32).T.astype(b16)
        d_query[side] = jnp.dot(turned, d_scores, preferred_element_type=f32) * scale
        if half:
            d_qkv[:, lanes] = d_query[...].T.astype(b16)

    def to_core():
        return pltpu.make_async_remote_copy(
            src_ref=d_pairs.at[:, :, pl.ds(2 * cells, 2 * cells)], dst_ref=by_core,
            send_sem=send.at[0], recv_sem=recv.at[0], device_id={"c": 1 - c}, device_id_type=MESH,
        )

    def to_y():
        return pltpu.make_async_remote_copy(
            src_ref=d_pairs.at[:, :, pl.ds(cells, cells)], dst_ref=by_y,
            send_sem=send.at[1], recv_sem=recv.at[1], device_id={"y": 1 - y}, device_id_type=MESH,
        )

    both = n_pairs // 2

    def beside(i, right, odd):
        p = i // 2
        late = (p + 1024 - both) // 1024

        @pl.when((p < both) | ((p < 3 * both) & (lax.rem(p, 2) == odd)))
        def _():
            backward(p - late * (p - both // 2 - p // 2), odd)

    def after(p):
        @pl.when(p == 3 * both)
        def _():
            to_core().start()

        @pl.when(p == 3 * both + 2)
        def _():
            to_core().wait_recv()

            def add(j, carry):
                for kind in (0, 1):
                    total = d_pairs[kind, j, : 2 * cells].astype(f32) + by_core[kind, j].astype(f32)
                    d_pairs[kind, j, : 2 * cells] = total.astype(b16)
                return carry

            lax.fori_loop(0, n_pairs, add, 0)
            to_y().start()

    scatter_kernel(
        n_h, sections, periods, left_starts, lefts, rights, out, scratch, [{"c": 1 - c}],
        lambda section, k: None, beside, after,
    )
    to_y().wait_recv()

    def add(j, carry):
        for kind in (0, 1):
            lanes = pl.ds(pl.multiple_of((kind + 1) * width + j * 128, 128), 128)
            total = d_pairs[kind, j, :cells].astype(f32) + by_y[kind, j].astype(f32)
            d_qkv[:, lanes] = total.astype(b16)
        return carry

    lax.fori_loop(0, n_pairs, add, 0)
    to_core().wait_send()
    to_y().wait_send()


def scatter_call(kernel, lefts, rights, operands, more_operands, out_shapes, out_specs, scratch, collective_id):
    periods = [own.shape[0] // CHUNK for own, *_ in rights]
    sections = [period * times for period, (*_, times) in zip(periods, rights)]
    n, cells = sum(sections), rights[0][0].shape[1]
    w = lefts.shape[1] // 4
    n_h = lax.axis_size("h")
    rows = w // n_h
    inner_h = n_h if rows % 16 == 0 else 1
    dma, bf16, f32 = pltpu.SemaphoreType.DMA, jnp.bfloat16, jnp.float32
    vmem, hbm = pl.BlockSpec(memory_space=pltpu.VMEM), pl.BlockSpec(memory_space=pl.ANY)
    others = max(inner_h - 1, 1)
    part_shape = jax.ShapeDtypeStruct((n, rows, CHUNK), f32)
    if inner_h == 1:
        part_shape = jax.ShapeDtypeStruct((n, w, CHUNK), bf16)
    part, *more = pl.pallas_call(
        functools.partial(kernel, inner_h, sections, periods),
        out_shape=[part_shape] + out_shapes,
        in_specs=[vmem] * (1 + len(operands)) + [hbm] * (2 * len(rights) + len(more_operands)),
        out_specs=[vmem] + out_specs,
        scratch_shapes=scratch
        + [
            pltpu.VMEM((3, CHUNK, 2 * cells), bf16),
            pltpu.VMEM((RING, 2 * w, CHUNK), f32),
            pltpu.VMEM((RING, 2 * w, CHUNK), bf16),
            pltpu.VMEM((n, 2 * w, CHUNK), bf16),
            pltpu.VMEM((RING, w, CHUNK), bf16),
            pltpu.VMEM((n, w, CHUNK), bf16),
            pltpu.VMEM((RING, w, CHUNK), bf16),
            pltpu.VMEM((n, others, w // inner_h, CHUNK), bf16),
            dma((3, 2)),
            dma((RING,)),
            dma((n,)),
            dma((RING,)),
            dma((n,)),
            dma((RING, others)),
            dma((n, others)),
        ],
        compiler_params=pltpu.CompilerParams(
            collective_id=collective_id, has_side_effects=True, vmem_limit_bytes=60 * 2**20
        ),
    )(lefts, *operands, *(half for pair in rights for half in pair[:2]), *more_operands)
    if inner_h == 1:
        part = lax.psum_scatter(part, "h", scatter_dimension=1, tiled=True).astype(f32)
    return part, *more


def scatter_product(lefts, left_starts, rights, vector, weights, product_type, with_sum, collective_id):
    (cells, features), columns = vector.shape, rights[-1][0].shape[0]
    dma = pltpu.SemaphoreType.DMA
    vmem, hbm = pl.BlockSpec(memory_space=pltpu.VMEM), pl.BlockSpec(memory_space=pl.ANY)

    def kernel(n_h, sections, periods, *refs):
        product_kernel(n_h, sections, periods, left_starts, len(weights), with_sum, *refs)

    return scatter_call(
        kernel,
        lefts,
        rights,
        [vector],
        weights,
        [jax.ShapeDtypeStruct((columns, cells), product_type)]
        + [jax.ShapeDtypeStruct((features, cells), jnp.float32)] * with_sum,
        [hbm] + [vmem] * with_sum,
        [
            pltpu.VMEM((3, features, CHUNK), jnp.bfloat16),
            pltpu.VMEM((2, CHUNK, cells), product_type),
            dma((3, len(weights))),
            dma((2,)),
        ],
        collective_id,
    )


def scatter_attention(lefts, left_starts, rights, query, pairs, d_out, log_total, seg, scale, collective_id):
    cells, width = query.shape
    bf16, vmem = jnp.bfloat16, pl.BlockSpec(memory_space=pltpu.VMEM)

    def kernel(n_h, sections, periods, *refs):
        attention_kernel(n_h, sections, periods, left_starts, scale, *refs)

    return scatter_call(
        kernel,
        lefts,
        rights,
        [query, pairs, d_out, log_total, seg[:, None], seg[None, :cells]],
        [],
        [jax.ShapeDtypeStruct((cells, 3 * width), bf16)],
        [vmem],
        [
            pltpu.VMEM((2, width // 128, 4 * cells, 128), bf16),
            pltpu.VMEM((2, width // 128, 2 * cells, 128), bf16),
            pltpu.VMEM((2, width // 128, cells, 128), bf16),
            pltpu.VMEM((128, cells), jnp.float32),
            pltpu.SemaphoreType.DMA((2,)),
            pltpu.SemaphoreType.DMA((2,)),
        ],
        collective_id,
    )


def own_half(left):
    half = left.shape[1] // 2
    return jnp.concatenate([left[:, :half], swap(left[:, half:], "c")], axis=0)


def left_of(left, pieces):
    left = own_half(relative(left, 1)).T
    n_h = lax.axis_size("h")
    left = left.reshape(4, n_h, pieces, -1, left.shape[1])
    return left.transpose(2, 0, 1, 3, 4).reshape(pieces, -1, left.shape[-1])


def both_cores(right, times=1):
    return right, swap(right, "c"), times


def columns_of(chunks):
    return chunks.transpose(1, 0, 2).reshape(chunks.shape[1], -1)


def on_device(
    counts,
    library,
    coords,
    lengths,
    cotangent,
    w_enc,
    w_qkv,
    w_out,
    gain_one,
    shift_one,
    w_up,
    w_down,
    gain_two,
    shift_two,
    w_dec,
):
    rows = counts.shape[0]
    width = w_qkv.shape[1] // 3
    heads = HEADS
    head_width = width // heads
    att_scale = head_width ** (-0.5)
    group_size = 4
    slots = rows * group_size
    scale = 10000.0 / library
    genes = counts.shape[1]
    padded = -(-genes // CHUNK) * CHUNK
    counts_f = counts.astype(jnp.float32)
    cot = jnp.pad(cotangent.T, ((0, padded - genes), (0, 0)))
    cot_pair = both_cores(cot)
    pe = by_owner(positions(coords, width), 1)
    ends = jnp.cumsum(lengths[0])
    group = [
        (lax.axis_index("y") ^ by_y) * 2 + (lax.axis_index("c") ^ by_c)
        for by_c in range(2)
        for by_y in range(2)
    ]
    place = jnp.concatenate([at * rows + jnp.arange(rows, dtype=jnp.int32) for at in group])
    seg_all = jnp.sum((place[:, None] >= ends[None, :]).astype(jnp.int32), axis=1)
    same = (seg_all[:rows, None] == seg_all[None, :])[None]
    vectors = jnp.stack([gain_one, shift_one, gain_two, shift_two], axis=1)
    vectors = jnp.pad(vectors, ((0, 0), (0, 124)))
    pad = ((0, 0), (0, padded - genes))
    quarter = padded // CHUNK // 4 * CHUNK
    gene_cuts = [0, quarter, 2 * quarter, 3 * quarter, padded]
    shards = [
        jnp.pad(w_enc.T, pad),
        jnp.concatenate([w_qkv, vectors], axis=1),
        by_owner(w_out, 1),
        by_owner(w_up, 1),
        by_owner(w_down, 1),
        jnp.pad(w_dec.T, pad),
    ]
    cuts = [gene_cuts, [0, width // 2 * 3, 3 * width + 128], [0, width]]
    cuts += [[0, 2 * width, 4 * width], [0, width // 2, width]]
    cuts += [[k * (padded // 1024) * 128 for k in range(8)] + [padded]]
    order = [(0, 0), (0, 1), (0, 2), (0, 3), (1, 0), (1, 1), (2, 0), (3, 0), (3, 1), (4, 0), (4, 1)]
    order += [(5, piece) for piece in range(8)]
    gathered, xb, h0, a1, query, kv_all = gather_all(
        shards, 5, cuts, order, counts.T, scale[None, :], pe.T, 0
    )
    xb_pair = both_cores(xb)
    enc_all, qkv_all, out_all, up_all, down_all = (
        w.reshape(-1, w.shape[-1]) for w in gathered[:5]
    )
    vectors = qkv_all[:, 3 * width :].astype(jnp.float32).T
    qkv_all = qkv_all[:, : 3 * width]
    g1f, b1f, g2f, b2f = vectors[0], vectors[1], vectors[2], vectors[3]
    kv_pairs, query_b = kv_all, query
    query = query.reshape(rows, heads, head_width)
    kv_all = kv_all.reshape(slots, -1)
    dec_own = gathered[5]
    middle = dec_own.shape[1] // 256 * 128
    by_x, by_y = swap(dec_own, "x"), swap(dec_own, "y")
    far = (swap(by_x[:, :middle], "y"), swap(by_y[:, middle:], "x"))
    dec_parts = [dec_own, by_y, by_x, jnp.concatenate(far, axis=1)]
    dec_parts += [swap(part, "c") for part in dec_parts]
    keys = kv_all[:, :width].reshape(slots, heads, head_width)
    values = kv_all[:, width:].reshape(slots, heads, head_width)

    def scores_of():
        raw = (
            jnp.einsum("qhd,khd->hqk", query, keys, preferred_element_type=jnp.float32) * att_scale
        )
        return jnp.where(same, raw, -1000000000.0)

    scores = scores_of()
    top = jnp.max(scores, axis=-1, keepdims=True)
    expo = jnp.exp(scores - top)
    total = jnp.sum(expo, axis=-1, keepdims=True)
    log_total = top + jnp.log(total)
    probs_b = (expo / total).astype(jnp.bfloat16)
    attended = jnp.einsum("hqk,khd->qhd", probs_b, values, preferred_element_type=jnp.float32)
    attended_b = attended.reshape(rows, width).astype(jnp.bfloat16)
    attended_b = by_owner(attended_b, 1)
    h1 = h0 + matmul(attended_b, out_all)
    a2 = layer_norm(h1, g2f, b2f).astype(jnp.bfloat16)
    hidden = matmul(a2, up_all)
    act, pull = jax.vjp(lambda v: jax.nn.gelu(v, approximate=False), hidden)
    act, slope = lax.optimization_barrier(
        (act.astype(jnp.bfloat16), pull(jnp.ones_like(hidden))[0])
    )
    h2 = h1 + matmul(act, down_all)
    hb = h2.astype(jnp.bfloat16)
    grad_dec, logits, dh2 = scatter_product(
        left_of(hb, 1), [0], [cot_pair], relative(hb, 1), dec_parts, jnp.bfloat16, True, 1
    )
    own_rows = grad_dec.shape[1]
    grad_dec = columns_of(grad_dec)[:, :genes].T
    logits = logits[:genes].T
    dh2 = relative(dh2, 0).T
    dfb = dh2.astype(jnp.bfloat16)
    d_act = contract_cols(dfb, down_all)
    d_hidden = (d_act * slope).astype(jnp.bfloat16)
    da2 = contract_cols(d_hidden, up_all)
    norm_pull = jax.vjp(layer_norm, h1, g2f, b2f)[1]
    dh1_norm, grad_gain_two, grad_shift_two = norm_pull(da2)
    dh1 = dh2 + dh1_norm
    dab = dh1.astype(jnp.bfloat16)
    d_attended = contract_cols(dab, out_all).astype(jnp.bfloat16)
    d_attended = from_owner(d_attended, 1)
    lefts = [left_of(a2, 1), left_of(act, act.shape[1] // width), left_of(attended_b, 1)]
    pieces = (4 * width,) + (width,) * 4
    rights = [both_cores(d_hidden.T), both_cores(dfb.T, 4), both_cores(dab.T)]
    grads, d_qkv = scatter_attention(
        jnp.concatenate(lefts, axis=0),
        [sum(pieces[:k]) // CHUNK for k in range(len(pieces) + 1)],
        rights,
        query_b,
        kv_pairs,
        d_attended,
        log_total[:, :, 0],
        seg_all,
        att_scale,
        2,
    )
    ends = [0]
    for columns in (4 * width, 4 * width, width):
        ends.append(ends[-1] + columns // CHUNK)
    grad_up, grad_down, grad_out = (grads[low:high] for low, high in zip(ends, ends[1:]))
    grad_up, grad_out = columns_of(grad_up), columns_of(grad_out)
    grad_down = grad_down.reshape(4, -1, own_rows, CHUNK).transpose(0, 2, 1, 3)
    grad_down = grad_down.reshape(4 * own_rows, -1)
    grad_out, grad_up, grad_down = (from_owner(g, 1) for g in (grad_out, grad_up, grad_down))
    da1 = contract_cols(d_qkv, qkv_all)
    first_pull = jax.vjp(layer_norm, h0, g1f, b1f)[1]
    dh0_norm, grad_gain_one, grad_shift_one = first_pull(da1)
    vectors_b = jnp.stack([grad_gain_one, grad_shift_one, grad_gain_two, grad_shift_two])
    vectors_b = jnp.pad(vectors_b, ((0, rows - 4), (0, 0))).astype(jnp.bfloat16)
    unit = jnp.eye(rows, dtype=jnp.bfloat16)
    dh0b = (dh1 + dh0_norm).astype(jnp.bfloat16)

    lefts = [left_of(a1, 1), left_of(vectors_b, 1), left_of(dh0b, 1)]
    grads, d_xb = scatter_product(
        jnp.concatenate(lefts, axis=0),
        [0, 3 * width // CHUNK, (3 * width + rows) // CHUNK],
        [both_cores(d_qkv.T), (unit, unit, 1), xb_pair],
        dh0b,
        [enc_all],
        jnp.float32,
        False,
        3,
    )
    ends = [0]
    for columns in (3 * width, rows):
        ends.append(ends[-1] + columns // CHUNK)
    grad_qkv, grad_vectors, grad_enc = (
        grads[low:high] for low, high in zip(ends, ends[1:] + [grads.shape[0]])
    )
    grad_qkv, grad_enc = columns_of(grad_qkv), columns_of(grad_enc)
    grad_gain_one, grad_shift_one, grad_gain_two, grad_shift_two = (
        grad_vectors[0, :, k] for k in range(4)
    )
    grad_enc = grad_enc[:, :genes].T
    d_xb = d_xb[:genes].T
    counts_grad = d_xb * scale[:, None] / (1.0 + counts_f * scale[:, None])
    return (
        logits,
        counts_grad,
        grad_enc,
        grad_qkv,
        grad_out,
        grad_gain_one,
        grad_shift_one,
        grad_up,
        grad_down,
        grad_gain_two,
        grad_shift_two,
        grad_dec,
    )


ALL = ("h", "x", "y", "c")


def solution(mesh):
    n_dp, n_fsdp = mesh.shape["dp"], mesh.shape["fsdp"]
    mesh = Mesh(mesh.devices.reshape((n_dp // 2, 2, 2, n_fsdp // 2)), ALL)
    placed = (
        P(ALL, None),
        P(ALL),
        P(None, ALL),
        P(("h", "x"), None),
        P(ALL, None),
        P(None, ALL),
        P(ALL, None),
        P(ALL, None),
        P(ALL),
        P(ALL),
        P(ALL, None),
        P(ALL, None),
        P(ALL),
        P(ALL),
        P(None, ALL),
    )
    return jax.shard_map(
        on_device,
        mesh=mesh,
        in_specs=placed,
        out_specs=(
            P(ALL, None),
            P(ALL, None),
            P(None, ALL),
            P(ALL, None),
            P(ALL, None),
            P(ALL),
            P(ALL),
            P(ALL, None),
            P(ALL, None),
            P(ALL),
            P(ALL),
            P(None, ALL),
        ),
        check_vma=False,
    )
```

```python
import functools
import math

import jax
import jax.numpy as jnp
from jax import lax
from jax.experimental import pallas as pl
from jax.experimental.pallas import tpu as pltpu
from jax.sharding import Mesh
from jax.sharding import PartitionSpec as P

HEADS = 16
MESH = pl.DeviceIdType.MESH
RING = 8
CHUNK = 256


eps = 1e-05


def layer_norm(value, gain, shift):
    mean = jnp.mean(value, axis=1, keepdims=True)
    centred = value - mean
    variance = jnp.mean(centred * centred, axis=1, keepdims=True)
    return centred * lax.rsqrt(variance + eps) * gain + shift


def positions(coords, width):
    quarter = width // 4
    freqs = 0.05 * jnp.exp(-jnp.arange(quarter, dtype=jnp.float32) * (math.log(10000.0) / quarter))
    along_x = coords[0].astype(jnp.float32)[:, None] * freqs[None, :]
    along_y = coords[1].astype(jnp.float32)[:, None] * freqs[None, :]
    return jnp.concatenate(
        [jnp.sin(along_x), jnp.cos(along_x), jnp.sin(along_y), jnp.cos(along_y)], axis=1
    )


def contract_rows(left, right):
    return lax.dot_general(
        left, right, (((0,), (0,)), ((), ())), preferred_element_type=jnp.float32
    )


def contract_cols(left, right):
    return lax.dot_general(
        left, right, (((1,), (1,)), ((), ())), preferred_element_type=jnp.float32
    )


def matmul(left, right):
    return jnp.dot(left, right, preferred_element_type=jnp.float32)


def swap(value, axis):
    return lax.ppermute(value, axis, [(0, 1), (1, 0)])


def by_owner(value, axis):
    n_h = lax.axis_size("h")
    at = value.shape
    block = at[axis] // (8 * n_h)
    split = value.reshape(at[:axis] + (n_h, 2, 2, 2, block) + at[axis + 1 :])
    order = list(range(axis)) + [axis + 3, axis + 1, axis + 2, axis, axis + 4]
    order += list(range(axis + 5, split.ndim))
    return split.transpose(order).reshape(at)


def from_owner(value, axis):
    n_h = lax.axis_size("h")
    at = value.shape
    block = at[axis] // (8 * n_h)
    split = value.reshape(at[:axis] + (2, 2, 2, n_h, block) + at[axis + 1 :])
    order = list(range(axis)) + [axis + 3, axis + 1, axis + 2, axis, axis + 4]
    order += list(range(axis + 5, split.ndim))
    return split.transpose(order).reshape(at)


def relative(value, axis):
    eighth = value.shape[axis] // 8
    mine = lax.axis_index("c") * 4 + lax.axis_index("x") * 2 + lax.axis_index("y")
    parts = [
        lax.dynamic_slice_in_dim(value, (mine ^ part) * eighth, eighth, axis) for part in range(8)
    ]
    return jnp.concatenate(parts, axis=axis)


def greet(peers):
    barrier = pltpu.get_barrier_semaphore()
    for peer in peers:
        pl.semaphore_signal(barrier, inc=1, device_id=peer, device_id_type=MESH)
    pl.semaphore_wait(barrier, len(peers))


def gather_kernel(n_h, jobs, n_full, shards, wholes, sems, between):
    own_sem, h_send, h_recv, send, recv = sems
    h, x, y, c = (lax.axis_index(name) for name in ("h", "x", "y", "c"))
    h = 0 if n_h == 1 else h
    to_x, to_y, to_c = {"x": 1 - x}, {"y": 1 - y}, {"c": 1 - c}
    greet([{"h": lax.rem(h + d, n_h)} for d in range(1, n_h)] + [to_x, to_y, to_c])

    def rows_of(job, at):
        array, low, high, _ = job
        rows = shards[array].shape[0]
        place = (pl.ds(at * rows, rows), pl.ds(low, high - low))
        return wholes[array].at[(c, x, y, *place) if array < n_full else place]

    def h_copy(j, d):
        array, low, high, _ = jobs[j]
        return pltpu.make_async_remote_copy(
            src_ref=shards[array].at[:, pl.ds(low, high - low)],
            dst_ref=rows_of(jobs[j], h),
            send_sem=h_send.at[j, d - 1],
            recv_sem=h_recv.at[j, d - 1],
            device_id={"h": lax.rem(h + d, n_h)},
            device_id_type=MESH,
        )

    def own_copy(j):
        array, low, high, _ = jobs[j]
        return pltpu.make_async_copy(
            shards[array].at[:, pl.ds(low, high - low)], rows_of(jobs[j], h), own_sem.at[j]
        )

    def block_copy(j, k, block, to, columns):
        view = wholes[jobs[j][0]].at[(*block, slice(None), pl.ds(columns[0], columns[1] - columns[0]))]
        return pltpu.make_async_remote_copy(
            src_ref=view,
            dst_ref=view,
            send_sem=send.at[j, k],
            recv_sem=recv.at[j, k],
            device_id=to,
            device_id_type=MESH,
        )

    own, by_x, by_y, far = (c, x, y), (c, 1 - x, y), (c, x, 1 - y), (c, 1 - x, 1 - y)

    def copy(j, k):
        _, low, high, middle = jobs[j]
        block, to, columns = [
            (own, to_x, (low, high)),
            (own, to_y, (low, high)),
            (own, to_c, (low, high)),
            (by_x, to_y, (low, middle)),
            (by_y, to_x, (middle, high)),
            (by_x, to_c, (low, high)),
            (by_y, to_c, (low, high)),
            (far, to_c, (low, high)),
        ][k]
        return block_copy(j, k, block, to, columns)

    def start_h(j):
        own_copy(j).start()
        for d in range(1, n_h):
            h_copy(j, d).start()

    whole = set()

    def landed(j):
        if j not in whole:
            whole.add(j)
            for k in (2, 5, 6, 7):
                copy(j, k).wait_recv()

    n = sum(array < n_full for array, *_ in jobs)
    ahead = 2
    for j in range(ahead):
        start_h(j)
    for step in range(n + 2):
        if step < n:
            own_copy(step).wait()
            for d in range(1, n_h):
                h_copy(step, d).wait_recv()
            for k in (0, 1, 2):
                copy(step, k).start()
            if step + ahead < len(jobs):
                start_h(step + ahead)
        if 0 <= step - 1 < n:
            for k in (0, 1):
                copy(step - 1, k).wait_recv()
            for k in (3, 4, 5, 6):
                copy(step - 1, k).start()
        if 0 <= step - 2 < n:
            for k in (3, 4):
                copy(step - 2, k).wait_recv()
            copy(step - 2, 7).start()
        between(step, landed)
    for j in range(n, len(jobs)):
        own_copy(j).wait()
        for d in range(1, n_h):
            h_copy(j, d).wait_recv()
    for j in range(len(jobs)):
        for d in range(1, n_h):
            h_copy(j, d).wait_send()
    for j in range(n):
        for k in range(8):
            copy(j, k).wait_send()
        landed(j)


def front_kernel(n_h, jobs, n_arrays, n_full, *refs):
    shards, (counts, tail, scale, pe) = refs[:n_arrays], refs[n_arrays : n_arrays + 4]
    rest = refs[n_arrays + 4 :]
    wholes, (xb, h0, a1, query, pairs) = rest[:n_arrays], rest[n_arrays : n_arrays + 5]
    (count_buf, enc_buf, xb_buf, total, qkv_buf, mine, count_sem, enc_sem, xb_sem, qkv_sem, kv_sem,
     kv_send, kv_recv, *sems) = rest[n_arrays + 5 :]
    y, c = lax.axis_index("y"), lax.axis_index("c")
    f32, b16 = jnp.float32, jnp.bfloat16
    width = h0.shape[1]
    n_chunks = xb.shape[0] // CHUNK
    by_chunk = lambda k: pl.ds(pl.multiple_of(k * CHUNK, CHUNK), CHUNK)

    def loads(k, last):
        slot = lax.rem(k, 2)
        source = tail if last else counts.at[by_chunk(k)]
        return (
            pltpu.make_async_copy(source, count_buf.at[slot], count_sem.at[slot]),
            pltpu.make_async_copy(
                wholes[0].at[:, :, :, :, by_chunk(k)], enc_buf.at[slot], enc_sem.at[slot]
            ),
        )

    def store(k):
        slot = lax.rem(k, 2)
        return pltpu.make_async_copy(xb_buf.at[slot], xb.at[by_chunk(k)], xb_sem.at[slot])

    def encode(k, first, last, low, high):
        slot = lax.rem(k, 2)
        for copy in loads(k, last):
            copy.wait()
        if not last:

            @pl.when(k + 1 < (high - 1 if high == n_chunks else high))
            def _():
                for copy in loads(k + 1, False):
                    copy.start()

        @pl.when(k >= low + 2)
        def _():
            store(k - 2).wait()

        value = jnp.log1p(count_buf[slot].astype(f32) * scale[...]).astype(b16)
        xb_buf[slot] = value
        store(k).start()
        term = jnp.dot(enc_buf[slot].reshape(width, CHUNK), value, preferred_element_type=f32)
        if first:

            @pl.when(k == 0)
            def _():
                total[...] = pe[...] + term

            @pl.when(k > 0)
            def _():
                total[...] += term

        else:
            total[...] += term

    def encode_job(low, high):
        low, high = low // CHUNK, high // CHUNK
        stop = high - 1 if high == n_chunks else high
        for copy in loads(jnp.int32(low), False):
            copy.start()

        def body(k, carry):
            encode(k, low == 0, False, low, high)
            return carry

        lax.fori_loop(low, stop, body, 0)
        if stop < high:
            for copy in loads(jnp.int32(stop), True):
                copy.start()
            encode(jnp.int32(stop), False, True, low, high)
        for k in range(max(low, high - 2), high):
            store(jnp.int32(k)).wait()

    def fetch_qkv():
        return pltpu.make_async_copy(wholes[1], qkv_buf, qkv_sem.at[0])

    def project():
        fetch_qkv().wait()
        vectors = qkv_buf[:, :, :, :, 3 * width :].reshape(width, 128).astype(f32)
        value = total[...]
        centred = value - jnp.mean(value, axis=0, keepdims=True)
        variance = jnp.mean(centred * centred, axis=0, keepdims=True)
        normed = centred * lax.rsqrt(variance + eps) * vectors[:, 0:1] + vectors[:, 1:2]
        h0[...] = value.T
        a1[...] = normed.T.astype(b16)

        def tile(k):
            weight = qkv_buf[:, :, :, :, by_chunk(k)].reshape(width, CHUNK)
            return jnp.dot(a1[...], weight, preferred_element_type=f32).astype(b16)

        def keys(k, carry):
            mine[:, by_chunk(k)] = tile(k + width // CHUNK)
            return carry

        lax.fori_loop(0, 2 * width // CHUNK, keys, 0)
        kv_own().start()
        kv_copy(0).start()

        def queries(k, carry):
            query[:, by_chunk(k)] = tile(k)
            return carry

        lax.fori_loop(0, width // CHUNK, queries, 0)

    def kv_own():
        return pltpu.make_async_copy(mine, pairs.at[0, 0], kv_sem.at[0])

    def kv_copy(k):
        return pltpu.make_async_remote_copy(
            src_ref=(mine, pairs.at[0])[k],
            dst_ref=(pairs.at[0, 1], pairs.at[1])[k],
            send_sem=kv_send.at[k],
            recv_sem=kv_recv.at[k],
            device_id=({"y": 1 - y}, {"c": 1 - c})[k],
            device_id_type=MESH,
        )

    arrays = [array for array, *_ in jobs]
    enc_jobs = [j for j, array in enumerate(arrays) if array == 0]
    qkv_jobs = [j for j, array in enumerate(arrays) if array == 1]
    at = max(qkv_jobs) + 3

    def between(step, landed):
        if step - 3 in enc_jobs:
            landed(step - 3)
            encode_job(*jobs[step - 3][1:3])
        if step == at:
            for j in qkv_jobs:
                landed(j)
            fetch_qkv().start()
            project()
        if step == at + 2:
            kv_own().wait()
            kv_copy(0).wait_recv()
            kv_copy(1).start()

    gather_kernel(n_h, jobs, n_full, shards, wholes, sems, between)
    kv_copy(0).wait_send()
    kv_copy(1).wait()


def gather_all(shards, n_full, cuts, order, counts, scale, pe, collective_id):
    n_h = lax.axis_size("h")
    if any(shard.shape[0] % 16 for shard in shards):
        shards = [lax.all_gather(s, "h", axis=0, tiled=True) for s in shards]
        n_h = 1
    jobs = []
    for array, piece in order:
        low, high = cuts[array][piece], cuts[array][piece + 1]
        jobs.append((array, low, high, low + (high - low) * 5 // 12 // 128 * 128))
    n, others, dma = len(jobs), max(n_h - 1, 1), pltpu.SemaphoreType.DMA
    shapes = [(n_h * s.shape[0], s.shape[1]) for s in shards]
    (genes, cells), width, padded = counts.shape, pe.shape[0], shards[0].shape[1]
    tail = counts[genes // CHUNK * CHUNK :]
    tail = jnp.pad(tail, ((0, CHUNK - tail.shape[0]), (0, 0)))
    bf16, f32 = jnp.bfloat16, jnp.float32
    vmem, hbm = pl.BlockSpec(memory_space=pltpu.VMEM), pl.BlockSpec(memory_space=pl.ANY)
    out = pl.pallas_call(
        functools.partial(front_kernel, n_h, jobs, len(shards), n_full),
        out_shape=[
            jax.ShapeDtypeStruct((2, 2, 2) + shape if k < n_full else shape, bf16)
            for k, shape in enumerate(shapes)
        ]
        + [
            jax.ShapeDtypeStruct((padded, cells), bf16),
            jax.ShapeDtypeStruct((cells, width), f32),
            jax.ShapeDtypeStruct((cells, width), bf16),
            jax.ShapeDtypeStruct((cells, width), bf16),
            jax.ShapeDtypeStruct((2, 2, cells, 2 * width), bf16),
        ],
        in_specs=[hbm] * (len(shards) + 2) + [vmem] * 2,
        out_specs=[hbm] * (len(shards) + 1) + [vmem] * 3 + [hbm],
        scratch_shapes=[
            pltpu.VMEM((2, CHUNK, cells), bf16),
            pltpu.VMEM((2, 2, 2, 2, width // 8, CHUNK), bf16),
            pltpu.VMEM((2, CHUNK, cells), bf16),
            pltpu.VMEM((width, cells), f32),
            pltpu.VMEM((2, 2, 2, width // 8, shards[1].shape[1]), bf16),
            pltpu.VMEM((cells, 2 * width), bf16),
            dma((2,)),
            dma((2,)),
            dma((2,)),
            dma((1,)),
            dma((1,)),
            dma((2,)),
            dma((2,)),
            dma((n,)),
            dma((n, others)),
            dma((n, others)),
            dma((n, 8)),
            dma((n, 8)),
        ],
        compiler_params=pltpu.CompilerParams(
            collective_id=collective_id, has_side_effects=True, vmem_limit_bytes=60 * 2**20
        ),
    )(*shards, counts, tail, scale, pe)
    return out[: len(shards)], *out[len(shards) :]


def scatter_kernel(
    n_h, sections, periods, left_starts, leaning, lefts, rights, out, scratch, peers, prefetch, beside, after
):
    (right_buf, part, own, s1, r1, s2, r2, s3, r3, own_h, s1_h, r1_h, s2_h, r2_h, s3_h, r3_h, load_sem, send1, recv1,
     send2, recv2, send3, recv3, send1_h, recv1_h, send2_h, recv2_h, send3_h, recv3_h) = scratch
    h, x, y = (lax.axis_index(name) for name in ("h", "x", "y"))
    to_x, to_y = {"x": 1 - x}, {"y": 1 - y}
    w = s3.shape[1]
    rows = w // n_h
    f32, b16 = jnp.float32, jnp.bfloat16
    starts = [sum(sections[:k]) for k in range(len(sections))]
    n = sum(sections)
    cells = right_buf.shape[2] // 2
    others = range(1, n_h)
    greet([{"h": lax.rem(h + d, n_h)} for d in others] + [to_x, to_y] + peers)

    def loads(i, section, k):
        slot = lax.rem(i, 3)
        return [
            pltpu.make_async_copy(
                rights[2 * section + half].at[chunk_of(k)],
                right_buf.at[slot, :, pl.ds(half * cells, cells)],
                load_sem.at[slot, half],
            )
            for half in (0, 1)
        ]

    def start_loads(i):
        for section, (start, count) in enumerate(zip(starts, sections)):

            @pl.when((i >= start) & (i < start + count))
            def _(section=section, start=start):
                for copy in loads(i, section, lax.rem(i - start, periods[section])):
                    copy.start()
                prefetch(section, i - start)

    def multiply(i, odd):
        for copy in loads(i, 0, 0):
            copy.wait()
        left = lefts[sum((i + 1024 - start) // 1024 for start in left_starts[1:]) if left_starts[1:] else 0]
        right = right_buf.at[lax.rem(i, 3)]
        part[...] = lax.dot_general(left, right[...], (((1,), (1,)), ((), ())), preferred_element_type=f32)

    def remote(source, target, send_sem, recv_sem, to):
        return pltpu.make_async_remote_copy(
            src_ref=source, dst_ref=target, send_sem=send_sem, recv_sem=recv_sem, device_id=to, device_id_type=MESH
        )

    class Links:
        def first(k, i, by_y):
            slot = lax.rem(k, RING)
            return remote(s1.at[slot], r1.at[i], send1.at[slot], recv1.at[i], to_y if by_y else to_x)

        def second(k, i, by_y):
            slot = lax.rem(k, RING)
            return remote(s2.at[slot], r2.at[i], send2.at[slot], recv2.at[i], to_x if by_y else to_y)

        def third(k, i, d):
            slot, to = lax.rem(k, RING), lax.rem(h + d, n_h)
            return remote(
                s3.at[slot, pl.ds(to * rows, rows)], r3.at[i, d - 1], send3.at[slot, d - 1], recv3.at[i, d - 1], {"h": to}
            )

        def start(k, i, by_y):
            slot = lax.rem(k, RING)

            @pl.when(k >= RING)
            def _():
                Links.first(k, i, by_y).wait_send()

            own[slot, :w] = part[:w]
            if by_y:
                own[slot, w:] = part[2 * w : 3 * w]
                s1[slot, :w] = part[w : 2 * w].astype(b16)
                s1[slot, w:] = part[3 * w :].astype(b16)
            else:
                own[slot, w:] = part[w : 2 * w]
                s1[slot] = part[2 * w :].astype(b16)
            Links.first(k, i, by_y).start()

        def pass_on(k, i, by_y):
            slot = lax.rem(k, RING)
            Links.first(k, i, by_y).wait_recv()

            @pl.when(k >= RING)
            def _():
                Links.second(k, i, by_y).wait_send()

            s2[slot] = (own[slot, w:] + r1[i, w:].astype(f32)).astype(b16)
            Links.second(k, i, by_y).start()

        def keep(k, i, by_y):
            slot = lax.rem(k, RING)
            Links.second(k, i, by_y).wait_recv()
            total = own[slot, :w] + r1[i, :w].astype(f32) + r2[i].astype(f32)
            if n_h == 1:
                out[i] = total.astype(b16)
                return

            @pl.when(k >= RING)
            def _():
                for d in others:
                    Links.third(k, i, d).wait_send()

            s3[slot] = total.astype(b16)
            for d in others:
                Links.third(k, i, d).start()

        def finish(k, i, by_y):
            if n_h == 1:
                return
            total = s3[lax.rem(k, RING), pl.ds(h * rows, rows)].astype(f32)
            for d in others:
                Links.third(k, i, d).wait_recv()
                total = total + r3[i, d - 1].astype(f32)
            out[i] = total

    class Along:
        def first(k, d):
            to = lax.rem(h + d, n_h)
            return remote(s1_h.at[k, :, to], r1_h.at[k, d - 1], send1_h.at[k, d - 1], recv1_h.at[k, d - 1], {"h": to})

        def second(k, by_y):
            return remote(s2_h.at[k], r2_h.at[k], send2_h.at[k], recv2_h.at[k], to_y if by_y else to_x)

        def third(k, by_y):
            return remote(s3_h.at[k], r3_h.at[k], send3_h.at[k], recv3_h.at[k], to_x if by_y else to_y)

        def start(k, i, by_y):
            for block in range(4):
                s1_h[k, block] = part[block * w : (block + 1) * w].reshape(n_h, rows, CHUNK).astype(b16)
                own_h[k, block] = part[pl.ds(block * w + h * rows, rows)]
            for d in others:
                Along.first(k, d).start()

        def pass_on(k, i, by_y):
            for d in others:
                Along.first(k, d).wait_recv()

            def total(block):
                return own_h[k, block] + sum(r1_h[k, d - 1, block].astype(f32) for d in others)

            mine, away = ((0, 2), (1, 3)) if by_y else ((0, 1), (2, 3))
            for place, block in enumerate(away):
                s2_h[k, place] = total(block).astype(b16)
            Along.second(k, by_y).start()
            for place, block in enumerate(mine):
                own_h[k, place] = total(block)

        def keep(k, i, by_y):
            Along.second(k, by_y).wait_recv()
            s3_h[k] = (own_h[k, 1] + r2_h[k, 1].astype(f32)).astype(b16)
            Along.third(k, by_y).start()

        def finish(k, i, by_y):
            Along.third(k, by_y).wait_recv()
            out[i] = own_h[k, 0] + r2_h[k, 0].astype(f32) + r3_h[k].astype(f32)

    pairs = (n + 1) // 2
    along = s1_h.shape[0] // 2 if n_h > 1 else 0
    stages = ("start", "pass_on", "keep", "finish")

    def step(p, carry):
        for lag, stage in enumerate(stages):
            q = p - lag
            turn = q // 8
            is_along = (lax.rem(q, 8) == 7) & (q < 8 * along)
            for odd in (0, 1):
                i = 2 * q + odd
                here = (i >= 0) & (i < n)
                if lag == 0:

                    @pl.when(here)
                    def _(i=i, odd=odd):
                        multiply(i, odd)

                k = i - 2 * turn if along else i
                leans = (lax.rem(q, 2) == 0) if leaning else False
                ways = [(0, here & ~is_along)] if not odd else [(1, here & ~is_along)]
                if odd and leaning:
                    ways = [(0, here & ~is_along & leans), (1, here & ~is_along & ~leans)]
                for by_y, when in ways:

                    @pl.when(when)
                    def _(k=k, i=i, by_y=by_y, stage=stage):
                        getattr(Links, stage)(k, i, by_y)

                if along:

                    @pl.when(here & is_along)
                    def _(i=i, odd=odd, turn=turn, stage=stage):
                        getattr(Along, stage)(2 * turn + odd, i, odd)

                if lag == 0:

                    @pl.when(here)
                    def _(i=i, odd=odd):
                        beside(i, right_buf.at[lax.rem(i, 3)], odd)
                        start_loads(i + 2)

        after(p)
        return carry

    start_loads(jnp.int32(0))
    start_loads(jnp.int32(1))
    lax.fori_loop(0, pairs + 3, step, 0)
    for k in range(max(n - 2 * along - RING, 0), n - 2 * along):
        Links.first(k, 0, 0).wait_send()
        Links.second(k, 0, 0).wait_send()
        for d in others:
            Links.third(k, 0, d).wait_send()
    for k in range(2 * along):
        for d in others:
            Along.first(k, d).wait_send()
        Along.second(k, 0).wait_send()
        Along.third(k, 0).wait_send()


def chunk_of(k):
    return pl.ds(pl.multiple_of(k * CHUNK, CHUNK), CHUNK)


def product_kernel(n_h, sections, periods, left_starts, n_weights, with_sum, *refs):
    lefts, vector = refs[:2]
    n_rights = 2 * len(sections)
    rights, weights = refs[2 : 2 + n_rights], refs[2 + n_rights : 2 + n_rights + n_weights]
    rest = refs[2 + n_rights + n_weights :]
    out, product = rest[:2]
    total_out = rest[2] if with_sum else None
    weight_buf, product_buf, weight_sem, product_sem, *scratch = rest[3 if with_sum else 2 :]
    begin, count = sum(sections[:-1]), sections[-1]
    cells = vector.shape[0]

    def weight_loads(k):
        slot = lax.rem(k, 3)
        size = weights[0].shape[0]
        return [
            pltpu.make_async_copy(
                weight.at[:, chunk_of(k)],
                weight_buf.at[slot, pl.ds(part * size, size)],
                weight_sem.at[slot, part],
            )
            for part, weight in enumerate(weights)
        ]

    def product_store(k):
        slot = lax.rem(k, 2)
        return pltpu.make_async_copy(product_buf.at[slot], product.at[chunk_of(k)], product_sem.at[slot])

    def prefetch(section, k):
        if section == len(sections) - 1:
            for copy in weight_loads(k):
                copy.start()

    def multiply(k, right):
        for copy in weight_loads(k):
            copy.wait()
        weight = weight_buf[lax.rem(k, 3)]

        @pl.when(k >= 2)
        def _():
            product_store(k - 2).wait()

        value = jnp.dot(vector[...], weight, preferred_element_type=jnp.float32)
        product_buf[lax.rem(k, 2)] = value.T.astype(product_buf.dtype)
        product_store(k).start()
        if with_sum:
            term = jnp.dot(weight, right[:, :cells], preferred_element_type=jnp.float32)

            @pl.when(k == 0)
            def _():
                total_out[...] = term

            @pl.when(k > 0)
            def _():
                total_out[...] += term

    def beside(i, right, odd):
        if begin == 0:
            multiply(i, right)
        else:

            @pl.when(i >= begin)
            def _():
                multiply(i - begin, right)

    scatter_kernel(
        n_h, sections, periods, left_starts, False, lefts, rights, out, scratch, [], prefetch, beside, lambda p: None
    )
    for k in range(max(count - 2, 0), count):
        product_store(k).wait()


def attention_kernel(n_h, sections, periods, left_starts, scale, *refs):
    lefts, query, pairs, d_out, log_total, seg_keys, seg_mine = refs[:7]
    n_rights = 2 * len(sections)
    rights = refs[7 : 7 + n_rights]
    out, d_qkv, d_pairs, by_core, by_y, d_query, send, recv, *scratch = refs[7 + n_rights :]
    y, c = lax.axis_index("y"), lax.axis_index("c")
    f32, b16 = jnp.float32, jnp.bfloat16
    cells, width = query.shape
    slots = 4 * cells
    n_pairs, head = width // 128, 64
    into = (((1,), (1,)), ((), ()))

    def backward(j, half):
        lanes = pl.ds(pl.multiple_of(j * 128, 128), 128)
        value_lanes = pl.ds(pl.multiple_of(width + j * 128, 128), 128)
        side = slice(half * head, (half + 1) * head)
        keys = pairs[:, :, :, lanes].reshape(slots, 128)[:, side]
        values = pairs[:, :, :, value_lanes].reshape(slots, 128)[:, side]
        mine, above = query[:, lanes][:, side], d_out[:, lanes][:, side]
        scores = lax.dot_general(keys, mine, into, preferred_element_type=f32) * scale
        scores = jnp.where(seg_keys[...] == seg_mine[...], scores, -1000000000.0)
        probs = jnp.exp(scores - log_total[pl.ds(2 * j + half, 1), :])
        d_probs = lax.dot_general(values, above, into, preferred_element_type=f32)
        inner = jnp.sum(probs * d_probs, axis=0, keepdims=True)
        d_scores = (probs * (d_probs - inner)).astype(b16)
        d_keys = jnp.dot(d_scores, mine, preferred_element_type=f32) * scale
        d_values = jnp.dot(probs.astype(b16), above, preferred_element_type=f32)
        d_pairs[0, j, :, side] = d_keys.astype(b16)
        d_pairs[1, j, :, side] = d_values.astype(b16)
        turned = keys.astype(f32).T.astype(b16)
        d_query[side] = jnp.dot(turned, d_scores, preferred_element_type=f32) * scale
        if half:
            d_qkv[:, lanes] = d_query[...].T.astype(b16)

    def to_core():
        return pltpu.make_async_remote_copy(
            src_ref=d_pairs.at[:, :, pl.ds(2 * cells, 2 * cells)], dst_ref=by_core,
            send_sem=send.at[0], recv_sem=recv.at[0], device_id={"c": 1 - c}, device_id_type=MESH,
        )

    def to_y():
        return pltpu.make_async_remote_copy(
            src_ref=d_pairs.at[:, :, pl.ds(cells, cells)], dst_ref=by_y,
            send_sem=send.at[1], recv_sem=recv.at[1], device_id={"y": 1 - y}, device_id_type=MESH,
        )

    def beside(i, right, odd):
        @pl.when(i < n_pairs)
        def _():
            backward(i, 0)
            backward(i, 1)

    def after(p):
        @pl.when(p == n_pairs // 2)
        def _():
            to_core().start()

        @pl.when(p == n_pairs // 2 + 2)
        def _():
            to_core().wait_recv()

            def add(j, carry):
                for kind in (0, 1):
                    total = d_pairs[kind, j, : 2 * cells].astype(f32) + by_core[kind, j].astype(f32)
                    d_pairs[kind, j, : 2 * cells] = total.astype(b16)
                return carry

            lax.fori_loop(0, n_pairs, add, 0)
            to_y().start()

    scatter_kernel(
        n_h, sections, periods, left_starts, True, lefts, rights, out, scratch, [{"c": 1 - c}],
        lambda section, k: None, beside, after,
    )
    to_y().wait_recv()

    def add(j, carry):
        for kind in (0, 1):
            lanes = pl.ds(pl.multiple_of((kind + 1) * width + j * 128, 128), 128)
            total = d_pairs[kind, j, :cells].astype(f32) + by_y[kind, j].astype(f32)
            d_qkv[:, lanes] = total.astype(b16)
        return carry

    lax.fori_loop(0, n_pairs, add, 0)
    to_core().wait_send()
    to_y().wait_send()


def scatter_call(kernel, lefts, rights, operands, more_operands, out_shapes, out_specs, scratch, collective_id):
    periods = [own.shape[0] // CHUNK for own, *_ in rights]
    sections = [period * times for period, (*_, times) in zip(periods, rights)]
    n, cells = sum(sections), rights[0][0].shape[1]
    w = lefts.shape[1] // 4
    n_h = lax.axis_size("h")
    rows = w // n_h
    inner_h = n_h if rows % 16 == 0 else 1
    dma, bf16, f32 = pltpu.SemaphoreType.DMA, jnp.bfloat16, jnp.float32
    vmem, hbm = pl.BlockSpec(memory_space=pltpu.VMEM), pl.BlockSpec(memory_space=pl.ANY)
    others, along = max(inner_h - 1, 1), max(2 * (n // 16), 2)
    part_shape = jax.ShapeDtypeStruct((n, rows, CHUNK), f32)
    if inner_h == 1:
        part_shape = jax.ShapeDtypeStruct((n, w, CHUNK), bf16)
    part, *more = pl.pallas_call(
        functools.partial(kernel, inner_h, sections, periods),
        out_shape=[part_shape] + out_shapes,
        in_specs=[vmem] * (1 + len(operands)) + [hbm] * (2 * len(rights) + len(more_operands)),
        out_specs=[vmem] + out_specs,
        scratch_shapes=scratch
        + [
            pltpu.VMEM((3, CHUNK, 2 * cells), bf16),
            pltpu.VMEM((4 * w, CHUNK), f32),
            pltpu.VMEM((RING, 2 * w, CHUNK), f32),
            pltpu.VMEM((RING, 2 * w, CHUNK), bf16),
            pltpu.VMEM((n, 2 * w, CHUNK), bf16),
            pltpu.VMEM((RING, w, CHUNK), bf16),
            pltpu.VMEM((n, w, CHUNK), bf16),
            pltpu.VMEM((RING, w, CHUNK), bf16),
            pltpu.VMEM((n, others, w // inner_h, CHUNK), bf16),
            pltpu.VMEM((along, 4, rows, CHUNK), f32),
            pltpu.VMEM((along, 4, inner_h, w // inner_h, CHUNK), bf16),
            pltpu.VMEM((along, others, 4, rows, CHUNK), bf16),
            pltpu.VMEM((along, 2, rows, CHUNK), bf16),
            pltpu.VMEM((along, 2, rows, CHUNK), bf16),
            pltpu.VMEM((along, rows, CHUNK), bf16),
            pltpu.VMEM((along, rows, CHUNK), bf16),
            dma((3, 2)),
            dma((RING,)),
            dma((n,)),
            dma((RING,)),
            dma((n,)),
            dma((RING, others)),
            dma((n, others)),
            dma((along, others)),
            dma((along, others)),
            dma((along,)),
            dma((along,)),
            dma((along,)),
            dma((along,)),
        ],
        compiler_params=pltpu.CompilerParams(
            collective_id=collective_id, has_side_effects=True, vmem_limit_bytes=60 * 2**20
        ),
    )(lefts, *operands, *(half for pair in rights for half in pair[:2]), *more_operands)
    if inner_h == 1:
        part = lax.psum_scatter(part, "h", scatter_dimension=1, tiled=True).astype(f32)
    return part, *more


def scatter_product(lefts, left_starts, rights, vector, weights, product_type, with_sum, collective_id):
    (cells, features), columns = vector.shape, rights[-1][0].shape[0]
    dma = pltpu.SemaphoreType.DMA
    vmem, hbm = pl.BlockSpec(memory_space=pltpu.VMEM), pl.BlockSpec(memory_space=pl.ANY)

    def kernel(n_h, sections, periods, *refs):
        product_kernel(n_h, sections, periods, left_starts, len(weights), with_sum, *refs)

    return scatter_call(
        kernel,
        lefts,
        rights,
        [vector],
        weights,
        [jax.ShapeDtypeStruct((columns, cells), product_type)]
        + [jax.ShapeDtypeStruct((features, cells), jnp.float32)] * with_sum,
        [hbm] + [vmem] * with_sum,
        [
            pltpu.VMEM((3, features, CHUNK), jnp.bfloat16),
            pltpu.VMEM((2, CHUNK, cells), product_type),
            dma((3, len(weights))),
            dma((2,)),
        ],
        collective_id,
    )


def scatter_attention(lefts, left_starts, rights, query, pairs, d_out, log_total, seg, scale, collective_id):
    cells, width = query.shape
    bf16, vmem = jnp.bfloat16, pl.BlockSpec(memory_space=pltpu.VMEM)

    def kernel(n_h, sections, periods, *refs):
        attention_kernel(n_h, sections, periods, left_starts, scale, *refs)

    return scatter_call(
        kernel,
        lefts,
        rights,
        [query, pairs, d_out, log_total, seg[:, None], seg[None, :cells]],
        [],
        [jax.ShapeDtypeStruct((cells, 3 * width), bf16)],
        [vmem],
        [
            pltpu.VMEM((2, width // 128, 4 * cells, 128), bf16),
            pltpu.VMEM((2, width // 128, 2 * cells, 128), bf16),
            pltpu.VMEM((2, width // 128, cells, 128), bf16),
            pltpu.VMEM((128, cells), jnp.float32),
            pltpu.SemaphoreType.DMA((2,)),
            pltpu.SemaphoreType.DMA((2,)),
        ],
        collective_id,
    )


def own_half(left):
    half = left.shape[1] // 2
    return jnp.concatenate([left[:, :half], swap(left[:, half:], "c")], axis=0)


def left_of(left, pieces):
    left = own_half(relative(left, 1)).T
    n_h = lax.axis_size("h")
    left = left.reshape(4, n_h, pieces, -1, left.shape[1])
    return left.transpose(2, 0, 1, 3, 4).reshape(pieces, -1, left.shape[-1])


def both_cores(right, times=1):
    return right, swap(right, "c"), times


def columns_of(chunks):
    return chunks.transpose(1, 0, 2).reshape(chunks.shape[1], -1)


def on_device(
    counts,
    library,
    coords,
    lengths,
    cotangent,
    w_enc,
    w_qkv,
    w_out,
    gain_one,
    shift_one,
    w_up,
    w_down,
    gain_two,
    shift_two,
    w_dec,
):
    rows = counts.shape[0]
    width = w_qkv.shape[1] // 3
    heads = HEADS
    head_width = width // heads
    att_scale = head_width ** (-0.5)
    group_size = 4
    slots = rows * group_size
    scale = 10000.0 / library
    genes = counts.shape[1]
    padded = -(-genes // CHUNK) * CHUNK
    counts_f = counts.astype(jnp.float32)
    cot = jnp.pad(cotangent.T, ((0, padded - genes), (0, 0)))
    cot_pair = both_cores(cot)
    pe = by_owner(positions(coords, width), 1)
    ends = jnp.cumsum(lengths[0])
    group = [
        (lax.axis_index("y") ^ by_y) * 2 + (lax.axis_index("c") ^ by_c)
        for by_c in range(2)
        for by_y in range(2)
    ]
    place = jnp.concatenate([at * rows + jnp.arange(rows, dtype=jnp.int32) for at in group])
    seg_all = jnp.sum((place[:, None] >= ends[None, :]).astype(jnp.int32), axis=1)
    same = (seg_all[:rows, None] == seg_all[None, :])[None]
    vectors = jnp.stack([gain_one, shift_one, gain_two, shift_two], axis=1)
    vectors = jnp.pad(vectors, ((0, 0), (0, 124)))
    pad = ((0, 0), (0, padded - genes))
    quarter = padded // CHUNK // 4 * CHUNK
    gene_cuts = [0, quarter, 2 * quarter, 3 * quarter, padded]
    shards = [
        jnp.pad(w_enc.T, pad),
        jnp.concatenate([w_qkv, vectors], axis=1),
        by_owner(w_out, 1),
        by_owner(w_up, 1),
        by_owner(w_down, 1),
        jnp.pad(w_dec.T, pad),
    ]
    cuts = [gene_cuts, [0, width // 2 * 3, 3 * width + 128], [0, width]]
    cuts += [[0, 2 * width, 4 * width], [0, width // 2, width]]
    cuts += [[0, padded]]
    order = [(0, 0), (0, 1), (0, 2), (0, 3), (1, 0), (1, 1), (2, 0), (3, 0), (3, 1), (4, 0), (4, 1), (5, 0)]
    gathered, xb, h0, a1, query, kv_all = gather_all(
        shards, 5, cuts, order, counts.T, scale[None, :], pe.T, 0
    )
    xb_pair = both_cores(xb)
    enc_all, qkv_all, out_all, up_all, down_all = (
        w.reshape(-1, w.shape[-1]) for w in gathered[:5]
    )
    vectors = qkv_all[:, 3 * width :].astype(jnp.float32).T
    qkv_all = qkv_all[:, : 3 * width]
    g1f, b1f, g2f, b2f = vectors[0], vectors[1], vectors[2], vectors[3]
    kv_pairs, query_b = kv_all, query
    query = query.reshape(rows, heads, head_width)
    kv_all = kv_all.reshape(slots, -1)
    dec_own = gathered[5]
    middle = dec_own.shape[1] // 256 * 128
    by_x, by_y = swap(dec_own, "x"), swap(dec_own, "y")
    far = (swap(by_x[:, :middle], "y"), swap(by_y[:, middle:], "x"))
    dec_parts = [dec_own, by_y, by_x, jnp.concatenate(far, axis=1)]
    dec_parts += [swap(part, "c") for part in dec_parts]
    keys = kv_all[:, :width].reshape(slots, heads, head_width)
    values = kv_all[:, width:].reshape(slots, heads, head_width)

    def scores_of():
        raw = (
            jnp.einsum("qhd,khd->hqk", query, keys, preferred_element_type=jnp.float32) * att_scale
        )
        return jnp.where(same, raw, -1000000000.0)

    scores = scores_of()
    top = jnp.max(scores, axis=-1, keepdims=True)
    expo = jnp.exp(scores - top)
    total = jnp.sum(expo, axis=-1, keepdims=True)
    log_total = top + jnp.log(total)
    probs_b = (expo / total).astype(jnp.bfloat16)
    attended = jnp.einsum("hqk,khd->qhd", probs_b, values, preferred_element_type=jnp.float32)
    attended_b = attended.reshape(rows, width).astype(jnp.bfloat16)
    attended_b = by_owner(attended_b, 1)
    h1 = h0 + matmul(attended_b, out_all)
    a2 = layer_norm(h1, g2f, b2f).astype(jnp.bfloat16)
    hidden = matmul(a2, up_all)
    act, pull = jax.vjp(lambda v: jax.nn.gelu(v, approximate=False), hidden)
    act, slope = lax.optimization_barrier(
        (act.astype(jnp.bfloat16), pull(jnp.ones_like(hidden))[0])
    )
    h2 = h1 + matmul(act, down_all)
    hb = h2.astype(jnp.bfloat16)
    grad_dec, logits, dh2 = scatter_product(
        left_of(hb, 1), [0], [cot_pair], relative(hb, 1), dec_parts, jnp.bfloat16, True, 1
    )
    own_rows = grad_dec.shape[1]
    grad_dec = columns_of(grad_dec)[:, :genes].T
    logits = logits[:genes].T
    dh2 = relative(dh2, 0).T
    dfb = dh2.astype(jnp.bfloat16)
    d_act = contract_cols(dfb, down_all)
    d_hidden = (d_act * slope).astype(jnp.bfloat16)
    da2 = contract_cols(d_hidden, up_all)
    norm_pull = jax.vjp(layer_norm, h1, g2f, b2f)[1]
    dh1_norm, grad_gain_two, grad_shift_two = norm_pull(da2)
    dh1 = dh2 + dh1_norm
    dab = dh1.astype(jnp.bfloat16)
    d_attended = contract_cols(dab, out_all).astype(jnp.bfloat16)
    d_attended = from_owner(d_attended, 1)
    lefts = [left_of(a2, 1), left_of(act, act.shape[1] // width), left_of(attended_b, 1)]
    pieces = (4 * width,) + (width,) * 4
    rights = [both_cores(d_hidden.T), both_cores(dfb.T, 4), both_cores(dab.T)]
    grads, d_qkv = scatter_attention(
        jnp.concatenate(lefts, axis=0),
        [sum(pieces[:k]) // CHUNK for k in range(len(pieces) + 1)],
        rights,
        query_b,
        kv_pairs,
        d_attended,
        log_total[:, :, 0],
        seg_all,
        att_scale,
        2,
    )
    ends = [0]
    for columns in (4 * width, 4 * width, width):
        ends.append(ends[-1] + columns // CHUNK)
    grad_up, grad_down, grad_out = (grads[low:high] for low, high in zip(ends, ends[1:]))
    grad_up, grad_out = columns_of(grad_up), columns_of(grad_out)
    grad_down = grad_down.reshape(4, -1, own_rows, CHUNK).transpose(0, 2, 1, 3)
    grad_down = grad_down.reshape(4 * own_rows, -1)
    grad_out, grad_up, grad_down = (from_owner(g, 1) for g in (grad_out, grad_up, grad_down))
    da1 = contract_cols(d_qkv, qkv_all)
    first_pull = jax.vjp(layer_norm, h0, g1f, b1f)[1]
    dh0_norm, grad_gain_one, grad_shift_one = first_pull(da1)
    vectors_b = jnp.stack([grad_gain_one, grad_shift_one, grad_gain_two, grad_shift_two])
    vectors_b = jnp.pad(vectors_b, ((0, rows - 4), (0, 0))).astype(jnp.bfloat16)
    unit = jnp.eye(rows, dtype=jnp.bfloat16)
    dh0b = (dh1 + dh0_norm).astype(jnp.bfloat16)

    lefts = [left_of(a1, 1), left_of(vectors_b, 1), left_of(dh0b, 1)]
    grads, d_xb = scatter_product(
        jnp.concatenate(lefts, axis=0),
        [0, 3 * width // CHUNK, (3 * width + rows) // CHUNK],
        [both_cores(d_qkv.T), (unit, unit, 1), xb_pair],
        dh0b,
        [enc_all],
        jnp.float32,
        False,
        3,
    )
    ends = [0]
    for columns in (3 * width, rows):
        ends.append(ends[-1] + columns // CHUNK)
    grad_qkv, grad_vectors, grad_enc = (
        grads[low:high] for low, high in zip(ends, ends[1:] + [grads.shape[0]])
    )
    grad_qkv, grad_enc = columns_of(grad_qkv), columns_of(grad_enc)
    grad_gain_one, grad_shift_one, grad_gain_two, grad_shift_two = (
        grad_vectors[0, :, k] for k in range(4)
    )
    grad_enc = grad_enc[:, :genes].T
    d_xb = d_xb[:genes].T
    counts_grad = d_xb * scale[:, None] / (1.0 + counts_f * scale[:, None])
    return (
        logits,
        counts_grad,
        grad_enc,
        grad_qkv,
        grad_out,
        grad_gain_one,
        grad_shift_one,
        grad_up,
        grad_down,
        grad_gain_two,
        grad_shift_two,
        grad_dec,
    )


ALL = ("h", "x", "y", "c")


def solution(mesh):
    n_dp, n_fsdp = mesh.shape["dp"], mesh.shape["fsdp"]
    mesh = Mesh(mesh.devices.reshape((n_dp // 2, 2, 2, n_fsdp // 2)), ALL)
    placed = (
        P(ALL, None),
        P(ALL),
        P(None, ALL),
        P(("h", "x"), None),
        P(ALL, None),
        P(None, ALL),
        P(ALL, None),
        P(ALL, None),
        P(ALL),
        P(ALL),
        P(ALL, None),
        P(ALL, None),
        P(ALL),
        P(ALL),
        P(None, ALL),
    )
    return jax.shard_map(
        on_device,
        mesh=mesh,
        in_specs=placed,
        out_specs=(
            P(ALL, None),
            P(ALL, None),
            P(None, ALL),
            P(ALL, None),
            P(ALL, None),
            P(ALL),
            P(ALL),
            P(ALL, None),
            P(ALL, None),
            P(ALL),
            P(ALL),
            P(None, ALL),
        ),
        check_vma=False,
    )
```

```python
import functools
import math

import jax
import jax.numpy as jnp
from jax import lax
from jax.experimental import pallas as pl
from jax.experimental.pallas import tpu as pltpu
from jax.sharding import Mesh
from jax.sharding import PartitionSpec as P

HEADS = 16
MESH = pl.DeviceIdType.MESH
RING = 8
CHUNK = 256


eps = 1e-05


def layer_norm(value, gain, shift):
    mean = jnp.mean(value, axis=1, keepdims=True)
    centred = value - mean
    variance = jnp.mean(centred * centred, axis=1, keepdims=True)
    return centred * lax.rsqrt(variance + eps) * gain + shift


def positions(coords, width):
    quarter = width // 4
    freqs = 0.05 * jnp.exp(-jnp.arange(quarter, dtype=jnp.float32) * (math.log(10000.0) / quarter))
    along_x = coords[0].astype(jnp.float32)[:, None] * freqs[None, :]
    along_y = coords[1].astype(jnp.float32)[:, None] * freqs[None, :]
    return jnp.concatenate(
        [jnp.sin(along_x), jnp.cos(along_x), jnp.sin(along_y), jnp.cos(along_y)], axis=1
    )


def contract_rows(left, right):
    return lax.dot_general(
        left, right, (((0,), (0,)), ((), ())), preferred_element_type=jnp.float32
    )


def contract_cols(left, right):
    return lax.dot_general(
        left, right, (((1,), (1,)), ((), ())), preferred_element_type=jnp.float32
    )


def matmul(left, right):
    return jnp.dot(left, right, preferred_element_type=jnp.float32)


def swap(value, axis):
    return lax.ppermute(value, axis, [(0, 1), (1, 0)])


def by_owner(value, axis):
    n_h = lax.axis_size("h")
    at = value.shape
    block = at[axis] // (8 * n_h)
    split = value.reshape(at[:axis] + (n_h, 2, 2, 2, block) + at[axis + 1 :])
    order = list(range(axis)) + [axis + 3, axis + 1, axis + 2, axis, axis + 4]
    order += list(range(axis + 5, split.ndim))
    return split.transpose(order).reshape(at)


def from_owner(value, axis):
    n_h = lax.axis_size("h")
    at = value.shape
    block = at[axis] // (8 * n_h)
    split = value.reshape(at[:axis] + (2, 2, 2, n_h, block) + at[axis + 1 :])
    order = list(range(axis)) + [axis + 3, axis + 1, axis + 2, axis, axis + 4]
    order += list(range(axis + 5, split.ndim))
    return split.transpose(order).reshape(at)


def relative(value, axis):
    eighth = value.shape[axis] // 8
    mine = lax.axis_index("c") * 4 + lax.axis_index("x") * 2 + lax.axis_index("y")
    parts = [
        lax.dynamic_slice_in_dim(value, (mine ^ part) * eighth, eighth, axis) for part in range(8)
    ]
    return jnp.concatenate(parts, axis=axis)


def greet(peers):
    barrier = pltpu.get_barrier_semaphore()
    for peer in peers:
        pl.semaphore_signal(barrier, inc=1, device_id=peer, device_id_type=MESH)
    pl.semaphore_wait(barrier, len(peers))


def gather_kernel(n_h, jobs, n_full, shards, wholes, sems, between):
    own_sem, h_send, h_recv, send, recv = sems
    h, x, y, c = (lax.axis_index(name) for name in ("h", "x", "y", "c"))
    h = 0 if n_h == 1 else h
    to_x, to_y, to_c = {"x": 1 - x}, {"y": 1 - y}, {"c": 1 - c}
    greet([{"h": lax.rem(h + d, n_h)} for d in range(1, n_h)] + [to_x, to_y, to_c])

    def rows_of(job, at):
        array, low, high, _ = job
        rows = shards[array].shape[0]
        place = (pl.ds(at * rows, rows), pl.ds(low, high - low))
        return wholes[array].at[(c, x, y, *place) if array < n_full else place]

    def h_copy(j, d):
        array, low, high, _ = jobs[j]
        return pltpu.make_async_remote_copy(
            src_ref=shards[array].at[:, pl.ds(low, high - low)],
            dst_ref=rows_of(jobs[j], h),
            send_sem=h_send.at[j, d - 1],
            recv_sem=h_recv.at[j, d - 1],
            device_id={"h": lax.rem(h + d, n_h)},
            device_id_type=MESH,
        )

    def own_copy(j):
        array, low, high, _ = jobs[j]
        return pltpu.make_async_copy(
            shards[array].at[:, pl.ds(low, high - low)], rows_of(jobs[j], h), own_sem.at[j]
        )

    def block_copy(j, k, block, to, columns):
        view = wholes[jobs[j][0]].at[(*block, slice(None), pl.ds(columns[0], columns[1] - columns[0]))]
        return pltpu.make_async_remote_copy(
            src_ref=view,
            dst_ref=view,
            send_sem=send.at[j, k],
            recv_sem=recv.at[j, k],
            device_id=to,
            device_id_type=MESH,
        )

    own, by_x, by_y, far = (c, x, y), (c, 1 - x, y), (c, x, 1 - y), (c, 1 - x, 1 - y)

    def copy(j, k):
        _, low, high, middle = jobs[j]
        block, to, columns = [
            (own, to_x, (low, high)),
            (own, to_y, (low, high)),
            (own, to_c, (low, high)),
            (by_x, to_y, (low, middle)),
            (by_y, to_x, (middle, high)),
            (by_x, to_c, (low, high)),
            (by_y, to_c, (low, high)),
            (far, to_c, (low, high)),
        ][k]
        return block_copy(j, k, block, to, columns)

    def start_h(j):
        own_copy(j).start()
        for d in range(1, n_h):
            h_copy(j, d).start()

    whole = set()

    def landed(j):
        if j not in whole:
            whole.add(j)
            for k in (2, 5, 6, 7):
                copy(j, k).wait_recv()

    n = sum(array < n_full for array, *_ in jobs)
    ahead = 2
    for j in range(ahead):
        start_h(j)
    for step in range(n + 2):
        if step < n:
            own_copy(step).wait()
            for d in range(1, n_h):
                h_copy(step, d).wait_recv()
            for k in (0, 1, 2):
                copy(step, k).start()
            if step + ahead < len(jobs):
                start_h(step + ahead)
        if 0 <= step - 1 < n:
            for k in (0, 1):
                copy(step - 1, k).wait_recv()
            for k in (3, 4, 5, 6):
                copy(step - 1, k).start()
        if 0 <= step - 2 < n:
            for k in (3, 4):
                copy(step - 2, k).wait_recv()
            copy(step - 2, 7).start()
        between(step, landed)
    for j in range(n, len(jobs)):
        own_copy(j).wait()
        for d in range(1, n_h):
            h_copy(j, d).wait_recv()
    for j in range(len(jobs)):
        for d in range(1, n_h):
            h_copy(j, d).wait_send()
    for j in range(n):
        for k in range(8):
            copy(j, k).wait_send()
        landed(j)


def front_kernel(n_h, jobs, n_arrays, n_full, *refs):
    shards, (counts, tail, scale, pe) = refs[:n_arrays], refs[n_arrays : n_arrays + 4]
    rest = refs[n_arrays + 4 :]
    wholes, (xb, h0, a1, query, pairs) = rest[:n_arrays], rest[n_arrays : n_arrays + 5]
    (count_buf, enc_buf, xb_buf, total, qkv_buf, mine, count_sem, enc_sem, xb_sem, qkv_sem, kv_sem,
     kv_send, kv_recv, *sems) = rest[n_arrays + 5 :]
    y, c = lax.axis_index("y"), lax.axis_index("c")
    f32, b16 = jnp.float32, jnp.bfloat16
    width = h0.shape[1]
    n_chunks = xb.shape[0] // CHUNK
    by_chunk = lambda k: pl.ds(pl.multiple_of(k * CHUNK, CHUNK), CHUNK)

    def loads(k, last):
        slot = lax.rem(k, 2)
        source = tail if last else counts.at[by_chunk(k)]
        return (
            pltpu.make_async_copy(source, count_buf.at[slot], count_sem.at[slot]),
            pltpu.make_async_copy(
                wholes[0].at[:, :, :, :, by_chunk(k)], enc_buf.at[slot], enc_sem.at[slot]
            ),
        )

    def store(k):
        slot = lax.rem(k, 2)
        return pltpu.make_async_copy(xb_buf.at[slot], xb.at[by_chunk(k)], xb_sem.at[slot])

    def encode(k, first, last, low, high):
        slot = lax.rem(k, 2)
        for copy in loads(k, last):
            copy.wait()
        if not last:

            @pl.when(k + 1 < (high - 1 if high == n_chunks else high))
            def _():
                for copy in loads(k + 1, False):
                    copy.start()

        @pl.when(k >= low + 2)
        def _():
            store(k - 2).wait()

        value = jnp.log1p(count_buf[slot].astype(f32) * scale[...]).astype(b16)
        xb_buf[slot] = value
        store(k).start()
        term = jnp.dot(enc_buf[slot].reshape(width, CHUNK), value, preferred_element_type=f32)
        if first:

            @pl.when(k == 0)
            def _():
                total[...] = pe[...] + term

            @pl.when(k > 0)
            def _():
                total[...] += term

        else:
            total[...] += term

    def encode_job(low, high):
        low, high = low // CHUNK, high // CHUNK
        stop = high - 1 if high == n_chunks else high
        for copy in loads(jnp.int32(low), False):
            copy.start()

        def body(k, carry):
            encode(k, low == 0, False, low, high)
            return carry

        lax.fori_loop(low, stop, body, 0)
        if stop < high:
            for copy in loads(jnp.int32(stop), True):
                copy.start()
            encode(jnp.int32(stop), False, True, low, high)
        for k in range(max(low, high - 2), high):
            store(jnp.int32(k)).wait()

    def fetch_qkv():
        return pltpu.make_async_copy(wholes[1], qkv_buf, qkv_sem.at[0])

    def project():
        fetch_qkv().wait()
        vectors = qkv_buf[:, :, :, :, 3 * width :].reshape(width, 128).astype(f32)
        value = total[...]
        centred = value - jnp.mean(value, axis=0, keepdims=True)
        variance = jnp.mean(centred * centred, axis=0, keepdims=True)
        normed = centred * lax.rsqrt(variance + eps) * vectors[:, 0:1] + vectors[:, 1:2]
        h0[...] = value.T
        a1[...] = normed.T.astype(b16)

        def tile(k):
            weight = qkv_buf[:, :, :, :, by_chunk(k)].reshape(width, CHUNK)
            return jnp.dot(a1[...], weight, preferred_element_type=f32).astype(b16)

        def keys(k, carry):
            mine[:, by_chunk(k)] = tile(k + width // CHUNK)
            return carry

        lax.fori_loop(0, 2 * width // CHUNK, keys, 0)
        kv_own().start()
        kv_copy(0).start()

        def queries(k, carry):
            query[:, by_chunk(k)] = tile(k)
            return carry

        lax.fori_loop(0, width // CHUNK, queries, 0)

    def kv_own():
        return pltpu.make_async_copy(mine, pairs.at[0, 0], kv_sem.at[0])

    def kv_copy(k):
        return pltpu.make_async_remote_copy(
            src_ref=(mine, pairs.at[0])[k],
            dst_ref=(pairs.at[0, 1], pairs.at[1])[k],
            send_sem=kv_send.at[k],
            recv_sem=kv_recv.at[k],
            device_id=({"y": 1 - y}, {"c": 1 - c})[k],
            device_id_type=MESH,
        )

    arrays = [array for array, *_ in jobs]
    enc_jobs = [j for j, array in enumerate(arrays) if array == 0]
    qkv_jobs = [j for j, array in enumerate(arrays) if array == 1]
    at = max(qkv_jobs) + 3

    def between(step, landed):
        if step - 3 in enc_jobs:
            landed(step - 3)
            encode_job(*jobs[step - 3][1:3])
        if step == at:
            for j in qkv_jobs:
                landed(j)
            fetch_qkv().start()
            project()
        if step == at + 2:
            kv_own().wait()
            kv_copy(0).wait_recv()
            kv_copy(1).start()

    gather_kernel(n_h, jobs, n_full, shards, wholes, sems, between)
    kv_copy(0).wait_send()
    kv_copy(1).wait()


def gather_all(shards, n_full, cuts, order, counts, scale, pe, collective_id):
    n_h = lax.axis_size("h")
    if any(shard.shape[0] % 16 for shard in shards):
        shards = [lax.all_gather(s, "h", axis=0, tiled=True) for s in shards]
        n_h = 1
    jobs = []
    for array, piece in order:
        low, high = cuts[array][piece], cuts[array][piece + 1]
        jobs.append((array, low, high, low + (high - low) // 256 * 128))
    n, others, dma = len(jobs), max(n_h - 1, 1), pltpu.SemaphoreType.DMA
    shapes = [(n_h * s.shape[0], s.shape[1]) for s in shards]
    (genes, cells), width, padded = counts.shape, pe.shape[0], shards[0].shape[1]
    tail = counts[genes // CHUNK * CHUNK :]
    tail = jnp.pad(tail, ((0, CHUNK - tail.shape[0]), (0, 0)))
    bf16, f32 = jnp.bfloat16, jnp.float32
    vmem, hbm = pl.BlockSpec(memory_space=pltpu.VMEM), pl.BlockSpec(memory_space=pl.ANY)
    out = pl.pallas_call(
        functools.partial(front_kernel, n_h, jobs, len(shards), n_full),
        out_shape=[
            jax.ShapeDtypeStruct((2, 2, 2) + shape if k < n_full else shape, bf16)
            for k, shape in enumerate(shapes)
        ]
        + [
            jax.ShapeDtypeStruct((padded, cells), bf16),
            jax.ShapeDtypeStruct((cells, width), f32),
            jax.ShapeDtypeStruct((cells, width), bf16),
            jax.ShapeDtypeStruct((cells, width), bf16),
            jax.ShapeDtypeStruct((2, 2, cells, 2 * width), bf16),
        ],
        in_specs=[hbm] * (len(shards) + 2) + [vmem] * 2,
        out_specs=[hbm] * (len(shards) + 1) + [vmem] * 3 + [hbm],
        scratch_shapes=[
            pltpu.VMEM((2, CHUNK, cells), bf16),
            pltpu.VMEM((2, 2, 2, 2, width // 8, CHUNK), bf16),
            pltpu.VMEM((2, CHUNK, cells), bf16),
            pltpu.VMEM((width, cells), f32),
            pltpu.VMEM((2, 2, 2, width // 8, shards[1].shape[1]), bf16),
            pltpu.VMEM((cells, 2 * width), bf16),
            dma((2,)),
            dma((2,)),
            dma((2,)),
            dma((1,)),
            dma((1,)),
            dma((2,)),
            dma((2,)),
            dma((n,)),
            dma((n, others)),
            dma((n, others)),
            dma((n, 8)),
            dma((n, 8)),
        ],
        compiler_params=pltpu.CompilerParams(
            collective_id=collective_id, has_side_effects=True, vmem_limit_bytes=60 * 2**20
        ),
    )(*shards, counts, tail, scale, pe)
    return out[: len(shards)], *out[len(shards) :]


def scatter_kernel(n_h, sections, periods, left_starts, lefts, rights, out, scratch, peers, prefetch, beside, after):
    (right_buf, own, s1, r1, s2, r2, s3, r3, load_sem, send1, recv1, send2, recv2, send3, recv3) = scratch
    h, x, y = (lax.axis_index(name) for name in ("h", "x", "y"))
    to_x, to_y = {"x": 1 - x}, {"y": 1 - y}
    w = s3.shape[1]
    rows = w // n_h
    f32, b16 = jnp.float32, jnp.bfloat16
    n_sections = len(sections)
    starts = [sum(sections[:k]) for k in range(n_sections)]
    n = sum(sections)
    cells = right_buf.shape[2] // 2
    greet([{"h": lax.rem(h + d, n_h)} for d in range(1, n_h)] + [to_x, to_y] + peers)

    def loads(i, section, k):
        slot = lax.rem(i, 3)
        return [
            pltpu.make_async_copy(
                rights[2 * section + half].at[chunk_of(k)],
                right_buf.at[slot, :, pl.ds(half * cells, cells)],
                load_sem.at[slot, half],
            )
            for half in (0, 1)
        ]

    def start_loads(i):
        for section, (start, count) in enumerate(zip(starts, sections)):

            @pl.when((i >= start) & (i < start + count))
            def _(section=section, start=start):
                for copy in loads(i, section, lax.rem(i - start, periods[section])):
                    copy.start()
                prefetch(section, i - start)

    def hop(i, source, target, send_sem, recv_sem, to):
        slot = lax.rem(i, RING)
        return pltpu.make_async_remote_copy(
            src_ref=source.at[slot], dst_ref=target.at[i], send_sem=send_sem.at[slot],
            recv_sem=recv_sem.at[i], device_id=to, device_id_type=MESH,
        )

    def first(i, odd):
        return hop(i, s1, r1, send1, recv1, to_y if odd else to_x)

    def second(i, odd):
        return hop(i, s2, r2, send2, recv2, to_x if odd else to_y)

    def third(i, d):
        to = lax.rem(h + d, n_h)
        slot = lax.rem(i, RING)
        return pltpu.make_async_remote_copy(
            src_ref=s3.at[slot, pl.ds(to * rows, rows)], dst_ref=r3.at[i, d - 1],
            send_sem=send3.at[slot, d - 1], recv_sem=recv3.at[i, d - 1],
            device_id={"h": to}, device_id_type=MESH,
        )

    def multiply(i, odd):
        slot = lax.rem(i, RING)
        for copy in loads(i, 0, 0):
            copy.wait()
        left = lefts[sum((i + 1024 - start) // 1024 for start in left_starts[1:]) if left_starts[1:] else 0]
        right = right_buf.at[lax.rem(i, 3)]

        @pl.when(i >= RING)
        def _():
            first(i - RING, odd).wait_send()

        part = lax.dot_general(left, right[...], (((1,), (1,)), ((), ())), preferred_element_type=f32)
        own[slot, :w] = part[:w]
        if odd:
            own[slot, w:] = part[2 * w : 3 * w]
            s1[slot, :w] = part[w : 2 * w].astype(b16)
            s1[slot, w:] = part[3 * w :].astype(b16)
        else:
            own[slot, w:] = part[w : 2 * w]
            s1[slot] = part[2 * w :].astype(b16)
        first(i, odd).start()

        beside(i, right, odd)
        start_loads(i + 2)

    def pass_on(i, odd):
        slot = lax.rem(i, RING)
        first(i, odd).wait_recv()

        @pl.when(i >= RING)
        def _():
            second(i - RING, odd).wait_send()

        s2[slot] = (own[slot, w:] + r1[i, w:].astype(f32)).astype(b16)
        second(i, odd).start()

    def keep(i, odd):
        slot = lax.rem(i, RING)
        second(i, odd).wait_recv()
        part = own[slot, :w] + r1[i, :w].astype(f32) + r2[i].astype(f32)
        if n_h == 1:
            out[i] = part.astype(b16)
            return

        @pl.when(i >= RING)
        def _():
            for d in range(1, n_h):
                third(i - RING, d).wait_send()

        s3[slot] = part.astype(b16)
        for d in range(1, n_h):
            third(i, d).start()

    def finish(i, odd):
        if n_h == 1:
            return
        total = s3[lax.rem(i, RING), pl.ds(h * rows, rows)].astype(f32)
        for d in range(1, n_h):
            third(i, d).wait_recv()
            total = total + r3[i, d - 1].astype(f32)
        out[i] = total

    start_loads(jnp.int32(0))
    start_loads(jnp.int32(1))
    pairs = (n + 1) // 2

    def step(p, carry):
        for lag, stage in enumerate((multiply, pass_on, keep, finish)):
            for odd in (0, 1):
                i = 2 * (p - lag) + odd

                @pl.when((i >= 0) & (i < n))
                def _(stage=stage, i=i, odd=odd):
                    stage(i, odd)

        after(p)
        return carry

    lax.fori_loop(0, pairs + 3, step, 0)
    for i in range(max(n - RING, 0), n):
        first(i, i % 2).wait_send()
        second(i, i % 2).wait_send()
        for d in range(1, n_h):
            third(i, d).wait_send()


def chunk_of(k):
    return pl.ds(pl.multiple_of(k * CHUNK, CHUNK), CHUNK)


def product_kernel(n_h, sections, periods, left_starts, n_weights, with_sum, *refs):
    lefts, vector = refs[:2]
    n_rights = 2 * len(sections)
    rights, weights = refs[2 : 2 + n_rights], refs[2 + n_rights : 2 + n_rights + n_weights]
    rest = refs[2 + n_rights + n_weights :]
    out, product = rest[:2]
    total_out = rest[2] if with_sum else None
    weight_buf, product_buf, weight_sem, product_sem, *scratch = rest[3 if with_sum else 2 :]
    begin, count = sum(sections[:-1]), sections[-1]
    cells = vector.shape[0]

    def weight_loads(k):
        slot = lax.rem(k, 3)
        size = weights[0].shape[0]
        return [
            pltpu.make_async_copy(
                weight.at[:, chunk_of(k)],
                weight_buf.at[slot, pl.ds(part * size, size)],
                weight_sem.at[slot, part],
            )
            for part, weight in enumerate(weights)
        ]

    def product_store(k):
        slot = lax.rem(k, 2)
        return pltpu.make_async_copy(product_buf.at[slot], product.at[chunk_of(k)], product_sem.at[slot])

    def prefetch(section, k):
        if section == len(sections) - 1:
            for copy in weight_loads(k):
                copy.start()

    def multiply(k, right):
        for copy in weight_loads(k):
            copy.wait()
        weight = weight_buf[lax.rem(k, 3)]

        @pl.when(k >= 2)
        def _():
            product_store(k - 2).wait()

        value = jnp.dot(vector[...], weight, preferred_element_type=jnp.float32)
        product_buf[lax.rem(k, 2)] = value.T.astype(product_buf.dtype)
        product_store(k).start()
        if with_sum:
            term = jnp.dot(weight, right[:, :cells], preferred_element_type=jnp.float32)

            @pl.when(k == 0)
            def _():
                total_out[...] = term

            @pl.when(k > 0)
            def _():
                total_out[...] += term

    def beside(i, right, odd):
        if begin == 0:
            multiply(i, right)
        else:

            @pl.when(i >= begin)
            def _():
                multiply(i - begin, right)

    scatter_kernel(
        n_h, sections, periods, left_starts, lefts, rights, out, scratch, [], prefetch, beside, lambda p: None
    )
    for k in range(max(count - 2, 0), count):
        product_store(k).wait()


def attention_kernel(n_h, sections, periods, left_starts, scale, *refs):
    lefts, query, pairs, d_out, log_total, seg_keys, seg_mine, h0, dh1, vectors, left_one = refs[:11]
    n_rights = 2 * len(sections)
    rights, weight = refs[11 : 11 + n_rights], refs[11 + n_rights]
    (out, turned_own, turned_other, lefts_next, dh0b, d_qkv, d_pairs, by_core, by_y, d_query, weight_buf, turned,
     da1, vector_rows, send_left, got_left, send, recv, local, *scratch) = refs[12 + n_rights :]
    x, y, c = (lax.axis_index(name) for name in ("x", "y", "c"))
    f32, b16 = jnp.float32, jnp.bfloat16
    cells, width = query.shape
    slots = 4 * cells
    n_pairs, head = width // 128, 64
    into = (((1,), (1,)), ((), ()))

    def backward(j, half):
        lanes = pl.ds(pl.multiple_of(j * 128, 128), 128)
        value_lanes = pl.ds(pl.multiple_of(width + j * 128, 128), 128)
        side = slice(half * head, (half + 1) * head)
        keys = pairs[:, :, :, lanes].reshape(slots, 128)[:, side]
        values = pairs[:, :, :, value_lanes].reshape(slots, 128)[:, side]
        mine, above = query[:, lanes][:, side], d_out[:, lanes][:, side]
        scores = lax.dot_general(keys, mine, into, preferred_element_type=f32) * scale
        scores = jnp.where(seg_keys[...] == seg_mine[...], scores, -1000000000.0)
        probs = jnp.exp(scores - log_total[pl.ds(2 * j + half, 1), :])
        d_probs = lax.dot_general(values, above, into, preferred_element_type=f32)
        inner = jnp.sum(probs * d_probs, axis=0, keepdims=True)
        d_scores = (probs * (d_probs - inner)).astype(b16)
        d_keys = jnp.dot(d_scores, mine, preferred_element_type=f32) * scale
        d_values = jnp.dot(probs.astype(b16), above, preferred_element_type=f32)
        d_pairs[0, j, :, side] = d_keys.astype(b16)
        d_pairs[1, j, :, side] = d_values.astype(b16)
        turned = keys.astype(f32).T.astype(b16)
        d_query[side] = jnp.dot(turned, d_scores, preferred_element_type=f32) * scale
        if half:
            d_qkv[:, lanes] = d_query[...].T.astype(b16)

    def to_core():
        return pltpu.make_async_remote_copy(
            src_ref=d_pairs.at[:, :, pl.ds(2 * cells, 2 * cells)], dst_ref=by_core,
            send_sem=send.at[0], recv_sem=recv.at[0], device_id={"c": 1 - c}, device_id_type=MESH,
        )

    def to_y():
        return pltpu.make_async_remote_copy(
            src_ref=d_pairs.at[:, :, pl.ds(cells, cells)], dst_ref=by_y,
            send_sem=send.at[1], recv_sem=recv.at[1], device_id={"y": 1 - y}, device_id_type=MESH,
        )

    def beside(i, right, odd):
        @pl.when(i < 2 * n_pairs)
        def _():
            backward(i // 2, odd)

    def fetch_weight():
        return pltpu.make_async_copy(weight, weight_buf, local.at[0])

    def keep_turned():
        return pltpu.make_async_copy(turned, turned_own, local.at[1])

    def send_turned():
        return pltpu.make_async_remote_copy(
            src_ref=turned, dst_ref=turned_other,
            send_sem=send.at[2], recv_sem=recv.at[2], device_id={"c": 1 - c}, device_id_type=MESH,
        )

    def to_other_left():
        return pltpu.make_async_remote_copy(
            src_ref=send_left, dst_ref=got_left,
            send_sem=send.at[3], recv_sem=recv.at[3], device_id={"c": 1 - c}, device_id_type=MESH,
        )

    def share():
        to_core().wait_recv()

        def add(j, carry):
            for kind in (0, 1):
                total = d_pairs[kind, j, : 2 * cells].astype(f32) + by_core[kind, j].astype(f32)
                d_pairs[kind, j, : 2 * cells] = total.astype(b16)
            return carry

        lax.fori_loop(0, n_pairs, add, 0)
        to_y().start()

    def collect():
        to_y().wait_recv()

        def add(j, carry):
            for kind in (0, 1):
                lanes = pl.ds(pl.multiple_of((kind + 1) * width + j * 128, 128), 128)
                total = d_pairs[kind, j, :cells].astype(f32) + by_y[kind, j].astype(f32)
                d_qkv[:, lanes] = total.astype(b16)
            return carry

        lax.fori_loop(0, n_pairs, add, 0)

    def turn():
        def tile(k, carry):
            turned[chunk_of(k)] = d_qkv[:, chunk_of(k)].astype(f32).T.astype(b16)
            return carry

        lax.fori_loop(0, 3 * width // CHUNK, tile, 0)
        keep_turned().start()
        send_turned().start()

    def project():
        fetch_weight().wait()
        for k in range(4):
            rows = weight_buf[k // 2, k % 2].reshape(width // 4, -1)[:, : 3 * width]
            da1[:, k * width // 4 : (k + 1) * width // 4] = lax.dot_general(
                d_qkv[...], rows, into, preferred_element_type=f32
            )

    def norm():
        value, above = h0[...], da1[...]
        centred = value - jnp.mean(value, axis=1, keepdims=True)
        inverse = lax.rsqrt(jnp.mean(centred * centred, axis=1, keepdims=True) + eps)
        normed = centred * inverse
        vector_rows[...] = jnp.zeros_like(vector_rows)
        vector_rows[0:1] = jnp.sum(above * normed, axis=0, keepdims=True)
        vector_rows[1:2] = jnp.sum(above, axis=0, keepdims=True)
        vector_rows[2:4] = vectors[1:3]
        above = above * vectors[0:1]
        inner = jnp.mean(above * normed, axis=1, keepdims=True)
        below = inverse * (above - jnp.mean(above, axis=1, keepdims=True) - normed * inner)
        dh0b[...] = (dh1[...] + below).astype(b16)

    def halves():
        for kind, source in enumerate((vector_rows, dh0b)):
            for part in range(8):
                eighth = (
                    lax.rem(c + part // 4, 2) * 4 + lax.rem(x + part // 2 % 2, 2) * 2 + lax.rem(y + part % 2, 2)
                )
                lanes = pl.ds(pl.multiple_of(eighth * (width // 8), width // 8), width // 8)
                block = source[:, lanes].astype(f32).T.astype(b16)
                rows = slice(part % 4 * (width // 8), (part % 4 + 1) * (width // 8))
                if part < 4:
                    lefts_next[1 + kind, rows, :cells] = block
                else:
                    send_left[kind, rows] = block
        to_other_left().start()

    def after(p):
        plan = {0: lambda: fetch_weight().start(), n_pairs: lambda: to_core().start(), n_pairs + 2: share}
        plan.update(zip(range(n_chunk_pairs - 2, n_chunk_pairs + 3), (collect, turn, project, norm, halves)))
        for when, action in plan.items():

            @pl.when(p == when)
            def _(action=action):
                action()

    n_chunk_pairs = (sum(sections) + 1) // 2
    scatter_kernel(
        n_h, sections, periods, left_starts, lefts, rights, out, scratch, [{"c": 1 - c}],
        lambda section, k: None, beside, after,
    )
    lefts_next[0] = left_one[...]
    to_other_left().wait_recv()
    for kind in (0, 1):
        lefts_next[1 + kind, :, cells:] = got_left[kind]
    keep_turned().wait()
    send_turned().wait()
    for copy in (to_core(), to_y(), to_other_left()):
        copy.wait_send()


def scatter_call(kernel, lefts, rights, operands, more_operands, out_shapes, out_specs, scratch, collective_id):
    periods = [own.shape[0] // CHUNK for own, *_ in rights]
    sections = [period * times for period, (*_, times) in zip(periods, rights)]
    n, cells = sum(sections), rights[0][0].shape[1]
    w = lefts.shape[1] // 4
    n_h = lax.axis_size("h")
    rows = w // n_h
    inner_h = n_h if rows % 16 == 0 else 1
    dma, bf16, f32 = pltpu.SemaphoreType.DMA, jnp.bfloat16, jnp.float32
    vmem, hbm = pl.BlockSpec(memory_space=pltpu.VMEM), pl.BlockSpec(memory_space=pl.ANY)
    others = max(inner_h - 1, 1)
    part_shape = jax.ShapeDtypeStruct((n, rows, CHUNK), f32)
    if inner_h == 1:
        part_shape = jax.ShapeDtypeStruct((n, w, CHUNK), bf16)
    part, *more = pl.pallas_call(
        functools.partial(kernel, inner_h, sections, periods),
        out_shape=[part_shape] + out_shapes,
        in_specs=[vmem] * (1 + len(operands)) + [hbm] * (2 * len(rights) + len(more_operands)),
        out_specs=[vmem] + out_specs,
        scratch_shapes=scratch
        + [
            pltpu.VMEM((3, CHUNK, 2 * cells), bf16),
            pltpu.VMEM((RING, 2 * w, CHUNK), f32),
            pltpu.VMEM((RING, 2 * w, CHUNK), bf16),
            pltpu.VMEM((n, 2 * w, CHUNK), bf16),
            pltpu.VMEM((RING, w, CHUNK), bf16),
            pltpu.VMEM((n, w, CHUNK), bf16),
            pltpu.VMEM((RING, w, CHUNK), bf16),
            pltpu.VMEM((n, others, w // inner_h, CHUNK), bf16),
            dma((3, 2)),
            dma((RING,)),
            dma((n,)),
            dma((RING,)),
            dma((n,)),
            dma((RING, others)),
            dma((n, others)),
        ],
        compiler_params=pltpu.CompilerParams(
            collective_id=collective_id, has_side_effects=True, vmem_limit_bytes=60 * 2**20
        ),
    )(lefts, *operands, *(half for pair in rights for half in pair[:2]), *more_operands)
    if inner_h == 1:
        part = lax.psum_scatter(part, "h", scatter_dimension=1, tiled=True).astype(f32)
    return part, *more


def scatter_product(lefts, left_starts, rights, vector, weights, product_type, with_sum, collective_id):
    (cells, features), columns = vector.shape, rights[-1][0].shape[0]
    dma = pltpu.SemaphoreType.DMA
    vmem, hbm = pl.BlockSpec(memory_space=pltpu.VMEM), pl.BlockSpec(memory_space=pl.ANY)

    def kernel(n_h, sections, periods, *refs):
        product_kernel(n_h, sections, periods, left_starts, len(weights), with_sum, *refs)

    return scatter_call(
        kernel,
        lefts,
        rights,
        [vector],
        weights,
        [jax.ShapeDtypeStruct((columns, cells), product_type)]
        + [jax.ShapeDtypeStruct((features, cells), jnp.float32)] * with_sum,
        [hbm] + [vmem] * with_sum,
        [
            pltpu.VMEM((3, features, CHUNK), jnp.bfloat16),
            pltpu.VMEM((2, CHUNK, cells), product_type),
            dma((3, len(weights))),
            dma((2,)),
        ],
        collective_id,
    )


def scatter_attention(lefts, left_starts, rights, operands, weight, scale, collective_id):
    cells, width = operands[0].shape
    bf16, f32, dma = jnp.bfloat16, jnp.float32, pltpu.SemaphoreType.DMA
    vmem, hbm = pl.BlockSpec(memory_space=pltpu.VMEM), pl.BlockSpec(memory_space=pl.ANY)

    def kernel(n_h, sections, periods, *refs):
        attention_kernel(n_h, sections, periods, left_starts, scale, *refs)

    return scatter_call(
        kernel,
        lefts,
        rights,
        operands,
        [weight],
        [
            jax.ShapeDtypeStruct((3 * width, cells), bf16),
            jax.ShapeDtypeStruct((3 * width, cells), bf16),
            jax.ShapeDtypeStruct((3,) + lefts.shape[1:], bf16),
            jax.ShapeDtypeStruct((cells, width), bf16),
        ],
        [hbm, hbm, vmem, vmem],
        [
            pltpu.VMEM((cells, 3 * width), bf16),
            pltpu.VMEM((2, width // 128, 4 * cells, 128), bf16),
            pltpu.VMEM((2, width // 128, 2 * cells, 128), bf16),
            pltpu.VMEM((2, width // 128, cells, 128), bf16),
            pltpu.VMEM((128, cells), f32),
            pltpu.VMEM(weight.shape, bf16),
            pltpu.VMEM((3 * width, cells), bf16),
            pltpu.VMEM((cells, width), f32),
            pltpu.VMEM((cells, width), f32),
            pltpu.VMEM((2, width // 2, cells), bf16),
            pltpu.VMEM((2, width // 2, cells), bf16),
            dma((4,)),
            dma((4,)),
            dma((2,)),
        ],
        collective_id,
    )


def own_half(left):
    half = left.shape[1] // 2
    return jnp.concatenate([left[:, :half], swap(left[:, half:], "c")], axis=0)


def left_of(left, pieces):
    left = own_half(relative(left, 1)).T
    n_h = lax.axis_size("h")
    left = left.reshape(4, n_h, pieces, -1, left.shape[1])
    return left.transpose(2, 0, 1, 3, 4).reshape(pieces, -1, left.shape[-1])


def both_cores(right, times=1):
    return right, swap(right, "c"), times


def columns_of(chunks):
    return chunks.transpose(1, 0, 2).reshape(chunks.shape[1], -1)


def on_device(
    counts,
    library,
    coords,
    lengths,
    cotangent,
    w_enc,
    w_qkv,
    w_out,
    gain_one,
    shift_one,
    w_up,
    w_down,
    gain_two,
    shift_two,
    w_dec,
):
    rows = counts.shape[0]
    width = w_qkv.shape[1] // 3
    heads = HEADS
    head_width = width // heads
    att_scale = head_width ** (-0.5)
    group_size = 4
    slots = rows * group_size
    scale = 10000.0 / library
    genes = counts.shape[1]
    padded = -(-genes // CHUNK) * CHUNK
    counts_f = counts.astype(jnp.float32)
    cot = jnp.pad(cotangent.T, ((0, padded - genes), (0, 0)))
    cot_pair = both_cores(cot)
    pe = by_owner(positions(coords, width), 1)
    ends = jnp.cumsum(lengths[0])
    group = [
        (lax.axis_index("y") ^ by_y) * 2 + (lax.axis_index("c") ^ by_c)
        for by_c in range(2)
        for by_y in range(2)
    ]
    place = jnp.concatenate([at * rows + jnp.arange(rows, dtype=jnp.int32) for at in group])
    seg_all = jnp.sum((place[:, None] >= ends[None, :]).astype(jnp.int32), axis=1)
    same = (seg_all[:rows, None] == seg_all[None, :])[None]
    vectors = jnp.stack([gain_one, shift_one, gain_two, shift_two], axis=1)
    vectors = jnp.pad(vectors, ((0, 0), (0, 124)))
    pad = ((0, 0), (0, padded - genes))
    quarter = padded // CHUNK // 4 * CHUNK
    gene_cuts = [0, quarter, 2 * quarter, 3 * quarter, padded]
    shards = [
        jnp.pad(w_enc.T, pad),
        jnp.concatenate([w_qkv, vectors], axis=1),
        by_owner(w_out, 1),
        by_owner(w_up, 1),
        by_owner(w_down, 1),
        jnp.pad(w_dec.T, pad),
    ]
    cuts = [gene_cuts, [0, width // 2 * 3, 3 * width + 128], [0, width]]
    cuts += [[0, 2 * width, 4 * width], [0, width // 2, width]]
    cuts += [[0, padded]]
    order = [(0, 0), (0, 1), (0, 2), (0, 3), (1, 0), (1, 1), (2, 0), (3, 0), (3, 1), (4, 0), (4, 1), (5, 0)]
    gathered, xb, h0, a1, query, kv_all = gather_all(
        shards, 5, cuts, order, counts.T, scale[None, :], pe.T, 0
    )
    xb_pair = both_cores(xb)
    enc_all, qkv_all, out_all, up_all, down_all = (
        w.reshape(-1, w.shape[-1]) for w in gathered[:5]
    )
    vectors = qkv_all[:, 3 * width :].astype(jnp.float32).T
    g1f, b1f, g2f, b2f = vectors[0], vectors[1], vectors[2], vectors[3]
    kv_pairs, query_b = kv_all, query
    query = query.reshape(rows, heads, head_width)
    kv_all = kv_all.reshape(slots, -1)
    dec_own = gathered[5]
    middle = dec_own.shape[1] // 256 * 128
    by_x, by_y = swap(dec_own, "x"), swap(dec_own, "y")
    far = (swap(by_x[:, :middle], "y"), swap(by_y[:, middle:], "x"))
    dec_parts = [dec_own, by_y, by_x, jnp.concatenate(far, axis=1)]
    dec_parts += [swap(part, "c") for part in dec_parts]
    keys = kv_all[:, :width].reshape(slots, heads, head_width)
    values = kv_all[:, width:].reshape(slots, heads, head_width)

    def scores_of():
        raw = (
            jnp.einsum("qhd,khd->hqk", query, keys, preferred_element_type=jnp.float32) * att_scale
        )
        return jnp.where(same, raw, -1000000000.0)

    scores = scores_of()
    top = jnp.max(scores, axis=-1, keepdims=True)
    expo = jnp.exp(scores - top)
    total = jnp.sum(expo, axis=-1, keepdims=True)
    log_total = top + jnp.log(total)
    probs_b = (expo / total).astype(jnp.bfloat16)
    attended = jnp.einsum("hqk,khd->qhd", probs_b, values, preferred_element_type=jnp.float32)
    attended_b = attended.reshape(rows, width).astype(jnp.bfloat16)
    attended_b = by_owner(attended_b, 1)
    h1 = h0 + matmul(attended_b, out_all)
    a2 = layer_norm(h1, g2f, b2f).astype(jnp.bfloat16)
    hidden = matmul(a2, up_all)
    act, pull = jax.vjp(lambda v: jax.nn.gelu(v, approximate=False), hidden)
    act, slope = lax.optimization_barrier(
        (act.astype(jnp.bfloat16), pull(jnp.ones_like(hidden))[0])
    )
    h2 = h1 + matmul(act, down_all)
    hb = h2.astype(jnp.bfloat16)
    grad_dec, logits, dh2 = scatter_product(
        left_of(hb, 1), [0], [cot_pair], relative(hb, 1), dec_parts, jnp.bfloat16, True, 1
    )
    own_rows = grad_dec.shape[1]
    grad_dec = columns_of(grad_dec)[:, :genes].T
    logits = logits[:genes].T
    dh2 = relative(dh2, 0).T
    dfb = dh2.astype(jnp.bfloat16)
    d_act = contract_cols(dfb, down_all)
    d_hidden = (d_act * slope).astype(jnp.bfloat16)
    da2 = contract_cols(d_hidden, up_all)
    norm_pull = jax.vjp(layer_norm, h1, g2f, b2f)[1]
    dh1_norm, grad_gain_two, grad_shift_two = norm_pull(da2)
    dh1 = dh2 + dh1_norm
    dab = dh1.astype(jnp.bfloat16)
    d_attended = contract_cols(dab, out_all).astype(jnp.bfloat16)
    d_attended = from_owner(d_attended, 1)
    lefts = [left_of(a2, 1), left_of(act, act.shape[1] // width), left_of(attended_b, 1)]
    pieces = (4 * width,) + (width,) * 4
    rights = [both_cores(d_hidden.T), both_cores(dfb.T, 4), both_cores(dab.T)]
    operands = [query_b, kv_pairs, d_attended, log_total[:, :, 0], seg_all[:, None], seg_all[None, :rows], h0, dh1]
    operands += [jnp.pad(jnp.stack([g1f, grad_gain_two, grad_shift_two]), ((0, 5), (0, 0))), left_of(a1, 1)[0]]
    grads, d_qkv, d_qkv_other, lefts, dh0b = scatter_attention(
        jnp.concatenate(lefts, axis=0),
        [sum(pieces[:k]) // CHUNK for k in range(len(pieces) + 1)],
        rights,
        operands,
        gathered[1],
        att_scale,
        2,
    )
    ends = [0]
    for columns in (4 * width, 4 * width, width):
        ends.append(ends[-1] + columns // CHUNK)
    grad_up, grad_down, grad_out = (grads[low:high] for low, high in zip(ends, ends[1:]))
    grad_up, grad_out = columns_of(grad_up), columns_of(grad_out)
    grad_down = grad_down.reshape(4, -1, own_rows, CHUNK).transpose(0, 2, 1, 3)
    grad_down = grad_down.reshape(4 * own_rows, -1)
    grad_out, grad_up, grad_down = (from_owner(g, 1) for g in (grad_out, grad_up, grad_down))
    unit = jnp.eye(rows, dtype=jnp.bfloat16)
    grads, d_xb = scatter_product(
        lefts,
        [0, 3 * width // CHUNK, (3 * width + rows) // CHUNK],
        [(d_qkv, d_qkv_other, 1), (unit, unit, 1), xb_pair],
        dh0b,
        [enc_all],
        jnp.float32,
        False,
        3,
    )
    ends = [0]
    for columns in (3 * width, rows):
        ends.append(ends[-1] + columns // CHUNK)
    grad_qkv, grad_vectors, grad_enc = (
        grads[low:high] for low, high in zip(ends, ends[1:] + [grads.shape[0]])
    )
    grad_qkv, grad_enc = columns_of(grad_qkv), columns_of(grad_enc)
    grad_gain_one, grad_shift_one, grad_gain_two, grad_shift_two = (
        grad_vectors[0, :, k] for k in range(4)
    )
    grad_enc = grad_enc[:, :genes].T
    d_xb = d_xb[:genes].T
    counts_grad = d_xb * scale[:, None] / (1.0 + counts_f * scale[:, None])
    return (
        logits,
        counts_grad,
        grad_enc,
        grad_qkv,
        grad_out,
        grad_gain_one,
        grad_shift_one,
        grad_up,
        grad_down,
        grad_gain_two,
        grad_shift_two,
        grad_dec,
    )


ALL = ("h", "x", "y", "c")


def solution(mesh):
    n_dp, n_fsdp = mesh.shape["dp"], mesh.shape["fsdp"]
    mesh = Mesh(mesh.devices.reshape((n_dp // 2, 2, 2, n_fsdp // 2)), ALL)
    placed = (
        P(ALL, None),
        P(ALL),
        P(None, ALL),
        P(("h", "x"), None),
        P(ALL, None),
        P(None, ALL),
        P(ALL, None),
        P(ALL, None),
        P(ALL),
        P(ALL),
        P(ALL, None),
        P(ALL, None),
        P(ALL),
        P(ALL),
        P(None, ALL),
    )
    return jax.shard_map(
        on_device,
        mesh=mesh,
        in_specs=placed,
        out_specs=(
            P(ALL, None),
            P(ALL, None),
            P(None, ALL),
            P(ALL, None),
            P(ALL, None),
            P(ALL),
            P(ALL),
            P(ALL, None),
            P(ALL, None),
            P(ALL),
            P(ALL),
            P(None, ALL),
        ),
        check_vma=False,
    )
```

```python
import functools
import math

import jax
import jax.numpy as jnp
from jax import lax
from jax.experimental import pallas as pl
from jax.experimental.pallas import tpu as pltpu
from jax.sharding import Mesh
from jax.sharding import PartitionSpec as P

HEADS = 16
MESH = pl.DeviceIdType.MESH
RING = 8
CHUNK = 256


eps = 1e-05


def layer_norm(value, gain, shift):
    mean = jnp.mean(value, axis=1, keepdims=True)
    centred = value - mean
    variance = jnp.mean(centred * centred, axis=1, keepdims=True)
    return centred * lax.rsqrt(variance + eps) * gain + shift


def positions(coords, width):
    quarter = width // 4
    freqs = 0.05 * jnp.exp(-jnp.arange(quarter, dtype=jnp.float32) * (math.log(10000.0) / quarter))
    along_x = coords[0].astype(jnp.float32)[:, None] * freqs[None, :]
    along_y = coords[1].astype(jnp.float32)[:, None] * freqs[None, :]
    return jnp.concatenate(
        [jnp.sin(along_x), jnp.cos(along_x), jnp.sin(along_y), jnp.cos(along_y)], axis=1
    )


def contract_rows(left, right):
    return lax.dot_general(
        left, right, (((0,), (0,)), ((), ())), preferred_element_type=jnp.float32
    )


def contract_cols(left, right):
    return lax.dot_general(
        left, right, (((1,), (1,)), ((), ())), preferred_element_type=jnp.float32
    )


def matmul(left, right):
    return jnp.dot(left, right, preferred_element_type=jnp.float32)


def swap(value, axis):
    return lax.ppermute(value, axis, [(0, 1), (1, 0)])


def by_owner(value, axis):
    n_h = lax.axis_size("h")
    at = value.shape
    block = at[axis] // (8 * n_h)
    split = value.reshape(at[:axis] + (n_h, 2, 2, 2, block) + at[axis + 1 :])
    order = list(range(axis)) + [axis + 3, axis + 1, axis + 2, axis, axis + 4]
    order += list(range(axis + 5, split.ndim))
    return split.transpose(order).reshape(at)


def from_owner(value, axis):
    n_h = lax.axis_size("h")
    at = value.shape
    block = at[axis] // (8 * n_h)
    split = value.reshape(at[:axis] + (2, 2, 2, n_h, block) + at[axis + 1 :])
    order = list(range(axis)) + [axis + 3, axis + 1, axis + 2, axis, axis + 4]
    order += list(range(axis + 5, split.ndim))
    return split.transpose(order).reshape(at)


def relative(value, axis):
    eighth = value.shape[axis] // 8
    mine = lax.axis_index("c") * 4 + lax.axis_index("x") * 2 + lax.axis_index("y")
    parts = [
        lax.dynamic_slice_in_dim(value, (mine ^ part) * eighth, eighth, axis) for part in range(8)
    ]
    return jnp.concatenate(parts, axis=axis)


def greet(peers):
    barrier = pltpu.get_barrier_semaphore()
    for peer in peers:
        pl.semaphore_signal(barrier, inc=1, device_id=peer, device_id_type=MESH)
    pl.semaphore_wait(barrier, len(peers))


def gather_kernel(n_h, jobs, n_full, shards, wholes, sems, between):
    own_sem, h_send, h_recv, send, recv = sems
    h, x, y, c = (lax.axis_index(name) for name in ("h", "x", "y", "c"))
    h = 0 if n_h == 1 else h
    to_x, to_y, to_c = {"x": 1 - x}, {"y": 1 - y}, {"c": 1 - c}
    greet([{"h": lax.rem(h + d, n_h)} for d in range(1, n_h)] + [to_x, to_y, to_c])

    def rows_of(job, at):
        array, low, high, _ = job
        rows = shards[array].shape[0]
        place = (pl.ds(at * rows, rows), pl.ds(low, high - low))
        return wholes[array].at[(c, x, y, *place) if array < n_full else place]

    def h_copy(j, d):
        array, low, high, _ = jobs[j]
        return pltpu.make_async_remote_copy(
            src_ref=shards[array].at[:, pl.ds(low, high - low)],
            dst_ref=rows_of(jobs[j], h),
            send_sem=h_send.at[j, d - 1],
            recv_sem=h_recv.at[j, d - 1],
            device_id={"h": lax.rem(h + d, n_h)},
            device_id_type=MESH,
        )

    def own_copy(j):
        array, low, high, _ = jobs[j]
        return pltpu.make_async_copy(
            shards[array].at[:, pl.ds(low, high - low)], rows_of(jobs[j], h), own_sem.at[j]
        )

    def block_copy(j, k, block, to, columns):
        view = wholes[jobs[j][0]].at[(*block, slice(None), pl.ds(columns[0], columns[1] - columns[0]))]
        return pltpu.make_async_remote_copy(
            src_ref=view,
            dst_ref=view,
            send_sem=send.at[j, k],
            recv_sem=recv.at[j, k],
            device_id=to,
            device_id_type=MESH,
        )

    own, by_x, by_y, far = (c, x, y), (c, 1 - x, y), (c, x, 1 - y), (c, 1 - x, 1 - y)

    def copy(j, k):
        _, low, high, middle = jobs[j]
        block, to, columns = [
            (own, to_x, (low, high)),
            (own, to_y, (low, high)),
            (own, to_c, (low, high)),
            (by_x, to_y, (low, middle)),
            (by_y, to_x, (middle, high)),
            (by_x, to_c, (low, high)),
            (by_y, to_c, (low, high)),
            (far, to_c, (low, high)),
        ][k]
        return block_copy(j, k, block, to, columns)

    def start_h(j):
        own_copy(j).start()
        for d in range(1, n_h):
            h_copy(j, d).start()

    whole = set()

    def landed(j):
        if j not in whole:
            whole.add(j)
            for k in (2, 5, 6, 7):
                copy(j, k).wait_recv()

    n = sum(array < n_full for array, *_ in jobs)
    ahead = 2
    for j in range(ahead):
        start_h(j)
    for step in range(n + 2):
        if step < n:
            own_copy(step).wait()
            for d in range(1, n_h):
                h_copy(step, d).wait_recv()
            for k in (0, 1, 2):
                copy(step, k).start()
            if step + ahead < len(jobs):
                start_h(step + ahead)
        if 0 <= step - 1 < n:
            for k in (0, 1):
                copy(step - 1, k).wait_recv()
            for k in (3, 4, 5, 6):
                copy(step - 1, k).start()
        if 0 <= step - 2 < n:
            for k in (3, 4):
                copy(step - 2, k).wait_recv()
            copy(step - 2, 7).start()
        between(step, landed)
    for j in range(n, len(jobs)):
        own_copy(j).wait()
        for d in range(1, n_h):
            h_copy(j, d).wait_recv()
    for j in range(len(jobs)):
        for d in range(1, n_h):
            h_copy(j, d).wait_send()
    for j in range(n):
        for k in range(8):
            copy(j, k).wait_send()
        landed(j)


def front_kernel(n_h, jobs, n_arrays, n_full, *refs):
    shards, (counts, tail, scale, pe) = refs[:n_arrays], refs[n_arrays : n_arrays + 4]
    rest = refs[n_arrays + 4 :]
    wholes, (xb, h0, a1, query, pairs) = rest[:n_arrays], rest[n_arrays : n_arrays + 5]
    (count_buf, enc_buf, xb_buf, total, qkv_buf, mine, count_sem, enc_sem, xb_sem, qkv_sem, kv_sem,
     kv_send, kv_recv, *sems) = rest[n_arrays + 5 :]
    y, c = lax.axis_index("y"), lax.axis_index("c")
    f32, b16 = jnp.float32, jnp.bfloat16
    width = h0.shape[1]
    n_chunks = xb.shape[0] // CHUNK
    by_chunk = lambda k: pl.ds(pl.multiple_of(k * CHUNK, CHUNK), CHUNK)

    def loads(k, last):
        slot = lax.rem(k, 2)
        source = tail if last else counts.at[by_chunk(k)]
        return (
            pltpu.make_async_copy(source, count_buf.at[slot], count_sem.at[slot]),
            pltpu.make_async_copy(
                wholes[0].at[:, :, :, :, by_chunk(k)], enc_buf.at[slot], enc_sem.at[slot]
            ),
        )

    def store(k):
        slot = lax.rem(k, 2)
        return pltpu.make_async_copy(xb_buf.at[slot], xb.at[by_chunk(k)], xb_sem.at[slot])

    def encode(k, first, last, low, high):
        slot = lax.rem(k, 2)
        for copy in loads(k, last):
            copy.wait()
        if not last:

            @pl.when(k + 1 < (high - 1 if high == n_chunks else high))
            def _():
                for copy in loads(k + 1, False):
                    copy.start()

        @pl.when(k >= low + 2)
        def _():
            store(k - 2).wait()

        value = jnp.log1p(count_buf[slot].astype(f32) * scale[...]).astype(b16)
        xb_buf[slot] = value
        store(k).start()
        term = jnp.dot(enc_buf[slot].reshape(width, CHUNK), value, preferred_element_type=f32)
        if first:

            @pl.when(k == 0)
            def _():
                total[...] = pe[...] + term

            @pl.when(k > 0)
            def _():
                total[...] += term

        else:
            total[...] += term

    def encode_job(low, high):
        low, high = low // CHUNK, high // CHUNK
        stop = high - 1 if high == n_chunks else high
        for copy in loads(jnp.int32(low), False):
            copy.start()

        def body(k, carry):
            encode(k, low == 0, False, low, high)
            return carry

        lax.fori_loop(low, stop, body, 0)
        if stop < high:
            for copy in loads(jnp.int32(stop), True):
                copy.start()
            encode(jnp.int32(stop), False, True, low, high)
        for k in range(max(low, high - 2), high):
            store(jnp.int32(k)).wait()

    def fetch_qkv():
        return pltpu.make_async_copy(wholes[1], qkv_buf, qkv_sem.at[0])

    def project():
        fetch_qkv().wait()
        vectors = qkv_buf[:, :, :, :, 3 * width :].reshape(width, 128).astype(f32)
        value = total[...]
        centred = value - jnp.mean(value, axis=0, keepdims=True)
        variance = jnp.mean(centred * centred, axis=0, keepdims=True)
        normed = centred * lax.rsqrt(variance + eps) * vectors[:, 0:1] + vectors[:, 1:2]
        h0[...] = value.T
        a1[...] = normed.T.astype(b16)

        def tile(k):
            weight = qkv_buf[:, :, :, :, by_chunk(k)].reshape(width, CHUNK)
            return jnp.dot(a1[...], weight, preferred_element_type=f32).astype(b16)

        def keys(k, carry):
            mine[:, by_chunk(k)] = tile(k + width // CHUNK)
            return carry

        lax.fori_loop(0, 2 * width // CHUNK, keys, 0)
        kv_own().start()
        kv_copy(0).start()

        def queries(k, carry):
            query[:, by_chunk(k)] = tile(k)
            return carry

        lax.fori_loop(0, width // CHUNK, queries, 0)

    def kv_own():
        return pltpu.make_async_copy(mine, pairs.at[0, 0], kv_sem.at[0])

    def kv_copy(k):
        return pltpu.make_async_remote_copy(
            src_ref=(mine, pairs.at[0])[k],
            dst_ref=(pairs.at[0, 1], pairs.at[1])[k],
            send_sem=kv_send.at[k],
            recv_sem=kv_recv.at[k],
            device_id=({"y": 1 - y}, {"c": 1 - c})[k],
            device_id_type=MESH,
        )

    arrays = [array for array, *_ in jobs]
    enc_jobs = [j for j, array in enumerate(arrays) if array == 0]
    qkv_jobs = [j for j, array in enumerate(arrays) if array == 1]
    at = max(qkv_jobs) + 3

    def between(step, landed):
        if step - 3 in enc_jobs:
            landed(step - 3)
            encode_job(*jobs[step - 3][1:3])
        if step == at:
            for j in qkv_jobs:
                landed(j)
            fetch_qkv().start()
            project()
        if step == at + 2:
            kv_own().wait()
            kv_copy(0).wait_recv()
            kv_copy(1).start()

    gather_kernel(n_h, jobs, n_full, shards, wholes, sems, between)
    kv_copy(0).wait_send()
    kv_copy(1).wait()


def gather_all(shards, n_full, cuts, order, counts, scale, pe, collective_id):
    n_h = lax.axis_size("h")
    if any(shard.shape[0] % 16 for shard in shards):
        shards = [lax.all_gather(s, "h", axis=0, tiled=True) for s in shards]
        n_h = 1
    jobs = []
    for array, piece in order:
        low, high = cuts[array][piece], cuts[array][piece + 1]
        jobs.append((array, low, high, low + (high - low) // 256 * 128))
    n, others, dma = len(jobs), max(n_h - 1, 1), pltpu.SemaphoreType.DMA
    shapes = [(n_h * s.shape[0], s.shape[1]) for s in shards]
    (genes, cells), width, padded = counts.shape, pe.shape[0], shards[0].shape[1]
    tail = counts[genes // CHUNK * CHUNK :]
    tail = jnp.pad(tail, ((0, CHUNK - tail.shape[0]), (0, 0)))
    bf16, f32 = jnp.bfloat16, jnp.float32
    vmem, hbm = pl.BlockSpec(memory_space=pltpu.VMEM), pl.BlockSpec(memory_space=pl.ANY)
    out = pl.pallas_call(
        functools.partial(front_kernel, n_h, jobs, len(shards), n_full),
        out_shape=[
            jax.ShapeDtypeStruct((2, 2, 2) + shape if k < n_full else shape, bf16)
            for k, shape in enumerate(shapes)
        ]
        + [
            jax.ShapeDtypeStruct((padded, cells), bf16),
            jax.ShapeDtypeStruct((cells, width), f32),
            jax.ShapeDtypeStruct((cells, width), bf16),
            jax.ShapeDtypeStruct((cells, width), bf16),
            jax.ShapeDtypeStruct((2, 2, cells, 2 * width), bf16),
        ],
        in_specs=[hbm] * (len(shards) + 2) + [vmem] * 2,
        out_specs=[hbm] * (len(shards) + 1) + [vmem] * 3 + [hbm],
        scratch_shapes=[
            pltpu.VMEM((2, CHUNK, cells), bf16),
            pltpu.VMEM((2, 2, 2, 2, width // 8, CHUNK), bf16),
            pltpu.VMEM((2, CHUNK, cells), bf16),
            pltpu.VMEM((width, cells), f32),
            pltpu.VMEM((2, 2, 2, width // 8, shards[1].shape[1]), bf16),
            pltpu.VMEM((cells, 2 * width), bf16),
            dma((2,)),
            dma((2,)),
            dma((2,)),
            dma((1,)),
            dma((1,)),
            dma((2,)),
            dma((2,)),
            dma((n,)),
            dma((n, others)),
            dma((n, others)),
            dma((n, 8)),
            dma((n, 8)),
        ],
        compiler_params=pltpu.CompilerParams(
            collective_id=collective_id, has_side_effects=True, vmem_limit_bytes=60 * 2**20
        ),
    )(*shards, counts, tail, scale, pe)
    return out[: len(shards)], *out[len(shards) :]


def scatter_kernel(n_h, sections, periods, left_starts, lefts, rights, out, scratch, peers, begin, prefetch, beside, after):
    (right_buf, own, s1, r1, s2, r2, s3, r3, load_sem, send1, recv1, send2, recv2, send3, recv3) = scratch
    h, x, y = (lax.axis_index(name) for name in ("h", "x", "y"))
    to_x, to_y = {"x": 1 - x}, {"y": 1 - y}
    w = s3.shape[1]
    rows = w // n_h
    f32, b16 = jnp.float32, jnp.bfloat16
    n_sections = len(sections)
    starts = [sum(sections[:k]) for k in range(n_sections)]
    n = sum(sections)
    cells = right_buf.shape[2] // 2
    greet([{"h": lax.rem(h + d, n_h)} for d in range(1, n_h)] + [to_x, to_y] + peers)
    begin()

    def loads(i, section, k):
        slot = lax.rem(i, 3)
        return [
            pltpu.make_async_copy(
                rights[2 * section + half].at[chunk_of(k)],
                right_buf.at[slot, :, pl.ds(half * cells, cells)],
                load_sem.at[slot, half],
            )
            for half in (0, 1)
        ]

    def start_loads(i):
        for section, (start, count) in enumerate(zip(starts, sections)):

            @pl.when((i >= start) & (i < start + count))
            def _(section=section, start=start):
                for copy in loads(i, section, lax.rem(i - start, periods[section])):
                    copy.start()
                prefetch(section, i - start)

    def hop(i, source, target, send_sem, recv_sem, to):
        slot = lax.rem(i, RING)
        return pltpu.make_async_remote_copy(
            src_ref=source.at[slot], dst_ref=target.at[i], send_sem=send_sem.at[slot],
            recv_sem=recv_sem.at[i], device_id=to, device_id_type=MESH,
        )

    def first(i, odd):
        return hop(i, s1, r1, send1, recv1, to_y if odd else to_x)

    def second(i, odd):
        return hop(i, s2, r2, send2, recv2, to_x if odd else to_y)

    def third(i, d):
        to = lax.rem(h + d, n_h)
        slot = lax.rem(i, RING)
        return pltpu.make_async_remote_copy(
            src_ref=s3.at[slot, pl.ds(to * rows, rows)], dst_ref=r3.at[i, d - 1],
            send_sem=send3.at[slot, d - 1], recv_sem=recv3.at[i, d - 1],
            device_id={"h": to}, device_id_type=MESH,
        )

    def multiply(i, odd):
        slot = lax.rem(i, RING)
        for copy in loads(i, 0, 0):
            copy.wait()
        left = lefts[sum((i + 1024 - start) // 1024 for start in left_starts[1:]) if left_starts[1:] else 0]
        right = right_buf.at[lax.rem(i, 3)]

        @pl.when(i >= RING)
        def _():
            first(i - RING, odd).wait_send()

        part = lax.dot_general(left, right[...], (((1,), (1,)), ((), ())), preferred_element_type=f32)
        own[slot, :w] = part[:w]
        if odd:
            own[slot, w:] = part[2 * w : 3 * w]
            s1[slot, :w] = part[w : 2 * w].astype(b16)
            s1[slot, w:] = part[3 * w :].astype(b16)
        else:
            own[slot, w:] = part[w : 2 * w]
            s1[slot] = part[2 * w :].astype(b16)
        first(i, odd).start()

        beside(i, right, odd)
        start_loads(i + 2)

    def pass_on(i, odd):
        slot = lax.rem(i, RING)
        first(i, odd).wait_recv()

        @pl.when(i >= RING)
        def _():
            second(i - RING, odd).wait_send()

        s2[slot] = (own[slot, w:] + r1[i, w:].astype(f32)).astype(b16)
        second(i, odd).start()

    def keep(i, odd):
        slot = lax.rem(i, RING)
        second(i, odd).wait_recv()
        part = own[slot, :w] + r1[i, :w].astype(f32) + r2[i].astype(f32)
        if n_h == 1:
            out[i] = part.astype(b16)
            return

        @pl.when(i >= RING)
        def _():
            for d in range(1, n_h):
                third(i - RING, d).wait_send()

        s3[slot] = part.astype(b16)
        for d in range(1, n_h):
            third(i, d).start()

    def finish(i, odd):
        if n_h == 1:
            return
        total = s3[lax.rem(i, RING), pl.ds(h * rows, rows)].astype(f32)
        for d in range(1, n_h):
            third(i, d).wait_recv()
            total = total + r3[i, d - 1].astype(f32)
        out[i] = total

    start_loads(jnp.int32(0))
    start_loads(jnp.int32(1))
    pairs = (n + 1) // 2

    def step(p, carry):
        for lag, stage in enumerate((multiply, pass_on, keep, finish)):
            for odd in (0, 1):
                i = 2 * (p - lag) + odd

                @pl.when((i >= 0) & (i < n))
                def _(stage=stage, i=i, odd=odd):
                    stage(i, odd)

        after(p)
        return carry

    lax.fori_loop(0, pairs + 3, step, 0)
    for i in range(max(n - RING, 0), n):
        first(i, i % 2).wait_send()
        second(i, i % 2).wait_send()
        for d in range(1, n_h):
            third(i, d).wait_send()


def chunk_of(k):
    return pl.ds(pl.multiple_of(k * CHUNK, CHUNK), CHUNK)


def eighth_of(part):
    c, x, y = (lax.axis_index(name) for name in ("c", "x", "y"))
    return lax.rem(c + part // 4, 2) * 4 + lax.rem(x + part // 2 % 2, 2) * 2 + lax.rem(y + part % 2, 2)


def product_kernel(n_h, sections, periods, left_starts, n_weights, *refs):
    lefts, vector = refs[:2]
    n_rights = 2 * len(sections)
    rights, weights = refs[2 : 2 + n_rights], refs[2 + n_rights : 2 + n_rights + n_weights]
    rest = refs[2 + n_rights + n_weights :]
    split = n_weights == 8
    out, product = rest[:2]
    summed, turned, *fetched = rest[2:6] if split else (None, None)
    rest = rest[6:] if split else rest[2:]
    total, swap_send, swap_recv = rest[:3] if split else (None, None, None)
    weight_buf, product_buf, weight_sem, product_sem, *scratch = rest[3:] if split else rest
    begin, count = sum(sections[:-1]), sections[-1]
    cells, features = vector.shape
    c = lax.axis_index("c")
    middle = weights[0].shape[1] // CHUNK
    spans = []
    if split:
        spans = [(0, 0, 2), (0, 2, 8), (0, 8, middle)]
        spans += [(1, 0, (count - middle) // 2), (1, (count - middle) // 2, count - middle)]

    def weight_loads(k, half, at):
        slot = lax.rem(k, 3)
        columns = chunk_of(at)
        sources = [weight.at[:, columns] for weight in weights]
        if split:
            sources = [weight.at[:, columns] for weight in weights[4 * half : 4 * half + 4]]
            sources += [fetched[half].at[part, :, columns] for part in range(4)]
        size = features // len(sources)
        return [
            pltpu.make_async_copy(
                source, weight_buf.at[slot, pl.ds(part * size, size)], weight_sem.at[slot, part]
            )
            for part, source in enumerate(sources)
        ]

    def swap_copy(span, part):
        half, low, high = spans[span]
        columns = pl.ds(low * CHUNK, (high - low) * CHUNK)
        return pltpu.make_async_remote_copy(
            src_ref=weights[4 * half + part].at[:, columns],
            dst_ref=fetched[half].at[part, :, columns],
            send_sem=swap_send.at[span, part],
            recv_sem=swap_recv.at[span, part],
            device_id={"c": 1 - c},
            device_id_type=MESH,
        )

    def start():
        for span in range(len(spans)):
            for part in range(4):
                swap_copy(span, part).start()

    def product_store(k):
        slot = lax.rem(k, 2)
        return pltpu.make_async_copy(product_buf.at[slot], product.at[chunk_of(k)], product_sem.at[slot])

    def prefetch(section, k):
        if section != len(sections) - 1:
            return
        if not split:
            for copy in weight_loads(k, 0, k):
                copy.start()
            return
        for span, (half, low, _) in enumerate(spans):

            @pl.when(k == half * middle + low)
            def _(span=span):
                for part in range(4):
                    swap_copy(span, part).wait_recv()

        for half, here in enumerate((k < middle, k >= middle)):

            @pl.when(here)
            def _(half=half):
                for copy in weight_loads(k, half, k - half * middle):
                    copy.start()

    def multiply(k, right):
        for copy in weight_loads(k, 0, 0):
            copy.wait()
        weight = weight_buf[lax.rem(k, 3)]

        @pl.when(k >= 2)
        def _():
            product_store(k - 2).wait()

        value = jnp.dot(vector[...], weight, preferred_element_type=jnp.float32)
        product_buf[lax.rem(k, 2)] = value.T.astype(product_buf.dtype)
        product_store(k).start()
        if split:
            term = jnp.dot(weight, right[:, :cells], preferred_element_type=jnp.float32)

            @pl.when(k == 0)
            def _():
                total[...] = term

            @pl.when(k > 0)
            def _():
                total[...] += term

    def beside(i, right, odd):
        if begin == 0:
            multiply(i, right)
        else:

            @pl.when(i >= begin)
            def _():
                multiply(i - begin, right)

    scatter_kernel(
        n_h, sections, periods, left_starts, lefts, rights, out, scratch, [{"c": 1 - c}] if split else [],
        start, prefetch, beside, lambda p: None,
    )
    for k in range(max(count - 2, 0), count):
        product_store(k).wait()
    if split:
        size = features // 8
        for part in range(8):
            block = total[part * size : (part + 1) * size]
            place = pl.ds(pl.multiple_of(eighth_of(part) * size, size), size)
            summed[:, place] = block.T
            turned[place] = block.astype(turned.dtype)
        for span in range(len(spans)):
            for part in range(4):
                swap_copy(span, part).wait_send()


def attention_kernel(n_h, sections, periods, left_starts, scale, *refs):
    lefts, query, pairs, d_out, log_total, seg_keys, seg_mine, h0, dh1, vectors, left_one = refs[:11]
    n_rights = 2 * len(sections)
    rights, weight = refs[11 : 11 + n_rights], refs[11 + n_rights]
    (out, turned_own, turned_other, lefts_next, dh0b, d_qkv, d_pairs, by_core, by_y, d_query, weight_buf, turned,
     da1, vector_rows, send_left, got_left, send, recv, local, *scratch) = refs[12 + n_rights :]
    y, c = lax.axis_index("y"), lax.axis_index("c")
    f32, b16 = jnp.float32, jnp.bfloat16
    cells, width = query.shape
    slots = 4 * cells
    n_pairs, head = width // 128, 64
    into = (((1,), (1,)), ((), ()))

    def backward(j, half):
        lanes = pl.ds(pl.multiple_of(j * 128, 128), 128)
        value_lanes = pl.ds(pl.multiple_of(width + j * 128, 128), 128)
        side = slice(half * head, (half + 1) * head)
        keys = pairs[:, :, :, lanes].reshape(slots, 128)[:, side]
        values = pairs[:, :, :, value_lanes].reshape(slots, 128)[:, side]
        mine, above = query[:, lanes][:, side], d_out[:, lanes][:, side]
        scores = lax.dot_general(keys, mine, into, preferred_element_type=f32) * scale
        scores = jnp.where(seg_keys[...] == seg_mine[...], scores, -1000000000.0)
        probs = jnp.exp(scores - log_total[pl.ds(2 * j + half, 1), :])
        d_probs = lax.dot_general(values, above, into, preferred_element_type=f32)
        inner = jnp.sum(probs * d_probs, axis=0, keepdims=True)
        d_scores = (probs * (d_probs - inner)).astype(b16)
        d_keys = jnp.dot(d_scores, mine, preferred_element_type=f32) * scale
        d_values = jnp.dot(probs.astype(b16), above, preferred_element_type=f32)
        d_pairs[0, j, :, side] = d_keys.astype(b16)
        d_pairs[1, j, :, side] = d_values.astype(b16)
        turned = keys.astype(f32).T.astype(b16)
        d_query[side] = jnp.dot(turned, d_scores, preferred_element_type=f32) * scale
        if half:
            d_qkv[:, lanes] = d_query[...].T.astype(b16)

    def to_core():
        return pltpu.make_async_remote_copy(
            src_ref=d_pairs.at[:, :, pl.ds(2 * cells, 2 * cells)], dst_ref=by_core,
            send_sem=send.at[0], recv_sem=recv.at[0], device_id={"c": 1 - c}, device_id_type=MESH,
        )

    def to_y():
        return pltpu.make_async_remote_copy(
            src_ref=d_pairs.at[:, :, pl.ds(cells, cells)], dst_ref=by_y,
            send_sem=send.at[1], recv_sem=recv.at[1], device_id={"y": 1 - y}, device_id_type=MESH,
        )

    def beside(i, right, odd):
        @pl.when(i < 2 * n_pairs)
        def _():
            backward(i // 2, odd)

    def fetch_weight():
        return pltpu.make_async_copy(weight, weight_buf, local.at[0])

    def keep_turned():
        return pltpu.make_async_copy(turned, turned_own, local.at[1])

    def send_turned():
        return pltpu.make_async_remote_copy(
            src_ref=turned, dst_ref=turned_other,
            send_sem=send.at[2], recv_sem=recv.at[2], device_id={"c": 1 - c}, device_id_type=MESH,
        )

    def to_other_left():
        return pltpu.make_async_remote_copy(
            src_ref=send_left, dst_ref=got_left,
            send_sem=send.at[3], recv_sem=recv.at[3], device_id={"c": 1 - c}, device_id_type=MESH,
        )

    def share():
        to_core().wait_recv()

        def add(j, carry):
            for kind in (0, 1):
                total = d_pairs[kind, j, : 2 * cells].astype(f32) + by_core[kind, j].astype(f32)
                d_pairs[kind, j, : 2 * cells] = total.astype(b16)
            return carry

        lax.fori_loop(0, n_pairs, add, 0)
        to_y().start()

    def collect():
        to_y().wait_recv()

        def add(j, carry):
            for kind in (0, 1):
                lanes = pl.ds(pl.multiple_of((kind + 1) * width + j * 128, 128), 128)
                total = d_pairs[kind, j, :cells].astype(f32) + by_y[kind, j].astype(f32)
                d_qkv[:, lanes] = total.astype(b16)
            return carry

        lax.fori_loop(0, n_pairs, add, 0)

    def turn():
        def tile(k, carry):
            turned[chunk_of(k)] = d_qkv[:, chunk_of(k)].astype(f32).T.astype(b16)
            return carry

        lax.fori_loop(0, 3 * width // CHUNK, tile, 0)
        keep_turned().start()
        send_turned().start()

    def project():
        fetch_weight().wait()
        for k in range(4):
            rows = weight_buf[k // 2, k % 2].reshape(width // 4, -1)[:, : 3 * width]
            da1[:, k * width // 4 : (k + 1) * width // 4] = lax.dot_general(
                d_qkv[...], rows, into, preferred_element_type=f32
            )

    def norm():
        value, above = h0[...], da1[...]
        centred = value - jnp.mean(value, axis=1, keepdims=True)
        inverse = lax.rsqrt(jnp.mean(centred * centred, axis=1, keepdims=True) + eps)
        normed = centred * inverse
        vector_rows[...] = jnp.zeros_like(vector_rows)
        vector_rows[0:1] = jnp.sum(above * normed, axis=0, keepdims=True)
        vector_rows[1:2] = jnp.sum(above, axis=0, keepdims=True)
        vector_rows[2:4] = vectors[1:3]
        above = above * vectors[0:1]
        inner = jnp.mean(above * normed, axis=1, keepdims=True)
        below = inverse * (above - jnp.mean(above, axis=1, keepdims=True) - normed * inner)
        dh0b[...] = (dh1[...] + below).astype(b16)

    def halves():
        for kind, source in enumerate((vector_rows, dh0b)):
            for part in range(8):
                lanes = pl.ds(pl.multiple_of(eighth_of(part) * (width // 8), width // 8), width // 8)
                block = source[:, lanes].astype(f32).T.astype(b16)
                rows = slice(part % 4 * (width // 8), (part % 4 + 1) * (width // 8))
                if part < 4:
                    lefts_next[1 + kind, rows, :cells] = block
                else:
                    send_left[kind, rows] = block
        to_other_left().start()

    def after(p):
        plan = {0: lambda: fetch_weight().start(), n_pairs: lambda: to_core().start(), n_pairs + 2: share}
        plan.update(zip(range(n_chunk_pairs - 2, n_chunk_pairs + 3), (collect, turn, project, norm, halves)))
        for when, action in plan.items():

            @pl.when(p == when)
            def _(action=action):
                action()

    n_chunk_pairs = (sum(sections) + 1) // 2
    scatter_kernel(
        n_h, sections, periods, left_starts, lefts, rights, out, scratch, [{"c": 1 - c}],
        lambda: None, lambda section, k: None, beside, after,
    )
    lefts_next[0] = left_one[...]
    to_other_left().wait_recv()
    for kind in (0, 1):
        lefts_next[1 + kind, :, cells:] = got_left[kind]
    keep_turned().wait()
    send_turned().wait()
    for copy in (to_core(), to_y(), to_other_left()):
        copy.wait_send()


def scatter_call(kernel, lefts, rights, operands, more_operands, out_shapes, out_specs, scratch, collective_id):
    periods = [own.shape[0] // CHUNK for own, *_ in rights]
    sections = [period * times for period, (*_, times) in zip(periods, rights)]
    n, cells = sum(sections), rights[0][0].shape[1]
    w = lefts.shape[1] // 4
    n_h = lax.axis_size("h")
    rows = w // n_h
    inner_h = n_h if rows % 16 == 0 else 1
    dma, bf16, f32 = pltpu.SemaphoreType.DMA, jnp.bfloat16, jnp.float32
    vmem, hbm = pl.BlockSpec(memory_space=pltpu.VMEM), pl.BlockSpec(memory_space=pl.ANY)
    others = max(inner_h - 1, 1)
    part_shape = jax.ShapeDtypeStruct((n, rows, CHUNK), f32)
    if inner_h == 1:
        part_shape = jax.ShapeDtypeStruct((n, w, CHUNK), bf16)
    part, *more = pl.pallas_call(
        functools.partial(kernel, inner_h, sections, periods),
        out_shape=[part_shape] + out_shapes,
        in_specs=[vmem] * (1 + len(operands)) + [hbm] * (2 * len(rights) + len(more_operands)),
        out_specs=[vmem] + out_specs,
        scratch_shapes=scratch
        + [
            pltpu.VMEM((3, CHUNK, 2 * cells), bf16),
            pltpu.VMEM((RING, 2 * w, CHUNK), f32),
            pltpu.VMEM((RING, 2 * w, CHUNK), bf16),
            pltpu.VMEM((n, 2 * w, CHUNK), bf16),
            pltpu.VMEM((RING, w, CHUNK), bf16),
            pltpu.VMEM((n, w, CHUNK), bf16),
            pltpu.VMEM((RING, w, CHUNK), bf16),
            pltpu.VMEM((n, others, w // inner_h, CHUNK), bf16),
            dma((3, 2)),
            dma((RING,)),
            dma((n,)),
            dma((RING,)),
            dma((n,)),
            dma((RING, others)),
            dma((n, others)),
        ],
        compiler_params=pltpu.CompilerParams(
            collective_id=collective_id, has_side_effects=True, vmem_limit_bytes=60 * 2**20
        ),
    )(lefts, *operands, *(half for pair in rights for half in pair[:2]), *more_operands)
    if inner_h == 1:
        part = lax.psum_scatter(part, "h", scatter_dimension=1, tiled=True).astype(f32)
    return part, *more


def scatter_product(lefts, left_starts, rights, vector, weights, product_type, collective_id):
    (cells, features), columns = vector.shape, rights[-1][0].shape[0]
    dma, bf16, f32 = pltpu.SemaphoreType.DMA, jnp.bfloat16, jnp.float32
    vmem, hbm = pl.BlockSpec(memory_space=pltpu.VMEM), pl.BlockSpec(memory_space=pl.ANY)
    shapes, specs, scratch = [jax.ShapeDtypeStruct((columns, cells), product_type)], [hbm], []
    if len(weights) == 8:
        shapes += [jax.ShapeDtypeStruct((cells, features), f32), jax.ShapeDtypeStruct((features, cells), bf16)]
        shapes += [jax.ShapeDtypeStruct((4,) + weights[k].shape, bf16) for k in (0, 4)]
        specs += [vmem, vmem, hbm, hbm]
        scratch = [pltpu.VMEM((features, cells), f32), dma((5, 4)), dma((5, 4))]

    def kernel(n_h, sections, periods, *refs):
        product_kernel(n_h, sections, periods, left_starts, len(weights), *refs)

    return scatter_call(
        kernel,
        lefts,
        rights,
        [vector],
        weights,
        shapes,
        specs,
        scratch
        + [
            pltpu.VMEM((3, features, CHUNK), bf16),
            pltpu.VMEM((2, CHUNK, cells), product_type),
            dma((3, len(weights))),
            dma((2,)),
        ],
        collective_id,
    )


def scatter_attention(lefts, left_starts, rights, operands, weight, scale, collective_id):
    cells, width = operands[0].shape
    bf16, f32, dma = jnp.bfloat16, jnp.float32, pltpu.SemaphoreType.DMA
    vmem, hbm = pl.BlockSpec(memory_space=pltpu.VMEM), pl.BlockSpec(memory_space=pl.ANY)

    def kernel(n_h, sections, periods, *refs):
        attention_kernel(n_h, sections, periods, left_starts, scale, *refs)

    return scatter_call(
        kernel,
        lefts,
        rights,
        operands,
        [weight],
        [
            jax.ShapeDtypeStruct((3 * width, cells), bf16),
            jax.ShapeDtypeStruct((3 * width, cells), bf16),
            jax.ShapeDtypeStruct((3,) + lefts.shape[1:], bf16),
            jax.ShapeDtypeStruct((cells, width), bf16),
        ],
        [hbm, hbm, vmem, vmem],
        [
            pltpu.VMEM((cells, 3 * width), bf16),
            pltpu.VMEM((2, width // 128, 4 * cells, 128), bf16),
            pltpu.VMEM((2, width // 128, 2 * cells, 128), bf16),
            pltpu.VMEM((2, width // 128, cells, 128), bf16),
            pltpu.VMEM((128, cells), f32),
            pltpu.VMEM(weight.shape, bf16),
            pltpu.VMEM((3 * width, cells), bf16),
            pltpu.VMEM((cells, width), f32),
            pltpu.VMEM((cells, width), f32),
            pltpu.VMEM((2, width // 2, cells), bf16),
            pltpu.VMEM((2, width // 2, cells), bf16),
            dma((4,)),
            dma((4,)),
            dma((2,)),
        ],
        collective_id,
    )


def own_half(left):
    half = left.shape[1] // 2
    return jnp.concatenate([left[:, :half], swap(left[:, half:], "c")], axis=0)


def left_of(left, pieces):
    left = own_half(relative(left, 1)).T
    n_h = lax.axis_size("h")
    left = left.reshape(4, n_h, pieces, -1, left.shape[1])
    return left.transpose(2, 0, 1, 3, 4).reshape(pieces, -1, left.shape[-1])


def both_cores(right, times=1):
    return right, swap(right, "c"), times


def columns_of(chunks):
    return chunks.transpose(1, 0, 2).reshape(chunks.shape[1], -1)


def on_device(
    counts,
    library,
    coords,
    lengths,
    cotangent,
    w_enc,
    w_qkv,
    w_out,
    gain_one,
    shift_one,
    w_up,
    w_down,
    gain_two,
    shift_two,
    w_dec,
):
    rows = counts.shape[0]
    width = w_qkv.shape[1] // 3
    heads = HEADS
    head_width = width // heads
    att_scale = head_width ** (-0.5)
    group_size = 4
    slots = rows * group_size
    scale = 10000.0 / library
    genes = counts.shape[1]
    padded = -(-genes // CHUNK) * CHUNK
    counts_f = counts.astype(jnp.float32)
    cot = jnp.pad(cotangent.T, ((0, padded - genes), (0, 0)))
    cot_pair = both_cores(cot)
    pe = by_owner(positions(coords, width), 1)
    ends = jnp.cumsum(lengths[0])
    group = [
        (lax.axis_index("y") ^ by_y) * 2 + (lax.axis_index("c") ^ by_c)
        for by_c in range(2)
        for by_y in range(2)
    ]
    place = jnp.concatenate([at * rows + jnp.arange(rows, dtype=jnp.int32) for at in group])
    seg_all = jnp.sum((place[:, None] >= ends[None, :]).astype(jnp.int32), axis=1)
    same = (seg_all[:rows, None] == seg_all[None, :])[None]
    vectors = jnp.stack([gain_one, shift_one, gain_two, shift_two], axis=1)
    vectors = jnp.pad(vectors, ((0, 0), (0, 124)))
    pad = ((0, 0), (0, padded - genes))
    quarter, middle = padded // CHUNK // 4 * CHUNK, padded // CHUNK // 2 * CHUNK
    gene_cuts = [0, quarter, 2 * quarter, 3 * quarter, padded]
    shards = [
        jnp.pad(w_enc.T, pad),
        jnp.concatenate([w_qkv, vectors], axis=1),
        by_owner(w_out, 1),
        by_owner(w_up, 1),
        by_owner(w_down, 1),
        w_dec.T[:, :middle],
        jnp.pad(w_dec.T[:, middle:], pad),
    ]
    cuts = [gene_cuts, [0, width // 2 * 3, 3 * width + 128], [0, width]]
    cuts += [[0, 2 * width, 4 * width], [0, width // 2, width]]
    cuts += [[0, middle], [0, padded - middle]]
    order = [(0, 0), (0, 1), (0, 2), (0, 3), (1, 0), (1, 1), (2, 0), (3, 0), (3, 1), (4, 0), (4, 1), (5, 0), (6, 0)]
    gathered, xb, h0, a1, query, kv_all = gather_all(
        shards, 5, cuts, order, counts.T, scale[None, :], pe.T, 0
    )
    xb_pair = both_cores(xb)
    enc_all, qkv_all, out_all, up_all, down_all = (
        w.reshape(-1, w.shape[-1]) for w in gathered[:5]
    )
    vectors = qkv_all[:, 3 * width :].astype(jnp.float32).T
    g1f, b1f, g2f, b2f = vectors[0], vectors[1], vectors[2], vectors[3]
    kv_pairs, query_b = kv_all, query
    query = query.reshape(rows, heads, head_width)
    kv_all = kv_all.reshape(slots, -1)
    dec_left, dec_right = gathered[5:]
    left_x, right_y = swap(dec_left, "x"), swap(dec_right, "y")
    left_y, right_x = swap(dec_left, "y"), swap(dec_right, "x")
    dec_parts = [dec_left, left_y, left_x, swap(left_x, "y")]
    dec_parts += [dec_right, right_y, right_x, swap(right_y, "x")]
    keys = kv_all[:, :width].reshape(slots, heads, head_width)
    values = kv_all[:, width:].reshape(slots, heads, head_width)

    def scores_of():
        raw = (
            jnp.einsum("qhd,khd->hqk", query, keys, preferred_element_type=jnp.float32) * att_scale
        )
        return jnp.where(same, raw, -1000000000.0)

    scores = scores_of()
    top = jnp.max(scores, axis=-1, keepdims=True)
    expo = jnp.exp(scores - top)
    total = jnp.sum(expo, axis=-1, keepdims=True)
    log_total = top + jnp.log(total)
    probs_b = (expo / total).astype(jnp.bfloat16)
    attended = jnp.einsum("hqk,khd->qhd", probs_b, values, preferred_element_type=jnp.float32)
    attended_b = attended.reshape(rows, width).astype(jnp.bfloat16)
    attended_b = by_owner(attended_b, 1)
    h1 = h0 + matmul(attended_b, out_all)
    a2 = layer_norm(h1, g2f, b2f).astype(jnp.bfloat16)
    hidden = matmul(a2, up_all)
    act, pull = jax.vjp(lambda v: jax.nn.gelu(v, approximate=False), hidden)
    act, slope = lax.optimization_barrier(
        (act.astype(jnp.bfloat16), pull(jnp.ones_like(hidden))[0])
    )
    h2 = h1 + matmul(act, down_all)
    hb = h2.astype(jnp.bfloat16)
    grad_dec, logits, dh2, dfb_turned, *_ = scatter_product(
        left_of(hb, 1), [0], [cot_pair], relative(hb, 1), dec_parts, jnp.bfloat16, 1
    )
    own_rows = grad_dec.shape[1]
    grad_dec = columns_of(grad_dec)[:, :genes].T
    logits = logits[:genes].T
    dfb = dh2.astype(jnp.bfloat16)
    d_act = contract_cols(dfb, down_all)
    d_hidden = (d_act * slope).astype(jnp.bfloat16)
    da2 = contract_cols(d_hidden, up_all)
    norm_pull = jax.vjp(layer_norm, h1, g2f, b2f)[1]
    dh1_norm, grad_gain_two, grad_shift_two = norm_pull(da2)
    dh1 = dh2 + dh1_norm
    dab = dh1.astype(jnp.bfloat16)
    d_attended = contract_cols(dab, out_all).astype(jnp.bfloat16)
    d_attended = from_owner(d_attended, 1)
    lefts = [left_of(a2, 1), left_of(act, act.shape[1] // width), left_of(attended_b, 1)]
    pieces = (4 * width,) + (width,) * 4
    rights = [both_cores(d_hidden.T), both_cores(dfb_turned, 4), both_cores(dab.T)]
    operands = [query_b, kv_pairs, d_attended, log_total[:, :, 0], seg_all[:, None], seg_all[None, :rows], h0, dh1]
    operands += [jnp.pad(jnp.stack([g1f, grad_gain_two, grad_shift_two]), ((0, 5), (0, 0))), left_of(a1, 1)[0]]
    grads, d_qkv, d_qkv_other, lefts, dh0b = scatter_attention(
        jnp.concatenate(lefts, axis=0),
        [sum(pieces[:k]) // CHUNK for k in range(len(pieces) + 1)],
        rights,
        operands,
        gathered[1],
        att_scale,
        2,
    )
    ends = [0]
    for columns in (4 * width, 4 * width, width):
        ends.append(ends[-1] + columns // CHUNK)
    grad_up, grad_down, grad_out = (grads[low:high] for low, high in zip(ends, ends[1:]))
    grad_up, grad_out = columns_of(grad_up), columns_of(grad_out)
    grad_down = grad_down.reshape(4, -1, own_rows, CHUNK).transpose(0, 2, 1, 3)
    grad_down = grad_down.reshape(4 * own_rows, -1)
    grad_out, grad_up, grad_down = (from_owner(g, 1) for g in (grad_out, grad_up, grad_down))
    unit = jnp.eye(rows, dtype=jnp.bfloat16)
    grads, d_xb = scatter_product(
        lefts,
        [0, 3 * width // CHUNK, (3 * width + rows) // CHUNK],
        [(d_qkv, d_qkv_other, 1), (unit, unit, 1), xb_pair],
        dh0b,
        [enc_all],
        jnp.float32,
        3,
    )
    ends = [0]
    for columns in (3 * width, rows):
        ends.append(ends[-1] + columns // CHUNK)
    grad_qkv, grad_vectors, grad_enc = (
        grads[low:high] for low, high in zip(ends, ends[1:] + [grads.shape[0]])
    )
    grad_qkv, grad_enc = columns_of(grad_qkv), columns_of(grad_enc)
    grad_gain_one, grad_shift_one, grad_gain_two, grad_shift_two = (
        grad_vectors[0, :, k] for k in range(4)
    )
    grad_enc = grad_enc[:, :genes].T
    d_xb = d_xb[:genes].T
    counts_grad = d_xb * scale[:, None] / (1.0 + counts_f * scale[:, None])
    return (
        logits,
        counts_grad,
        grad_enc,
        grad_qkv,
        grad_out,
        grad_gain_one,
        grad_shift_one,
        grad_up,
        grad_down,
        grad_gain_two,
        grad_shift_two,
        grad_dec,
    )


ALL = ("h", "x", "y", "c")


def solution(mesh):
    n_dp, n_fsdp = mesh.shape["dp"], mesh.shape["fsdp"]
    mesh = Mesh(mesh.devices.reshape((n_dp // 2, 2, 2, n_fsdp // 2)), ALL)
    placed = (
        P(ALL, None),
        P(ALL),
        P(None, ALL),
        P(("h", "x"), None),
        P(ALL, None),
        P(None, ALL),
        P(ALL, None),
        P(ALL, None),
        P(ALL),
        P(ALL),
        P(ALL, None),
        P(ALL, None),
        P(ALL),
        P(ALL),
        P(None, ALL),
    )
    return jax.shard_map(
        on_device,
        mesh=mesh,
        in_specs=placed,
        out_specs=(
            P(ALL, None),
            P(ALL, None),
            P(None, ALL),
            P(ALL, None),
            P(ALL, None),
            P(ALL),
            P(ALL),
            P(ALL, None),
            P(ALL, None),
            P(ALL),
            P(ALL),
            P(None, ALL),
        ),
        check_vma=False,
    )
```

```python
import functools
import math

import jax
import jax.numpy as jnp
from jax import lax
from jax.experimental import pallas as pl
from jax.experimental.pallas import tpu as pltpu
from jax.sharding import Mesh
from jax.sharding import PartitionSpec as P

HEADS = 16
MESH = pl.DeviceIdType.MESH
RING = 8
CHUNK = 256


eps = 1e-05


def layer_norm(value, gain, shift):
    mean = jnp.mean(value, axis=1, keepdims=True)
    centred = value - mean
    variance = jnp.mean(centred * centred, axis=1, keepdims=True)
    return centred * lax.rsqrt(variance + eps) * gain + shift


def positions(coords, width):
    quarter = width // 4
    freqs = 0.05 * jnp.exp(-jnp.arange(quarter, dtype=jnp.float32) * (math.log(10000.0) / quarter))
    along_x = coords[0].astype(jnp.float32)[:, None] * freqs[None, :]
    along_y = coords[1].astype(jnp.float32)[:, None] * freqs[None, :]
    return jnp.concatenate(
        [jnp.sin(along_x), jnp.cos(along_x), jnp.sin(along_y), jnp.cos(along_y)], axis=1
    )


def contract_cols(left, right):
    return lax.dot_general(
        left, right, (((1,), (1,)), ((), ())), preferred_element_type=jnp.float32
    )


def swap(value, axis):
    return lax.ppermute(value, axis, [(0, 1), (1, 0)])


def by_owner(value, axis):
    n_h = lax.axis_size("h")
    at = value.shape
    block = at[axis] // (8 * n_h)
    split = value.reshape(at[:axis] + (n_h, 2, 2, 2, block) + at[axis + 1 :])
    order = list(range(axis)) + [axis + 3, axis + 1, axis + 2, axis, axis + 4]
    order += list(range(axis + 5, split.ndim))
    return split.transpose(order).reshape(at)


def from_owner(value, axis):
    n_h = lax.axis_size("h")
    at = value.shape
    block = at[axis] // (8 * n_h)
    split = value.reshape(at[:axis] + (2, 2, 2, n_h, block) + at[axis + 1 :])
    order = list(range(axis)) + [axis + 3, axis + 1, axis + 2, axis, axis + 4]
    order += list(range(axis + 5, split.ndim))
    return split.transpose(order).reshape(at)


def greet(peers):
    barrier = pltpu.get_barrier_semaphore()
    for peer in peers:
        pl.semaphore_signal(barrier, inc=1, device_id=peer, device_id_type=MESH)
    pl.semaphore_wait(barrier, len(peers))


def gather_kernel(n_h, jobs, n_full, shards, wholes, sems, between):
    own_sem, h_send, h_recv, send, recv = sems
    h, x, y, c = (lax.axis_index(name) for name in ("h", "x", "y", "c"))
    h = 0 if n_h == 1 else h
    to_x, to_y, to_c = {"x": 1 - x}, {"y": 1 - y}, {"c": 1 - c}
    greet([{"h": lax.rem(h + d, n_h)} for d in range(1, n_h)] + [to_x, to_y, to_c])

    def rows_of(job, at):
        array, low, high, _ = job
        rows = shards[array].shape[0]
        place = (pl.ds(at * rows, rows), pl.ds(low, high - low))
        return wholes[array].at[(c, x, y, *place) if array < n_full else place]

    def h_copy(j, d):
        array, low, high, _ = jobs[j]
        return pltpu.make_async_remote_copy(
            src_ref=shards[array].at[:, pl.ds(low, high - low)],
            dst_ref=rows_of(jobs[j], h),
            send_sem=h_send.at[j, d - 1],
            recv_sem=h_recv.at[j, d - 1],
            device_id={"h": lax.rem(h + d, n_h)},
            device_id_type=MESH,
        )

    def own_copy(j):
        array, low, high, _ = jobs[j]
        return pltpu.make_async_copy(
            shards[array].at[:, pl.ds(low, high - low)], rows_of(jobs[j], h), own_sem.at[j]
        )

    def block_copy(j, k, block, to, columns):
        view = wholes[jobs[j][0]].at[(*block, slice(None), pl.ds(columns[0], columns[1] - columns[0]))]
        return pltpu.make_async_remote_copy(
            src_ref=view,
            dst_ref=view,
            send_sem=send.at[j, k],
            recv_sem=recv.at[j, k],
            device_id=to,
            device_id_type=MESH,
        )

    own, by_x, by_y, far = (c, x, y), (c, 1 - x, y), (c, x, 1 - y), (c, 1 - x, 1 - y)

    def copy(j, k):
        _, low, high, middle = jobs[j]
        block, to, columns = [
            (own, to_x, (low, high)),
            (own, to_y, (low, high)),
            (own, to_c, (low, high)),
            (by_x, to_y, (low, middle)),
            (by_y, to_x, (middle, high)),
            (by_x, to_c, (low, high)),
            (by_y, to_c, (low, high)),
            (far, to_c, (low, high)),
        ][k]
        return block_copy(j, k, block, to, columns)

    def start_h(j):
        own_copy(j).start()
        for d in range(1, n_h):
            h_copy(j, d).start()

    whole = set()

    def landed(j):
        if j not in whole:
            whole.add(j)
            for k in (2, 5, 6, 7):
                copy(j, k).wait_recv()

    n = sum(array < n_full for array, *_ in jobs)
    ahead = 2
    for j in range(ahead):
        start_h(j)
    for step in range(n + 2):
        if step < n:
            own_copy(step).wait()
            for d in range(1, n_h):
                h_copy(step, d).wait_recv()
            for k in (0, 1, 2):
                copy(step, k).start()
            if step + ahead < len(jobs):
                start_h(step + ahead)
        if 0 <= step - 1 < n:
            for k in (0, 1):
                copy(step - 1, k).wait_recv()
            for k in (3, 4, 5, 6):
                copy(step - 1, k).start()
        if 0 <= step - 2 < n:
            for k in (3, 4):
                copy(step - 2, k).wait_recv()
            copy(step - 2, 7).start()
        between(step, landed)
    for j in range(n, len(jobs)):
        own_copy(j).wait()
        for d in range(1, n_h):
            h_copy(j, d).wait_recv()
    for j in range(len(jobs)):
        for d in range(1, n_h):
            h_copy(j, d).wait_send()
    for j in range(n):
        for k in range(8):
            copy(j, k).wait_send()
        landed(j)


def gene_tail(counts):
    tail = counts[counts.shape[0] // CHUNK * CHUNK :]
    return jnp.pad(tail, ((0, CHUNK - tail.shape[0]), (0, 0)))


def eighth_of(part):
    c, x, y = (lax.axis_index(name) for name in ("c", "x", "y"))
    return lax.rem(c + part // 4, 2) * 4 + lax.rem(x + part // 2 % 2, 2) * 2 + lax.rem(y + part % 2, 2)


def front_kernel(n_h, jobs, n_arrays, n_full, owners, scale_s, *refs):
    shards = refs[:n_arrays]
    counts, cot, tail, cot_tail, scale, pe, seg_keys, seg_mine = refs[n_arrays : n_arrays + 8]
    rest = refs[n_arrays + 8 :]
    wholes = rest[:n_arrays]
    (xb, xb_other, cot_own, cot_other, pairs, lefts, left_one, left_last, h0, query, log_total, h1, slope,
     act, hb) = rest[n_arrays : n_arrays + 15]
    (a1, a2, plain, attended, turned, gains, perm, count_buf, enc_buf, xb_buf, total, qkv_buf, mine, pairs_buf, out_buf,
     up_buf, down_buf, own_left, send_left, count_sem, enc_sem, xb_sem, fetch_sem, kv_sem, kv_send, kv_recv, cot_sem,
     cot_send, cot_recv, left_sem, left_send, left_recv, *sems) = rest[n_arrays + 15 :]
    y, c = lax.axis_index("y"), lax.axis_index("c")
    to_core = {"c": 1 - c}
    f32, b16 = jnp.float32, jnp.bfloat16
    cells, width = h0.shape
    slots, head = 4 * cells, 64
    n_pairs = width // 128
    n_chunks = xb.shape[0] // CHUNK
    by_chunk = lambda k: pl.ds(pl.multiple_of(k * CHUNK, CHUNK), CHUNK)

    def loads(k, last):
        slot = lax.rem(k, 2)
        source = tail if last else counts.at[by_chunk(k)]
        return (
            pltpu.make_async_copy(source, count_buf.at[slot], count_sem.at[slot]),
            pltpu.make_async_copy(
                wholes[0].at[:, :, :, :, by_chunk(k)], enc_buf.at[slot], enc_sem.at[slot]
            ),
        )

    def store(k):
        slot = lax.rem(k, 2)
        return pltpu.make_async_copy(xb_buf.at[slot], xb.at[by_chunk(k)], xb_sem.at[slot])

    def encode(k, first, last, low, high):
        slot = lax.rem(k, 2)
        for copy in loads(k, last):
            copy.wait()
        if not last:

            @pl.when(k + 1 < (high - 1 if high == n_chunks else high))
            def _():
                for copy in loads(k + 1, False):
                    copy.start()

        @pl.when(k >= low + 2)
        def _():
            store(k - 2).wait()

        value = jnp.log1p(count_buf[slot].astype(f32) * scale[...]).astype(b16)
        xb_buf[slot] = value
        store(k).start()
        term = jnp.dot(enc_buf[slot].reshape(width, CHUNK), value, preferred_element_type=f32)
        if first:

            @pl.when(k == 0)
            def _():
                total[...] = pe[...] + term

            @pl.when(k > 0)
            def _():
                total[...] += term

        else:
            total[...] += term

    def encode_job(low, high):
        low, high = low // CHUNK, high // CHUNK
        stop = high - 1 if high == n_chunks else high
        for copy in loads(jnp.int32(low), False):
            copy.start()

        def body(k, carry):
            encode(k, low == 0, False, low, high)
            return carry

        lax.fori_loop(low, stop, body, 0)
        if stop < high:
            for copy in loads(jnp.int32(stop), True):
                copy.start()
            encode(jnp.int32(stop), False, True, low, high)
        for k in range(max(low, high - 2), high):
            store(jnp.int32(k)).wait()

    def fetch(k):
        buffer = (qkv_buf, out_buf, up_buf, down_buf)[k]
        return pltpu.make_async_copy(wholes[1 + k], buffer, fetch_sem.at[k])

    def project():
        fetch(0).wait()
        vectors = qkv_buf[:, :, :, :, 3 * width :].reshape(width, 128).astype(f32)
        value = total[...]
        centred = value - jnp.mean(value, axis=0, keepdims=True)
        variance = jnp.mean(centred * centred, axis=0, keepdims=True)
        normed = centred * lax.rsqrt(variance + eps) * vectors[:, 0:1] + vectors[:, 1:2]
        gains[...] = vectors.T[0:8]
        h0[...] = value.T
        a1[...] = normed.T.astype(b16)

        def tile(k):
            weight = qkv_buf[:, :, :, :, by_chunk(k)].reshape(width, CHUNK)
            return jnp.dot(a1[...], weight, preferred_element_type=f32).astype(b16)

        def keys(k, carry):
            mine[:, by_chunk(k)] = tile(k + width // CHUNK)
            return carry

        lax.fori_loop(0, 2 * width // CHUNK, keys, 0)
        kv_own().start()
        kv_copy(0).start()

        def queries(k, carry):
            query[:, by_chunk(k)] = tile(k)
            return carry

        lax.fori_loop(0, width // CHUNK, queries, 0)

    def kv_own():
        return pltpu.make_async_copy(mine, pairs.at[0, 0], kv_sem.at[0])

    def kv_copy(k):
        return pltpu.make_async_remote_copy(
            src_ref=(mine, pairs.at[0])[k],
            dst_ref=(pairs.at[0, 1], pairs.at[1])[k],
            send_sem=kv_send.at[k],
            recv_sem=kv_recv.at[k],
            device_id=({"y": 1 - y}, {"c": 1 - c})[k],
            device_id_type=MESH,
        )

    def swap_cot(k):
        source = (cot.at[pl.ds(0, (n_chunks - 1) * CHUNK)], cot_tail)[k]
        place = pl.ds((n_chunks - 1) * CHUNK * k, ((n_chunks - 1) * CHUNK, CHUNK)[k])
        return (
            pltpu.make_async_copy(source, cot_own.at[place], cot_sem.at[k]),
            pltpu.make_async_remote_copy(
                src_ref=source, dst_ref=cot_other.at[place], send_sem=cot_send.at[k], recv_sem=cot_recv.at[k],
                device_id=to_core, device_id_type=MESH,
            ),
        )

    def swap_xb():
        return pltpu.make_async_remote_copy(
            src_ref=xb, dst_ref=xb_other, send_sem=cot_send.at[2], recv_sem=cot_recv.at[2],
            device_id=to_core, device_id_type=MESH,
        )

    def make_perm():
        place = lax.broadcasted_iota(jnp.int32, (8, width), 1)
        size = width // 8 // owners
        within, at = lax.rem(place, size), lax.div(place, size)
        at_h, at = lax.rem(at, owners), lax.div(at, owners)
        wanted = at_h * 8 + lax.rem(lax.div(at, 2), 2) * 4 + lax.rem(at, 2) * 2 + lax.div(at, 4)
        wanted = (wanted * size + within)[0:1]
        for k in range(width // CHUNK):
            row = lax.broadcasted_iota(jnp.int32, (CHUNK, width), 0) + k * CHUNK
            perm[k * CHUNK : (k + 1) * CHUNK] = jnp.where(row == wanted, 1.0, 0.0).astype(b16)

    def fetch_pairs():
        return pltpu.make_async_copy(pairs, pairs_buf, kv_sem.at[1])

    def attend(j, carry):
        lanes = by_lanes(j)
        keys = pairs_buf[:, :, :, lanes].reshape(slots, 128)
        values = pairs_buf[:, :, :, by_lanes(n_pairs + j)].reshape(slots, 128).astype(f32).T.astype(b16)
        for half in (0, 1):
            side = slice(half * head, (half + 1) * head)
            scores = lax.dot_general(
                keys[:, side], query[:, lanes][:, side], (((1,), (1,)), ((), ())), preferred_element_type=f32
            )
            scores = jnp.where(seg_keys[...] == seg_mine[...], scores * scale_s, -1000000000.0)
            top = jnp.max(scores, axis=0, keepdims=True)
            expo = jnp.exp(scores - top)
            whole = jnp.sum(expo, axis=0, keepdims=True)
            log_total[pl.ds(2 * j + half, 1), :] = top + jnp.log(whole)
            probs = (expo * (1.0 / whole)).astype(b16)
            turned[side] = jnp.dot(values[side], probs, preferred_element_type=f32)
        plain[:, lanes] = turned[...].T.astype(b16)
        return carry

    def by_lanes(j):
        return pl.ds(pl.multiple_of(j * 128, 128), 128)

    def leave_attention():
        attended[...] = jnp.dot(plain[...], perm[...], preferred_element_type=f32).astype(b16)
        fetch(1).wait()
        for k in range(width // CHUNK):
            columns = slice(k * CHUNK, (k + 1) * CHUNK)
            weight = out_buf[:, :, :, :, columns].reshape(width, CHUNK)
            h1[:, columns] = h0[:, columns] + jnp.dot(attended[...], weight, preferred_element_type=f32)
        value = h1[...]
        centred = value - jnp.mean(value, axis=1, keepdims=True)
        variance = jnp.mean(centred * centred, axis=1, keepdims=True)
        a2[...] = (centred * lax.rsqrt(variance + eps) * gains[2:3] + gains[3:4]).astype(b16)

    def widen(k, carry):
        weight = up_buf[:, :, :, :, by_chunk(k)].reshape(width, CHUNK)
        value = jnp.dot(a2[...], weight, preferred_element_type=f32)
        share = 0.5 * (1.0 + lax.erf(value * (0.5**0.5)))
        act[:, by_chunk(k)] = (value * share).astype(b16)
        slope[:, by_chunk(k)] = share + value * jnp.exp(-0.5 * value * value) * (2.0 * math.pi) ** -0.5
        return carry

    def narrow(k, carry):
        weight = down_buf[:, :, :, :, by_chunk(k)].reshape(4 * width, CHUNK)
        value = h1[:, by_chunk(k)] + jnp.dot(act[...], weight, preferred_element_type=f32)
        hb[:, by_chunk(k)] = value.astype(b16)
        return carry

    def left_copies(k):
        target = (lefts.at[pl.ds(0, 6)], left_one, left_last)[k]
        source = pl.ds((0, 6, 7)[k], (6, 1, 1)[k])
        return (
            pltpu.make_async_copy(own_left.at[source], target.at[:, :, pl.ds(0, cells)], left_sem.at[k]),
            pltpu.make_async_remote_copy(
                src_ref=send_left.at[source], dst_ref=target.at[:, :, pl.ds(cells, cells)],
                send_sem=left_send.at[k], recv_sem=left_recv.at[k], device_id=to_core, device_id_type=MESH,
            ),
        )

    def make_left(source, k):
        size = source.shape[1] // 8
        pieces = size // (width // 8)
        step = size // owners // pieces
        for part in range(8):
            lanes = pl.ds(pl.multiple_of(eighth_of(part) * size, size), size)
            block = source[:, lanes].astype(f32).T.astype(b16)
            target = own_left if part < 4 else send_left
            base = part % 4 * (width // 8)
            if pieces == 1:
                target[k, base : base + size] = block
                continue
            for piece in range(pieces):
                for at in range(owners):
                    rows = block[(at * pieces + piece) * step : (at * pieces + piece + 1) * step]
                    target[k + piece, base + at * step : base + (at + 1) * step] = rows

    arrays = [array for array, *_ in jobs]
    last_of = [max(j for j, array in enumerate(arrays) if array == k) for k in range(5)]
    enc_jobs = [j for j, array in enumerate(arrays) if array == 0]
    at = last_of[1] + 3

    def between(step, landed):
        if step == 0:
            for k in (0, 1):
                for copy in swap_cot(k):
                    copy.start()
        if step == 1:
            make_perm()
        if step - 3 in enc_jobs:
            landed(step - 3)
            encode_job(*jobs[step - 3][1:3])
        if step == enc_jobs[-1] + 3:
            swap_xb().start()
        if step == at:
            for j in range(last_of[1] + 1):
                landed(j)
            fetch(0).start()
            project()
        if step == at + 2:
            kv_own().wait()
            kv_copy(0).wait_recv()
            kv_copy(1).start()
            make_left(a1, 6)
            for copy in left_copies(1):
                copy.start()
        if step == at + 3:
            for j in range(last_of[3] + 1):
                landed(j)
            fetch(1).start()
            fetch(2).start()
            kv_copy(1).wait_recv()
            fetch_pairs().start()
            fetch_pairs().wait()
            lax.fori_loop(0, n_pairs // 2, attend, 0)
        if step == at + 4:
            lax.fori_loop(n_pairs // 2, n_pairs, attend, 0)
        if step == at + 5:
            for j in range(last_of[4] + 1):
                landed(j)
            fetch(3).start()
            leave_attention()
            fetch(2).wait()
            lax.fori_loop(0, 2 * width // CHUNK, widen, 0)
        if step == at + 6:
            lax.fori_loop(2 * width // CHUNK, 4 * width // CHUNK, widen, 0)
        if step == at + 7:
            fetch(3).wait()
            lax.fori_loop(0, width // CHUNK, narrow, 0)
            make_left(hb, 7)
            for copy in left_copies(2):
                copy.start()
        if step == at + 8:
            make_left(a2, 0)
            make_left(act, 1)
            make_left(attended, 5)
            for copy in left_copies(0):
                copy.start()

    gather_kernel(n_h, jobs, n_full, shards, wholes, sems, between)
    kv_copy(0).wait_send()
    kv_copy(1).wait_send()
    for k in (0, 1):
        for copy in swap_cot(k):
            copy.wait()
    swap_xb().wait()
    for k in range(3):
        for copy in left_copies(k):
            copy.wait()


def gather_all(shards, cuts, order, counts, cot, scale, pe, seg, scale_s, collective_id):
    owners = n_h = lax.axis_size("h")
    if any(shard.shape[0] % 16 for shard in shards):
        shards = [lax.all_gather(s, "h", axis=0, tiled=True) for s in shards]
        n_h = 1
    jobs = []
    for array, piece in order:
        low, high = cuts[array][piece], cuts[array][piece + 1]
        jobs.append((array, low, high, low + (high - low) // 256 * 128))
    n, others, dma = len(jobs), max(n_h - 1, 1), pltpu.SemaphoreType.DMA
    shapes = [(n_h * s.shape[0], s.shape[1]) for s in shards]
    (genes, cells), width, padded = counts.shape, pe.shape[0], shards[0].shape[1]
    slots, half = seg.shape[0], width // 2
    bf16, f32 = jnp.bfloat16, jnp.float32
    vmem, hbm = pl.BlockSpec(memory_space=pltpu.VMEM), pl.BlockSpec(memory_space=pl.ANY)
    shape = jax.ShapeDtypeStruct
    hbm_out = [shape((padded, cells), bf16)] * 4 + [shape((2, 2, cells, 2 * width), bf16)]
    hbm_out += [shape((k, half, 2 * cells), bf16) for k in (6, 1, 1)]
    vmem_out = [
        shape((cells, width), f32),
        shape((cells, width), bf16),
        shape((width // 64, cells), f32),
        shape((cells, width), f32),
        shape((cells, 4 * width), f32),
        shape((cells, 4 * width), bf16),
        shape((cells, width), bf16),
    ]
    eighth = width // 8
    out = pl.pallas_call(
        functools.partial(front_kernel, n_h, jobs, len(shards), len(shards), owners, scale_s),
        out_shape=[shape((2, 2, 2) + k, bf16) for k in shapes] + hbm_out + vmem_out,
        in_specs=[hbm] * (len(shards) + 4) + [vmem] * 4,
        out_specs=[hbm] * (len(shards) + len(hbm_out)) + [vmem] * len(vmem_out),
        scratch_shapes=[
            pltpu.VMEM((cells, width), bf16),
            pltpu.VMEM((cells, width), bf16),
            pltpu.VMEM((cells, width), bf16),
            pltpu.VMEM((cells, width), bf16),
            pltpu.VMEM((128, cells), f32),
            pltpu.VMEM((8, width), f32),
            pltpu.VMEM((width, width), bf16),
            pltpu.VMEM((2, CHUNK, cells), bf16),
            pltpu.VMEM((2, 2, 2, 2, eighth, CHUNK), bf16),
            pltpu.VMEM((2, CHUNK, cells), bf16),
            pltpu.VMEM((width, cells), f32),
            pltpu.VMEM((2, 2, 2, eighth, shards[1].shape[1]), bf16),
            pltpu.VMEM((cells, 2 * width), bf16),
            pltpu.VMEM((2, 2, cells, 2 * width), bf16),
            pltpu.VMEM((2, 2, 2, eighth, width), bf16),
            pltpu.VMEM((2, 2, 2, eighth, 4 * width), bf16),
            pltpu.VMEM((2, 2, 2, 4 * eighth, width), bf16),
            pltpu.VMEM((8, half, cells), bf16),
            pltpu.VMEM((8, half, cells), bf16),
            dma((2,)),
            dma((2,)),
            dma((2,)),
            dma((4,)),
            dma((2,)),
            dma((2,)),
            dma((2,)),
            dma((2,)),
            dma((3,)),
            dma((3,)),
            dma((3,)),
            dma((3,)),
            dma((3,)),
            dma((n,)),
            dma((n, others)),
            dma((n, others)),
            dma((n, 8)),
            dma((n, 8)),
        ],
        compiler_params=pltpu.CompilerParams(
            collective_id=collective_id, has_side_effects=True, vmem_limit_bytes=63 * 2**20
        ),
    )(
        *shards, counts, cot, gene_tail(counts), gene_tail(cot), scale, pe, seg[:, None], seg[None, :cells]
    )
    return out[: len(shards)], *out[len(shards) :]


def scatter_kernel(n_h, sections, periods, left_starts, lefts, rights, out, scratch, peers, prefetch, beside, after):
    (right_buf, own, s1, r1, s2, r2, s3, r3, load_sem, send1, recv1, send2, recv2, send3, recv3) = scratch
    h, x, y = (lax.axis_index(name) for name in ("h", "x", "y"))
    to_x, to_y = {"x": 1 - x}, {"y": 1 - y}
    w = s3.shape[1]
    rows = w // n_h
    f32, b16 = jnp.float32, jnp.bfloat16
    n_sections = len(sections)
    starts = [sum(sections[:k]) for k in range(n_sections)]
    n = sum(sections)
    cells = right_buf.shape[2] // 2
    greet([{"h": lax.rem(h + d, n_h)} for d in range(1, n_h)] + [to_x, to_y] + peers)

    def loads(i, section, k):
        slot = lax.rem(i, 3)
        return [
            pltpu.make_async_copy(
                rights[2 * section + half].at[chunk_of(k)],
                right_buf.at[slot, :, pl.ds(half * cells, cells)],
                load_sem.at[slot, half],
            )
            for half in (0, 1)
        ]

    def start_loads(i):
        for section, (start, count) in enumerate(zip(starts, sections)):

            @pl.when((i >= start) & (i < start + count))
            def _(section=section, start=start):
                for copy in loads(i, section, lax.rem(i - start, periods[section])):
                    copy.start()
                prefetch(section, i - start)

    def hop(i, source, target, send_sem, recv_sem, to):
        slot = lax.rem(i, RING)
        return pltpu.make_async_remote_copy(
            src_ref=source.at[slot], dst_ref=target.at[i], send_sem=send_sem.at[slot],
            recv_sem=recv_sem.at[i], device_id=to, device_id_type=MESH,
        )

    def first(i, odd):
        return hop(i, s1, r1, send1, recv1, to_y if odd else to_x)

    def second(i, odd):
        return hop(i, s2, r2, send2, recv2, to_x if odd else to_y)

    def third(i, d):
        to = lax.rem(h + d, n_h)
        slot = lax.rem(i, RING)
        return pltpu.make_async_remote_copy(
            src_ref=s3.at[slot, pl.ds(to * rows, rows)], dst_ref=r3.at[i, d - 1],
            send_sem=send3.at[slot, d - 1], recv_sem=recv3.at[i, d - 1],
            device_id={"h": to}, device_id_type=MESH,
        )

    def multiply(i, odd):
        slot = lax.rem(i, RING)
        for copy in loads(i, 0, 0):
            copy.wait()
        left = lefts[sum((i + 1024 - start) // 1024 for start in left_starts[1:]) if left_starts[1:] else 0]
        right = right_buf.at[lax.rem(i, 3)]

        @pl.when(i >= RING)
        def _():
            first(i - RING, odd).wait_send()

        part = lax.dot_general(left, right[...], (((1,), (1,)), ((), ())), preferred_element_type=f32)
        own[slot, :w] = part[:w]
        if odd:
            own[slot, w:] = part[2 * w : 3 * w]
            s1[slot, :w] = part[w : 2 * w].astype(b16)
            s1[slot, w:] = part[3 * w :].astype(b16)
        else:
            own[slot, w:] = part[w : 2 * w]
            s1[slot] = part[2 * w :].astype(b16)
        first(i, odd).start()

        beside(i, right, odd)
        start_loads(i + 2)

    def pass_on(i, odd):
        slot = lax.rem(i, RING)
        first(i, odd).wait_recv()

        @pl.when(i >= RING)
        def _():
            second(i - RING, odd).wait_send()

        s2[slot] = (own[slot, w:] + r1[i, w:].astype(f32)).astype(b16)
        second(i, odd).start()

    def keep(i, odd):
        slot = lax.rem(i, RING)
        second(i, odd).wait_recv()
        part = own[slot, :w] + r1[i, :w].astype(f32) + r2[i].astype(f32)
        if n_h == 1:
            out[i] = part.astype(b16)
            return

        @pl.when(i >= RING)
        def _():
            for d in range(1, n_h):
                third(i - RING, d).wait_send()

        s3[slot] = part.astype(b16)
        for d in range(1, n_h):
            third(i, d).start()

    def finish(i, odd):
        if n_h == 1:
            return
        total = s3[lax.rem(i, RING), pl.ds(h * rows, rows)].astype(f32)
        for d in range(1, n_h):
            third(i, d).wait_recv()
            total = total + r3[i, d - 1].astype(f32)
        out[i] = total

    start_loads(jnp.int32(0))
    start_loads(jnp.int32(1))
    pairs = (n + 1) // 2

    def step(p, carry):
        for lag, stage in enumerate((multiply, pass_on, keep, finish)):
            for odd in (0, 1):
                i = 2 * (p - lag) + odd

                @pl.when((i >= 0) & (i < n))
                def _(stage=stage, i=i, odd=odd):
                    stage(i, odd)

        after(p)
        return carry

    lax.fori_loop(0, pairs + 3, step, 0)
    for i in range(max(n - RING, 0), n):
        first(i, i % 2).wait_send()
        second(i, i % 2).wait_send()
        for d in range(1, n_h):
            third(i, d).wait_send()


def chunk_of(k):
    return pl.ds(pl.multiple_of(k * CHUNK, CHUNK), CHUNK)


def product_kernel(n_h, sections, periods, left_starts, n_weights, with_sum, *refs):
    lefts, vector = refs[:2]
    n_rights = 2 * len(sections)
    rights, weights = refs[2 : 2 + n_rights], refs[2 + n_rights : 2 + n_rights + n_weights]
    rest = refs[2 + n_rights + n_weights :]
    out, product = rest[:2]
    total_out = rest[2] if with_sum else None
    weight_buf, product_buf, weight_sem, product_sem, *scratch = rest[3 if with_sum else 2 :]
    begin, count = sum(sections[:-1]), sections[-1]
    cells = vector.shape[0]

    def weight_loads(k):
        slot = lax.rem(k, 3)
        size = weights[0].shape[0]
        return [
            pltpu.make_async_copy(
                weight.at[:, chunk_of(k)],
                weight_buf.at[slot, pl.ds(part * size, size)],
                weight_sem.at[slot, part],
            )
            for part, weight in enumerate(weights)
        ]

    def product_store(k):
        slot = lax.rem(k, 2)
        return pltpu.make_async_copy(product_buf.at[slot], product.at[chunk_of(k)], product_sem.at[slot])

    def prefetch(section, k):
        if section == len(sections) - 1:
            for copy in weight_loads(k):
                copy.start()

    def multiply(k, right):
        for copy in weight_loads(k):
            copy.wait()
        weight = weight_buf[lax.rem(k, 3)]

        @pl.when(k >= 2)
        def _():
            product_store(k - 2).wait()

        value = jnp.dot(vector[...], weight, preferred_element_type=jnp.float32)
        product_buf[lax.rem(k, 2)] = value.T.astype(product_buf.dtype)
        product_store(k).start()
        if with_sum:
            term = jnp.dot(weight, right[:, :cells], preferred_element_type=jnp.float32)

            @pl.when(k == 0)
            def _():
                total_out[...] = term

            @pl.when(k > 0)
            def _():
                total_out[...] += term

    def beside(i, right, odd):
        if begin == 0:
            multiply(i, right)
        else:

            @pl.when(i >= begin)
            def _():
                multiply(i - begin, right)

    scatter_kernel(
        n_h, sections, periods, left_starts, lefts, rights, out, scratch, [], prefetch, beside, lambda p: None
    )
    for k in range(max(count - 2, 0), count):
        product_store(k).wait()


def attention_kernel(n_h, sections, periods, left_starts, scale, *refs):
    lefts, query, pairs, d_out, log_total, seg_keys, seg_mine, h0, dh1, vectors, left_one = refs[:11]
    n_rights = 2 * len(sections)
    rights, weight = refs[11 : 11 + n_rights], refs[11 + n_rights]
    (out, turned_own, turned_other, lefts_next, dh0b, d_qkv, d_pairs, by_core, by_y, d_query, weight_buf, turned,
     da1, vector_rows, send_left, got_left, send, recv, local, *scratch) = refs[12 + n_rights :]
    y, c = lax.axis_index("y"), lax.axis_index("c")
    f32, b16 = jnp.float32, jnp.bfloat16
    cells, width = query.shape
    slots = 4 * cells
    n_pairs, head = width // 128, 64
    into = (((1,), (1,)), ((), ()))

    def backward(j, half):
        lanes = pl.ds(pl.multiple_of(j * 128, 128), 128)
        value_lanes = pl.ds(pl.multiple_of(width + j * 128, 128), 128)
        side = slice(half * head, (half + 1) * head)
        keys = pairs[:, :, :, lanes].reshape(slots, 128)[:, side]
        values = pairs[:, :, :, value_lanes].reshape(slots, 128)[:, side]
        mine, above = query[:, lanes][:, side], d_out[:, lanes][:, side]
        scores = lax.dot_general(keys, mine, into, preferred_element_type=f32) * scale
        scores = jnp.where(seg_keys[...] == seg_mine[...], scores, -1000000000.0)
        probs = jnp.exp(scores - log_total[pl.ds(2 * j + half, 1), :])
        d_probs = lax.dot_general(values, above, into, preferred_element_type=f32)
        inner = jnp.sum(probs * d_probs, axis=0, keepdims=True)
        d_scores = (probs * (d_probs - inner)).astype(b16)
        d_keys = jnp.dot(d_scores, mine, preferred_element_type=f32) * scale
        d_values = jnp.dot(probs.astype(b16), above, preferred_element_type=f32)
        d_pairs[0, j, :, side] = d_keys.astype(b16)
        d_pairs[1, j, :, side] = d_values.astype(b16)
        turned = keys.astype(f32).T.astype(b16)
        d_query[side] = jnp.dot(turned, d_scores, preferred_element_type=f32) * scale
        if half:
            d_qkv[:, lanes] = d_query[...].T.astype(b16)

    def to_core():
        return pltpu.make_async_remote_copy(
            src_ref=d_pairs.at[:, :, pl.ds(2 * cells, 2 * cells)], dst_ref=by_core,
            send_sem=send.at[0], recv_sem=recv.at[0], device_id={"c": 1 - c}, device_id_type=MESH,
        )

    def to_y():
        return pltpu.make_async_remote_copy(
            src_ref=d_pairs.at[:, :, pl.ds(cells, cells)], dst_ref=by_y,
            send_sem=send.at[1], recv_sem=recv.at[1], device_id={"y": 1 - y}, device_id_type=MESH,
        )

    def beside(i, right, odd):
        @pl.when(i < 2 * n_pairs)
        def _():
            backward(i // 2, odd)

    def fetch_weight():
        return pltpu.make_async_copy(weight, weight_buf, local.at[0])

    def keep_turned():
        return pltpu.make_async_copy(turned, turned_own, local.at[1])

    def send_turned():
        return pltpu.make_async_remote_copy(
            src_ref=turned, dst_ref=turned_other,
            send_sem=send.at[2], recv_sem=recv.at[2], device_id={"c": 1 - c}, device_id_type=MESH,
        )

    def to_other_left():
        return pltpu.make_async_remote_copy(
            src_ref=send_left, dst_ref=got_left,
            send_sem=send.at[3], recv_sem=recv.at[3], device_id={"c": 1 - c}, device_id_type=MESH,
        )

    def share():
        to_core().wait_recv()

        def add(j, carry):
            for kind in (0, 1):
                total = d_pairs[kind, j, : 2 * cells].astype(f32) + by_core[kind, j].astype(f32)
                d_pairs[kind, j, : 2 * cells] = total.astype(b16)
            return carry

        lax.fori_loop(0, n_pairs, add, 0)
        to_y().start()

    def collect():
        to_y().wait_recv()

        def add(j, carry):
            for kind in (0, 1):
                lanes = pl.ds(pl.multiple_of((kind + 1) * width + j * 128, 128), 128)
                total = d_pairs[kind, j, :cells].astype(f32) + by_y[kind, j].astype(f32)
                d_qkv[:, lanes] = total.astype(b16)
            return carry

        lax.fori_loop(0, n_pairs, add, 0)

    def turn():
        def tile(k, carry):
            turned[chunk_of(k)] = d_qkv[:, chunk_of(k)].astype(f32).T.astype(b16)
            return carry

        lax.fori_loop(0, 3 * width // CHUNK, tile, 0)
        keep_turned().start()
        send_turned().start()

    def project():
        fetch_weight().wait()
        for k in range(4):
            rows = weight_buf[k // 2, k % 2].reshape(width // 4, -1)[:, : 3 * width]
            da1[:, k * width // 4 : (k + 1) * width // 4] = lax.dot_general(
                d_qkv[...], rows, into, preferred_element_type=f32
            )

    def norm():
        value, above = h0[...], da1[...]
        centred = value - jnp.mean(value, axis=1, keepdims=True)
        inverse = lax.rsqrt(jnp.mean(centred * centred, axis=1, keepdims=True) + eps)
        normed = centred * inverse
        vector_rows[...] = jnp.zeros_like(vector_rows)
        vector_rows[0:1] = jnp.sum(above * normed, axis=0, keepdims=True)
        vector_rows[1:2] = jnp.sum(above, axis=0, keepdims=True)
        vector_rows[2:4] = vectors[1:3]
        above = above * vectors[0:1]
        inner = jnp.mean(above * normed, axis=1, keepdims=True)
        below = inverse * (above - jnp.mean(above, axis=1, keepdims=True) - normed * inner)
        dh0b[...] = (dh1[...] + below).astype(b16)

    def halves():
        for kind, source in enumerate((vector_rows, dh0b)):
            for part in range(8):
                lanes = pl.ds(pl.multiple_of(eighth_of(part) * (width // 8), width // 8), width // 8)
                block = source[:, lanes].astype(f32).T.astype(b16)
                rows = slice(part % 4 * (width // 8), (part % 4 + 1) * (width // 8))
                if part < 4:
                    lefts_next[1 + kind, rows, :cells] = block
                else:
                    send_left[kind, rows] = block
        to_other_left().start()

    def after(p):
        plan = {0: lambda: fetch_weight().start(), n_pairs: lambda: to_core().start(), n_pairs + 2: share}
        plan.update(zip(range(n_chunk_pairs - 2, n_chunk_pairs + 3), (collect, turn, project, norm, halves)))
        for when, action in plan.items():

            @pl.when(p == when)
            def _(action=action):
                action()

    n_chunk_pairs = (sum(sections) + 1) // 2
    scatter_kernel(
        n_h, sections, periods, left_starts, lefts, rights, out, scratch, [{"c": 1 - c}],
        lambda section, k: None, beside, after,
    )
    lefts_next[0] = left_one[...]
    to_other_left().wait_recv()
    for kind in (0, 1):
        lefts_next[1 + kind, :, cells:] = got_left[kind]
    keep_turned().wait()
    send_turned().wait()
    for copy in (to_core(), to_y(), to_other_left()):
        copy.wait_send()


def scatter_call(kernel, lefts, rights, operands, more_operands, out_shapes, out_specs, scratch, collective_id):
    periods = [own.shape[0] // CHUNK for own, *_ in rights]
    sections = [period * times for period, (*_, times) in zip(periods, rights)]
    n, cells = sum(sections), rights[0][0].shape[1]
    w = lefts.shape[1] // 4
    n_h = lax.axis_size("h")
    rows = w // n_h
    inner_h = n_h if rows % 16 == 0 else 1
    dma, bf16, f32 = pltpu.SemaphoreType.DMA, jnp.bfloat16, jnp.float32
    vmem, hbm = pl.BlockSpec(memory_space=pltpu.VMEM), pl.BlockSpec(memory_space=pl.ANY)
    others = max(inner_h - 1, 1)
    part_shape = jax.ShapeDtypeStruct((n, rows, CHUNK), f32)
    if inner_h == 1:
        part_shape = jax.ShapeDtypeStruct((n, w, CHUNK), bf16)
    part, *more = pl.pallas_call(
        functools.partial(kernel, inner_h, sections, periods),
        out_shape=[part_shape] + out_shapes,
        in_specs=[vmem] * (1 + len(operands)) + [hbm] * (2 * len(rights) + len(more_operands)),
        out_specs=[vmem] + out_specs,
        scratch_shapes=scratch
        + [
            pltpu.VMEM((3, CHUNK, 2 * cells), bf16),
            pltpu.VMEM((RING, 2 * w, CHUNK), f32),
            pltpu.VMEM((RING, 2 * w, CHUNK), bf16),
            pltpu.VMEM((n, 2 * w, CHUNK), bf16),
            pltpu.VMEM((RING, w, CHUNK), bf16),
            pltpu.VMEM((n, w, CHUNK), bf16),
            pltpu.VMEM((RING, w, CHUNK), bf16),
            pltpu.VMEM((n, others, w // inner_h, CHUNK), bf16),
            dma((3, 2)),
            dma((RING,)),
            dma((n,)),
            dma((RING,)),
            dma((n,)),
            dma((RING, others)),
            dma((n, others)),
        ],
        compiler_params=pltpu.CompilerParams(
            collective_id=collective_id, has_side_effects=True, vmem_limit_bytes=60 * 2**20
        ),
    )(lefts, *operands, *(half for pair in rights for half in pair[:2]), *more_operands)
    if inner_h == 1:
        part = lax.psum_scatter(part, "h", scatter_dimension=1, tiled=True).astype(f32)
    return part, *more


def scatter_product(lefts, left_starts, rights, vector, weights, product_type, with_sum, collective_id):
    (cells, features), columns = vector.shape, rights[-1][0].shape[0]
    dma = pltpu.SemaphoreType.DMA
    vmem, hbm = pl.BlockSpec(memory_space=pltpu.VMEM), pl.BlockSpec(memory_space=pl.ANY)

    def kernel(n_h, sections, periods, *refs):
        product_kernel(n_h, sections, periods, left_starts, len(weights), with_sum, *refs)

    return scatter_call(
        kernel,
        lefts,
        rights,
        [vector],
        weights,
        [jax.ShapeDtypeStruct((columns, cells), product_type)]
        + [jax.ShapeDtypeStruct((features, cells), jnp.float32)] * with_sum,
        [hbm] + [vmem] * with_sum,
        [
            pltpu.VMEM((3, features, CHUNK), jnp.bfloat16),
            pltpu.VMEM((2, CHUNK, cells), product_type),
            dma((3, len(weights))),
            dma((2,)),
        ],
        collective_id,
    )


def scatter_attention(lefts, left_starts, rights, operands, weight, scale, collective_id):
    cells, width = operands[0].shape
    bf16, f32, dma = jnp.bfloat16, jnp.float32, pltpu.SemaphoreType.DMA
    vmem, hbm = pl.BlockSpec(memory_space=pltpu.VMEM), pl.BlockSpec(memory_space=pl.ANY)

    def kernel(n_h, sections, periods, *refs):
        attention_kernel(n_h, sections, periods, left_starts, scale, *refs)

    return scatter_call(
        kernel,
        lefts,
        rights,
        operands,
        [weight],
        [
            jax.ShapeDtypeStruct((3 * width, cells), bf16),
            jax.ShapeDtypeStruct((3 * width, cells), bf16),
            jax.ShapeDtypeStruct((3,) + lefts.shape[1:], bf16),
            jax.ShapeDtypeStruct((cells, width), bf16),
        ],
        [hbm, hbm, vmem, vmem],
        [
            pltpu.VMEM((cells, 3 * width), bf16),
            pltpu.VMEM((2, width // 128, 4 * cells, 128), bf16),
            pltpu.VMEM((2, width // 128, 2 * cells, 128), bf16),
            pltpu.VMEM((2, width // 128, cells, 128), bf16),
            pltpu.VMEM((128, cells), f32),
            pltpu.VMEM(weight.shape, bf16),
            pltpu.VMEM((3 * width, cells), bf16),
            pltpu.VMEM((cells, width), f32),
            pltpu.VMEM((cells, width), f32),
            pltpu.VMEM((2, width // 2, cells), bf16),
            pltpu.VMEM((2, width // 2, cells), bf16),
            dma((4,)),
            dma((4,)),
            dma((2,)),
        ],
        collective_id,
    )


def both_cores(right, times=1):
    return right, swap(right, "c"), times


def columns_of(chunks):
    return chunks.transpose(1, 0, 2).reshape(chunks.shape[1], -1)


def on_device(
    counts,
    library,
    coords,
    lengths,
    cotangent,
    w_enc,
    w_qkv,
    w_out,
    gain_one,
    shift_one,
    w_up,
    w_down,
    gain_two,
    shift_two,
    w_dec,
):
    rows = counts.shape[0]
    width = w_qkv.shape[1] // 3
    att_scale = (width // HEADS) ** (-0.5)
    group_size = 4
    slots = rows * group_size
    scale = 10000.0 / library
    genes = counts.shape[1]
    padded = -(-genes // CHUNK) * CHUNK
    counts_f = counts.astype(jnp.float32)
    pe = by_owner(positions(coords, width), 1)
    ends = jnp.cumsum(lengths[0])
    group = [
        (lax.axis_index("y") ^ by_y) * 2 + (lax.axis_index("c") ^ by_c)
        for by_c in range(2)
        for by_y in range(2)
    ]
    place = jnp.concatenate([at * rows + jnp.arange(rows, dtype=jnp.int32) for at in group])
    seg_all = jnp.sum((place[:, None] >= ends[None, :]).astype(jnp.int32), axis=1)
    vectors = jnp.stack([gain_one, shift_one, gain_two, shift_two], axis=1)
    vectors = jnp.pad(vectors, ((0, 0), (0, 124)))
    pad = ((0, 0), (0, padded - genes))
    quarter = padded // CHUNK // 4 * CHUNK
    gene_cuts = [0, quarter, 2 * quarter, 3 * quarter, padded]
    shards = [
        jnp.pad(w_enc.T, pad),
        jnp.concatenate([w_qkv, vectors], axis=1),
        by_owner(w_out, 1),
        by_owner(w_up, 1),
        by_owner(w_down, 1),
        jnp.pad(w_dec.T, pad),
    ]
    cuts = [gene_cuts, [0, width // 2 * 3, 3 * width + 128], [0, width]]
    cuts += [[0, 2 * width, 4 * width], [0, width // 2, width]]
    cuts += [gene_cuts]
    order = [(0, 0), (0, 1), (0, 2), (0, 3), (1, 0), (1, 1), (2, 0), (3, 0), (3, 1), (4, 0), (4, 1)]
    order += [(5, 0), (5, 1), (5, 2), (5, 3)]
    (gathered, xb, xb_other, cot, cot_other, kv_pairs, lefts, left_one, left_last, h0, query, log_total, h1, slope, _,
     hb) = gather_all(
        shards, cuts, order, counts.T, cotangent.T, scale[None, :], pe.T, seg_all, att_scale, 0
    )
    enc_all, qkv_all, out_all, up_all, down_all, dec_all = (
        w.reshape(-1, w.shape[-1]) for w in gathered
    )
    vectors = qkv_all[:, 3 * width :].astype(jnp.float32).T
    g1f, b1f, g2f, b2f = vectors[0], vectors[1], vectors[2], vectors[3]
    grad_dec, logits, dh2 = scatter_product(
        left_last, [0], [(cot, cot_other, 1)], hb, [dec_all], jnp.bfloat16, True, 1
    )
    own_rows = grad_dec.shape[1]
    grad_dec = columns_of(grad_dec)[:, :genes].T
    logits = logits[:genes].T
    dfb_turned = dh2.astype(jnp.bfloat16)
    dh2 = dh2.T
    dfb = dfb_turned.T
    d_act = contract_cols(dfb, down_all)
    d_hidden = (d_act * slope).astype(jnp.bfloat16)
    da2 = contract_cols(d_hidden, up_all)
    norm_pull = jax.vjp(layer_norm, h1, g2f, b2f)[1]
    dh1_norm, grad_gain_two, grad_shift_two = norm_pull(da2)
    dh1 = dh2 + dh1_norm
    dab = dh1.astype(jnp.bfloat16)
    d_attended = contract_cols(dab, out_all).astype(jnp.bfloat16)
    d_attended = from_owner(d_attended, 1)
    pieces = (4 * width,) + (width,) * 4
    rights = [both_cores(d_hidden.T), both_cores(dfb_turned, 4), both_cores(dab.T)]
    operands = [query, kv_pairs, d_attended, log_total, seg_all[:, None], seg_all[None, :rows], h0, dh1]
    operands += [jnp.pad(jnp.stack([g1f, grad_gain_two, grad_shift_two]), ((0, 5), (0, 0))), left_one[0]]
    grads, d_qkv, d_qkv_other, lefts, dh0b = scatter_attention(
        lefts,
        [sum(pieces[:k]) // CHUNK for k in range(len(pieces) + 1)],
        rights,
        operands,
        gathered[1],
        att_scale,
        2,
    )
    ends = [0]
    for columns in (4 * width, 4 * width, width):
        ends.append(ends[-1] + columns // CHUNK)
    grad_up, grad_down, grad_out = (grads[low:high] for low, high in zip(ends, ends[1:]))
    grad_up, grad_out = columns_of(grad_up), columns_of(grad_out)
    grad_down = grad_down.reshape(4, -1, own_rows, CHUNK).transpose(0, 2, 1, 3)
    grad_down = grad_down.reshape(4 * own_rows, -1)
    grad_out, grad_up, grad_down = (from_owner(g, 1) for g in (grad_out, grad_up, grad_down))
    unit = jnp.eye(rows, dtype=jnp.bfloat16)
    grads, d_xb = scatter_product(
        lefts,
        [0, 3 * width // CHUNK, (3 * width + rows) // CHUNK],
        [(d_qkv, d_qkv_other, 1), (unit, unit, 1), (xb, xb_other, 1)],
        dh0b,
        [enc_all],
        jnp.float32,
        False,
        3,
    )
    ends = [0]
    for columns in (3 * width, rows):
        ends.append(ends[-1] + columns // CHUNK)
    grad_qkv, grad_vectors, grad_enc = (
        grads[low:high] for low, high in zip(ends, ends[1:] + [grads.shape[0]])
    )
    grad_qkv, grad_enc = columns_of(grad_qkv), columns_of(grad_enc)
    grad_gain_one, grad_shift_one, grad_gain_two, grad_shift_two = (
        grad_vectors[0, :, k] for k in range(4)
    )
    grad_enc = grad_enc[:, :genes].T
    d_xb = d_xb[:genes].T
    counts_grad = d_xb * scale[:, None] / (1.0 + counts_f * scale[:, None])
    return (
        logits,
        counts_grad,
        grad_enc,
        grad_qkv,
        grad_out,
        grad_gain_one,
        grad_shift_one,
        grad_up,
        grad_down,
        grad_gain_two,
        grad_shift_two,
        grad_dec,
    )


ALL = ("h", "x", "y", "c")


def solution(mesh):
    n_dp, n_fsdp = mesh.shape["dp"], mesh.shape["fsdp"]
    mesh = Mesh(mesh.devices.reshape((n_dp // 2, 2, 2, n_fsdp // 2)), ALL)
    placed = (
        P(ALL, None),
        P(ALL),
        P(None, ALL),
        P(("h", "x"), None),
        P(ALL, None),
        P(None, ALL),
        P(ALL, None),
        P(ALL, None),
        P(ALL),
        P(ALL),
        P(ALL, None),
        P(ALL, None),
        P(ALL),
        P(ALL),
        P(None, ALL),
    )
    return jax.shard_map(
        on_device,
        mesh=mesh,
        in_specs=placed,
        out_specs=(
            P(ALL, None),
            P(ALL, None),
            P(None, ALL),
            P(ALL, None),
            P(ALL, None),
            P(ALL),
            P(ALL),
            P(ALL, None),
            P(ALL, None),
            P(ALL),
            P(ALL),
            P(None, ALL),
        ),
        check_vma=False,
    )
```

```python
import functools
import math

import jax
import jax.numpy as jnp
from jax import lax
from jax.experimental import pallas as pl
from jax.experimental.pallas import tpu as pltpu
from jax.sharding import Mesh
from jax.sharding import PartitionSpec as P

HEADS = 16
MESH = pl.DeviceIdType.MESH
RING = 8
CHUNK = 256


eps = 1e-05


def layer_norm(value, gain, shift):
    mean = jnp.mean(value, axis=1, keepdims=True)
    centred = value - mean
    variance = jnp.mean(centred * centred, axis=1, keepdims=True)
    return centred * lax.rsqrt(variance + eps) * gain + shift


def positions(coords, width):
    quarter = width // 4
    freqs = 0.05 * jnp.exp(-jnp.arange(quarter, dtype=jnp.float32) * (math.log(10000.0) / quarter))
    along_x = coords[0].astype(jnp.float32)[:, None] * freqs[None, :]
    along_y = coords[1].astype(jnp.float32)[:, None] * freqs[None, :]
    return jnp.concatenate(
        [jnp.sin(along_x), jnp.cos(along_x), jnp.sin(along_y), jnp.cos(along_y)], axis=1
    )


def contract_cols(left, right):
    return lax.dot_general(
        left, right, (((1,), (1,)), ((), ())), preferred_element_type=jnp.float32
    )


def swap(value, axis):
    return lax.ppermute(value, axis, [(0, 1), (1, 0)])


def by_owner(value, axis):
    n_h = lax.axis_size("h")
    at = value.shape
    block = at[axis] // (8 * n_h)
    split = value.reshape(at[:axis] + (n_h, 2, 2, 2, block) + at[axis + 1 :])
    order = list(range(axis)) + [axis + 3, axis + 1, axis + 2, axis, axis + 4]
    order += list(range(axis + 5, split.ndim))
    return split.transpose(order).reshape(at)


def from_owner(value, axis):
    n_h = lax.axis_size("h")
    at = value.shape
    block = at[axis] // (8 * n_h)
    split = value.reshape(at[:axis] + (2, 2, 2, n_h, block) + at[axis + 1 :])
    order = list(range(axis)) + [axis + 3, axis + 1, axis + 2, axis, axis + 4]
    order += list(range(axis + 5, split.ndim))
    return split.transpose(order).reshape(at)


def greet(peers):
    barrier = pltpu.get_barrier_semaphore()
    for peer in peers:
        pl.semaphore_signal(barrier, inc=1, device_id=peer, device_id_type=MESH)
    pl.semaphore_wait(barrier, len(peers))


def gather_kernel(n_h, jobs, n_full, shards, wholes, sems, between):
    own_sem, h_send, h_recv, send, recv = sems
    h, x, y, c = (lax.axis_index(name) for name in ("h", "x", "y", "c"))
    h = 0 if n_h == 1 else h
    to_x, to_y, to_c = {"x": 1 - x}, {"y": 1 - y}, {"c": 1 - c}
    greet([{"h": lax.rem(h + d, n_h)} for d in range(1, n_h)] + [to_x, to_y, to_c])

    def rows_of(job, at):
        array, low, high, _ = job
        rows = shards[array].shape[0]
        place = (pl.ds(at * rows, rows), pl.ds(low, high - low))
        return wholes[array].at[(c, x, y, *place) if array < n_full else place]

    def h_copy(j, d):
        array, low, high, _ = jobs[j]
        return pltpu.make_async_remote_copy(
            src_ref=shards[array].at[:, pl.ds(low, high - low)],
            dst_ref=rows_of(jobs[j], h),
            send_sem=h_send.at[j, d - 1],
            recv_sem=h_recv.at[j, d - 1],
            device_id={"h": lax.rem(h + d, n_h)},
            device_id_type=MESH,
        )

    def own_copy(j):
        array, low, high, _ = jobs[j]
        return pltpu.make_async_copy(
            shards[array].at[:, pl.ds(low, high - low)], rows_of(jobs[j], h), own_sem.at[j]
        )

    def block_copy(j, k, block, to, columns):
        view = wholes[jobs[j][0]].at[(*block, slice(None), pl.ds(columns[0], columns[1] - columns[0]))]
        return pltpu.make_async_remote_copy(
            src_ref=view,
            dst_ref=view,
            send_sem=send.at[j, k],
            recv_sem=recv.at[j, k],
            device_id=to,
            device_id_type=MESH,
        )

    own, by_x, by_y, far = (c, x, y), (c, 1 - x, y), (c, x, 1 - y), (c, 1 - x, 1 - y)

    def copy(j, k):
        _, low, high, middle = jobs[j]
        block, to, columns = [
            (own, to_x, (low, high)),
            (own, to_y, (low, high)),
            (own, to_c, (low, high)),
            (by_x, to_y, (low, middle)),
            (by_y, to_x, (middle, high)),
            (by_x, to_c, (low, high)),
            (by_y, to_c, (low, high)),
            (far, to_c, (low, high)),
        ][k]
        return block_copy(j, k, block, to, columns)

    def start_h(j):
        own_copy(j).start()
        for d in range(1, n_h):
            h_copy(j, d).start()

    whole = set()

    def landed(j):
        if j not in whole:
            whole.add(j)
            for k in (2, 5, 6, 7):
                copy(j, k).wait_recv()

    n = sum(array < n_full for array, *_ in jobs)
    ahead = 2
    for j in range(ahead):
        start_h(j)
    for step in range(n + 2):
        if step < n:
            own_copy(step).wait()
            for d in range(1, n_h):
                h_copy(step, d).wait_recv()
            for k in (0, 1, 2):
                copy(step, k).start()
            if step + ahead < len(jobs):
                start_h(step + ahead)
        if 0 <= step - 1 < n:
            for k in (0, 1):
                copy(step - 1, k).wait_recv()
            for k in (3, 4, 5, 6):
                copy(step - 1, k).start()
        if 0 <= step - 2 < n:
            for k in (3, 4):
                copy(step - 2, k).wait_recv()
            copy(step - 2, 7).start()
        between(step, landed)
    for j in range(n, len(jobs)):
        own_copy(j).wait()
        for d in range(1, n_h):
            h_copy(j, d).wait_recv()
    for j in range(len(jobs)):
        for d in range(1, n_h):
            h_copy(j, d).wait_send()
    for j in range(n):
        for k in range(8):
            copy(j, k).wait_send()
        landed(j)


def gene_tail(counts):
    tail = counts[counts.shape[0] // CHUNK * CHUNK :]
    return jnp.pad(tail, ((0, CHUNK - tail.shape[0]), (0, 0)))


def eighth_of(part):
    c, x, y = (lax.axis_index(name) for name in ("c", "x", "y"))
    return lax.rem(c + part // 4, 2) * 4 + lax.rem(x + part // 2 % 2, 2) * 2 + lax.rem(y + part % 2, 2)


def front_kernel(n_h, jobs, n_arrays, n_full, owners, scale_s, *refs):
    shards = refs[:n_arrays]
    counts, cot, tail, cot_tail, scale, pe, seg_keys, seg_mine = refs[n_arrays : n_arrays + 8]
    rest = refs[n_arrays + 8 :]
    wholes = rest[:n_arrays]
    (xb, xb_other, cot_other, pairs, lefts, left_one, left_last, h0, query, log_total, h1, slope,
     act, hb) = rest[n_arrays : n_arrays + 14]
    (a1, a2, plain, attended, turned, gains, perm, count_buf, enc_buf, xb_buf, total, qkv_buf, mine, pairs_buf, out_buf,
     up_buf, down_buf, own_left, send_left, count_sem, enc_sem, xb_sem, fetch_sem, kv_sem, kv_send, kv_recv,
     cot_send, cot_recv, left_sem, left_send, left_recv, *sems) = rest[n_arrays + 14 :]
    y, c = lax.axis_index("y"), lax.axis_index("c")
    to_core = {"c": 1 - c}
    f32, b16 = jnp.float32, jnp.bfloat16
    cells, width = h0.shape
    slots, head = 4 * cells, 64
    n_pairs = width // 128
    n_chunks = xb.shape[0] // CHUNK
    by_chunk = lambda k: pl.ds(pl.multiple_of(k * CHUNK, CHUNK), CHUNK)

    def loads(k, last):
        slot = lax.rem(k, 2)
        source = tail if last else counts.at[by_chunk(k)]
        return (
            pltpu.make_async_copy(source, count_buf.at[slot], count_sem.at[slot]),
            pltpu.make_async_copy(
                wholes[0].at[:, :, :, :, by_chunk(k)], enc_buf.at[slot], enc_sem.at[slot]
            ),
        )

    def store(k):
        slot = lax.rem(k, 2)
        return pltpu.make_async_copy(xb_buf.at[slot], xb.at[by_chunk(k)], xb_sem.at[slot])

    def encode(k, first, last, low, high):
        slot = lax.rem(k, 2)
        for copy in loads(k, last):
            copy.wait()
        if not last:

            @pl.when(k + 1 < (high - 1 if high == n_chunks else high))
            def _():
                for copy in loads(k + 1, False):
                    copy.start()

        @pl.when(k >= low + 2)
        def _():
            store(k - 2).wait()

        value = jnp.log1p(count_buf[slot].astype(f32) * scale[...]).astype(b16)
        xb_buf[slot] = value
        store(k).start()
        term = jnp.dot(enc_buf[slot].reshape(width, CHUNK), value, preferred_element_type=f32)
        if first:

            @pl.when(k == 0)
            def _():
                total[...] = pe[...] + term

            @pl.when(k > 0)
            def _():
                total[...] += term

        else:
            total[...] += term

    def encode_job(low, high):
        low, high = low // CHUNK, high // CHUNK
        stop = high - 1 if high == n_chunks else high
        for copy in loads(jnp.int32(low), False):
            copy.start()

        def body(k, carry):
            encode(k, low == 0, False, low, high)
            return carry

        lax.fori_loop(low, stop, body, 0)
        if stop < high:
            for copy in loads(jnp.int32(stop), True):
                copy.start()
            encode(jnp.int32(stop), False, True, low, high)
        for k in range(max(low, high - 2), high):
            store(jnp.int32(k)).wait()

    def fetch(k):
        buffer = (qkv_buf, out_buf, up_buf, down_buf)[k]
        return pltpu.make_async_copy(wholes[1 + k], buffer, fetch_sem.at[k])

    def project():
        fetch(0).wait()
        vectors = qkv_buf[:, :, :, :, 3 * width :].reshape(width, 128).astype(f32)
        value = total[...]
        centred = value - jnp.mean(value, axis=0, keepdims=True)
        variance = jnp.mean(centred * centred, axis=0, keepdims=True)
        normed = centred * lax.rsqrt(variance + eps) * vectors[:, 0:1] + vectors[:, 1:2]
        gains[...] = vectors.T[0:8]
        h0[...] = value.T
        a1[...] = normed.T.astype(b16)

        def tile(k):
            weight = qkv_buf[:, :, :, :, by_chunk(k)].reshape(width, CHUNK)
            return jnp.dot(a1[...], weight, preferred_element_type=f32).astype(b16)

        def keys(k, carry):
            mine[:, by_chunk(k)] = tile(k + width // CHUNK)
            return carry

        lax.fori_loop(0, 2 * width // CHUNK, keys, 0)
        kv_own().start()
        kv_copy(0).start()

        def queries(k, carry):
            query[:, by_chunk(k)] = tile(k)
            return carry

        lax.fori_loop(0, width // CHUNK, queries, 0)

    def kv_own():
        return pltpu.make_async_copy(mine, pairs.at[0, 0], kv_sem.at[0])

    def kv_copy(k):
        return pltpu.make_async_remote_copy(
            src_ref=(mine, pairs.at[0])[k],
            dst_ref=(pairs.at[0, 1], pairs.at[1])[k],
            send_sem=kv_send.at[k],
            recv_sem=kv_recv.at[k],
            device_id=({"y": 1 - y}, {"c": 1 - c})[k],
            device_id_type=MESH,
        )

    def swap_cot(k):
        source = (cot.at[pl.ds(0, (n_chunks - 1) * CHUNK)], cot_tail)[k]
        place = pl.ds((n_chunks - 1) * CHUNK * k, ((n_chunks - 1) * CHUNK, CHUNK)[k])
        return pltpu.make_async_remote_copy(
            src_ref=source, dst_ref=cot_other.at[place], send_sem=cot_send.at[k], recv_sem=cot_recv.at[k],
            device_id=to_core, device_id_type=MESH,
        )

    def swap_xb():
        return pltpu.make_async_remote_copy(
            src_ref=xb, dst_ref=xb_other, send_sem=cot_send.at[2], recv_sem=cot_recv.at[2],
            device_id=to_core, device_id_type=MESH,
        )

    def make_perm():
        place = lax.broadcasted_iota(jnp.int32, (8, width), 1)
        size = width // 8 // owners
        within, at = lax.rem(place, size), lax.div(place, size)
        at_h, at = lax.rem(at, owners), lax.div(at, owners)
        wanted = at_h * 8 + lax.rem(lax.div(at, 2), 2) * 4 + lax.rem(at, 2) * 2 + lax.div(at, 4)
        wanted = (wanted * size + within)[0:1]
        for k in range(width // CHUNK):
            row = lax.broadcasted_iota(jnp.int32, (CHUNK, width), 0) + k * CHUNK
            perm[k * CHUNK : (k + 1) * CHUNK] = jnp.where(row == wanted, 1.0, 0.0).astype(b16)

    def fetch_pairs():
        return pltpu.make_async_copy(pairs, pairs_buf, kv_sem.at[1])

    def attend(j, carry):
        lanes = by_lanes(j)
        keys = pairs_buf[:, :, :, lanes].reshape(slots, 128)
        values = pairs_buf[:, :, :, by_lanes(n_pairs + j)].reshape(slots, 128).astype(f32).T.astype(b16)
        for half in (0, 1):
            side = slice(half * head, (half + 1) * head)
            scores = lax.dot_general(
                keys[:, side], query[:, lanes][:, side], (((1,), (1,)), ((), ())), preferred_element_type=f32
            )
            scores = jnp.where(seg_keys[...] == seg_mine[...], scores * scale_s, -1000000000.0)
            top = jnp.max(scores, axis=0, keepdims=True)
            expo = jnp.exp(scores - top)
            whole = jnp.sum(expo, axis=0, keepdims=True)
            log_total[pl.ds(2 * j + half, 1), :] = top + jnp.log(whole)
            probs = (expo * (1.0 / whole)).astype(b16)
            turned[side] = jnp.dot(values[side], probs, preferred_element_type=f32)
        plain[:, lanes] = turned[...].T.astype(b16)
        return carry

    def by_lanes(j):
        return pl.ds(pl.multiple_of(j * 128, 128), 128)

    def leave_attention():
        attended[...] = jnp.dot(plain[...], perm[...], preferred_element_type=f32).astype(b16)
        fetch(1).wait()
        for k in range(width // CHUNK):
            columns = slice(k * CHUNK, (k + 1) * CHUNK)
            weight = out_buf[:, :, :, :, columns].reshape(width, CHUNK)
            h1[:, columns] = h0[:, columns] + jnp.dot(attended[...], weight, preferred_element_type=f32)
        value = h1[...]
        centred = value - jnp.mean(value, axis=1, keepdims=True)
        variance = jnp.mean(centred * centred, axis=1, keepdims=True)
        a2[...] = (centred * lax.rsqrt(variance + eps) * gains[2:3] + gains[3:4]).astype(b16)

    def widen(k, carry):
        weight = up_buf[:, :, :, :, by_chunk(k)].reshape(width, CHUNK)
        value = jnp.dot(a2[...], weight, preferred_element_type=f32)
        share = 0.5 * (1.0 + lax.erf(value * (0.5**0.5)))
        act[:, by_chunk(k)] = (value * share).astype(b16)
        slope[:, by_chunk(k)] = share + value * jnp.exp(-0.5 * value * value) * (2.0 * math.pi) ** -0.5
        return carry

    def narrow(k, carry):
        weight = down_buf[:, :, :, :, by_chunk(k)].reshape(4 * width, CHUNK)
        value = h1[:, by_chunk(k)] + jnp.dot(act[...], weight, preferred_element_type=f32)
        hb[:, by_chunk(k)] = value.astype(b16)
        return carry

    def left_copies(k):
        target = (lefts.at[pl.ds(0, 6)], left_one, left_last)[k]
        source = pl.ds((0, 6, 7)[k], (6, 1, 1)[k])
        return (
            pltpu.make_async_copy(own_left.at[source], target.at[:, :, pl.ds(0, cells)], left_sem.at[k]),
            pltpu.make_async_remote_copy(
                src_ref=send_left.at[source], dst_ref=target.at[:, :, pl.ds(cells, cells)],
                send_sem=left_send.at[k], recv_sem=left_recv.at[k], device_id=to_core, device_id_type=MESH,
            ),
        )

    def make_left(source, k):
        size = source.shape[1] // 8
        pieces = size // (width // 8)
        step = size // owners // pieces
        for part in range(8):
            lanes = pl.ds(pl.multiple_of(eighth_of(part) * size, size), size)
            block = source[:, lanes].astype(f32).T.astype(b16)
            target = own_left if part < 4 else send_left
            base = part % 4 * (width // 8)
            if pieces == 1:
                target[k, base : base + size] = block
                continue
            for piece in range(pieces):
                for at in range(owners):
                    rows = block[(at * pieces + piece) * step : (at * pieces + piece + 1) * step]
                    target[k + piece, base + at * step : base + (at + 1) * step] = rows

    arrays = [array for array, *_ in jobs]
    last_of = [max(j for j, array in enumerate(arrays) if array == k) for k in range(5)]
    enc_jobs = [j for j, array in enumerate(arrays) if array == 0]
    at = last_of[1] + 3

    def between(step, landed):
        if step == 0:
            for k in (0, 1):
                swap_cot(k).start()
        if step == 1:
            make_perm()
        if step - 3 in enc_jobs:
            landed(step - 3)
            encode_job(*jobs[step - 3][1:3])
        if step == enc_jobs[-1] + 3:
            swap_xb().start()
        if step == at:
            for j in range(last_of[1] + 1):
                landed(j)
            fetch(0).start()
            project()
        if step == at + 2:
            kv_own().wait()
            kv_copy(0).wait_recv()
            kv_copy(1).start()
            make_left(a1, 6)
            for copy in left_copies(1):
                copy.start()
        if step == at + 3:
            for j in range(last_of[3] + 1):
                landed(j)
            fetch(1).start()
            fetch(2).start()
            kv_copy(1).wait_recv()
            fetch_pairs().start()
            fetch_pairs().wait()
            lax.fori_loop(0, n_pairs // 2, attend, 0)
        if step == at + 4:
            lax.fori_loop(n_pairs // 2, n_pairs, attend, 0)
        if step == at + 5:
            for j in range(last_of[4] + 1):
                landed(j)
            fetch(3).start()
            leave_attention()
            fetch(2).wait()
            lax.fori_loop(0, 2 * width // CHUNK, widen, 0)
        if step == at + 6:
            lax.fori_loop(2 * width // CHUNK, 4 * width // CHUNK, widen, 0)
        if step == at + 7:
            fetch(3).wait()
            lax.fori_loop(0, width // CHUNK, narrow, 0)
            make_left(hb, 7)
            for copy in left_copies(2):
                copy.start()
        if step == at + 8:
            make_left(a2, 0)
            make_left(act, 1)
            make_left(attended, 5)
            for copy in left_copies(0):
                copy.start()

    gather_kernel(n_h, jobs, n_full, shards, wholes, sems, between)
    kv_copy(0).wait_send()
    kv_copy(1).wait_send()
    for k in (0, 1):
        swap_cot(k).wait()
    swap_xb().wait()
    for k in range(3):
        for copy in left_copies(k):
            copy.wait()


def gather_all(shards, cuts, order, counts, cot, scale, pe, seg, scale_s, collective_id):
    owners = n_h = lax.axis_size("h")
    if any(shard.shape[0] % 16 for shard in shards):
        shards = [lax.all_gather(s, "h", axis=0, tiled=True) for s in shards]
        n_h = 1
    jobs = []
    for array, piece in order:
        low, high = cuts[array][piece], cuts[array][piece + 1]
        jobs.append((array, low, high, low + (high - low) // 256 * 128))
    n, others, dma = len(jobs), max(n_h - 1, 1), pltpu.SemaphoreType.DMA
    shapes = [(n_h * s.shape[0], s.shape[1]) for s in shards]
    (genes, cells), width, padded = counts.shape, pe.shape[0], shards[0].shape[1]
    slots, half = seg.shape[0], width // 2
    bf16, f32 = jnp.bfloat16, jnp.float32
    vmem, hbm = pl.BlockSpec(memory_space=pltpu.VMEM), pl.BlockSpec(memory_space=pl.ANY)
    shape = jax.ShapeDtypeStruct
    hbm_out = [shape((padded, cells), bf16)] * 3 + [shape((2, 2, cells, 2 * width), bf16)]
    hbm_out += [shape((k, half, 2 * cells), bf16) for k in (6, 1, 1)]
    vmem_out = [
        shape((cells, width), f32),
        shape((cells, width), bf16),
        shape((width // 64, cells), f32),
        shape((cells, width), f32),
        shape((cells, 4 * width), f32),
        shape((cells, 4 * width), bf16),
        shape((cells, width), bf16),
    ]
    eighth = width // 8
    out = pl.pallas_call(
        functools.partial(front_kernel, n_h, jobs, len(shards), len(shards), owners, scale_s),
        out_shape=[shape((2, 2, 2) + k, bf16) for k in shapes] + hbm_out + vmem_out,
        in_specs=[hbm] * (len(shards) + 4) + [vmem] * 4,
        out_specs=[hbm] * (len(shards) + len(hbm_out)) + [vmem] * len(vmem_out),
        scratch_shapes=[
            pltpu.VMEM((cells, width), bf16),
            pltpu.VMEM((cells, width), bf16),
            pltpu.VMEM((cells, width), bf16),
            pltpu.VMEM((cells, width), bf16),
            pltpu.VMEM((128, cells), f32),
            pltpu.VMEM((8, width), f32),
            pltpu.VMEM((width, width), bf16),
            pltpu.VMEM((2, CHUNK, cells), bf16),
            pltpu.VMEM((2, 2, 2, 2, eighth, CHUNK), bf16),
            pltpu.VMEM((2, CHUNK, cells), bf16),
            pltpu.VMEM((width, cells), f32),
            pltpu.VMEM((2, 2, 2, eighth, shards[1].shape[1]), bf16),
            pltpu.VMEM((cells, 2 * width), bf16),
            pltpu.VMEM((2, 2, cells, 2 * width), bf16),
            pltpu.VMEM((2, 2, 2, eighth, width), bf16),
            pltpu.VMEM((2, 2, 2, eighth, 4 * width), bf16),
            pltpu.VMEM((2, 2, 2, 4 * eighth, width), bf16),
            pltpu.VMEM((8, half, cells), bf16),
            pltpu.VMEM((8, half, cells), bf16),
            dma((2,)),
            dma((2,)),
            dma((2,)),
            dma((4,)),
            dma((2,)),
            dma((2,)),
            dma((2,)),
            dma((3,)),
            dma((3,)),
            dma((3,)),
            dma((3,)),
            dma((3,)),
            dma((n,)),
            dma((n, others)),
            dma((n, others)),
            dma((n, 8)),
            dma((n, 8)),
        ],
        compiler_params=pltpu.CompilerParams(
            collective_id=collective_id, has_side_effects=True, vmem_limit_bytes=63 * 2**20
        ),
    )(
        *shards, counts, cot, gene_tail(counts), gene_tail(cot), scale, pe, seg[:, None], seg[None, :cells]
    )
    return out[: len(shards)], *out[len(shards) :]


def scatter_kernel(n_h, sections, periods, left_starts, lefts, rights, tail, out, scratch, peers, prefetch, beside, after):
    (right_buf, own, s1, r1, s2, r2, s3, r3, load_sem, send1, recv1, send2, recv2, send3, recv3) = scratch
    h, x, y = (lax.axis_index(name) for name in ("h", "x", "y"))
    to_x, to_y = {"x": 1 - x}, {"y": 1 - y}
    w = s3.shape[1]
    rows = w // n_h
    f32, b16 = jnp.float32, jnp.bfloat16
    n_sections = len(sections)
    starts = [sum(sections[:k]) for k in range(n_sections)]
    n = sum(sections)
    cells = right_buf.shape[2] // 2
    greet([{"h": lax.rem(h + d, n_h)} for d in range(1, n_h)] + [to_x, to_y] + peers)

    def loads(i, section, k, last=False):
        slot = lax.rem(i, 3)
        return [
            pltpu.make_async_copy(
                tail if last and not half else rights[2 * section + half].at[chunk_of(k)],
                right_buf.at[slot, :, pl.ds(half * cells, cells)],
                load_sem.at[slot, half],
            )
            for half in (0, 1)
        ]

    def start_loads(i):
        for section, (start, count) in enumerate(zip(starts, sections)):

            @pl.when((i >= start) & (i < start + count))
            def _(section=section, start=start):
                k = lax.rem(i - start, periods[section])
                ends = [(False, k >= 0)]
                if tail is not None:
                    ends = [(False, k < periods[section] - 1), (True, k == periods[section] - 1)]
                for last, here in ends:

                    @pl.when(here)
                    def _(last=last):
                        for copy in loads(i, section, k, last):
                            copy.start()

                prefetch(section, i - start)

    def hop(i, source, target, send_sem, recv_sem, to):
        slot = lax.rem(i, RING)
        return pltpu.make_async_remote_copy(
            src_ref=source.at[slot], dst_ref=target.at[i], send_sem=send_sem.at[slot],
            recv_sem=recv_sem.at[i], device_id=to, device_id_type=MESH,
        )

    def first(i, odd):
        return hop(i, s1, r1, send1, recv1, to_y if odd else to_x)

    def second(i, odd):
        return hop(i, s2, r2, send2, recv2, to_x if odd else to_y)

    def third(i, d):
        to = lax.rem(h + d, n_h)
        slot = lax.rem(i, RING)
        return pltpu.make_async_remote_copy(
            src_ref=s3.at[slot, pl.ds(to * rows, rows)], dst_ref=r3.at[i, d - 1],
            send_sem=send3.at[slot, d - 1], recv_sem=recv3.at[i, d - 1],
            device_id={"h": to}, device_id_type=MESH,
        )

    def multiply(i, odd):
        slot = lax.rem(i, RING)
        for copy in loads(i, 0, 0):
            copy.wait()
        left = lefts[sum((i + 1024 - start) // 1024 for start in left_starts[1:]) if left_starts[1:] else 0]
        right = right_buf.at[lax.rem(i, 3)]

        @pl.when(i >= RING)
        def _():
            first(i - RING, odd).wait_send()

        part = lax.dot_general(left, right[...], (((1,), (1,)), ((), ())), preferred_element_type=f32)
        own[slot, :w] = part[:w]
        if odd:
            own[slot, w:] = part[2 * w : 3 * w]
            s1[slot, :w] = part[w : 2 * w].astype(b16)
            s1[slot, w:] = part[3 * w :].astype(b16)
        else:
            own[slot, w:] = part[w : 2 * w]
            s1[slot] = part[2 * w :].astype(b16)
        first(i, odd).start()

        beside(i, right, odd)
        start_loads(i + 2)

    def pass_on(i, odd):
        slot = lax.rem(i, RING)
        first(i, odd).wait_recv()

        @pl.when(i >= RING)
        def _():
            second(i - RING, odd).wait_send()

        s2[slot] = (own[slot, w:] + r1[i, w:].astype(f32)).astype(b16)
        second(i, odd).start()

    def keep(i, odd):
        slot = lax.rem(i, RING)
        second(i, odd).wait_recv()
        part = own[slot, :w] + r1[i, :w].astype(f32) + r2[i].astype(f32)
        if n_h == 1:
            out[i] = part.astype(b16)
            return

        @pl.when(i >= RING)
        def _():
            for d in range(1, n_h):
                third(i - RING, d).wait_send()

        s3[slot] = part.astype(b16)
        for d in range(1, n_h):
            third(i, d).start()

    def finish(i, odd):
        if n_h == 1:
            return
        total = s3[lax.rem(i, RING), pl.ds(h * rows, rows)].astype(f32)
        for d in range(1, n_h):
            third(i, d).wait_recv()
            total = total + r3[i, d - 1].astype(f32)
        out[i] = total

    start_loads(jnp.int32(0))
    start_loads(jnp.int32(1))
    pairs = (n + 1) // 2

    def step(p, carry):
        for lag, stage in enumerate((multiply, pass_on, keep, finish)):
            for odd in (0, 1):
                i = 2 * (p - lag) + odd

                @pl.when((i >= 0) & (i < n))
                def _(stage=stage, i=i, odd=odd):
                    stage(i, odd)

        after(p)
        return carry

    lax.fori_loop(0, pairs + 3, step, 0)
    for i in range(max(n - RING, 0), n):
        first(i, i % 2).wait_send()
        second(i, i % 2).wait_send()
        for d in range(1, n_h):
            third(i, d).wait_send()


def chunk_of(k):
    return pl.ds(pl.multiple_of(k * CHUNK, CHUNK), CHUNK)


def product_kernel(n_h, sections, periods, left_starts, n_weights, with_sum, *refs):
    lefts, vector = refs[:2]
    n_rights = 2 * len(sections)
    rights, weights = refs[2 : 2 + n_rights], refs[2 + n_rights : 2 + n_rights + n_weights]
    rest = refs[2 + n_rights + n_weights :]
    tail, rest = (rest[0], rest[1:]) if with_sum else (None, rest)
    out, product = rest[:2]
    total_out = rest[2] if with_sum else None
    weight_buf, product_buf, weight_sem, product_sem, *scratch = rest[3 if with_sum else 2 :]
    begin, count = sum(sections[:-1]), sections[-1]
    cells = vector.shape[0]

    def weight_loads(k):
        slot = lax.rem(k, 3)
        size = weights[0].shape[0]
        return [
            pltpu.make_async_copy(
                weight.at[:, chunk_of(k)],
                weight_buf.at[slot, pl.ds(part * size, size)],
                weight_sem.at[slot, part],
            )
            for part, weight in enumerate(weights)
        ]

    def product_store(k):
        slot = lax.rem(k, 2)
        return pltpu.make_async_copy(product_buf.at[slot], product.at[chunk_of(k)], product_sem.at[slot])

    def prefetch(section, k):
        if section == len(sections) - 1:
            for copy in weight_loads(k):
                copy.start()

    def multiply(k, right):
        for copy in weight_loads(k):
            copy.wait()
        weight = weight_buf[lax.rem(k, 3)]

        @pl.when(k >= 2)
        def _():
            product_store(k - 2).wait()

        value = jnp.dot(vector[...], weight, preferred_element_type=jnp.float32)
        product_buf[lax.rem(k, 2)] = value.T.astype(product_buf.dtype)
        product_store(k).start()
        if with_sum:
            term = jnp.dot(weight, right[:, :cells], preferred_element_type=jnp.float32)

            @pl.when(k == 0)
            def _():
                total_out[...] = term

            @pl.when(k > 0)
            def _():
                total_out[...] += term

    def beside(i, right, odd):
        if begin == 0:
            multiply(i, right)
        else:

            @pl.when(i >= begin)
            def _():
                multiply(i - begin, right)

    scatter_kernel(
        n_h, sections, periods, left_starts, lefts, rights, tail, out, scratch, [], prefetch, beside, lambda p: None
    )
    for k in range(max(count - 2, 0), count):
        product_store(k).wait()


def attention_kernel(n_h, sections, periods, left_starts, scale, *refs):
    lefts, query, pairs, d_out, log_total, seg_keys, seg_mine, h0, dh1, vectors, left_one = refs[:11]
    n_rights = 2 * len(sections)
    rights, weight = refs[11 : 11 + n_rights], refs[11 + n_rights]
    (out, turned_own, turned_other, lefts_next, dh0b, d_qkv, d_pairs, by_core, by_y, d_query, weight_buf, turned,
     da1, vector_rows, send_left, got_left, send, recv, local, *scratch) = refs[12 + n_rights :]
    y, c = lax.axis_index("y"), lax.axis_index("c")
    f32, b16 = jnp.float32, jnp.bfloat16
    cells, width = query.shape
    slots = 4 * cells
    n_pairs, head = width // 128, 64
    into = (((1,), (1,)), ((), ()))

    def backward(j, half):
        lanes = pl.ds(pl.multiple_of(j * 128, 128), 128)
        value_lanes = pl.ds(pl.multiple_of(width + j * 128, 128), 128)
        side = slice(half * head, (half + 1) * head)
        keys = pairs[:, :, :, lanes].reshape(slots, 128)[:, side]
        values = pairs[:, :, :, value_lanes].reshape(slots, 128)[:, side]
        mine, above = query[:, lanes][:, side], d_out[:, lanes][:, side]
        scores = lax.dot_general(keys, mine, into, preferred_element_type=f32) * scale
        scores = jnp.where(seg_keys[...] == seg_mine[...], scores, -1000000000.0)
        probs = jnp.exp(scores - log_total[pl.ds(2 * j + half, 1), :])
        d_probs = lax.dot_general(values, above, into, preferred_element_type=f32)
        inner = jnp.sum(probs * d_probs, axis=0, keepdims=True)
        d_scores = (probs * (d_probs - inner)).astype(b16)
        d_keys = jnp.dot(d_scores, mine, preferred_element_type=f32) * scale
        d_values = jnp.dot(probs.astype(b16), above, preferred_element_type=f32)
        d_pairs[0, j, :, side] = d_keys.astype(b16)
        d_pairs[1, j, :, side] = d_values.astype(b16)
        turned = keys.astype(f32).T.astype(b16)
        d_query[side] = jnp.dot(turned, d_scores, preferred_element_type=f32) * scale
        if half:
            d_qkv[:, lanes] = d_query[...].T.astype(b16)

    def to_core():
        return pltpu.make_async_remote_copy(
            src_ref=d_pairs.at[:, :, pl.ds(2 * cells, 2 * cells)], dst_ref=by_core,
            send_sem=send.at[0], recv_sem=recv.at[0], device_id={"c": 1 - c}, device_id_type=MESH,
        )

    def to_y():
        return pltpu.make_async_remote_copy(
            src_ref=d_pairs.at[:, :, pl.ds(cells, cells)], dst_ref=by_y,
            send_sem=send.at[1], recv_sem=recv.at[1], device_id={"y": 1 - y}, device_id_type=MESH,
        )

    def beside(i, right, odd):
        @pl.when(i < 2 * n_pairs)
        def _():
            backward(i // 2, odd)

    def fetch_weight():
        return pltpu.make_async_copy(weight, weight_buf, local.at[0])

    def keep_turned():
        return pltpu.make_async_copy(turned, turned_own, local.at[1])

    def send_turned():
        return pltpu.make_async_remote_copy(
            src_ref=turned, dst_ref=turned_other,
            send_sem=send.at[2], recv_sem=recv.at[2], device_id={"c": 1 - c}, device_id_type=MESH,
        )

    def to_other_left():
        return pltpu.make_async_remote_copy(
            src_ref=send_left, dst_ref=got_left,
            send_sem=send.at[3], recv_sem=recv.at[3], device_id={"c": 1 - c}, device_id_type=MESH,
        )

    def share():
        to_core().wait_recv()

        def add(j, carry):
            for kind in (0, 1):
                total = d_pairs[kind, j, : 2 * cells].astype(f32) + by_core[kind, j].astype(f32)
                d_pairs[kind, j, : 2 * cells] = total.astype(b16)
            return carry

        lax.fori_loop(0, n_pairs, add, 0)
        to_y().start()

    def collect():
        to_y().wait_recv()

        def add(j, carry):
            for kind in (0, 1):
                lanes = pl.ds(pl.multiple_of((kind + 1) * width + j * 128, 128), 128)
                total = d_pairs[kind, j, :cells].astype(f32) + by_y[kind, j].astype(f32)
                d_qkv[:, lanes] = total.astype(b16)
            return carry

        lax.fori_loop(0, n_pairs, add, 0)

    def turn():
        def tile(k, carry):
            turned[chunk_of(k)] = d_qkv[:, chunk_of(k)].astype(f32).T.astype(b16)
            return carry

        lax.fori_loop(0, 3 * width // CHUNK, tile, 0)
        keep_turned().start()
        send_turned().start()

    def project():
        fetch_weight().wait()
        for k in range(4):
            rows = weight_buf[k // 2, k % 2].reshape(width // 4, -1)[:, : 3 * width]
            da1[:, k * width // 4 : (k + 1) * width // 4] = lax.dot_general(
                d_qkv[...], rows, into, preferred_element_type=f32
            )

    def norm():
        value, above = h0[...], da1[...]
        centred = value - jnp.mean(value, axis=1, keepdims=True)
        inverse = lax.rsqrt(jnp.mean(centred * centred, axis=1, keepdims=True) + eps)
        normed = centred * inverse
        vector_rows[...] = jnp.zeros_like(vector_rows)
        vector_rows[0:1] = jnp.sum(above * normed, axis=0, keepdims=True)
        vector_rows[1:2] = jnp.sum(above, axis=0, keepdims=True)
        vector_rows[2:4] = vectors[1:3]
        above = above * vectors[0:1]
        inner = jnp.mean(above * normed, axis=1, keepdims=True)
        below = inverse * (above - jnp.mean(above, axis=1, keepdims=True) - normed * inner)
        dh0b[...] = (dh1[...] + below).astype(b16)

    def halves():
        for kind, source in enumerate((vector_rows, dh0b)):
            for part in range(8):
                lanes = pl.ds(pl.multiple_of(eighth_of(part) * (width // 8), width // 8), width // 8)
                block = source[:, lanes].astype(f32).T.astype(b16)
                rows = slice(part % 4 * (width // 8), (part % 4 + 1) * (width // 8))
                if part < 4:
                    lefts_next[1 + kind, rows, :cells] = block
                else:
                    send_left[kind, rows] = block
        to_other_left().start()

    def after(p):
        plan = {0: lambda: fetch_weight().start(), n_pairs: lambda: to_core().start(), n_pairs + 2: share}
        plan.update(zip(range(n_chunk_pairs - 2, n_chunk_pairs + 3), (collect, turn, project, norm, halves)))
        for when, action in plan.items():

            @pl.when(p == when)
            def _(action=action):
                action()

    n_chunk_pairs = (sum(sections) + 1) // 2
    scatter_kernel(
        n_h, sections, periods, left_starts, lefts, rights, None, out, scratch, [{"c": 1 - c}],
        lambda section, k: None, beside, after,
    )
    lefts_next[0] = left_one[...]
    to_other_left().wait_recv()
    for kind in (0, 1):
        lefts_next[1 + kind, :, cells:] = got_left[kind]
    keep_turned().wait()
    send_turned().wait()
    for copy in (to_core(), to_y(), to_other_left()):
        copy.wait_send()


def scatter_call(kernel, lefts, rights, operands, more_operands, out_shapes, out_specs, scratch, collective_id):
    periods = [other.shape[0] // CHUNK for _, other, _ in rights]
    sections = [period * times for period, (*_, times) in zip(periods, rights)]
    n, cells = sum(sections), rights[0][0].shape[1]
    w = lefts.shape[1] // 4
    n_h = lax.axis_size("h")
    rows = w // n_h
    inner_h = n_h if rows % 16 == 0 else 1
    dma, bf16, f32 = pltpu.SemaphoreType.DMA, jnp.bfloat16, jnp.float32
    vmem, hbm = pl.BlockSpec(memory_space=pltpu.VMEM), pl.BlockSpec(memory_space=pl.ANY)
    others = max(inner_h - 1, 1)
    part_shape = jax.ShapeDtypeStruct((n, rows, CHUNK), f32)
    if inner_h == 1:
        part_shape = jax.ShapeDtypeStruct((n, w, CHUNK), bf16)
    part, *more = pl.pallas_call(
        functools.partial(kernel, inner_h, sections, periods),
        out_shape=[part_shape] + out_shapes,
        in_specs=[vmem] * (1 + len(operands)) + [hbm] * (2 * len(rights) + len(more_operands)),
        out_specs=[vmem] + out_specs,
        scratch_shapes=scratch
        + [
            pltpu.VMEM((3, CHUNK, 2 * cells), bf16),
            pltpu.VMEM((RING, 2 * w, CHUNK), f32),
            pltpu.VMEM((RING, 2 * w, CHUNK), bf16),
            pltpu.VMEM((n, 2 * w, CHUNK), bf16),
            pltpu.VMEM((RING, w, CHUNK), bf16),
            pltpu.VMEM((n, w, CHUNK), bf16),
            pltpu.VMEM((RING, w, CHUNK), bf16),
            pltpu.VMEM((n, others, w // inner_h, CHUNK), bf16),
            dma((3, 2)),
            dma((RING,)),
            dma((n,)),
            dma((RING,)),
            dma((n,)),
            dma((RING, others)),
            dma((n, others)),
        ],
        compiler_params=pltpu.CompilerParams(
            collective_id=collective_id, has_side_effects=True, vmem_limit_bytes=60 * 2**20
        ),
    )(lefts, *operands, *(half for pair in rights for half in pair[:2]), *more_operands)
    if inner_h == 1:
        part = lax.psum_scatter(part, "h", scatter_dimension=1, tiled=True).astype(f32)
    return part, *more


def scatter_product(lefts, left_starts, rights, vector, weights, product_type, with_sum, collective_id):
    (cells, features), columns = vector.shape, rights[-1][1].shape[0]
    dma = pltpu.SemaphoreType.DMA
    vmem, hbm = pl.BlockSpec(memory_space=pltpu.VMEM), pl.BlockSpec(memory_space=pl.ANY)

    def kernel(n_h, sections, periods, *refs):
        product_kernel(n_h, sections, periods, left_starts, len(weights) - with_sum, with_sum, *refs)

    return scatter_call(
        kernel,
        lefts,
        rights,
        [vector],
        weights,
        [jax.ShapeDtypeStruct((columns, cells), product_type)]
        + [jax.ShapeDtypeStruct((features, cells), jnp.float32)] * with_sum,
        [hbm] + [vmem] * with_sum,
        [
            pltpu.VMEM((3, features, CHUNK), jnp.bfloat16),
            pltpu.VMEM((2, CHUNK, cells), product_type),
            dma((3, len(weights))),
            dma((2,)),
        ],
        collective_id,
    )


def scatter_attention(lefts, left_starts, rights, operands, weight, scale, collective_id):
    cells, width = operands[0].shape
    bf16, f32, dma = jnp.bfloat16, jnp.float32, pltpu.SemaphoreType.DMA
    vmem, hbm = pl.BlockSpec(memory_space=pltpu.VMEM), pl.BlockSpec(memory_space=pl.ANY)

    def kernel(n_h, sections, periods, *refs):
        attention_kernel(n_h, sections, periods, left_starts, scale, *refs)

    return scatter_call(
        kernel,
        lefts,
        rights,
        operands,
        [weight],
        [
            jax.ShapeDtypeStruct((3 * width, cells), bf16),
            jax.ShapeDtypeStruct((3 * width, cells), bf16),
            jax.ShapeDtypeStruct((3,) + lefts.shape[1:], bf16),
            jax.ShapeDtypeStruct((cells, width), bf16),
        ],
        [hbm, hbm, vmem, vmem],
        [
            pltpu.VMEM((cells, 3 * width), bf16),
            pltpu.VMEM((2, width // 128, 4 * cells, 128), bf16),
            pltpu.VMEM((2, width // 128, 2 * cells, 128), bf16),
            pltpu.VMEM((2, width // 128, cells, 128), bf16),
            pltpu.VMEM((128, cells), f32),
            pltpu.VMEM(weight.shape, bf16),
            pltpu.VMEM((3 * width, cells), bf16),
            pltpu.VMEM((cells, width), f32),
            pltpu.VMEM((cells, width), f32),
            pltpu.VMEM((2, width // 2, cells), bf16),
            pltpu.VMEM((2, width // 2, cells), bf16),
            dma((4,)),
            dma((4,)),
            dma((2,)),
        ],
        collective_id,
    )


def both_cores(right, times=1):
    return right, swap(right, "c"), times


def columns_of(chunks):
    return chunks.transpose(1, 0, 2).reshape(chunks.shape[1], -1)


def on_device(
    counts,
    library,
    coords,
    lengths,
    cotangent,
    w_enc,
    w_qkv,
    w_out,
    gain_one,
    shift_one,
    w_up,
    w_down,
    gain_two,
    shift_two,
    w_dec,
):
    rows = counts.shape[0]
    width = w_qkv.shape[1] // 3
    att_scale = (width // HEADS) ** (-0.5)
    group_size = 4
    slots = rows * group_size
    scale = 10000.0 / library
    genes = counts.shape[1]
    padded = -(-genes // CHUNK) * CHUNK
    counts_f = counts.astype(jnp.float32)
    pe = by_owner(positions(coords, width), 1)
    ends = jnp.cumsum(lengths[0])
    group = [
        (lax.axis_index("y") ^ by_y) * 2 + (lax.axis_index("c") ^ by_c)
        for by_c in range(2)
        for by_y in range(2)
    ]
    place = jnp.concatenate([at * rows + jnp.arange(rows, dtype=jnp.int32) for at in group])
    seg_all = jnp.sum((place[:, None] >= ends[None, :]).astype(jnp.int32), axis=1)
    vectors = jnp.stack([gain_one, shift_one, gain_two, shift_two], axis=1)
    vectors = jnp.pad(vectors, ((0, 0), (0, 124)))
    pad = ((0, 0), (0, padded - genes))
    quarter = padded // CHUNK // 4 * CHUNK
    gene_cuts = [0, quarter, 2 * quarter, 3 * quarter, padded]
    shards = [
        jnp.pad(w_enc.T, pad),
        jnp.concatenate([w_qkv, vectors], axis=1),
        by_owner(w_out, 1),
        by_owner(w_up, 1),
        by_owner(w_down, 1),
        jnp.pad(w_dec.T, pad),
    ]
    cuts = [gene_cuts, [0, width // 2 * 3, 3 * width + 128], [0, width]]
    cuts += [[0, 2 * width, 4 * width], [0, width // 2, width]]
    cuts += [gene_cuts]
    order = [(0, 0), (0, 1), (0, 2), (0, 3), (1, 0), (1, 1), (2, 0), (3, 0), (3, 1), (4, 0), (4, 1)]
    order += [(5, 0), (5, 1), (5, 2), (5, 3)]
    (gathered, xb, xb_other, cot_other, kv_pairs, lefts, left_one, left_last, h0, query, log_total, h1, slope, _,
     hb) = gather_all(
        shards, cuts, order, counts.T, cotangent.T, scale[None, :], pe.T, seg_all, att_scale, 0
    )
    enc_all, qkv_all, out_all, up_all, down_all, dec_all = (
        w.reshape(-1, w.shape[-1]) for w in gathered
    )
    vectors = qkv_all[:, 3 * width :].astype(jnp.float32).T
    g1f, b1f, g2f, b2f = vectors[0], vectors[1], vectors[2], vectors[3]
    grad_dec, logits, dh2 = scatter_product(
        left_last, [0], [(cotangent.T, cot_other, 1)], hb, [dec_all, gene_tail(cotangent.T)], jnp.bfloat16, True, 1
    )
    own_rows = grad_dec.shape[1]
    grad_dec = columns_of(grad_dec)[:, :genes].T
    logits = logits[:genes].T
    dfb_turned = dh2.astype(jnp.bfloat16)
    dh2 = dh2.T
    dfb = dfb_turned.T
    d_act = contract_cols(dfb, down_all)
    d_hidden = (d_act * slope).astype(jnp.bfloat16)
    da2 = contract_cols(d_hidden, up_all)
    norm_pull = jax.vjp(layer_norm, h1, g2f, b2f)[1]
    dh1_norm, grad_gain_two, grad_shift_two = norm_pull(da2)
    dh1 = dh2 + dh1_norm
    dab = dh1.astype(jnp.bfloat16)
    d_attended = contract_cols(dab, out_all).astype(jnp.bfloat16)
    d_attended = from_owner(d_attended, 1)
    pieces = (4 * width,) + (width,) * 4
    rights = [both_cores(d_hidden.T), both_cores(dfb_turned, 4), both_cores(dab.T)]
    operands = [query, kv_pairs, d_attended, log_total, seg_all[:, None], seg_all[None, :rows], h0, dh1]
    operands += [jnp.pad(jnp.stack([g1f, grad_gain_two, grad_shift_two]), ((0, 5), (0, 0))), left_one[0]]
    grads, d_qkv, d_qkv_other, lefts, dh0b = scatter_attention(
        lefts,
        [sum(pieces[:k]) // CHUNK for k in range(len(pieces) + 1)],
        rights,
        operands,
        gathered[1],
        att_scale,
        2,
    )
    ends = [0]
    for columns in (4 * width, 4 * width, width):
        ends.append(ends[-1] + columns // CHUNK)
    grad_up, grad_down, grad_out = (grads[low:high] for low, high in zip(ends, ends[1:]))
    grad_up, grad_out = columns_of(grad_up), columns_of(grad_out)
    grad_down = grad_down.reshape(4, -1, own_rows, CHUNK).transpose(0, 2, 1, 3)
    grad_down = grad_down.reshape(4 * own_rows, -1)
    grad_out, grad_up, grad_down = (from_owner(g, 1) for g in (grad_out, grad_up, grad_down))
    unit = jnp.eye(rows, dtype=jnp.bfloat16)
    grads, d_xb = scatter_product(
        lefts,
        [0, 3 * width // CHUNK, (3 * width + rows) // CHUNK],
        [(d_qkv, d_qkv_other, 1), (unit, unit, 1), (xb, xb_other, 1)],
        dh0b,
        [enc_all],
        jnp.float32,
        False,
        3,
    )
    ends = [0]
    for columns in (3 * width, rows):
        ends.append(ends[-1] + columns // CHUNK)
    grad_qkv, grad_vectors, grad_enc = (
        grads[low:high] for low, high in zip(ends, ends[1:] + [grads.shape[0]])
    )
    grad_qkv, grad_enc = columns_of(grad_qkv), columns_of(grad_enc)
    grad_gain_one, grad_shift_one, grad_gain_two, grad_shift_two = (
        grad_vectors[0, :, k] for k in range(4)
    )
    grad_enc = grad_enc[:, :genes].T
    d_xb = d_xb[:genes].T
    counts_grad = d_xb * scale[:, None] / (1.0 + counts_f * scale[:, None])
    return (
        logits,
        counts_grad,
        grad_enc,
        grad_qkv,
        grad_out,
        grad_gain_one,
        grad_shift_one,
        grad_up,
        grad_down,
        grad_gain_two,
        grad_shift_two,
        grad_dec,
    )


ALL = ("h", "x", "y", "c")


def solution(mesh):
    n_dp, n_fsdp = mesh.shape["dp"], mesh.shape["fsdp"]
    mesh = Mesh(mesh.devices.reshape((n_dp // 2, 2, 2, n_fsdp // 2)), ALL)
    placed = (
        P(ALL, None),
        P(ALL),
        P(None, ALL),
        P(("h", "x"), None),
        P(ALL, None),
        P(None, ALL),
        P(ALL, None),
        P(ALL, None),
        P(ALL),
        P(ALL),
        P(ALL, None),
        P(ALL, None),
        P(ALL),
        P(ALL),
        P(None, ALL),
    )
    return jax.shard_map(
        on_device,
        mesh=mesh,
        in_specs=placed,
        out_specs=(
            P(ALL, None),
            P(ALL, None),
            P(None, ALL),
            P(ALL, None),
            P(ALL, None),
            P(ALL),
            P(ALL),
            P(ALL, None),
            P(ALL, None),
            P(ALL),
            P(ALL),
            P(None, ALL),
        ),
        check_vma=False,
    )
```

```python
import functools
import math

import jax
import jax.numpy as jnp
from jax import lax
from jax.experimental import pallas as pl
from jax.experimental.pallas import tpu as pltpu
from jax.sharding import Mesh
from jax.sharding import PartitionSpec as P

HEADS = 16
MESH = pl.DeviceIdType.MESH
RING = 8
CHUNK = 256


eps = 1e-05


def layer_norm(value, gain, shift):
    mean = jnp.mean(value, axis=1, keepdims=True)
    centred = value - mean
    variance = jnp.mean(centred * centred, axis=1, keepdims=True)
    return centred * lax.rsqrt(variance + eps) * gain + shift


def positions(coords, width):
    quarter = width // 4
    freqs = 0.05 * jnp.exp(-jnp.arange(quarter, dtype=jnp.float32) * (math.log(10000.0) / quarter))
    along_x = coords[0].astype(jnp.float32)[:, None] * freqs[None, :]
    along_y = coords[1].astype(jnp.float32)[:, None] * freqs[None, :]
    return jnp.concatenate(
        [jnp.sin(along_x), jnp.cos(along_x), jnp.sin(along_y), jnp.cos(along_y)], axis=1
    )


def contract_cols(left, right):
    return lax.dot_general(
        left, right, (((1,), (1,)), ((), ())), preferred_element_type=jnp.float32
    )


def swap(value, axis):
    return lax.ppermute(value, axis, [(0, 1), (1, 0)])


def by_owner(value, axis):
    n_h = lax.axis_size("h")
    at = value.shape
    block = at[axis] // (8 * n_h)
    split = value.reshape(at[:axis] + (n_h, 2, 2, 2, block) + at[axis + 1 :])
    order = list(range(axis)) + [axis + 3, axis + 1, axis + 2, axis, axis + 4]
    order += list(range(axis + 5, split.ndim))
    return split.transpose(order).reshape(at)


def from_owner(value, axis):
    n_h = lax.axis_size("h")
    at = value.shape
    block = at[axis] // (8 * n_h)
    split = value.reshape(at[:axis] + (2, 2, 2, n_h, block) + at[axis + 1 :])
    order = list(range(axis)) + [axis + 3, axis + 1, axis + 2, axis, axis + 4]
    order += list(range(axis + 5, split.ndim))
    return split.transpose(order).reshape(at)


def greet(peers):
    barrier = pltpu.get_barrier_semaphore()
    for peer in peers:
        pl.semaphore_signal(barrier, inc=1, device_id=peer, device_id_type=MESH)
    pl.semaphore_wait(barrier, len(peers))


def gather_kernel(n_h, jobs, n_full, shards, wholes, sems, between):
    own_sem, h_send, h_recv, send, recv = sems
    h, x, y, c = (lax.axis_index(name) for name in ("h", "x", "y", "c"))
    h = 0 if n_h == 1 else h
    to_x, to_y, to_c = {"x": 1 - x}, {"y": 1 - y}, {"c": 1 - c}
    greet([{"h": lax.rem(h + d, n_h)} for d in range(1, n_h)] + [to_x, to_y, to_c])

    def rows_of(job, at):
        array, low, high, _ = job
        rows = shards[array].shape[0]
        place = (pl.ds(at * rows, rows), pl.ds(low, high - low))
        return wholes[array].at[(c, x, y, *place) if array < n_full else place]

    def h_copy(j, d):
        array, low, high, _ = jobs[j]
        return pltpu.make_async_remote_copy(
            src_ref=shards[array].at[:, pl.ds(low, high - low)],
            dst_ref=rows_of(jobs[j], h),
            send_sem=h_send.at[j, d - 1],
            recv_sem=h_recv.at[j, d - 1],
            device_id={"h": lax.rem(h + d, n_h)},
            device_id_type=MESH,
        )

    def own_copy(j):
        array, low, high, _ = jobs[j]
        return pltpu.make_async_copy(
            shards[array].at[:, pl.ds(low, high - low)], rows_of(jobs[j], h), own_sem.at[j]
        )

    def block_copy(j, k, block, to, columns):
        view = wholes[jobs[j][0]].at[(*block, slice(None), pl.ds(columns[0], columns[1] - columns[0]))]
        return pltpu.make_async_remote_copy(
            src_ref=view,
            dst_ref=view,
            send_sem=send.at[j, k],
            recv_sem=recv.at[j, k],
            device_id=to,
            device_id_type=MESH,
        )

    own, by_x, by_y, far = (c, x, y), (c, 1 - x, y), (c, x, 1 - y), (c, 1 - x, 1 - y)

    def copy(j, k):
        _, low, high, middle = jobs[j]
        block, to, columns = [
            (own, to_x, (low, high)),
            (own, to_y, (low, high)),
            (own, to_c, (low, high)),
            (by_x, to_y, (low, middle)),
            (by_y, to_x, (middle, high)),
            (by_x, to_c, (low, high)),
            (by_y, to_c, (low, high)),
            (far, to_c, (low, high)),
        ][k]
        return block_copy(j, k, block, to, columns)

    def start_h(j):
        own_copy(j).start()
        for d in range(1, n_h):
            h_copy(j, d).start()

    whole = set()

    def landed(j):
        if j not in whole:
            whole.add(j)
            for k in (2, 5, 6, 7):
                copy(j, k).wait_recv()

    n = sum(array < n_full for array, *_ in jobs)
    ahead = 2
    for j in range(ahead):
        start_h(j)
    for step in range(n + 2):
        if step < n:
            own_copy(step).wait()
            for d in range(1, n_h):
                h_copy(step, d).wait_recv()
            for k in (0, 1, 2):
                copy(step, k).start()
            if step + ahead < len(jobs):
                start_h(step + ahead)
        if 0 <= step - 1 < n:
            for k in (0, 1):
                copy(step - 1, k).wait_recv()
            for k in (3, 4, 5, 6):
                copy(step - 1, k).start()
        if 0 <= step - 2 < n:
            for k in (3, 4):
                copy(step - 2, k).wait_recv()
            copy(step - 2, 7).start()
        between(step, landed)
    for j in range(n, len(jobs)):
        own_copy(j).wait()
        for d in range(1, n_h):
            h_copy(j, d).wait_recv()
    for j in range(len(jobs)):
        for d in range(1, n_h):
            h_copy(j, d).wait_send()
    for j in range(n):
        for k in range(8):
            copy(j, k).wait_send()
        landed(j)


def gene_tail(counts):
    tail = counts[counts.shape[0] // CHUNK * CHUNK :]
    return jnp.pad(tail, ((0, CHUNK - tail.shape[0]), (0, 0)))


def eighth_of(part):
    c, x, y = (lax.axis_index(name) for name in ("c", "x", "y"))
    return lax.rem(c + part // 4, 2) * 4 + lax.rem(x + part // 2 % 2, 2) * 2 + lax.rem(y + part % 2, 2)


def front_kernel(n_h, jobs, n_arrays, n_full, owners, scale_s, *refs):
    shards = refs[:n_arrays]
    counts, cot, tail, cot_tail, scale, pe, seg_keys, seg_mine = refs[n_arrays : n_arrays + 8]
    rest = refs[n_arrays + 8 :]
    wholes = rest[:n_arrays]
    (xb, xb_other, cot_other, pairs, lefts, left_one, left_last, h0, query, log_total, h1, slope,
     act, hb) = rest[n_arrays : n_arrays + 14]
    (a1, a2, plain, attended, turned, gains, perm, count_buf, enc_buf, xb_buf, total, qkv_buf, mine, pairs_buf, out_buf,
     up_buf, down_buf, own_left, send_left, count_sem, enc_sem, xb_sem, fetch_sem, kv_sem, kv_send, kv_recv,
     cot_send, cot_recv, left_sem, left_send, left_recv, *sems) = rest[n_arrays + 14 :]
    y, c = lax.axis_index("y"), lax.axis_index("c")
    to_core = {"c": 1 - c}
    f32, b16 = jnp.float32, jnp.bfloat16
    cells, width = h0.shape
    slots, head = 4 * cells, 64
    n_pairs = width // 128
    n_chunks = xb.shape[0] // CHUNK
    by_chunk = lambda k: pl.ds(pl.multiple_of(k * CHUNK, CHUNK), CHUNK)

    def loads(k, last):
        slot = lax.rem(k, 2)
        source = tail if last else counts.at[by_chunk(k)]
        return (
            pltpu.make_async_copy(source, count_buf.at[slot], count_sem.at[slot]),
            pltpu.make_async_copy(
                wholes[0].at[:, :, :, :, by_chunk(k)], enc_buf.at[slot], enc_sem.at[slot]
            ),
        )

    def store(k):
        slot = lax.rem(k, 2)
        return pltpu.make_async_copy(xb_buf.at[slot], xb.at[by_chunk(k)], xb_sem.at[slot])

    def encode(k, first, last, low, high):
        slot = lax.rem(k, 2)
        for copy in loads(k, last):
            copy.wait()
        if not last:

            @pl.when(k + 1 < (high - 1 if high == n_chunks else high))
            def _():
                for copy in loads(k + 1, False):
                    copy.start()

        @pl.when(k >= low + 2)
        def _():
            store(k - 2).wait()

        value = jnp.log1p(count_buf[slot].astype(f32) * scale[...]).astype(b16)
        xb_buf[slot] = value
        store(k).start()
        term = jnp.dot(enc_buf[slot].reshape(width, CHUNK), value, preferred_element_type=f32)
        if first:

            @pl.when(k == 0)
            def _():
                total[...] = pe[...] + term

            @pl.when(k > 0)
            def _():
                total[...] += term

        else:
            total[...] += term

    def encode_job(low, high):
        low, high = low // CHUNK, high // CHUNK
        stop = high - 1 if high == n_chunks else high
        for copy in loads(jnp.int32(low), False):
            copy.start()

        def body(k, carry):
            encode(k, low == 0, False, low, high)
            return carry

        lax.fori_loop(low, stop, body, 0)
        if stop < high:
            for copy in loads(jnp.int32(stop), True):
                copy.start()
            encode(jnp.int32(stop), False, True, low, high)
        for k in range(max(low, high - 2), high):
            store(jnp.int32(k)).wait()

    def fetch(k):
        buffer = (qkv_buf, out_buf, up_buf, down_buf)[k]
        return pltpu.make_async_copy(wholes[1 + k], buffer, fetch_sem.at[k])

    def project():
        fetch(0).wait()
        vectors = qkv_buf[:, :, :, :, 3 * width :].reshape(width, 128).astype(f32)
        value = total[...]
        centred = value - jnp.mean(value, axis=0, keepdims=True)
        variance = jnp.mean(centred * centred, axis=0, keepdims=True)
        normed = centred * lax.rsqrt(variance + eps) * vectors[:, 0:1] + vectors[:, 1:2]
        gains[...] = vectors.T[0:8]
        h0[...] = value.T
        a1[...] = normed.T.astype(b16)

        def tile(k):
            weight = qkv_buf[:, :, :, :, by_chunk(k)].reshape(width, CHUNK)
            return jnp.dot(a1[...], weight, preferred_element_type=f32).astype(b16)

        def keys(k, carry):
            mine[:, by_chunk(k)] = tile(k + width // CHUNK)
            return carry

        lax.fori_loop(0, 2 * width // CHUNK, keys, 0)
        kv_own().start()
        kv_copy(0).start()

        def queries(k, carry):
            query[:, by_chunk(k)] = tile(k)
            return carry

        lax.fori_loop(0, width // CHUNK, queries, 0)

    def kv_own():
        return pltpu.make_async_copy(mine, pairs.at[0, 0], kv_sem.at[0])

    def kv_copy(k):
        return pltpu.make_async_remote_copy(
            src_ref=(mine, pairs.at[0])[k],
            dst_ref=(pairs.at[0, 1], pairs.at[1])[k],
            send_sem=kv_send.at[k],
            recv_sem=kv_recv.at[k],
            device_id=({"y": 1 - y}, {"c": 1 - c})[k],
            device_id_type=MESH,
        )

    def swap_cot(k):
        source = (cot.at[pl.ds(0, (n_chunks - 1) * CHUNK)], cot_tail)[k]
        place = pl.ds((n_chunks - 1) * CHUNK * k, ((n_chunks - 1) * CHUNK, CHUNK)[k])
        return pltpu.make_async_remote_copy(
            src_ref=source, dst_ref=cot_other.at[place], send_sem=cot_send.at[k], recv_sem=cot_recv.at[k],
            device_id=to_core, device_id_type=MESH,
        )

    def swap_xb():
        return pltpu.make_async_remote_copy(
            src_ref=xb, dst_ref=xb_other, send_sem=cot_send.at[2], recv_sem=cot_recv.at[2],
            device_id=to_core, device_id_type=MESH,
        )

    def make_perm():
        place = lax.broadcasted_iota(jnp.int32, (8, width), 1)
        size = width // 8 // owners
        within, at = lax.rem(place, size), lax.div(place, size)
        at_h, at = lax.rem(at, owners), lax.div(at, owners)
        wanted = at_h * 8 + lax.rem(lax.div(at, 2), 2) * 4 + lax.rem(at, 2) * 2 + lax.div(at, 4)
        wanted = (wanted * size + within)[0:1]
        for k in range(width // CHUNK):
            row = lax.broadcasted_iota(jnp.int32, (CHUNK, width), 0) + k * CHUNK
            perm[k * CHUNK : (k + 1) * CHUNK] = jnp.where(row == wanted, 1.0, 0.0).astype(b16)

    def fetch_pairs():
        return pltpu.make_async_copy(pairs, pairs_buf, kv_sem.at[1])

    def attend(j, carry):
        lanes = by_lanes(j)
        keys = pairs_buf[:, :, :, lanes].reshape(slots, 128)
        values = pairs_buf[:, :, :, by_lanes(n_pairs + j)].reshape(slots, 128).astype(f32).T.astype(b16)
        for half in (0, 1):
            side = slice(half * head, (half + 1) * head)
            scores = lax.dot_general(
                keys[:, side], query[:, lanes][:, side], (((1,), (1,)), ((), ())), preferred_element_type=f32
            )
            scores = jnp.where(seg_keys[...] == seg_mine[...], scores * scale_s, -1000000000.0)
            top = jnp.max(scores, axis=0, keepdims=True)
            expo = jnp.exp(scores - top)
            whole = jnp.sum(expo, axis=0, keepdims=True)
            log_total[pl.ds(2 * j + half, 1), :] = top + jnp.log(whole)
            probs = (expo * (1.0 / whole)).astype(b16)
            turned[side] = jnp.dot(values[side], probs, preferred_element_type=f32)
        plain[:, lanes] = turned[...].T.astype(b16)
        return carry

    def by_lanes(j):
        return pl.ds(pl.multiple_of(j * 128, 128), 128)

    def leave_attention():
        attended[...] = jnp.dot(plain[...], perm[...], preferred_element_type=f32).astype(b16)
        fetch(1).wait()
        for k in range(width // CHUNK):
            columns = slice(k * CHUNK, (k + 1) * CHUNK)
            weight = out_buf[:, :, :, :, columns].reshape(width, CHUNK)
            h1[:, columns] = h0[:, columns] + jnp.dot(attended[...], weight, preferred_element_type=f32)
        value = h1[...]
        centred = value - jnp.mean(value, axis=1, keepdims=True)
        variance = jnp.mean(centred * centred, axis=1, keepdims=True)
        a2[...] = (centred * lax.rsqrt(variance + eps) * gains[2:3] + gains[3:4]).astype(b16)

    def widen(k, carry):
        weight = up_buf[:, :, :, :, by_chunk(k)].reshape(width, CHUNK)
        value = jnp.dot(a2[...], weight, preferred_element_type=f32)
        share = 0.5 * (1.0 + lax.erf(value * (0.5**0.5)))
        act[:, by_chunk(k)] = (value * share).astype(b16)
        steep = share + value * jnp.exp(-0.5 * value * value) * (2.0 * math.pi) ** -0.5
        slope[by_chunk(k)] = steep.T
        return carry

    def narrow(k, carry):
        weight = down_buf[:, :, :, :, by_chunk(k)].reshape(4 * width, CHUNK)
        value = h1[:, by_chunk(k)] + jnp.dot(act[...], weight, preferred_element_type=f32)
        hb[:, by_chunk(k)] = value.astype(b16)
        return carry

    def left_copies(k):
        target = (lefts.at[pl.ds(0, 6)], left_one, left_last)[k]
        source = pl.ds((0, 6, 7)[k], (6, 1, 1)[k])
        return (
            pltpu.make_async_copy(own_left.at[source], target.at[:, :, pl.ds(0, cells)], left_sem.at[k]),
            pltpu.make_async_remote_copy(
                src_ref=send_left.at[source], dst_ref=target.at[:, :, pl.ds(cells, cells)],
                send_sem=left_send.at[k], recv_sem=left_recv.at[k], device_id=to_core, device_id_type=MESH,
            ),
        )

    def make_left(source, k):
        size = source.shape[1] // 8
        pieces = size // (width // 8)
        step = size // owners // pieces
        for part in range(8):
            lanes = pl.ds(pl.multiple_of(eighth_of(part) * size, size), size)
            block = source[:, lanes].astype(f32).T.astype(b16)
            target = own_left if part < 4 else send_left
            base = part % 4 * (width // 8)
            if pieces == 1:
                target[k, base : base + size] = block
                continue
            for piece in range(pieces):
                for at in range(owners):
                    rows = block[(at * pieces + piece) * step : (at * pieces + piece + 1) * step]
                    target[k + piece, base + at * step : base + (at + 1) * step] = rows

    arrays = [array for array, *_ in jobs]
    last_of = [max(j for j, array in enumerate(arrays) if array == k) for k in range(5)]
    enc_jobs = [j for j, array in enumerate(arrays) if array == 0]
    at = last_of[1] + 3

    def between(step, landed):
        if step == 0:
            for k in (0, 1):
                swap_cot(k).start()
        if step == 1:
            make_perm()
        if step - 3 in enc_jobs:
            landed(step - 3)
            encode_job(*jobs[step - 3][1:3])
        if step == enc_jobs[-1] + 3:
            swap_xb().start()
        if step == at:
            for j in range(last_of[1] + 1):
                landed(j)
            fetch(0).start()
            project()
        if step == at + 2:
            kv_own().wait()
            kv_copy(0).wait_recv()
            kv_copy(1).start()
            make_left(a1, 6)
            for copy in left_copies(1):
                copy.start()
        if step == at + 3:
            for j in range(last_of[3] + 1):
                landed(j)
            fetch(1).start()
            fetch(2).start()
            kv_copy(1).wait_recv()
            fetch_pairs().start()
            fetch_pairs().wait()
            lax.fori_loop(0, n_pairs // 2, attend, 0)
        if step == at + 4:
            lax.fori_loop(n_pairs // 2, n_pairs, attend, 0)
        if step == at + 5:
            for j in range(last_of[4] + 1):
                landed(j)
            fetch(3).start()
            leave_attention()
            fetch(2).wait()
            lax.fori_loop(0, 2 * width // CHUNK, widen, 0)
        if step == at + 6:
            lax.fori_loop(2 * width // CHUNK, 4 * width // CHUNK, widen, 0)
        if step == at + 7:
            fetch(3).wait()
            lax.fori_loop(0, width // CHUNK, narrow, 0)
            make_left(hb, 7)
            for copy in left_copies(2):
                copy.start()
        if step == at + 8:
            make_left(a2, 0)
            make_left(act, 1)
            make_left(attended, 5)
            for copy in left_copies(0):
                copy.start()

    gather_kernel(n_h, jobs, n_full, shards, wholes, sems, between)
    kv_copy(0).wait_send()
    kv_copy(1).wait_send()
    for k in (0, 1):
        swap_cot(k).wait()
    swap_xb().wait()
    for k in range(3):
        for copy in left_copies(k):
            copy.wait()


def gather_all(shards, cuts, order, counts, cot, scale, pe, seg, scale_s, collective_id):
    owners = n_h = lax.axis_size("h")
    if any(shard.shape[0] % 16 for shard in shards):
        shards = [lax.all_gather(s, "h", axis=0, tiled=True) for s in shards]
        n_h = 1
    jobs = []
    for array, piece in order:
        low, high = cuts[array][piece], cuts[array][piece + 1]
        jobs.append((array, low, high, low + (high - low) // (512 if array in (3, 4) else 256) * 128))
    n, others, dma = len(jobs), max(n_h - 1, 1), pltpu.SemaphoreType.DMA
    shapes = [(n_h * s.shape[0], s.shape[1]) for s in shards]
    (genes, cells), width, padded = counts.shape, pe.shape[0], shards[0].shape[1]
    slots, half = seg.shape[0], width // 2
    bf16, f32 = jnp.bfloat16, jnp.float32
    vmem, hbm = pl.BlockSpec(memory_space=pltpu.VMEM), pl.BlockSpec(memory_space=pl.ANY)
    shape = jax.ShapeDtypeStruct
    hbm_out = [shape((padded, cells), bf16)] * 3 + [shape((2, 2, cells, 2 * width), bf16)]
    hbm_out += [shape((k, half, 2 * cells), bf16) for k in (6, 1, 1)]
    vmem_out = [
        shape((cells, width), f32),
        shape((cells, width), bf16),
        shape((width // 64, cells), f32),
        shape((cells, width), f32),
        shape((4 * width, cells), f32),
        shape((cells, 4 * width), bf16),
        shape((cells, width), bf16),
    ]
    eighth = width // 8
    out = pl.pallas_call(
        functools.partial(front_kernel, n_h, jobs, len(shards), len(shards), owners, scale_s),
        out_shape=[shape((2, 2, 2) + k, bf16) for k in shapes] + hbm_out + vmem_out,
        in_specs=[vmem] * len(shards) + [hbm] * 4 + [vmem] * 4,
        out_specs=[hbm] * (len(shards) + len(hbm_out)) + [vmem] * len(vmem_out),
        scratch_shapes=[
            pltpu.VMEM((cells, width), bf16),
            pltpu.VMEM((cells, width), bf16),
            pltpu.VMEM((cells, width), bf16),
            pltpu.VMEM((cells, width), bf16),
            pltpu.VMEM((128, cells), f32),
            pltpu.VMEM((8, width), f32),
            pltpu.VMEM((width, width), bf16),
            pltpu.VMEM((2, CHUNK, cells), bf16),
            pltpu.VMEM((2, 2, 2, 2, eighth, CHUNK), bf16),
            pltpu.VMEM((2, CHUNK, cells), bf16),
            pltpu.VMEM((width, cells), f32),
            pltpu.VMEM((2, 2, 2, eighth, shards[1].shape[1]), bf16),
            pltpu.VMEM((cells, 2 * width), bf16),
            pltpu.VMEM((2, 2, cells, 2 * width), bf16),
            pltpu.VMEM((2, 2, 2, eighth, width), bf16),
            pltpu.VMEM((2, 2, 2, eighth, 4 * width), bf16),
            pltpu.VMEM((2, 2, 2, 4 * eighth, width), bf16),
            pltpu.VMEM((8, half, cells), bf16),
            pltpu.VMEM((8, half, cells), bf16),
            dma((2,)),
            dma((2,)),
            dma((2,)),
            dma((4,)),
            dma((2,)),
            dma((2,)),
            dma((2,)),
            dma((3,)),
            dma((3,)),
            dma((3,)),
            dma((3,)),
            dma((3,)),
            dma((n,)),
            dma((n, others)),
            dma((n, others)),
            dma((n, 8)),
            dma((n, 8)),
        ],
        compiler_params=pltpu.CompilerParams(
            collective_id=collective_id, has_side_effects=True, vmem_limit_bytes=63 * 2**20
        ),
    )(
        *shards, counts, cot, gene_tail(counts), gene_tail(cot), scale, pe, seg[:, None], seg[None, :cells]
    )
    return out[: len(shards)], *out[len(shards) :]


def scatter_kernel(n_h, sections, periods, left_starts, lefts, rights, tail, out, scratch, peers, prefetch, beside, after):
    (right_buf, own, s1, r1, s2, r2, s3, r3, load_sem, send1, recv1, send2, recv2, send3, recv3) = scratch
    h, x, y = (lax.axis_index(name) for name in ("h", "x", "y"))
    to_x, to_y = {"x": 1 - x}, {"y": 1 - y}
    w = s3.shape[1]
    rows = w // n_h
    f32, b16 = jnp.float32, jnp.bfloat16
    n_sections = len(sections)
    starts = [sum(sections[:k]) for k in range(n_sections)]
    n = sum(sections)
    cells = right_buf.shape[2] // 2
    greet([{"h": lax.rem(h + d, n_h)} for d in range(1, n_h)] + [to_x, to_y] + peers)

    def loads(i, section, k, last=False):
        slot = lax.rem(i, 3)
        return [
            pltpu.make_async_copy(
                tail if last and not half else rights[2 * section + half].at[chunk_of(k)],
                right_buf.at[slot, :, pl.ds(half * cells, cells)],
                load_sem.at[slot, half],
            )
            for half in (0, 1)
        ]

    def start_loads(i):
        for section, (start, count) in enumerate(zip(starts, sections)):

            @pl.when((i >= start) & (i < start + count))
            def _(section=section, start=start):
                k = lax.rem(i - start, periods[section])
                ends = [(False, k >= 0)]
                if tail is not None:
                    ends = [(False, k < periods[section] - 1), (True, k == periods[section] - 1)]
                for last, here in ends:

                    @pl.when(here)
                    def _(last=last):
                        for copy in loads(i, section, k, last):
                            copy.start()

                prefetch(section, i - start)

    def hop(i, source, target, send_sem, recv_sem, to):
        slot = lax.rem(i, RING)
        return pltpu.make_async_remote_copy(
            src_ref=source.at[slot], dst_ref=target.at[i], send_sem=send_sem.at[slot],
            recv_sem=recv_sem.at[i], device_id=to, device_id_type=MESH,
        )

    def first(i, odd):
        return hop(i, s1, r1, send1, recv1, to_y if odd else to_x)

    def second(i, odd):
        return hop(i, s2, r2, send2, recv2, to_x if odd else to_y)

    def third(i, d):
        to = lax.rem(h + d, n_h)
        slot = lax.rem(i, RING)
        return pltpu.make_async_remote_copy(
            src_ref=s3.at[slot, pl.ds(to * rows, rows)], dst_ref=r3.at[i, d - 1],
            send_sem=send3.at[slot, d - 1], recv_sem=recv3.at[i, d - 1],
            device_id={"h": to}, device_id_type=MESH,
        )

    def multiply(i, odd):
        slot = lax.rem(i, RING)
        for copy in loads(i, 0, 0):
            copy.wait()
        left = lefts[sum((i + 1024 - start) // 1024 for start in left_starts[1:]) if left_starts[1:] else 0]
        right = right_buf.at[lax.rem(i, 3)]

        @pl.when(i >= RING)
        def _():
            first(i - RING, odd).wait_send()

        part = lax.dot_general(left, right[...], (((1,), (1,)), ((), ())), preferred_element_type=f32)
        own[slot, :w] = part[:w]
        if odd:
            own[slot, w:] = part[2 * w : 3 * w]
            s1[slot, :w] = part[w : 2 * w].astype(b16)
            s1[slot, w:] = part[3 * w :].astype(b16)
        else:
            own[slot, w:] = part[w : 2 * w]
            s1[slot] = part[2 * w :].astype(b16)
        first(i, odd).start()

        beside(i, right, odd)
        start_loads(i + 2)

    def pass_on(i, odd):
        slot = lax.rem(i, RING)
        first(i, odd).wait_recv()

        @pl.when(i >= RING)
        def _():
            second(i - RING, odd).wait_send()

        s2[slot] = (own[slot, w:] + r1[i, w:].astype(f32)).astype(b16)
        second(i, odd).start()

    def keep(i, odd):
        slot = lax.rem(i, RING)
        second(i, odd).wait_recv()
        part = own[slot, :w] + r1[i, :w].astype(f32) + r2[i].astype(f32)
        if n_h == 1:
            out[i] = part.astype(b16)
            return

        @pl.when(i >= RING)
        def _():
            for d in range(1, n_h):
                third(i - RING, d).wait_send()

        s3[slot] = part.astype(b16)
        for d in range(1, n_h):
            third(i, d).start()

    def finish(i, odd):
        if n_h == 1:
            return
        total = s3[lax.rem(i, RING), pl.ds(h * rows, rows)].astype(f32)
        for d in range(1, n_h):
            third(i, d).wait_recv()
            total = total + r3[i, d - 1].astype(f32)
        out[i] = total

    start_loads(jnp.int32(0))
    start_loads(jnp.int32(1))
    pairs = (n + 1) // 2

    def step(p, carry):
        for lag, stage in enumerate((multiply, pass_on, keep, finish)):
            for odd in (0, 1):
                i = 2 * (p - lag) + odd

                @pl.when((i >= 0) & (i < n))
                def _(stage=stage, i=i, odd=odd):
                    stage(i, odd)

        after(p)
        return carry

    lax.fori_loop(0, pairs + 3, step, 0)
    for i in range(max(n - RING, 0), n):
        first(i, i % 2).wait_send()
        second(i, i % 2).wait_send()
        for d in range(1, n_h):
            third(i, d).wait_send()


def chunk_of(k):
    return pl.ds(pl.multiple_of(k * CHUNK, CHUNK), CHUNK)


def product_kernel(n_h, sections, periods, left_starts, n_weights, with_sum, *refs):
    lefts, vector = refs[:2]
    n_rights = 2 * len(sections)
    rights, weights = refs[2 : 2 + n_rights], refs[2 + n_rights : 2 + n_rights + n_weights]
    rest = refs[2 + n_rights + n_weights :]
    tail, rest = (rest[0], rest[1:]) if with_sum else (None, rest)
    out, product = rest[:2]
    total_out = rest[2] if with_sum else None
    weight_buf, product_buf, weight_sem, product_sem, *scratch = rest[3 if with_sum else 2 :]
    begin, count = sum(sections[:-1]), sections[-1]
    cells = vector.shape[0]

    def weight_loads(k):
        slot = lax.rem(k, 3)
        size = weights[0].shape[0]
        return [
            pltpu.make_async_copy(
                weight.at[:, chunk_of(k)],
                weight_buf.at[slot, pl.ds(part * size, size)],
                weight_sem.at[slot, part],
            )
            for part, weight in enumerate(weights)
        ]

    def product_store(k):
        slot = lax.rem(k, 2)
        return pltpu.make_async_copy(product_buf.at[slot], product.at[chunk_of(k)], product_sem.at[slot])

    def prefetch(section, k):
        if section == len(sections) - 1:
            for copy in weight_loads(k):
                copy.start()

    def multiply(k, right):
        for copy in weight_loads(k):
            copy.wait()
        weight = weight_buf[lax.rem(k, 3)]

        @pl.when(k >= 2)
        def _():
            product_store(k - 2).wait()

        value = jnp.dot(vector[...], weight, preferred_element_type=jnp.float32)
        product_buf[lax.rem(k, 2)] = value.T.astype(product_buf.dtype)
        product_store(k).start()
        if with_sum:
            term = jnp.dot(weight, right[:, :cells], preferred_element_type=jnp.float32)

            @pl.when(k == 0)
            def _():
                total_out[...] = term

            @pl.when(k > 0)
            def _():
                total_out[...] += term

    def beside(i, right, odd):
        if begin == 0:
            multiply(i, right)
        else:

            @pl.when(i >= begin)
            def _():
                multiply(i - begin, right)

    scatter_kernel(
        n_h, sections, periods, left_starts, lefts, rights, tail, out, scratch, [], prefetch, beside, lambda p: None
    )
    for k in range(max(count - 2, 0), count):
        product_store(k).wait()


def attention_kernel(n_h, sections, periods, left_starts, scale, *refs):
    lefts, query, pairs, d_out, log_total, seg_keys, seg_mine, h0, dh1, vectors, left_one = refs[:11]
    n_rights = 2 * len(sections)
    rights, weight = refs[11 : 11 + n_rights], refs[11 + n_rights]
    (out, turned_own, turned_other, lefts_next, dh0b, d_qkv, d_pairs, by_core, by_y, d_query, weight_buf, turned,
     da1, vector_rows, send_left, got_left, send, recv, local, *scratch) = refs[12 + n_rights :]
    y, c = lax.axis_index("y"), lax.axis_index("c")
    f32, b16 = jnp.float32, jnp.bfloat16
    cells, width = query.shape
    slots = 4 * cells
    n_pairs, head = width // 128, 64
    into = (((1,), (1,)), ((), ()))

    def backward(j, half):
        lanes = pl.ds(pl.multiple_of(j * 128, 128), 128)
        value_lanes = pl.ds(pl.multiple_of(width + j * 128, 128), 128)
        side = slice(half * head, (half + 1) * head)
        keys = pairs[:, :, :, lanes].reshape(slots, 128)[:, side]
        values = pairs[:, :, :, value_lanes].reshape(slots, 128)[:, side]
        mine, above = query[:, lanes][:, side], d_out[:, lanes][:, side]
        scores = lax.dot_general(keys, mine, into, preferred_element_type=f32) * scale
        scores = jnp.where(seg_keys[...] == seg_mine[...], scores, -1000000000.0)
        probs = jnp.exp(scores - log_total[pl.ds(2 * j + half, 1), :])
        d_probs = lax.dot_general(values, above, into, preferred_element_type=f32)
        inner = jnp.sum(probs * d_probs, axis=0, keepdims=True)
        d_scores = (probs * (d_probs - inner)).astype(b16)
        d_keys = jnp.dot(d_scores, mine, preferred_element_type=f32) * scale
        d_values = jnp.dot(probs.astype(b16), above, preferred_element_type=f32)
        d_pairs[0, j, :, side] = d_keys.astype(b16)
        d_pairs[1, j, :, side] = d_values.astype(b16)
        turned = keys.astype(f32).T.astype(b16)
        d_query[side] = jnp.dot(turned, d_scores, preferred_element_type=f32) * scale
        if half:
            d_qkv[:, lanes] = d_query[...].T.astype(b16)

    def to_core():
        return pltpu.make_async_remote_copy(
            src_ref=d_pairs.at[:, :, pl.ds(2 * cells, 2 * cells)], dst_ref=by_core,
            send_sem=send.at[0], recv_sem=recv.at[0], device_id={"c": 1 - c}, device_id_type=MESH,
        )

    def to_y():
        return pltpu.make_async_remote_copy(
            src_ref=d_pairs.at[:, :, pl.ds(cells, cells)], dst_ref=by_y,
            send_sem=send.at[1], recv_sem=recv.at[1], device_id={"y": 1 - y}, device_id_type=MESH,
        )

    def beside(i, right, odd):
        @pl.when(i < 2 * n_pairs)
        def _():
            backward(i // 2, odd)

    def fetch_weight():
        return pltpu.make_async_copy(weight, weight_buf, local.at[0])

    def keep_turned():
        return pltpu.make_async_copy(turned, turned_own, local.at[1])

    def send_turned():
        return pltpu.make_async_remote_copy(
            src_ref=turned, dst_ref=turned_other,
            send_sem=send.at[2], recv_sem=recv.at[2], device_id={"c": 1 - c}, device_id_type=MESH,
        )

    def to_other_left():
        return pltpu.make_async_remote_copy(
            src_ref=send_left, dst_ref=got_left,
            send_sem=send.at[3], recv_sem=recv.at[3], device_id={"c": 1 - c}, device_id_type=MESH,
        )

    def share():
        to_core().wait_recv()

        def add(j, carry):
            for kind in (0, 1):
                total = d_pairs[kind, j, : 2 * cells].astype(f32) + by_core[kind, j].astype(f32)
                d_pairs[kind, j, : 2 * cells] = total.astype(b16)
            return carry

        lax.fori_loop(0, n_pairs, add, 0)
        to_y().start()

    def collect():
        to_y().wait_recv()

        def add(j, carry):
            for kind in (0, 1):
                lanes = pl.ds(pl.multiple_of((kind + 1) * width + j * 128, 128), 128)
                total = d_pairs[kind, j, :cells].astype(f32) + by_y[kind, j].astype(f32)
                d_qkv[:, lanes] = total.astype(b16)
            return carry

        lax.fori_loop(0, n_pairs, add, 0)

    def turn():
        def tile(k, carry):
            turned[chunk_of(k)] = d_qkv[:, chunk_of(k)].astype(f32).T.astype(b16)
            return carry

        lax.fori_loop(0, 3 * width // CHUNK, tile, 0)
        keep_turned().start()
        send_turned().start()

    def project():
        fetch_weight().wait()
        for k in range(4):
            rows = weight_buf[k // 2, k % 2].reshape(width // 4, -1)[:, : 3 * width]
            da1[:, k * width // 4 : (k + 1) * width // 4] = lax.dot_general(
                d_qkv[...], rows, into, preferred_element_type=f32
            )

    def norm():
        value, above = h0[...], da1[...]
        centred = value - jnp.mean(value, axis=1, keepdims=True)
        inverse = lax.rsqrt(jnp.mean(centred * centred, axis=1, keepdims=True) + eps)
        normed = centred * inverse
        vector_rows[...] = jnp.zeros_like(vector_rows)
        vector_rows[0:1] = jnp.sum(above * normed, axis=0, keepdims=True)
        vector_rows[1:2] = jnp.sum(above, axis=0, keepdims=True)
        vector_rows[2:4] = vectors[1:3]
        above = above * vectors[0:1]
        inner = jnp.mean(above * normed, axis=1, keepdims=True)
        below = inverse * (above - jnp.mean(above, axis=1, keepdims=True) - normed * inner)
        dh0b[...] = (dh1[...] + below).astype(b16)

    def halves():
        for kind, source in enumerate((vector_rows, dh0b)):
            for part in range(8):
                lanes = pl.ds(pl.multiple_of(eighth_of(part) * (width // 8), width // 8), width // 8)
                block = source[:, lanes].astype(f32).T.astype(b16)
                rows = slice(part % 4 * (width // 8), (part % 4 + 1) * (width // 8))
                if part < 4:
                    lefts_next[1 + kind, rows, :cells] = block
                else:
                    send_left[kind, rows] = block
        to_other_left().start()

    def after(p):
        plan = {0: lambda: fetch_weight().start(), n_pairs: lambda: to_core().start(), n_pairs + 2: share}
        plan.update(zip(range(n_chunk_pairs - 2, n_chunk_pairs + 3), (collect, turn, project, norm, halves)))
        for when, action in plan.items():

            @pl.when(p == when)
            def _(action=action):
                action()

    n_chunk_pairs = (sum(sections) + 1) // 2
    scatter_kernel(
        n_h, sections, periods, left_starts, lefts, rights, None, out, scratch, [{"c": 1 - c}],
        lambda section, k: None, beside, after,
    )
    lefts_next[0] = left_one[...]
    to_other_left().wait_recv()
    for kind in (0, 1):
        lefts_next[1 + kind, :, cells:] = got_left[kind]
    keep_turned().wait()
    send_turned().wait()
    for copy in (to_core(), to_y(), to_other_left()):
        copy.wait_send()


def scatter_call(kernel, lefts, rights, operands, more_operands, out_shapes, out_specs, scratch, collective_id):
    periods = [other.shape[0] // CHUNK for _, other, _ in rights]
    sections = [period * times for period, (*_, times) in zip(periods, rights)]
    n, cells = sum(sections), rights[0][0].shape[1]
    w = lefts.shape[1] // 4
    n_h = lax.axis_size("h")
    rows = w // n_h
    inner_h = n_h if rows % 16 == 0 else 1
    dma, bf16, f32 = pltpu.SemaphoreType.DMA, jnp.bfloat16, jnp.float32
    vmem, hbm = pl.BlockSpec(memory_space=pltpu.VMEM), pl.BlockSpec(memory_space=pl.ANY)
    others = max(inner_h - 1, 1)
    part_shape = jax.ShapeDtypeStruct((n, rows, CHUNK), f32)
    if inner_h == 1:
        part_shape = jax.ShapeDtypeStruct((n, w, CHUNK), bf16)
    part, *more = pl.pallas_call(
        functools.partial(kernel, inner_h, sections, periods),
        out_shape=[part_shape] + out_shapes,
        in_specs=[vmem] * (1 + len(operands)) + [hbm] * (2 * len(rights) + len(more_operands)),
        out_specs=[vmem] + out_specs,
        scratch_shapes=scratch
        + [
            pltpu.VMEM((3, CHUNK, 2 * cells), bf16),
            pltpu.VMEM((RING, 2 * w, CHUNK), f32),
            pltpu.VMEM((RING, 2 * w, CHUNK), bf16),
            pltpu.VMEM((n, 2 * w, CHUNK), bf16),
            pltpu.VMEM((RING, w, CHUNK), bf16),
            pltpu.VMEM((n, w, CHUNK), bf16),
            pltpu.VMEM((RING, w, CHUNK), bf16),
            pltpu.VMEM((n, others, w // inner_h, CHUNK), bf16),
            dma((3, 2)),
            dma((RING,)),
            dma((n,)),
            dma((RING,)),
            dma((n,)),
            dma((RING, others)),
            dma((n, others)),
        ],
        compiler_params=pltpu.CompilerParams(
            collective_id=collective_id, has_side_effects=True, vmem_limit_bytes=60 * 2**20
        ),
    )(lefts, *operands, *(half for pair in rights for half in pair[:2]), *more_operands)
    if inner_h == 1:
        part = lax.psum_scatter(part, "h", scatter_dimension=1, tiled=True).astype(f32)
    return part, *more


def scatter_product(lefts, left_starts, rights, vector, weights, product_type, with_sum, collective_id):
    (cells, features), columns = vector.shape, rights[-1][1].shape[0]
    dma = pltpu.SemaphoreType.DMA
    vmem, hbm = pl.BlockSpec(memory_space=pltpu.VMEM), pl.BlockSpec(memory_space=pl.ANY)

    def kernel(n_h, sections, periods, *refs):
        product_kernel(n_h, sections, periods, left_starts, len(weights) - with_sum, with_sum, *refs)

    return scatter_call(
        kernel,
        lefts,
        rights,
        [vector],
        weights,
        [jax.ShapeDtypeStruct((columns, cells), product_type)]
        + [jax.ShapeDtypeStruct((features, cells), jnp.float32)] * with_sum,
        [hbm] + [vmem] * with_sum,
        [
            pltpu.VMEM((3, features, CHUNK), jnp.bfloat16),
            pltpu.VMEM((2, CHUNK, cells), product_type),
            dma((3, len(weights))),
            dma((2,)),
        ],
        collective_id,
    )


def scatter_attention(lefts, left_starts, rights, operands, weight, scale, collective_id):
    cells, width = operands[0].shape
    bf16, f32, dma = jnp.bfloat16, jnp.float32, pltpu.SemaphoreType.DMA
    vmem, hbm = pl.BlockSpec(memory_space=pltpu.VMEM), pl.BlockSpec(memory_space=pl.ANY)

    def kernel(n_h, sections, periods, *refs):
        attention_kernel(n_h, sections, periods, left_starts, scale, *refs)

    return scatter_call(
        kernel,
        lefts,
        rights,
        operands,
        [weight],
        [
            jax.ShapeDtypeStruct((3 * width, cells), bf16),
            jax.ShapeDtypeStruct((3 * width, cells), bf16),
            jax.ShapeDtypeStruct((3,) + lefts.shape[1:], bf16),
            jax.ShapeDtypeStruct((cells, width), bf16),
        ],
        [hbm, hbm, vmem, vmem],
        [
            pltpu.VMEM((cells, 3 * width), bf16),
            pltpu.VMEM((2, width // 128, 4 * cells, 128), bf16),
            pltpu.VMEM((2, width // 128, 2 * cells, 128), bf16),
            pltpu.VMEM((2, width // 128, cells, 128), bf16),
            pltpu.VMEM((128, cells), f32),
            pltpu.VMEM(weight.shape, bf16),
            pltpu.VMEM((3 * width, cells), bf16),
            pltpu.VMEM((cells, width), f32),
            pltpu.VMEM((cells, width), f32),
            pltpu.VMEM((2, width // 2, cells), bf16),
            pltpu.VMEM((2, width // 2, cells), bf16),
            dma((4,)),
            dma((4,)),
            dma((2,)),
        ],
        collective_id,
    )


def both_cores(right, times=1):
    return right, swap(right, "c"), times


def columns_of(chunks):
    return chunks.transpose(1, 0, 2).reshape(chunks.shape[1], -1)


def on_device(
    counts,
    library,
    coords,
    lengths,
    cotangent,
    w_enc,
    w_qkv,
    w_out,
    gain_one,
    shift_one,
    w_up,
    w_down,
    gain_two,
    shift_two,
    w_dec,
):
    rows = counts.shape[0]
    width = w_qkv.shape[1] // 3
    att_scale = (width // HEADS) ** (-0.5)
    group_size = 4
    slots = rows * group_size
    scale = 10000.0 / library
    genes = counts.shape[1]
    padded = -(-genes // CHUNK) * CHUNK
    counts_f = counts.astype(jnp.float32)
    pe = by_owner(positions(coords, width), 1)
    ends = jnp.cumsum(lengths[0])
    group = [
        (lax.axis_index("y") ^ by_y) * 2 + (lax.axis_index("c") ^ by_c)
        for by_c in range(2)
        for by_y in range(2)
    ]
    place = jnp.concatenate([at * rows + jnp.arange(rows, dtype=jnp.int32) for at in group])
    seg_all = jnp.sum((place[:, None] >= ends[None, :]).astype(jnp.int32), axis=1)
    vectors = jnp.stack([gain_one, shift_one, gain_two, shift_two], axis=1)
    vectors = jnp.pad(vectors, ((0, 0), (0, 124)))
    pad = ((0, 0), (0, padded - genes))
    quarter = padded // CHUNK // 4 * CHUNK
    gene_cuts = [0, quarter, 2 * quarter, 3 * quarter, padded]
    shards = [
        jnp.pad(w_enc.T, pad),
        jnp.concatenate([w_qkv, vectors], axis=1),
        by_owner(w_out, 1),
        by_owner(w_up, 1),
        by_owner(w_down, 1),
        jnp.pad(w_dec.T, pad),
    ]
    cuts = [gene_cuts, [0, width // 2 * 3, 3 * width + 128], [0, width]]
    cuts += [[0, 2 * width, 4 * width], [0, width // 2, width]]
    cuts += [gene_cuts]
    order = [(0, 0), (0, 1), (0, 2), (0, 3), (1, 0), (1, 1), (2, 0), (3, 0), (3, 1), (4, 0), (4, 1)]
    order += [(5, 0), (5, 1), (5, 2), (5, 3)]
    (gathered, xb, xb_other, cot_other, kv_pairs, lefts, left_one, left_last, h0, query, log_total, h1, slope, _,
     hb) = gather_all(
        shards, cuts, order, counts.T, cotangent.T, scale[None, :], pe.T, seg_all, att_scale, 0
    )
    enc_all, qkv_all, out_all, up_all, down_all, dec_all = (
        w.reshape(-1, w.shape[-1]) for w in gathered
    )
    vectors = qkv_all[:, 3 * width :].astype(jnp.float32).T
    g1f, b1f, g2f, b2f = vectors[0], vectors[1], vectors[2], vectors[3]
    grad_dec, logits, dh2 = scatter_product(
        left_last, [0], [(cotangent.T, cot_other, 1)], hb, [dec_all, gene_tail(cotangent.T)], jnp.bfloat16, True, 1
    )
    own_rows = grad_dec.shape[1]
    grad_dec = columns_of(grad_dec)[:, :genes].T
    logits = logits[:genes].T
    dfb_turned = dh2.astype(jnp.bfloat16)
    dh2 = dh2.T
    dfb = dfb_turned.T
    d_act = contract_cols(dfb, down_all)
    d_hidden = (d_act * slope.T).astype(jnp.bfloat16)
    da2 = contract_cols(d_hidden, up_all)
    norm_pull = jax.vjp(layer_norm, h1, g2f, b2f)[1]
    dh1_norm, grad_gain_two, grad_shift_two = norm_pull(da2)
    dh1 = dh2 + dh1_norm
    dab = dh1.astype(jnp.bfloat16)
    d_attended = contract_cols(dab, out_all).astype(jnp.bfloat16)
    d_attended = from_owner(d_attended, 1)
    pieces = (4 * width,) + (width,) * 4
    rights = [both_cores(d_hidden.T), both_cores(dfb_turned, 4), both_cores(dab.T)]
    operands = [query, kv_pairs, d_attended, log_total, seg_all[:, None], seg_all[None, :rows], h0, dh1]
    operands += [jnp.pad(jnp.stack([g1f, grad_gain_two, grad_shift_two]), ((0, 5), (0, 0))), left_one[0]]
    grads, d_qkv, d_qkv_other, lefts, dh0b = scatter_attention(
        lefts,
        [sum(pieces[:k]) // CHUNK for k in range(len(pieces) + 1)],
        rights,
        operands,
        gathered[1],
        att_scale,
        2,
    )
    ends = [0]
    for columns in (4 * width, 4 * width, width):
        ends.append(ends[-1] + columns // CHUNK)
    grad_up, grad_down, grad_out = (grads[low:high] for low, high in zip(ends, ends[1:]))
    n_h = lax.axis_size("h")
    by_half = (2, 2, 2, 2, own_rows, n_h // 2, -1)
    grad_up = grad_up.reshape(by_half).transpose(4, 3, 5, 1, 2, 0, 6).reshape(own_rows, -1)
    by_pair = (-1, 2, 2, own_rows, 2, n_h, width // (8 * n_h))
    grad_out, grad_down = (
        g.reshape(by_pair).transpose(0, 3, 5, 2, 4, 1, 6).reshape(-1, width) for g in (grad_out, grad_down)
    )
    unit = jnp.eye(rows, dtype=jnp.bfloat16)
    grads, d_xb = scatter_product(
        lefts,
        [0, 3 * width // CHUNK, (3 * width + rows) // CHUNK],
        [(d_qkv, d_qkv_other, 1), (unit, unit, 1), (xb, xb_other, 1)],
        dh0b,
        [enc_all],
        jnp.float32,
        False,
        3,
    )
    ends = [0]
    for columns in (3 * width, rows):
        ends.append(ends[-1] + columns // CHUNK)
    grad_qkv, grad_vectors, grad_enc = (
        grads[low:high] for low, high in zip(ends, ends[1:] + [grads.shape[0]])
    )
    grad_qkv, grad_enc = columns_of(grad_qkv), columns_of(grad_enc)
    grad_gain_one, grad_shift_one, grad_gain_two, grad_shift_two = (
        grad_vectors[0, :, k] for k in range(4)
    )
    grad_enc = grad_enc[:, :genes].T
    d_xb = d_xb[:genes].T
    counts_grad = d_xb * scale[:, None] / (1.0 + counts_f * scale[:, None])
    return (
        logits,
        counts_grad,
        grad_enc,
        grad_qkv,
        grad_out,
        grad_gain_one,
        grad_shift_one,
        grad_up,
        grad_down,
        grad_gain_two,
        grad_shift_two,
        grad_dec,
    )


ALL = ("h", "x", "y", "c")


def solution(mesh):
    n_dp, n_fsdp = mesh.shape["dp"], mesh.shape["fsdp"]
    mesh = Mesh(mesh.devices.reshape((n_dp // 2, 2, 2, n_fsdp // 2)), ALL)
    placed = (
        P(ALL, None),
        P(ALL),
        P(None, ALL),
        P(("h", "x"), None),
        P(ALL, None),
        P(None, ALL),
        P(ALL, None),
        P(ALL, None),
        P(ALL),
        P(ALL),
        P(ALL, None),
        P(ALL, None),
        P(ALL),
        P(ALL),
        P(None, ALL),
    )
    return jax.shard_map(
        on_device,
        mesh=mesh,
        in_specs=placed,
        out_specs=(
            P(ALL, None),
            P(ALL, None),
            P(None, ALL),
            P(ALL, None),
            P(ALL, None),
            P(ALL),
            P(ALL),
            P(ALL, None),
            P(ALL, None),
            P(ALL),
            P(ALL),
            P(None, ALL),
        ),
        check_vma=False,
    )
```

```python
import functools
import math

import jax
import jax.numpy as jnp
from jax import lax
from jax.experimental import pallas as pl
from jax.experimental.pallas import tpu as pltpu
from jax.sharding import Mesh
from jax.sharding import PartitionSpec as P

HEADS = 16
MESH = pl.DeviceIdType.MESH
RING = 8
CHUNK = 256


eps = 1e-05


def layer_norm(value, gain, shift):
    mean = jnp.mean(value, axis=1, keepdims=True)
    centred = value - mean
    variance = jnp.mean(centred * centred, axis=1, keepdims=True)
    return centred * lax.rsqrt(variance + eps) * gain + shift


def positions(coords, width):
    quarter = width // 4
    freqs = 0.05 * jnp.exp(-jnp.arange(quarter, dtype=jnp.float32) * (math.log(10000.0) / quarter))
    along_x = coords[0].astype(jnp.float32)[:, None] * freqs[None, :]
    along_y = coords[1].astype(jnp.float32)[:, None] * freqs[None, :]
    return jnp.concatenate(
        [jnp.sin(along_x), jnp.cos(along_x), jnp.sin(along_y), jnp.cos(along_y)], axis=1
    )


def contract_cols(left, right):
    return lax.dot_general(
        left, right, (((1,), (1,)), ((), ())), preferred_element_type=jnp.float32
    )


def swap(value, axis):
    return lax.ppermute(value, axis, [(0, 1), (1, 0)])


def by_owner(value, axis):
    n_h = lax.axis_size("h")
    at = value.shape
    block = at[axis] // (8 * n_h)
    split = value.reshape(at[:axis] + (n_h, 2, 2, 2, block) + at[axis + 1 :])
    order = list(range(axis)) + [axis + 3, axis + 1, axis + 2, axis, axis + 4]
    order += list(range(axis + 5, split.ndim))
    return split.transpose(order).reshape(at)


def from_owner(value, axis):
    n_h = lax.axis_size("h")
    at = value.shape
    block = at[axis] // (8 * n_h)
    split = value.reshape(at[:axis] + (2, 2, 2, n_h, block) + at[axis + 1 :])
    order = list(range(axis)) + [axis + 3, axis + 1, axis + 2, axis, axis + 4]
    order += list(range(axis + 5, split.ndim))
    return split.transpose(order).reshape(at)


def greet(peers):
    barrier = pltpu.get_barrier_semaphore()
    for peer in peers:
        pl.semaphore_signal(barrier, inc=1, device_id=peer, device_id_type=MESH)
    pl.semaphore_wait(barrier, len(peers))


def gather_kernel(n_h, jobs, n_full, shards, wholes, sems, between):
    own_sem, h_send, h_recv, send, recv = sems
    h, x, y, c = (lax.axis_index(name) for name in ("h", "x", "y", "c"))
    h = 0 if n_h == 1 else h
    to_x, to_y, to_c = {"x": 1 - x}, {"y": 1 - y}, {"c": 1 - c}
    greet([{"h": lax.rem(h + d, n_h)} for d in range(1, n_h)] + [to_x, to_y, to_c])

    def rows_of(job, at):
        array, low, high, _ = job
        rows = shards[array].shape[0]
        place = (pl.ds(at * rows, rows), pl.ds(low, high - low))
        return wholes[array].at[(c, x, y, *place) if array < n_full else place]

    def h_copy(j, d):
        array, low, high, _ = jobs[j]
        return pltpu.make_async_remote_copy(
            src_ref=shards[array].at[:, pl.ds(low, high - low)],
            dst_ref=rows_of(jobs[j], h),
            send_sem=h_send.at[j, d - 1],
            recv_sem=h_recv.at[j, d - 1],
            device_id={"h": lax.rem(h + d, n_h)},
            device_id_type=MESH,
        )

    def own_copy(j):
        array, low, high, _ = jobs[j]
        return pltpu.make_async_copy(
            shards[array].at[:, pl.ds(low, high - low)], rows_of(jobs[j], h), own_sem.at[j]
        )

    def block_copy(j, k, block, to, columns):
        view = wholes[jobs[j][0]].at[(*block, slice(None), pl.ds(columns[0], columns[1] - columns[0]))]
        return pltpu.make_async_remote_copy(
            src_ref=view,
            dst_ref=view,
            send_sem=send.at[j, k],
            recv_sem=recv.at[j, k],
            device_id=to,
            device_id_type=MESH,
        )

    own, by_x, by_y, far = (c, x, y), (c, 1 - x, y), (c, x, 1 - y), (c, 1 - x, 1 - y)

    def copy(j, k):
        _, low, high, middle = jobs[j]
        block, to, columns = [
            (own, to_x, (low, high)),
            (own, to_y, (low, high)),
            (own, to_c, (low, high)),
            (by_x, to_y, (low, middle)),
            (by_y, to_x, (middle, high)),
            (by_x, to_c, (low, high)),
            (by_y, to_c, (low, high)),
            (far, to_c, (low, high)),
        ][k]
        return block_copy(j, k, block, to, columns)

    def start_h(j):
        own_copy(j).start()
        for d in range(1, n_h):
            h_copy(j, d).start()

    whole = set()

    def landed(j):
        if j not in whole:
            whole.add(j)
            for k in (2, 5, 6, 7):
                copy(j, k).wait_recv()

    n = sum(array < n_full for array, *_ in jobs)
    ahead = 2
    for j in range(ahead):
        start_h(j)
    for step in range(n + 2):
        if step < n:
            own_copy(step).wait()
            for d in range(1, n_h):
                h_copy(step, d).wait_recv()
            for k in (0, 1, 2):
                copy(step, k).start()
            if step + ahead < len(jobs):
                start_h(step + ahead)
        if 0 <= step - 1 < n:
            for k in (0, 1):
                copy(step - 1, k).wait_recv()
            for k in (3, 4, 5, 6):
                copy(step - 1, k).start()
        if 0 <= step - 2 < n:
            for k in (3, 4):
                copy(step - 2, k).wait_recv()
            copy(step - 2, 7).start()
        between(step, landed)
    for j in range(n, len(jobs)):
        own_copy(j).wait()
        for d in range(1, n_h):
            h_copy(j, d).wait_recv()
    for j in range(len(jobs)):
        for d in range(1, n_h):
            h_copy(j, d).wait_send()
    for j in range(n):
        for k in range(8):
            copy(j, k).wait_send()
        landed(j)


def gene_tail(counts):
    tail = counts[counts.shape[0] // CHUNK * CHUNK :]
    return jnp.pad(tail, ((0, CHUNK - tail.shape[0]), (0, 0)))


def eighth_of(part):
    c, x, y = (lax.axis_index(name) for name in ("c", "x", "y"))
    return lax.rem(c + part // 4, 2) * 4 + lax.rem(x + part // 2 % 2, 2) * 2 + lax.rem(y + part % 2, 2)


def front_kernel(n_h, jobs, n_arrays, n_full, owners, scale_s, *refs):
    shards = refs[:n_arrays]
    counts, cot, tail, cot_tail, scale, pe, seg_keys, seg_mine = refs[n_arrays : n_arrays + 8]
    rest = refs[n_arrays + 8 :]
    wholes = rest[:n_arrays]
    (xb, xb_other, cot_other, pairs, lefts, left_one, left_last, h0, query, log_total, h1, slope,
     act, hb) = rest[n_arrays : n_arrays + 14]
    (a1, a2, plain, attended, turned, gains, perm, count_buf, enc_buf, xb_buf, total, qkv_buf, mine, pairs_buf, out_buf,
     up_buf, down_buf, own_left, send_left, count_sem, enc_sem, xb_sem, fetch_sem, kv_sem, kv_send, kv_recv,
     cot_send, cot_recv, left_sem, left_send, left_recv, *sems) = rest[n_arrays + 14 :]
    y, c = lax.axis_index("y"), lax.axis_index("c")
    to_core = {"c": 1 - c}
    f32, b16 = jnp.float32, jnp.bfloat16
    cells, width = h0.shape
    slots, head = 4 * cells, 64
    n_pairs = width // 128
    n_chunks = xb.shape[0] // CHUNK
    by_chunk = lambda k: pl.ds(pl.multiple_of(k * CHUNK, CHUNK), CHUNK)

    def loads(k, last):
        slot = lax.rem(k, 2)
        source = tail if last else counts.at[by_chunk(k)]
        return (
            pltpu.make_async_copy(source, count_buf.at[slot], count_sem.at[slot]),
            pltpu.make_async_copy(
                wholes[0].at[:, :, :, :, by_chunk(k)], enc_buf.at[slot], enc_sem.at[slot]
            ),
        )

    def store(k):
        slot = lax.rem(k, 2)
        return pltpu.make_async_copy(xb_buf.at[slot], xb.at[by_chunk(k)], xb_sem.at[slot])

    def encode(k, first, last, low, high):
        slot = lax.rem(k, 2)
        for copy in loads(k, last):
            copy.wait()
        if not last:

            @pl.when(k + 1 < (high - 1 if high == n_chunks else high))
            def _():
                for copy in loads(k + 1, False):
                    copy.start()

        @pl.when(k >= low + 2)
        def _():
            store(k - 2).wait()

        value = jnp.log1p(count_buf[slot].astype(f32) * scale[...]).astype(b16)
        xb_buf[slot] = value
        store(k).start()
        term = jnp.dot(enc_buf[slot].reshape(width, CHUNK), value, preferred_element_type=f32)
        if first:

            @pl.when(k == 0)
            def _():
                total[...] = pe[...] + term

            @pl.when(k > 0)
            def _():
                total[...] += term

        else:
            total[...] += term

    def encode_job(low, high):
        low, high = low // CHUNK, high // CHUNK
        stop = high - 1 if high == n_chunks else high
        for copy in loads(jnp.int32(low), False):
            copy.start()

        def body(k, carry):
            encode(k, low == 0, False, low, high)
            return carry

        lax.fori_loop(low, stop, body, 0)
        if stop < high:
            for copy in loads(jnp.int32(stop), True):
                copy.start()
            encode(jnp.int32(stop), False, True, low, high)
        for k in range(max(low, high - 2), high):
            store(jnp.int32(k)).wait()

    def fetch(k):
        buffer = (qkv_buf, out_buf, up_buf, down_buf)[k]
        return pltpu.make_async_copy(wholes[1 + k], buffer, fetch_sem.at[k])

    def project():
        fetch(0).wait()
        vectors = qkv_buf[:, :, :, :, 3 * width :].reshape(width, 128).astype(f32)
        value = total[...]
        centred = value - jnp.mean(value, axis=0, keepdims=True)
        variance = jnp.mean(centred * centred, axis=0, keepdims=True)
        normed = centred * lax.rsqrt(variance + eps) * vectors[:, 0:1] + vectors[:, 1:2]
        gains[...] = vectors.T[0:8]
        h0[...] = value.T
        a1[...] = normed.T.astype(b16)

        def tile(k):
            weight = qkv_buf[:, :, :, :, by_chunk(k)].reshape(width, CHUNK)
            return jnp.dot(a1[...], weight, preferred_element_type=f32).astype(b16)

        def keys(k, carry):
            mine[:, by_chunk(k)] = tile(k + width // CHUNK)
            return carry

        lax.fori_loop(0, 2 * width // CHUNK, keys, 0)
        kv_own().start()
        kv_copy(0).start()

        def queries(k, carry):
            query[:, by_chunk(k)] = tile(k)
            return carry

        lax.fori_loop(0, width // CHUNK, queries, 0)

    def kv_own():
        return pltpu.make_async_copy(mine, pairs.at[0, 0], kv_sem.at[0])

    def kv_copy(k):
        return pltpu.make_async_remote_copy(
            src_ref=(mine, pairs.at[0])[k],
            dst_ref=(pairs.at[0, 1], pairs.at[1])[k],
            send_sem=kv_send.at[k],
            recv_sem=kv_recv.at[k],
            device_id=({"y": 1 - y}, {"c": 1 - c})[k],
            device_id_type=MESH,
        )

    def swap_cot(k):
        source = (cot.at[pl.ds(0, (n_chunks - 1) * CHUNK)], cot_tail)[k]
        place = pl.ds((n_chunks - 1) * CHUNK * k, ((n_chunks - 1) * CHUNK, CHUNK)[k])
        return pltpu.make_async_remote_copy(
            src_ref=source, dst_ref=cot_other.at[place], send_sem=cot_send.at[k], recv_sem=cot_recv.at[k],
            device_id=to_core, device_id_type=MESH,
        )

    def swap_xb():
        return pltpu.make_async_remote_copy(
            src_ref=xb, dst_ref=xb_other, send_sem=cot_send.at[2], recv_sem=cot_recv.at[2],
            device_id=to_core, device_id_type=MESH,
        )

    def make_perm():
        place = lax.broadcasted_iota(jnp.int32, (8, width), 1)
        size = width // 8 // owners
        within, at = lax.rem(place, size), lax.div(place, size)
        at_h, at = lax.rem(at, owners), lax.div(at, owners)
        wanted = at_h * 8 + lax.rem(lax.div(at, 2), 2) * 4 + lax.rem(at, 2) * 2 + lax.div(at, 4)
        wanted = (wanted * size + within)[0:1]
        for k in range(width // CHUNK):
            row = lax.broadcasted_iota(jnp.int32, (CHUNK, width), 0) + k * CHUNK
            perm[k * CHUNK : (k + 1) * CHUNK] = jnp.where(row == wanted, 1.0, 0.0).astype(b16)

    def fetch_pairs():
        return pltpu.make_async_copy(pairs, pairs_buf, kv_sem.at[1])

    def attend(j, carry):
        lanes = by_lanes(j)
        keys = pairs_buf[:, :, :, lanes].reshape(slots, 128)
        values = pairs_buf[:, :, :, by_lanes(n_pairs + j)].reshape(slots, 128).astype(f32).T.astype(b16)
        for half in (0, 1):
            side = slice(half * head, (half + 1) * head)
            scores = lax.dot_general(
                keys[:, side], query[:, lanes][:, side], (((1,), (1,)), ((), ())), preferred_element_type=f32
            )
            scores = jnp.where(seg_keys[...] == seg_mine[...], scores * scale_s, -1000000000.0)
            top = jnp.max(scores, axis=0, keepdims=True)
            expo = jnp.exp(scores - top)
            whole = jnp.sum(expo, axis=0, keepdims=True)
            log_total[pl.ds(2 * j + half, 1), :] = top + jnp.log(whole)
            probs = (expo * (1.0 / whole)).astype(b16)
            turned[side] = jnp.dot(values[side], probs, preferred_element_type=f32)
        plain[:, lanes] = turned[...].T.astype(b16)
        return carry

    def by_lanes(j):
        return pl.ds(pl.multiple_of(j * 128, 128), 128)

    def leave_attention():
        attended[...] = jnp.dot(plain[...], perm[...], preferred_element_type=f32).astype(b16)
        fetch(1).wait()
        for k in range(width // CHUNK):
            columns = slice(k * CHUNK, (k + 1) * CHUNK)
            weight = out_buf[:, :, :, :, columns].reshape(width, CHUNK)
            h1[:, columns] = h0[:, columns] + jnp.dot(attended[...], weight, preferred_element_type=f32)
        value = h1[...]
        centred = value - jnp.mean(value, axis=1, keepdims=True)
        variance = jnp.mean(centred * centred, axis=1, keepdims=True)
        a2[...] = (centred * lax.rsqrt(variance + eps) * gains[2:3] + gains[3:4]).astype(b16)

    def widen(k, carry):
        weight = up_buf[:, :, :, :, by_chunk(k)].reshape(width, CHUNK)
        value = jnp.dot(a2[...], weight, preferred_element_type=f32)
        share = 0.5 * (1.0 + lax.erf(value * (0.5**0.5)))
        act[:, by_chunk(k)] = (value * share).astype(b16)
        steep = share + value * jnp.exp(-0.5 * value * value) * (2.0 * math.pi) ** -0.5
        slope[by_chunk(k)] = steep.T
        return carry

    def narrow(k, carry):
        weight = down_buf[:, :, :, :, by_chunk(k)].reshape(4 * width, CHUNK)
        value = h1[:, by_chunk(k)] + jnp.dot(act[...], weight, preferred_element_type=f32)
        hb[:, by_chunk(k)] = value.astype(b16)
        return carry

    def left_copies(k):
        target = (lefts.at[pl.ds(0, 6)], left_one, left_last)[k]
        source = pl.ds((0, 6, 7)[k], (6, 1, 1)[k])
        return (
            pltpu.make_async_copy(own_left.at[source], target.at[:, :, pl.ds(0, cells)], left_sem.at[k]),
            pltpu.make_async_remote_copy(
                src_ref=send_left.at[source], dst_ref=target.at[:, :, pl.ds(cells, cells)],
                send_sem=left_send.at[k], recv_sem=left_recv.at[k], device_id=to_core, device_id_type=MESH,
            ),
        )

    def make_left(source, k):
        size = source.shape[1] // 8
        pieces = size // (width // 8)
        step = size // owners // pieces
        for part in range(8):
            lanes = pl.ds(pl.multiple_of(eighth_of(part) * size, size), size)
            block = source[:, lanes].astype(f32).T.astype(b16)
            target = own_left if part < 4 else send_left
            base = part % 4 * (width // 8)
            if pieces == 1:
                target[k, base : base + size] = block
                continue
            for piece in range(pieces):
                for at in range(owners):
                    rows = block[(at * pieces + piece) * step : (at * pieces + piece + 1) * step]
                    target[k + piece, base + at * step : base + (at + 1) * step] = rows

    arrays = [array for array, *_ in jobs]
    last_of = [max(j for j, array in enumerate(arrays) if array == k) for k in range(5)]
    enc_jobs = [j for j, array in enumerate(arrays) if array == 0]
    at = last_of[1] + 3

    def between(step, landed):
        if step == 0:
            for k in (0, 1):
                swap_cot(k).start()
        if step == 1:
            make_perm()
        if step - 3 in enc_jobs:
            landed(step - 3)
            encode_job(*jobs[step - 3][1:3])
        if step == enc_jobs[-1] + 3:
            swap_xb().start()
        if step == at:
            for j in range(last_of[1] + 1):
                landed(j)
            fetch(0).start()
            project()
        if step == at + 2:
            kv_own().wait()
            kv_copy(0).wait_recv()
            kv_copy(1).start()
            make_left(a1, 6)
            for copy in left_copies(1):
                copy.start()
        if step == at + 3:
            for j in range(last_of[3] + 1):
                landed(j)
            fetch(1).start()
            fetch(2).start()
            kv_copy(1).wait_recv()
            fetch_pairs().start()
            fetch_pairs().wait()
            lax.fori_loop(0, n_pairs // 2, attend, 0)
        if step == at + 4:
            lax.fori_loop(n_pairs // 2, n_pairs, attend, 0)
        if step == at + 5:
            for j in range(last_of[4] + 1):
                landed(j)
            fetch(3).start()
            leave_attention()
            fetch(2).wait()
            lax.fori_loop(0, 2 * width // CHUNK, widen, 0)
        if step == at + 6:
            lax.fori_loop(2 * width // CHUNK, 4 * width // CHUNK, widen, 0)
        if step == at + 7:
            fetch(3).wait()
            lax.fori_loop(0, width // CHUNK, narrow, 0)
            make_left(hb, 7)
            for copy in left_copies(2):
                copy.start()
        if step == at + 8:
            make_left(a2, 0)
            make_left(act, 1)
            make_left(attended, 5)
            for copy in left_copies(0):
                copy.start()

    gather_kernel(n_h, jobs, n_full, shards, wholes, sems, between)
    kv_copy(0).wait_send()
    kv_copy(1).wait_send()
    for k in (0, 1):
        swap_cot(k).wait()
    swap_xb().wait()
    for k in range(3):
        for copy in left_copies(k):
            copy.wait()


def gather_all(shards, cuts, order, counts, cot, scale, pe, seg, scale_s, collective_id):
    owners = n_h = lax.axis_size("h")
    if any(shard.shape[0] % 16 for shard in shards):
        shards = [lax.all_gather(s, "h", axis=0, tiled=True) for s in shards]
        n_h = 1
    jobs = []
    for array, piece in order:
        low, high = cuts[array][piece], cuts[array][piece + 1]
        jobs.append((array, low, high, low + (high - low) // (512 if array in (3, 4) else 256) * 128))
    n, others, dma = len(jobs), max(n_h - 1, 1), pltpu.SemaphoreType.DMA
    shapes = [(n_h * s.shape[0], s.shape[1]) for s in shards]
    (genes, cells), width, padded = counts.shape, pe.shape[0], shards[0].shape[1]
    slots, half = seg.shape[0], width // 2
    bf16, f32 = jnp.bfloat16, jnp.float32
    vmem, hbm = pl.BlockSpec(memory_space=pltpu.VMEM), pl.BlockSpec(memory_space=pl.ANY)
    shape = jax.ShapeDtypeStruct
    hbm_out = [shape((padded, cells), bf16)] * 3 + [shape((2, 2, cells, 2 * width), bf16)]
    hbm_out += [shape((k, half, 2 * cells), bf16) for k in (6, 1, 1)]
    vmem_out = [
        shape((cells, width), f32),
        shape((cells, width), bf16),
        shape((width // 64, cells), f32),
        shape((cells, width), f32),
        shape((4 * width, cells), f32),
        shape((cells, 4 * width), bf16),
        shape((cells, width), bf16),
    ]
    eighth = width // 8
    out = pl.pallas_call(
        functools.partial(front_kernel, n_h, jobs, len(shards), len(shards), owners, scale_s),
        out_shape=[shape((2, 2, 2) + k, bf16) for k in shapes] + hbm_out + vmem_out,
        in_specs=[vmem] * len(shards) + [hbm] * 4 + [vmem] * 4,
        out_specs=[hbm] * (len(shards) + len(hbm_out)) + [vmem] * len(vmem_out),
        scratch_shapes=[
            pltpu.VMEM((cells, width), bf16),
            pltpu.VMEM((cells, width), bf16),
            pltpu.VMEM((cells, width), bf16),
            pltpu.VMEM((cells, width), bf16),
            pltpu.VMEM((128, cells), f32),
            pltpu.VMEM((8, width), f32),
            pltpu.VMEM((width, width), bf16),
            pltpu.VMEM((2, CHUNK, cells), bf16),
            pltpu.VMEM((2, 2, 2, 2, eighth, CHUNK), bf16),
            pltpu.VMEM((2, CHUNK, cells), bf16),
            pltpu.VMEM((width, cells), f32),
            pltpu.VMEM((2, 2, 2, eighth, shards[1].shape[1]), bf16),
            pltpu.VMEM((cells, 2 * width), bf16),
            pltpu.VMEM((2, 2, cells, 2 * width), bf16),
            pltpu.VMEM((2, 2, 2, eighth, width), bf16),
            pltpu.VMEM((2, 2, 2, eighth, 4 * width), bf16),
            pltpu.VMEM((2, 2, 2, 4 * eighth, width), bf16),
            pltpu.VMEM((8, half, cells), bf16),
            pltpu.VMEM((8, half, cells), bf16),
            dma((2,)),
            dma((2,)),
            dma((2,)),
            dma((4,)),
            dma((2,)),
            dma((2,)),
            dma((2,)),
            dma((3,)),
            dma((3,)),
            dma((3,)),
            dma((3,)),
            dma((3,)),
            dma((n,)),
            dma((n, others)),
            dma((n, others)),
            dma((n, 8)),
            dma((n, 8)),
        ],
        compiler_params=pltpu.CompilerParams(
            collective_id=collective_id, has_side_effects=True, vmem_limit_bytes=63 * 2**20
        ),
    )(
        *shards, counts, cot, gene_tail(counts), gene_tail(cot), scale, pe, seg[:, None], seg[None, :cells]
    )
    return out[: len(shards)], *out[len(shards) :]


def scatter_kernel(n_h, sections, periods, left_starts, lefts, rights, tail, out, scratch, peers, prefetch, beside, after):
    (right_buf, own, s1, r1, s2, r2, s3, r3, load_sem, send1, recv1, send2, recv2, send3, recv3) = scratch
    h, x, y = (lax.axis_index(name) for name in ("h", "x", "y"))
    to_x, to_y = {"x": 1 - x}, {"y": 1 - y}
    w = s3.shape[1]
    rows = w // n_h
    f32, b16 = jnp.float32, jnp.bfloat16
    n_sections = len(sections)
    starts = [sum(sections[:k]) for k in range(n_sections)]
    n = sum(sections)
    cells = right_buf.shape[2] // 2
    greet([{"h": lax.rem(h + d, n_h)} for d in range(1, n_h)] + [to_x, to_y] + peers)

    def loads(i, section, k, last=False):
        slot = lax.rem(i, 3)
        return [
            pltpu.make_async_copy(
                tail if last and not half else rights[2 * section + half].at[chunk_of(k)],
                right_buf.at[slot, :, pl.ds(half * cells, cells)],
                load_sem.at[slot, half],
            )
            for half in (0, 1)
        ]

    def start_loads(i):
        for section, (start, count) in enumerate(zip(starts, sections)):

            @pl.when((i >= start) & (i < start + count))
            def _(section=section, start=start):
                k = lax.rem(i - start, periods[section])
                ends = [(False, k >= 0)]
                if tail is not None:
                    ends = [(False, k < periods[section] - 1), (True, k == periods[section] - 1)]
                for last, here in ends:

                    @pl.when(here)
                    def _(last=last):
                        for copy in loads(i, section, k, last):
                            copy.start()

                prefetch(section, i - start)

    def hop(i, source, target, send_sem, recv_sem, to):
        slot = lax.rem(i, RING)
        return pltpu.make_async_remote_copy(
            src_ref=source.at[slot], dst_ref=target.at[i], send_sem=send_sem.at[slot],
            recv_sem=recv_sem.at[i], device_id=to, device_id_type=MESH,
        )

    def first(i, odd):
        return hop(i, s1, r1, send1, recv1, to_y if odd else to_x)

    def second(i, odd):
        return hop(i, s2, r2, send2, recv2, to_x if odd else to_y)

    def third(i, d):
        to = lax.rem(h + d, n_h)
        slot = lax.rem(i, RING)
        return pltpu.make_async_remote_copy(
            src_ref=s3.at[slot, pl.ds(to * rows, rows)], dst_ref=r3.at[i, d - 1],
            send_sem=send3.at[slot, d - 1], recv_sem=recv3.at[i, d - 1],
            device_id={"h": to}, device_id_type=MESH,
        )

    def multiply(i, odd):
        slot = lax.rem(i, RING)
        for copy in loads(i, 0, 0):
            copy.wait()
        left = lefts[sum((i + 1024 - start) // 1024 for start in left_starts[1:]) if left_starts[1:] else 0]
        right = right_buf.at[lax.rem(i, 3)]

        @pl.when(i >= RING)
        def _():
            first(i - RING, odd).wait_send()

        part = lax.dot_general(left, right[...], (((1,), (1,)), ((), ())), preferred_element_type=f32)
        own[slot, :w] = part[:w]
        if odd:
            own[slot, w:] = part[2 * w : 3 * w]
            s1[slot, :w] = part[w : 2 * w].astype(b16)
            s1[slot, w:] = part[3 * w :].astype(b16)
        else:
            own[slot, w:] = part[w : 2 * w]
            s1[slot] = part[2 * w :].astype(b16)
        first(i, odd).start()

        beside(i, right, odd)
        start_loads(i + 2)

    def pass_on(i, odd):
        slot = lax.rem(i, RING)
        first(i, odd).wait_recv()

        @pl.when(i >= RING)
        def _():
            second(i - RING, odd).wait_send()

        s2[slot] = (own[slot, w:] + r1[i, w:].astype(f32)).astype(b16)
        second(i, odd).start()

    def keep(i, odd):
        slot = lax.rem(i, RING)
        second(i, odd).wait_recv()
        part = own[slot, :w] + r1[i, :w].astype(f32) + r2[i].astype(f32)
        if n_h == 1:
            out[i] = part.astype(b16)
            return

        @pl.when(i >= RING)
        def _():
            for d in range(1, n_h):
                third(i - RING, d).wait_send()

        s3[slot] = part.astype(b16)
        for d in range(1, n_h):
            third(i, d).start()

    def finish(i, odd):
        if n_h == 1:
            return
        total = s3[lax.rem(i, RING), pl.ds(h * rows, rows)].astype(f32)
        for d in range(1, n_h):
            third(i, d).wait_recv()
            total = total + r3[i, d - 1].astype(f32)
        out[i] = total

    start_loads(jnp.int32(0))
    start_loads(jnp.int32(1))
    pairs = (n + 1) // 2

    def step(p, carry):
        for lag, stage in enumerate((multiply, pass_on, keep, finish)):
            for odd in (0, 1):
                i = 2 * (p - lag) + odd

                @pl.when((i >= 0) & (i < n))
                def _(stage=stage, i=i, odd=odd):
                    stage(i, odd)

        after(p)
        return carry

    lax.fori_loop(0, pairs + 3, step, 0)
    for i in range(max(n - RING, 0), n):
        first(i, i % 2).wait_send()
        second(i, i % 2).wait_send()
        for d in range(1, n_h):
            third(i, d).wait_send()


def chunk_of(k):
    return pl.ds(pl.multiple_of(k * CHUNK, CHUNK), CHUNK)


def product_kernel(n_h, sections, periods, left_starts, n_weights, with_sum, *refs):
    lefts, vector = refs[:2]
    n_rights = 2 * len(sections)
    rights, weights = refs[2 : 2 + n_rights], refs[2 + n_rights : 2 + n_rights + n_weights]
    rest = refs[2 + n_rights + n_weights :]
    tail, rest = (rest[0], rest[1:]) if with_sum else (None, rest)
    out, product = rest[:2]
    total_out = rest[2] if with_sum else None
    weight_buf, product_buf, weight_sem, product_sem, *scratch = rest[3 if with_sum else 2 :]
    begin, count = sum(sections[:-1]), sections[-1]
    cells = vector.shape[0]

    def weight_loads(k):
        slot = lax.rem(k, 3)
        size = weights[0].shape[0]
        return [
            pltpu.make_async_copy(
                weight.at[:, chunk_of(k)],
                weight_buf.at[slot, pl.ds(part * size, size)],
                weight_sem.at[slot, part],
            )
            for part, weight in enumerate(weights)
        ]

    def product_store(k):
        slot = lax.rem(k, 2)
        return pltpu.make_async_copy(product_buf.at[slot], product.at[chunk_of(k)], product_sem.at[slot])

    def prefetch(section, k):
        if section == len(sections) - 1:
            for copy in weight_loads(k):
                copy.start()

    def multiply(k, right):
        for copy in weight_loads(k):
            copy.wait()
        weight = weight_buf[lax.rem(k, 3)]

        @pl.when(k >= 2)
        def _():
            product_store(k - 2).wait()

        value = jnp.dot(vector[...], weight, preferred_element_type=jnp.float32)
        product_buf[lax.rem(k, 2)] = value.T.astype(product_buf.dtype)
        product_store(k).start()
        if with_sum:
            term = jnp.dot(weight, right[:, :cells], preferred_element_type=jnp.float32)

            @pl.when(k == 0)
            def _():
                total_out[...] = term

            @pl.when(k > 0)
            def _():
                total_out[...] += term

    def beside(i, right, odd):
        if begin == 0:
            multiply(i, right)
        else:

            @pl.when(i >= begin)
            def _():
                multiply(i - begin, right)

    scatter_kernel(
        n_h, sections, periods, left_starts, lefts, rights, tail, out, scratch, [], prefetch, beside, lambda p: None
    )
    for k in range(max(count - 2, 0), count):
        product_store(k).wait()


def order_columns(target, chunks, first, n_h):
    columns, rows = target.shape[1], chunks.shape[1]
    block = columns // (8 * n_h)
    for run in range(target.shape[0] // rows):
        for k in range(8 * n_h):
            at, h = k // n_h, k % n_h
            place = (h * 8 + at // 2 % 2 * 4 + at % 2 * 2 + at // 4) * block
            chunk, start = k * block // CHUNK, k * block % CHUNK
            target[run * rows : (run + 1) * rows, place : place + block] = chunks[
                first + run * columns // CHUNK + chunk, :, start : start + block
            ]


def attention_kernel(n_h, sections, periods, left_starts, scale, *refs):
    lefts, query, pairs, d_out, log_total, seg_keys, seg_mine, h0, dh1, vectors, left_one = refs[:11]
    n_rights = 2 * len(sections)
    rights, weight = refs[11 : 11 + n_rights], refs[11 + n_rights]
    (out, turned_own, turned_other, lefts_next, dh0b, grad_up, grad_down, grad_out, d_qkv, d_pairs, by_core, by_y, d_query, weight_buf, turned,
     da1, vector_rows, send_left, got_left, send, recv, local, *scratch) = refs[12 + n_rights :]
    y, c = lax.axis_index("y"), lax.axis_index("c")
    f32, b16 = jnp.float32, jnp.bfloat16
    cells, width = query.shape
    slots = 4 * cells
    n_pairs, head = width // 128, 64
    into = (((1,), (1,)), ((), ()))

    def backward(j, half):
        lanes = pl.ds(pl.multiple_of(j * 128, 128), 128)
        value_lanes = pl.ds(pl.multiple_of(width + j * 128, 128), 128)
        side = slice(half * head, (half + 1) * head)
        keys = pairs[:, :, :, lanes].reshape(slots, 128)[:, side]
        values = pairs[:, :, :, value_lanes].reshape(slots, 128)[:, side]
        mine, above = query[:, lanes][:, side], d_out[:, lanes][:, side]
        scores = lax.dot_general(keys, mine, into, preferred_element_type=f32) * scale
        scores = jnp.where(seg_keys[...] == seg_mine[...], scores, -1000000000.0)
        probs = jnp.exp(scores - log_total[pl.ds(2 * j + half, 1), :])
        d_probs = lax.dot_general(values, above, into, preferred_element_type=f32)
        inner = jnp.sum(probs * d_probs, axis=0, keepdims=True)
        d_scores = (probs * (d_probs - inner)).astype(b16)
        d_keys = jnp.dot(d_scores, mine, preferred_element_type=f32) * scale
        d_values = jnp.dot(probs.astype(b16), above, preferred_element_type=f32)
        d_pairs[0, j, :, side] = d_keys.astype(b16)
        d_pairs[1, j, :, side] = d_values.astype(b16)
        turned = keys.astype(f32).T.astype(b16)
        d_query[side] = jnp.dot(turned, d_scores, preferred_element_type=f32) * scale
        if half:
            d_qkv[:, lanes] = d_query[...].T.astype(b16)

    def to_core():
        return pltpu.make_async_remote_copy(
            src_ref=d_pairs.at[:, :, pl.ds(2 * cells, 2 * cells)], dst_ref=by_core,
            send_sem=send.at[0], recv_sem=recv.at[0], device_id={"c": 1 - c}, device_id_type=MESH,
        )

    def to_y():
        return pltpu.make_async_remote_copy(
            src_ref=d_pairs.at[:, :, pl.ds(cells, cells)], dst_ref=by_y,
            send_sem=send.at[1], recv_sem=recv.at[1], device_id={"y": 1 - y}, device_id_type=MESH,
        )

    def beside(i, right, odd):
        @pl.when(i < 2 * n_pairs)
        def _():
            backward(i // 2, odd)

    def fetch_weight():
        return pltpu.make_async_copy(weight, weight_buf, local.at[0])

    def keep_turned():
        return pltpu.make_async_copy(turned, turned_own, local.at[1])

    def send_turned():
        return pltpu.make_async_remote_copy(
            src_ref=turned, dst_ref=turned_other,
            send_sem=send.at[2], recv_sem=recv.at[2], device_id={"c": 1 - c}, device_id_type=MESH,
        )

    def to_other_left():
        return pltpu.make_async_remote_copy(
            src_ref=send_left, dst_ref=got_left,
            send_sem=send.at[3], recv_sem=recv.at[3], device_id={"c": 1 - c}, device_id_type=MESH,
        )

    def share():
        to_core().wait_recv()

        def add(j, carry):
            for kind in (0, 1):
                total = d_pairs[kind, j, : 2 * cells].astype(f32) + by_core[kind, j].astype(f32)
                d_pairs[kind, j, : 2 * cells] = total.astype(b16)
            return carry

        lax.fori_loop(0, n_pairs, add, 0)
        to_y().start()

    def collect():
        to_y().wait_recv()

        def add(j, carry):
            for kind in (0, 1):
                lanes = pl.ds(pl.multiple_of((kind + 1) * width + j * 128, 128), 128)
                total = d_pairs[kind, j, :cells].astype(f32) + by_y[kind, j].astype(f32)
                d_qkv[:, lanes] = total.astype(b16)
            return carry

        lax.fori_loop(0, n_pairs, add, 0)

    def turn():
        def tile(k, carry):
            turned[chunk_of(k)] = d_qkv[:, chunk_of(k)].astype(f32).T.astype(b16)
            return carry

        lax.fori_loop(0, 3 * width // CHUNK, tile, 0)
        keep_turned().start()
        send_turned().start()

    def project():
        fetch_weight().wait()
        for k in range(4):
            rows = weight_buf[k // 2, k % 2].reshape(width // 4, -1)[:, : 3 * width]
            da1[:, k * width // 4 : (k + 1) * width // 4] = lax.dot_general(
                d_qkv[...], rows, into, preferred_element_type=f32
            )

    def norm():
        value, above = h0[...], da1[...]
        centred = value - jnp.mean(value, axis=1, keepdims=True)
        inverse = lax.rsqrt(jnp.mean(centred * centred, axis=1, keepdims=True) + eps)
        normed = centred * inverse
        vector_rows[...] = jnp.zeros_like(vector_rows)
        vector_rows[0:1] = jnp.sum(above * normed, axis=0, keepdims=True)
        vector_rows[1:2] = jnp.sum(above, axis=0, keepdims=True)
        vector_rows[2:4] = vectors[1:3]
        above = above * vectors[0:1]
        inner = jnp.mean(above * normed, axis=1, keepdims=True)
        below = inverse * (above - jnp.mean(above, axis=1, keepdims=True) - normed * inner)
        dh0b[...] = (dh1[...] + below).astype(b16)

    def halves():
        for kind, source in enumerate((vector_rows, dh0b)):
            for part in range(8):
                lanes = pl.ds(pl.multiple_of(eighth_of(part) * (width // 8), width // 8), width // 8)
                block = source[:, lanes].astype(f32).T.astype(b16)
                rows = slice(part % 4 * (width // 8), (part % 4 + 1) * (width // 8))
                if part < 4:
                    lefts_next[1 + kind, rows, :cells] = block
                else:
                    send_left[kind, rows] = block
        to_other_left().start()

    def after(p):
        plan = {0: lambda: fetch_weight().start(), n_pairs: lambda: to_core().start(), n_pairs + 2: share}
        plan.update(zip(range(n_chunk_pairs - 2, n_chunk_pairs + 3), (collect, turn, project, norm, halves)))
        for when, action in plan.items():

            @pl.when(p == when)
            def _(action=action):
                action()

    n_chunk_pairs = (sum(sections) + 1) // 2
    scatter_kernel(
        n_h, sections, periods, left_starts, lefts, rights, None, out, scratch, [{"c": 1 - c}],
        lambda section, k: None, beside, after,
    )
    lefts_next[0] = left_one[...]
    to_other_left().wait_recv()
    for kind in (0, 1):
        lefts_next[1 + kind, :, cells:] = got_left[kind]
    if n_h > 1:
        order_columns(grad_up, out, 0, n_h)
        order_columns(grad_down, out, 4 * width // CHUNK, n_h)
        order_columns(grad_out, out, 8 * width // CHUNK, n_h)
    keep_turned().wait()
    send_turned().wait()
    for copy in (to_core(), to_y(), to_other_left()):
        copy.wait_send()


def scatter_call(kernel, lefts, rights, operands, more_operands, out_shapes, out_specs, scratch, collective_id):
    periods = [other.shape[0] // CHUNK for _, other, _ in rights]
    sections = [period * times for period, (*_, times) in zip(periods, rights)]
    n, cells = sum(sections), rights[0][0].shape[1]
    w = lefts.shape[1] // 4
    n_h = lax.axis_size("h")
    rows = w // n_h
    inner_h = n_h if rows % 16 == 0 else 1
    dma, bf16, f32 = pltpu.SemaphoreType.DMA, jnp.bfloat16, jnp.float32
    vmem, hbm = pl.BlockSpec(memory_space=pltpu.VMEM), pl.BlockSpec(memory_space=pl.ANY)
    others = max(inner_h - 1, 1)
    part_shape = jax.ShapeDtypeStruct((n, rows, CHUNK), f32)
    if inner_h == 1:
        part_shape = jax.ShapeDtypeStruct((n, w, CHUNK), bf16)
    part, *more = pl.pallas_call(
        functools.partial(kernel, inner_h, sections, periods),
        out_shape=[part_shape] + out_shapes,
        in_specs=[vmem] * (1 + len(operands)) + [hbm] * (2 * len(rights) + len(more_operands)),
        out_specs=[vmem] + out_specs,
        scratch_shapes=scratch
        + [
            pltpu.VMEM((3, CHUNK, 2 * cells), bf16),
            pltpu.VMEM((RING, 2 * w, CHUNK), f32),
            pltpu.VMEM((RING, 2 * w, CHUNK), bf16),
            pltpu.VMEM((n, 2 * w, CHUNK), bf16),
            pltpu.VMEM((RING, w, CHUNK), bf16),
            pltpu.VMEM((n, w, CHUNK), bf16),
            pltpu.VMEM((RING, w, CHUNK), bf16),
            pltpu.VMEM((n, others, w // inner_h, CHUNK), bf16),
            dma((3, 2)),
            dma((RING,)),
            dma((n,)),
            dma((RING,)),
            dma((n,)),
            dma((RING, others)),
            dma((n, others)),
        ],
        compiler_params=pltpu.CompilerParams(
            collective_id=collective_id, has_side_effects=True, vmem_limit_bytes=60 * 2**20
        ),
    )(lefts, *operands, *(half for pair in rights for half in pair[:2]), *more_operands)
    if inner_h == 1:
        part = lax.psum_scatter(part, "h", scatter_dimension=1, tiled=True).astype(f32)
    return part, *more


def scatter_product(lefts, left_starts, rights, vector, weights, product_type, with_sum, collective_id):
    (cells, features), columns = vector.shape, rights[-1][1].shape[0]
    dma = pltpu.SemaphoreType.DMA
    vmem, hbm = pl.BlockSpec(memory_space=pltpu.VMEM), pl.BlockSpec(memory_space=pl.ANY)

    def kernel(n_h, sections, periods, *refs):
        product_kernel(n_h, sections, periods, left_starts, len(weights) - with_sum, with_sum, *refs)

    return scatter_call(
        kernel,
        lefts,
        rights,
        [vector],
        weights,
        [jax.ShapeDtypeStruct((columns, cells), product_type)]
        + [jax.ShapeDtypeStruct((features, cells), jnp.float32)] * with_sum,
        [hbm] + [vmem] * with_sum,
        [
            pltpu.VMEM((3, features, CHUNK), jnp.bfloat16),
            pltpu.VMEM((2, CHUNK, cells), product_type),
            dma((3, len(weights))),
            dma((2,)),
        ],
        collective_id,
    )


def scatter_attention(lefts, left_starts, rights, operands, weight, scale, collective_id):
    cells, width = operands[0].shape
    own_rows = width // (8 * lax.axis_size("h"))
    bf16, f32, dma = jnp.bfloat16, jnp.float32, pltpu.SemaphoreType.DMA
    vmem, hbm = pl.BlockSpec(memory_space=pltpu.VMEM), pl.BlockSpec(memory_space=pl.ANY)

    def kernel(n_h, sections, periods, *refs):
        attention_kernel(n_h, sections, periods, left_starts, scale, *refs)

    return scatter_call(
        kernel,
        lefts,
        rights,
        operands,
        [weight],
        [
            jax.ShapeDtypeStruct((3 * width, cells), bf16),
            jax.ShapeDtypeStruct((3 * width, cells), bf16),
            jax.ShapeDtypeStruct((3,) + lefts.shape[1:], bf16),
            jax.ShapeDtypeStruct((cells, width), bf16),
            jax.ShapeDtypeStruct((own_rows, 4 * width), f32),
            jax.ShapeDtypeStruct((4 * own_rows, width), f32),
            jax.ShapeDtypeStruct((own_rows, width), f32),
        ],
        [hbm, hbm, vmem, vmem, vmem, vmem, vmem],
        [
            pltpu.VMEM((cells, 3 * width), bf16),
            pltpu.VMEM((2, width // 128, 4 * cells, 128), bf16),
            pltpu.VMEM((2, width // 128, 2 * cells, 128), bf16),
            pltpu.VMEM((2, width // 128, cells, 128), bf16),
            pltpu.VMEM((128, cells), f32),
            pltpu.VMEM(weight.shape, bf16),
            pltpu.VMEM((3 * width, cells), bf16),
            pltpu.VMEM((cells, width), f32),
            pltpu.VMEM((cells, width), f32),
            pltpu.VMEM((2, width // 2, cells), bf16),
            pltpu.VMEM((2, width // 2, cells), bf16),
            dma((4,)),
            dma((4,)),
            dma((2,)),
        ],
        collective_id,
    )


def both_cores(right, times=1):
    return right, swap(right, "c"), times


def columns_of(chunks):
    return chunks.transpose(1, 0, 2).reshape(chunks.shape[1], -1)


def on_device(
    counts,
    library,
    coords,
    lengths,
    cotangent,
    w_enc,
    w_qkv,
    w_out,
    gain_one,
    shift_one,
    w_up,
    w_down,
    gain_two,
    shift_two,
    w_dec,
):
    rows = counts.shape[0]
    width = w_qkv.shape[1] // 3
    att_scale = (width // HEADS) ** (-0.5)
    group_size = 4
    slots = rows * group_size
    scale = 10000.0 / library
    genes = counts.shape[1]
    padded = -(-genes // CHUNK) * CHUNK
    counts_f = counts.astype(jnp.float32)
    pe = by_owner(positions(coords, width), 1)
    ends = jnp.cumsum(lengths[0])
    group = [
        (lax.axis_index("y") ^ by_y) * 2 + (lax.axis_index("c") ^ by_c)
        for by_c in range(2)
        for by_y in range(2)
    ]
    place = jnp.concatenate([at * rows + jnp.arange(rows, dtype=jnp.int32) for at in group])
    seg_all = jnp.sum((place[:, None] >= ends[None, :]).astype(jnp.int32), axis=1)
    vectors = jnp.stack([gain_one, shift_one, gain_two, shift_two], axis=1)
    vectors = jnp.pad(vectors, ((0, 0), (0, 124)))
    pad = ((0, 0), (0, padded - genes))
    quarter = padded // CHUNK // 4 * CHUNK
    gene_cuts = [0, quarter, 2 * quarter, 3 * quarter, padded]
    shards = [
        jnp.pad(w_enc.T, pad),
        jnp.concatenate([w_qkv, vectors], axis=1),
        by_owner(w_out, 1),
        by_owner(w_up, 1),
        by_owner(w_down, 1),
        jnp.pad(w_dec.T, pad),
    ]
    cuts = [gene_cuts, [0, width // 2 * 3, 3 * width + 128], [0, width]]
    cuts += [[0, 2 * width, 4 * width], [0, width // 2, width]]
    cuts += [gene_cuts]
    order = [(0, 0), (0, 1), (0, 2), (0, 3), (1, 0), (1, 1), (2, 0), (3, 0), (3, 1), (4, 0), (4, 1)]
    order += [(5, 0), (5, 1), (5, 2), (5, 3)]
    (gathered, xb, xb_other, cot_other, kv_pairs, lefts, left_one, left_last, h0, query, log_total, h1, slope, _,
     hb) = gather_all(
        shards, cuts, order, counts.T, cotangent.T, scale[None, :], pe.T, seg_all, att_scale, 0
    )
    enc_all, qkv_all, out_all, up_all, down_all, dec_all = (
        w.reshape(-1, w.shape[-1]) for w in gathered
    )
    vectors = qkv_all[:, 3 * width :].astype(jnp.float32).T
    g1f, b1f, g2f, b2f = vectors[0], vectors[1], vectors[2], vectors[3]
    grad_dec, logits, dh2 = scatter_product(
        left_last, [0], [(cotangent.T, cot_other, 1)], hb, [dec_all, gene_tail(cotangent.T)], jnp.bfloat16, True, 1
    )
    own_rows = grad_dec.shape[1]
    grad_dec = columns_of(grad_dec)[:, :genes].T
    logits = logits[:genes].T
    dfb_turned = dh2.astype(jnp.bfloat16)
    dh2 = dh2.T
    dfb = dfb_turned.T
    d_act = contract_cols(dfb, down_all)
    d_hidden = (d_act * slope.T).astype(jnp.bfloat16)
    da2 = contract_cols(d_hidden, up_all)
    norm_pull = jax.vjp(layer_norm, h1, g2f, b2f)[1]
    dh1_norm, grad_gain_two, grad_shift_two = norm_pull(da2)
    dh1 = dh2 + dh1_norm
    dab = dh1.astype(jnp.bfloat16)
    d_attended = contract_cols(dab, out_all).astype(jnp.bfloat16)
    d_attended = from_owner(d_attended, 1)
    pieces = (4 * width,) + (width,) * 4
    rights = [both_cores(d_hidden.T), both_cores(dfb_turned, 4), both_cores(dab.T)]
    operands = [query, kv_pairs, d_attended, log_total, seg_all[:, None], seg_all[None, :rows], h0, dh1]
    operands += [jnp.pad(jnp.stack([g1f, grad_gain_two, grad_shift_two]), ((0, 5), (0, 0))), left_one[0]]
    grads, d_qkv, d_qkv_other, lefts, dh0b, *ordered = scatter_attention(
        lefts,
        [sum(pieces[:k]) // CHUNK for k in range(len(pieces) + 1)],
        rights,
        operands,
        gathered[1],
        att_scale,
        2,
    )
    if own_rows % 16 == 0:
        grad_up, grad_down, grad_out = ordered
    else:
        ends = [0]
        for columns in (4 * width, 4 * width, width):
            ends.append(ends[-1] + columns // CHUNK)
        grad_up, grad_down, grad_out = (grads[low:high] for low, high in zip(ends, ends[1:]))
        n_h = lax.axis_size("h")
        by_half = (2, 2, 2, 2, own_rows, n_h // 2, -1)
        grad_up = grad_up.reshape(by_half).transpose(4, 3, 5, 1, 2, 0, 6).reshape(own_rows, -1)
        by_pair = (-1, 2, 2, own_rows, 2, n_h, width // (8 * n_h))
        grad_out, grad_down = (
            g.reshape(by_pair).transpose(0, 3, 5, 2, 4, 1, 6).reshape(-1, width) for g in (grad_out, grad_down)
        )
    unit = jnp.eye(rows, dtype=jnp.bfloat16)
    grads, d_xb = scatter_product(
        lefts,
        [0, 3 * width // CHUNK, (3 * width + rows) // CHUNK],
        [(d_qkv, d_qkv_other, 1), (unit, unit, 1), (xb, xb_other, 1)],
        dh0b,
        [enc_all],
        jnp.float32,
        False,
        3,
    )
    ends = [0]
    for columns in (3 * width, rows):
        ends.append(ends[-1] + columns // CHUNK)
    grad_qkv, grad_vectors, grad_enc = (
        grads[low:high] for low, high in zip(ends, ends[1:] + [grads.shape[0]])
    )
    grad_qkv, grad_enc = columns_of(grad_qkv), columns_of(grad_enc)
    grad_gain_one, grad_shift_one, grad_gain_two, grad_shift_two = (
        grad_vectors[0, :, k] for k in range(4)
    )
    grad_enc = grad_enc[:, :genes].T
    d_xb = d_xb[:genes].T
    counts_grad = d_xb * scale[:, None] / (1.0 + counts_f * scale[:, None])
    return (
        logits,
        counts_grad,
        grad_enc,
        grad_qkv,
        grad_out,
        grad_gain_one,
        grad_shift_one,
        grad_up,
        grad_down,
        grad_gain_two,
        grad_shift_two,
        grad_dec,
    )


ALL = ("h", "x", "y", "c")


def solution(mesh):
    n_dp, n_fsdp = mesh.shape["dp"], mesh.shape["fsdp"]
    mesh = Mesh(mesh.devices.reshape((n_dp // 2, 2, 2, n_fsdp // 2)), ALL)
    placed = (
        P(ALL, None),
        P(ALL),
        P(None, ALL),
        P(("h", "x"), None),
        P(ALL, None),
        P(None, ALL),
        P(ALL, None),
        P(ALL, None),
        P(ALL),
        P(ALL),
        P(ALL, None),
        P(ALL, None),
        P(ALL),
        P(ALL),
        P(None, ALL),
    )
    return jax.shard_map(
        on_device,
        mesh=mesh,
        in_specs=placed,
        out_specs=(
            P(ALL, None),
            P(ALL, None),
            P(None, ALL),
            P(ALL, None),
            P(ALL, None),
            P(ALL),
            P(ALL),
            P(ALL, None),
            P(ALL, None),
            P(ALL),
            P(ALL),
            P(None, ALL),
        ),
        check_vma=False,
    )
```

```python
import functools
import math

import jax
import jax.numpy as jnp
from jax import lax
from jax.experimental import pallas as pl
from jax.experimental.pallas import tpu as pltpu
from jax.sharding import Mesh
from jax.sharding import PartitionSpec as P

HEADS = 16
MESH = pl.DeviceIdType.MESH
RING = 8
CHUNK = 256


eps = 1e-05


def layer_norm(value, gain, shift):
    mean = jnp.mean(value, axis=1, keepdims=True)
    centred = value - mean
    variance = jnp.mean(centred * centred, axis=1, keepdims=True)
    return centred * lax.rsqrt(variance + eps) * gain + shift


def positions(coords, width):
    quarter = width // 4
    freqs = 0.05 * jnp.exp(-jnp.arange(quarter, dtype=jnp.float32) * (math.log(10000.0) / quarter))
    along_x = coords[0].astype(jnp.float32)[:, None] * freqs[None, :]
    along_y = coords[1].astype(jnp.float32)[:, None] * freqs[None, :]
    return jnp.concatenate(
        [jnp.sin(along_x), jnp.cos(along_x), jnp.sin(along_y), jnp.cos(along_y)], axis=1
    )


def contract_cols(left, right):
    return lax.dot_general(
        left, right, (((1,), (1,)), ((), ())), preferred_element_type=jnp.float32
    )


def swap(value, axis):
    return lax.ppermute(value, axis, [(0, 1), (1, 0)])


def by_owner(value, axis):
    n_h = lax.axis_size("h")
    at = value.shape
    block = at[axis] // (8 * n_h)
    split = value.reshape(at[:axis] + (n_h, 2, 2, 2, block) + at[axis + 1 :])
    order = list(range(axis)) + [axis + 3, axis + 1, axis + 2, axis, axis + 4]
    order += list(range(axis + 5, split.ndim))
    return split.transpose(order).reshape(at)


def from_owner(value, axis):
    n_h = lax.axis_size("h")
    at = value.shape
    block = at[axis] // (8 * n_h)
    split = value.reshape(at[:axis] + (2, 2, 2, n_h, block) + at[axis + 1 :])
    order = list(range(axis)) + [axis + 3, axis + 1, axis + 2, axis, axis + 4]
    order += list(range(axis + 5, split.ndim))
    return split.transpose(order).reshape(at)


def greet(peers):
    barrier = pltpu.get_barrier_semaphore()
    for peer in peers:
        pl.semaphore_signal(barrier, inc=1, device_id=peer, device_id_type=MESH)
    pl.semaphore_wait(barrier, len(peers))


def gather_kernel(n_h, jobs, n_full, shards, wholes, sems, between):
    own_sem, h_send, h_recv, send, recv = sems
    h, x, y, c = (lax.axis_index(name) for name in ("h", "x", "y", "c"))
    h = 0 if n_h == 1 else h
    to_x, to_y, to_c = {"x": 1 - x}, {"y": 1 - y}, {"c": 1 - c}
    greet([{"h": lax.rem(h + d, n_h)} for d in range(1, n_h)] + [to_x, to_y, to_c])

    def rows_of(job, at):
        array, low, high, _ = job
        rows = shards[array].shape[0]
        place = (pl.ds(at * rows, rows), pl.ds(low, high - low))
        return wholes[array].at[(c, x, y, *place) if array < n_full else place]

    def h_copy(j, d):
        array, low, high, _ = jobs[j]
        return pltpu.make_async_remote_copy(
            src_ref=shards[array].at[:, pl.ds(low, high - low)],
            dst_ref=rows_of(jobs[j], h),
            send_sem=h_send.at[j, d - 1],
            recv_sem=h_recv.at[j, d - 1],
            device_id={"h": lax.rem(h + d, n_h)},
            device_id_type=MESH,
        )

    def own_copy(j):
        array, low, high, _ = jobs[j]
        return pltpu.make_async_copy(
            shards[array].at[:, pl.ds(low, high - low)], rows_of(jobs[j], h), own_sem.at[j]
        )

    def block_copy(j, k, block, to, columns):
        view = wholes[jobs[j][0]].at[(*block, slice(None), pl.ds(columns[0], columns[1] - columns[0]))]
        return pltpu.make_async_remote_copy(
            src_ref=view,
            dst_ref=view,
            send_sem=send.at[j, k],
            recv_sem=recv.at[j, k],
            device_id=to,
            device_id_type=MESH,
        )

    own, by_x, by_y, far = (c, x, y), (c, 1 - x, y), (c, x, 1 - y), (c, 1 - x, 1 - y)

    def copy(j, k):
        _, low, high, middle = jobs[j]
        block, to, columns = [
            (own, to_x, (low, high)),
            (own, to_y, (low, high)),
            (own, to_c, (low, high)),
            (by_x, to_y, (low, middle)),
            (by_y, to_x, (middle, high)),
            (by_x, to_c, (low, high)),
            (by_y, to_c, (low, high)),
            (far, to_c, (low, high)),
        ][k]
        return block_copy(j, k, block, to, columns)

    def start_h(j):
        own_copy(j).start()
        for d in range(1, n_h):
            h_copy(j, d).start()

    whole = set()

    def landed(j):
        if j not in whole:
            whole.add(j)
            for k in (2, 5, 6, 7):
                copy(j, k).wait_recv()

    n = sum(array < n_full for array, *_ in jobs)
    ahead = 2
    for j in range(ahead):
        start_h(j)
    for step in range(n + 2):
        if step < n:
            own_copy(step).wait()
            for d in range(1, n_h):
                h_copy(step, d).wait_recv()
            for k in (0, 1, 2):
                copy(step, k).start()
            if step + ahead < len(jobs):
                start_h(step + ahead)
        if 0 <= step - 1 < n:
            for k in (0, 1):
                copy(step - 1, k).wait_recv()
            for k in (3, 4, 5, 6):
                copy(step - 1, k).start()
        if 0 <= step - 2 < n:
            for k in (3, 4):
                copy(step - 2, k).wait_recv()
            copy(step - 2, 7).start()
        between(step, landed)
    for j in range(n, len(jobs)):
        own_copy(j).wait()
        for d in range(1, n_h):
            h_copy(j, d).wait_recv()
    for j in range(len(jobs)):
        for d in range(1, n_h):
            h_copy(j, d).wait_send()
    for j in range(n):
        for k in range(8):
            copy(j, k).wait_send()
        landed(j)


def gene_tail(counts):
    tail = counts[counts.shape[0] // CHUNK * CHUNK :]
    return jnp.pad(tail, ((0, CHUNK - tail.shape[0]), (0, 0)))


def eighth_of(part):
    c, x, y = (lax.axis_index(name) for name in ("c", "x", "y"))
    return lax.rem(c + part // 4, 2) * 4 + lax.rem(x + part // 2 % 2, 2) * 2 + lax.rem(y + part % 2, 2)


def front_kernel(n_h, jobs, n_arrays, n_full, owners, scale_s, *refs):
    shards = refs[:n_arrays]
    counts, cot, tail, cot_tail, scale, pe, seg_keys, seg_mine = refs[n_arrays : n_arrays + 8]
    rest = refs[n_arrays + 8 :]
    wholes = rest[:n_arrays]
    (xb, xb_other, cot_other, pairs, lefts, left_one, left_last, h0, query, log_total, h1, slope,
     act, hb) = rest[n_arrays : n_arrays + 14]
    (a1, a2, plain, attended, turned, gains, perm, count_buf, enc_buf, xb_buf, total, qkv_buf, mine, pairs_buf, out_buf,
     up_buf, down_buf, own_left, send_left, count_sem, enc_sem, xb_sem, fetch_sem, kv_sem, kv_send, kv_recv,
     cot_send, cot_recv, left_sem, left_send, left_recv, *sems) = rest[n_arrays + 14 :]
    y, c = lax.axis_index("y"), lax.axis_index("c")
    to_core = {"c": 1 - c}
    f32, b16 = jnp.float32, jnp.bfloat16
    cells, width = h0.shape
    slots, head = 4 * cells, 64
    n_pairs = width // 128
    n_chunks = xb.shape[0] // CHUNK
    by_chunk = lambda k: pl.ds(pl.multiple_of(k * CHUNK, CHUNK), CHUNK)

    def loads(k, last):
        slot = lax.rem(k, 2)
        source = tail if last else counts.at[by_chunk(k)]
        return (
            pltpu.make_async_copy(source, count_buf.at[slot], count_sem.at[slot]),
            pltpu.make_async_copy(
                wholes[0].at[:, :, :, :, by_chunk(k)], enc_buf.at[slot], enc_sem.at[slot]
            ),
        )

    def store(k):
        slot = lax.rem(k, 2)
        return pltpu.make_async_copy(xb_buf.at[slot], xb.at[by_chunk(k)], xb_sem.at[slot])

    def encode(k, first, last, low, high):
        slot = lax.rem(k, 2)
        for copy in loads(k, last):
            copy.wait()
        if not last:

            @pl.when(k + 1 < (high - 1 if high == n_chunks else high))
            def _():
                for copy in loads(k + 1, False):
                    copy.start()

        @pl.when(k >= low + 2)
        def _():
            store(k - 2).wait()

        value = jnp.log1p(count_buf[slot].astype(f32) * scale[...]).astype(b16)
        xb_buf[slot] = value
        store(k).start()
        term = jnp.dot(enc_buf[slot].reshape(width, CHUNK), value, preferred_element_type=f32)
        if first:

            @pl.when(k == 0)
            def _():
                total[...] = pe[...] + term

            @pl.when(k > 0)
            def _():
                total[...] += term

        else:
            total[...] += term

    def encode_job(low, high):
        low, high = low // CHUNK, high // CHUNK
        stop = high - 1 if high == n_chunks else high
        for copy in loads(jnp.int32(low), False):
            copy.start()

        def body(k, carry):
            encode(k, low == 0, False, low, high)
            return carry

        lax.fori_loop(low, stop, body, 0)
        if stop < high:
            for copy in loads(jnp.int32(stop), True):
                copy.start()
            encode(jnp.int32(stop), False, True, low, high)
        for k in range(max(low, high - 2), high):
            store(jnp.int32(k)).wait()

    def fetch(k):
        buffer = (qkv_buf, out_buf, up_buf, down_buf)[k]
        return pltpu.make_async_copy(wholes[1 + k], buffer, fetch_sem.at[k])

    def project():
        fetch(0).wait()
        vectors = qkv_buf[:, :, :, :, 3 * width :].reshape(width, 128).astype(f32)
        value = total[...]
        centred = value - jnp.mean(value, axis=0, keepdims=True)
        variance = jnp.mean(centred * centred, axis=0, keepdims=True)
        normed = centred * lax.rsqrt(variance + eps) * vectors[:, 0:1] + vectors[:, 1:2]
        gains[...] = vectors.T[0:8]
        h0[...] = value.T
        a1[...] = normed.T.astype(b16)

        def tile(k):
            weight = qkv_buf[:, :, :, :, by_chunk(k)].reshape(width, CHUNK)
            return jnp.dot(a1[...], weight, preferred_element_type=f32).astype(b16)

        def keys(k, carry):
            mine[:, by_chunk(k)] = tile(k + width // CHUNK)
            return carry

        lax.fori_loop(0, 2 * width // CHUNK, keys, 0)
        kv_own().start()
        kv_copy(0).start()

        def queries(k, carry):
            query[:, by_chunk(k)] = tile(k)
            return carry

        lax.fori_loop(0, width // CHUNK, queries, 0)

    def kv_own():
        return pltpu.make_async_copy(mine, pairs.at[0, 0], kv_sem.at[0])

    def kv_copy(k):
        return pltpu.make_async_remote_copy(
            src_ref=(mine, pairs.at[0])[k],
            dst_ref=(pairs.at[0, 1], pairs.at[1])[k],
            send_sem=kv_send.at[k],
            recv_sem=kv_recv.at[k],
            device_id=({"y": 1 - y}, {"c": 1 - c})[k],
            device_id_type=MESH,
        )

    def swap_cot(k):
        source = (cot.at[pl.ds(0, (n_chunks - 1) * CHUNK)], cot_tail)[k]
        place = pl.ds((n_chunks - 1) * CHUNK * k, ((n_chunks - 1) * CHUNK, CHUNK)[k])
        return pltpu.make_async_remote_copy(
            src_ref=source, dst_ref=cot_other.at[place], send_sem=cot_send.at[k], recv_sem=cot_recv.at[k],
            device_id=to_core, device_id_type=MESH,
        )

    def swap_xb():
        return pltpu.make_async_remote_copy(
            src_ref=xb, dst_ref=xb_other, send_sem=cot_send.at[2], recv_sem=cot_recv.at[2],
            device_id=to_core, device_id_type=MESH,
        )

    def make_perm():
        place = lax.broadcasted_iota(jnp.int32, (8, width), 1)
        size = width // 8 // owners
        within, at = lax.rem(place, size), lax.div(place, size)
        at_h, at = lax.rem(at, owners), lax.div(at, owners)
        wanted = at_h * 8 + lax.rem(lax.div(at, 2), 2) * 4 + lax.rem(at, 2) * 2 + lax.div(at, 4)
        wanted = (wanted * size + within)[0:1]
        for k in range(width // CHUNK):
            row = lax.broadcasted_iota(jnp.int32, (CHUNK, width), 0) + k * CHUNK
            perm[k * CHUNK : (k + 1) * CHUNK] = jnp.where(row == wanted, 1.0, 0.0).astype(b16)

    def fetch_pairs():
        return pltpu.make_async_copy(pairs, pairs_buf, kv_sem.at[1])

    def attend(j, carry):
        lanes = by_lanes(j)
        keys = pairs_buf[:, :, :, lanes].reshape(slots, 128)
        values = pairs_buf[:, :, :, by_lanes(n_pairs + j)].reshape(slots, 128).astype(f32).T.astype(b16)
        for half in (0, 1):
            side = slice(half * head, (half + 1) * head)
            scores = lax.dot_general(
                keys[:, side], query[:, lanes][:, side], (((1,), (1,)), ((), ())), preferred_element_type=f32
            )
            scores = jnp.where(seg_keys[...] == seg_mine[...], scores * scale_s, -1000000000.0)
            top = jnp.max(scores, axis=0, keepdims=True)
            expo = jnp.exp(scores - top)
            whole = jnp.sum(expo, axis=0, keepdims=True)
            log_total[pl.ds(2 * j + half, 1), :] = top + jnp.log(whole)
            probs = (expo * (1.0 / whole)).astype(b16)
            turned[side] = jnp.dot(values[side], probs, preferred_element_type=f32)
        plain[:, lanes] = turned[...].T.astype(b16)
        return carry

    def by_lanes(j):
        return pl.ds(pl.multiple_of(j * 128, 128), 128)

    def leave_attention():
        attended[...] = jnp.dot(plain[...], perm[...], preferred_element_type=f32).astype(b16)
        fetch(1).wait()
        for k in range(width // CHUNK):
            columns = slice(k * CHUNK, (k + 1) * CHUNK)
            weight = out_buf[:, :, :, :, columns].reshape(width, CHUNK)
            h1[:, columns] = h0[:, columns] + jnp.dot(attended[...], weight, preferred_element_type=f32)
        value = h1[...]
        centred = value - jnp.mean(value, axis=1, keepdims=True)
        variance = jnp.mean(centred * centred, axis=1, keepdims=True)
        a2[...] = (centred * lax.rsqrt(variance + eps) * gains[2:3] + gains[3:4]).astype(b16)

    def widen(k, carry):
        weight = up_buf[:, :, :, :, by_chunk(k)].reshape(width, CHUNK)
        value = jnp.dot(a2[...], weight, preferred_element_type=f32)
        share = 0.5 * (1.0 + lax.erf(value * (0.5**0.5)))
        act[:, by_chunk(k)] = (value * share).astype(b16)
        steep = share + value * jnp.exp(-0.5 * value * value) * (2.0 * math.pi) ** -0.5
        slope[by_chunk(k)] = steep.T
        return carry

    def narrow(k, carry):
        weight = down_buf[:, :, :, :, by_chunk(k)].reshape(4 * width, CHUNK)
        value = h1[:, by_chunk(k)] + jnp.dot(act[...], weight, preferred_element_type=f32)
        hb[:, by_chunk(k)] = value.astype(b16)
        return carry

    def left_copies(k):
        target = (lefts.at[pl.ds(0, 6)], left_one, left_last)[k]
        source = pl.ds((0, 6, 7)[k], (6, 1, 1)[k])
        return (
            pltpu.make_async_copy(own_left.at[source], target.at[:, :, pl.ds(0, cells)], left_sem.at[k]),
            pltpu.make_async_remote_copy(
                src_ref=send_left.at[source], dst_ref=target.at[:, :, pl.ds(cells, cells)],
                send_sem=left_send.at[k], recv_sem=left_recv.at[k], device_id=to_core, device_id_type=MESH,
            ),
        )

    def make_left(source, k):
        size = source.shape[1] // 8
        pieces = size // (width // 8)
        step = size // owners // pieces
        for part in range(8):
            lanes = pl.ds(pl.multiple_of(eighth_of(part) * size, size), size)
            block = source[:, lanes].astype(f32).T.astype(b16)
            target = own_left if part < 4 else send_left
            base = part % 4 * (width // 8)
            if pieces == 1:
                target[k, base : base + size] = block
                continue
            for piece in range(pieces):
                for at in range(owners):
                    rows = block[(at * pieces + piece) * step : (at * pieces + piece + 1) * step]
                    target[k + piece, base + at * step : base + (at + 1) * step] = rows

    arrays = [array for array, *_ in jobs]
    last_of = [max(j for j, array in enumerate(arrays) if array == k) for k in range(5)]
    enc_jobs = [j for j, array in enumerate(arrays) if array == 0]
    at = last_of[1] + 3

    def between(step, landed):
        if step == 0:
            for k in (0, 1):
                swap_cot(k).start()
        if step == 1:
            make_perm()
        if step - 3 in enc_jobs:
            landed(step - 3)
            encode_job(*jobs[step - 3][1:3])
        if step == enc_jobs[-1] + 3:
            swap_xb().start()
        if step == at:
            for j in range(last_of[1] + 1):
                landed(j)
            fetch(0).start()
            project()
        if step == at + 2:
            kv_own().wait()
            kv_copy(0).wait_recv()
            kv_copy(1).start()
            make_left(a1, 6)
            for copy in left_copies(1):
                copy.start()
        if step == at + 3:
            for j in range(last_of[3] + 1):
                landed(j)
            fetch(1).start()
            fetch(2).start()
            kv_copy(1).wait_recv()
            fetch_pairs().start()
            fetch_pairs().wait()
            lax.fori_loop(0, n_pairs // 2, attend, 0)
        if step == at + 4:
            lax.fori_loop(n_pairs // 2, n_pairs, attend, 0)
        if step == at + 5:
            for j in range(last_of[4] + 1):
                landed(j)
            fetch(3).start()
            leave_attention()
            fetch(2).wait()
            lax.fori_loop(0, 2 * width // CHUNK, widen, 0)
        if step == at + 6:
            lax.fori_loop(2 * width // CHUNK, 4 * width // CHUNK, widen, 0)
        if step == at + 7:
            fetch(3).wait()
            lax.fori_loop(0, width // CHUNK, narrow, 0)
            make_left(hb, 7)
            for copy in left_copies(2):
                copy.start()
        if step == at + 8:
            make_left(a2, 0)
            make_left(act, 1)
            make_left(attended, 5)
            for copy in left_copies(0):
                copy.start()

    gather_kernel(n_h, jobs, n_full, shards, wholes, sems, between)
    kv_copy(0).wait_send()
    kv_copy(1).wait_send()
    for k in (0, 1):
        swap_cot(k).wait()
    swap_xb().wait()
    for k in range(3):
        for copy in left_copies(k):
            copy.wait()


def gather_all(shards, cuts, order, counts, cot, scale, pe, seg, scale_s, collective_id):
    owners = n_h = lax.axis_size("h")
    if any(shard.shape[0] % 16 for shard in shards):
        shards = [lax.all_gather(s, "h", axis=0, tiled=True) for s in shards]
        n_h = 1
    jobs = []
    for array, piece in order:
        low, high = cuts[array][piece], cuts[array][piece + 1]
        jobs.append((array, low, high, low + (high - low) // (512 if array in (3, 4) else 256) * 128))
    n, others, dma = len(jobs), max(n_h - 1, 1), pltpu.SemaphoreType.DMA
    shapes = [(n_h * s.shape[0], s.shape[1]) for s in shards]
    (genes, cells), width, padded = counts.shape, pe.shape[0], shards[0].shape[1]
    slots, half = seg.shape[0], width // 2
    bf16, f32 = jnp.bfloat16, jnp.float32
    vmem, hbm = pl.BlockSpec(memory_space=pltpu.VMEM), pl.BlockSpec(memory_space=pl.ANY)
    shape = jax.ShapeDtypeStruct
    hbm_out = [shape((padded, cells), bf16)] * 3 + [shape((2, 2, cells, 2 * width), bf16)]
    hbm_out += [shape((k, half, 2 * cells), bf16) for k in (6, 1, 1)]
    vmem_out = [
        shape((cells, width), f32),
        shape((cells, width), bf16),
        shape((width // 64, cells), f32),
        shape((cells, width), f32),
        shape((4 * width, cells), f32),
        shape((cells, 4 * width), bf16),
        shape((cells, width), bf16),
    ]
    eighth = width // 8
    out = pl.pallas_call(
        functools.partial(front_kernel, n_h, jobs, len(shards), len(shards), owners, scale_s),
        out_shape=[shape((2, 2, 2) + k, bf16) for k in shapes] + hbm_out + vmem_out,
        in_specs=[vmem] * len(shards) + [hbm] * 4 + [vmem] * 4,
        out_specs=[hbm] * (len(shards) + len(hbm_out)) + [vmem] * len(vmem_out),
        scratch_shapes=[
            pltpu.VMEM((cells, width), bf16),
            pltpu.VMEM((cells, width), bf16),
            pltpu.VMEM((cells, width), bf16),
            pltpu.VMEM((cells, width), bf16),
            pltpu.VMEM((128, cells), f32),
            pltpu.VMEM((8, width), f32),
            pltpu.VMEM((width, width), bf16),
            pltpu.VMEM((2, CHUNK, cells), bf16),
            pltpu.VMEM((2, 2, 2, 2, eighth, CHUNK), bf16),
            pltpu.VMEM((2, CHUNK, cells), bf16),
            pltpu.VMEM((width, cells), f32),
            pltpu.VMEM((2, 2, 2, eighth, shards[1].shape[1]), bf16),
            pltpu.VMEM((cells, 2 * width), bf16),
            pltpu.VMEM((2, 2, cells, 2 * width), bf16),
            pltpu.VMEM((2, 2, 2, eighth, width), bf16),
            pltpu.VMEM((2, 2, 2, eighth, 4 * width), bf16),
            pltpu.VMEM((2, 2, 2, 4 * eighth, width), bf16),
            pltpu.VMEM((8, half, cells), bf16),
            pltpu.VMEM((8, half, cells), bf16),
            dma((2,)),
            dma((2,)),
            dma((2,)),
            dma((4,)),
            dma((2,)),
            dma((2,)),
            dma((2,)),
            dma((3,)),
            dma((3,)),
            dma((3,)),
            dma((3,)),
            dma((3,)),
            dma((n,)),
            dma((n, others)),
            dma((n, others)),
            dma((n, 8)),
            dma((n, 8)),
        ],
        compiler_params=pltpu.CompilerParams(
            collective_id=collective_id, has_side_effects=True, vmem_limit_bytes=63 * 2**20
        ),
    )(
        *shards, counts, cot, gene_tail(counts), gene_tail(cot), scale, pe, seg[:, None], seg[None, :cells]
    )
    return out[: len(shards)], *out[len(shards) :]


def scatter_kernel(n_h, sections, periods, left_starts, lefts, rights, tail, out, scratch, peers, prefetch, beside, after):
    (right_buf, own, s1, r1, s2, r2, s3, r3, load_sem, send1, recv1, send2, recv2, send3, recv3) = scratch
    h, x, y = (lax.axis_index(name) for name in ("h", "x", "y"))
    to_x, to_y = {"x": 1 - x}, {"y": 1 - y}
    w = s3.shape[1]
    rows = w // n_h
    f32, b16 = jnp.float32, jnp.bfloat16
    n_sections = len(sections)
    starts = [sum(sections[:k]) for k in range(n_sections)]
    n = sum(sections)
    cells = right_buf.shape[2] // 2
    greet([{"h": lax.rem(h + d, n_h)} for d in range(1, n_h)] + [to_x, to_y] + peers)

    def loads(i, section, k, last=False):
        slot = lax.rem(i, 3)
        return [
            pltpu.make_async_copy(
                tail if last and not half else rights[2 * section + half].at[chunk_of(k)],
                right_buf.at[slot, :, pl.ds(half * cells, cells)],
                load_sem.at[slot, half],
            )
            for half in (0, 1)
        ]

    def start_loads(i):
        for section, (start, count) in enumerate(zip(starts, sections)):

            @pl.when((i >= start) & (i < start + count))
            def _(section=section, start=start):
                k = lax.rem(i - start, periods[section])
                ends = [(False, k >= 0)]
                if tail is not None:
                    ends = [(False, k < periods[section] - 1), (True, k == periods[section] - 1)]
                for last, here in ends:

                    @pl.when(here)
                    def _(last=last):
                        for copy in loads(i, section, k, last):
                            copy.start()

                prefetch(section, i - start)

    def hop(i, source, target, send_sem, recv_sem, to):
        slot = lax.rem(i, RING)
        return pltpu.make_async_remote_copy(
            src_ref=source.at[slot], dst_ref=target.at[i], send_sem=send_sem.at[slot],
            recv_sem=recv_sem.at[i], device_id=to, device_id_type=MESH,
        )

    def first(i, odd):
        return hop(i, s1, r1, send1, recv1, to_y if odd else to_x)

    def second(i, odd):
        return hop(i, s2, r2, send2, recv2, to_x if odd else to_y)

    def third(i, d):
        to = lax.rem(h + d, n_h)
        slot = lax.rem(i, RING)
        return pltpu.make_async_remote_copy(
            src_ref=s3.at[slot, pl.ds(to * rows, rows)], dst_ref=r3.at[i, d - 1],
            send_sem=send3.at[slot, d - 1], recv_sem=recv3.at[i, d - 1],
            device_id={"h": to}, device_id_type=MESH,
        )

    def multiply(i, odd):
        slot = lax.rem(i, RING)
        for copy in loads(i, 0, 0):
            copy.wait()
        left = lefts[sum((i + 1024 - start) // 1024 for start in left_starts[1:]) if left_starts[1:] else 0]
        right = right_buf.at[lax.rem(i, 3)]

        @pl.when(i >= RING)
        def _():
            first(i - RING, odd).wait_send()

        part = lax.dot_general(left, right[...], (((1,), (1,)), ((), ())), preferred_element_type=f32)
        own[slot, :w] = part[:w]
        if odd:
            own[slot, w:] = part[2 * w : 3 * w]
            s1[slot, :w] = part[w : 2 * w].astype(b16)
            s1[slot, w:] = part[3 * w :].astype(b16)
        else:
            own[slot, w:] = part[w : 2 * w]
            s1[slot] = part[2 * w :].astype(b16)
        first(i, odd).start()

        beside(i, right, odd)
        start_loads(i + 2)

    def pass_on(i, odd):
        slot = lax.rem(i, RING)
        first(i, odd).wait_recv()

        @pl.when(i >= RING)
        def _():
            second(i - RING, odd).wait_send()

        s2[slot] = (own[slot, w:] + r1[i, w:].astype(f32)).astype(b16)
        second(i, odd).start()

    def keep(i, odd):
        slot = lax.rem(i, RING)
        second(i, odd).wait_recv()
        part = own[slot, :w] + r1[i, :w].astype(f32) + r2[i].astype(f32)
        if n_h == 1:
            out[i] = part.astype(b16)
            return

        @pl.when(i >= RING)
        def _():
            for d in range(1, n_h):
                third(i - RING, d).wait_send()

        s3[slot] = part.astype(b16)
        for d in range(1, n_h):
            third(i, d).start()

    def finish(i, odd):
        if n_h == 1:
            return
        total = s3[lax.rem(i, RING), pl.ds(h * rows, rows)].astype(f32)
        for d in range(1, n_h):
            third(i, d).wait_recv()
            total = total + r3[i, d - 1].astype(f32)
        out[i] = total

    start_loads(jnp.int32(0))
    start_loads(jnp.int32(1))
    pairs = (n + 1) // 2

    def step(p, carry):
        for lag, stage in enumerate((multiply, pass_on, keep, finish)):
            for odd in (0, 1):
                i = 2 * (p - lag) + odd

                @pl.when((i >= 0) & (i < n))
                def _(stage=stage, i=i, odd=odd):
                    stage(i, odd)

        after(p)
        return carry

    lax.fori_loop(0, pairs + 3, step, 0)
    for i in range(max(n - RING, 0), n):
        first(i, i % 2).wait_send()
        second(i, i % 2).wait_send()
        for d in range(1, n_h):
            third(i, d).wait_send()


def chunk_of(k):
    return pl.ds(pl.multiple_of(k * CHUNK, CHUNK), CHUNK)


def product_kernel(n_h, sections, periods, left_starts, n_weights, with_sum, *refs):
    lefts, vector = refs[:2]
    n_rights = 2 * len(sections)
    rights, weights = refs[2 : 2 + n_rights], refs[2 + n_rights : 2 + n_rights + n_weights]
    rest = refs[2 + n_rights + n_weights :]
    tail, rest = (rest[0], rest[1:]) if with_sum else (None, rest)
    out, product = rest[:2]
    total_out, rounded = rest[2:4] if with_sum else (None, None)
    weight_buf, product_buf, weight_sem, product_sem, *scratch = rest[4 if with_sum else 2 :]
    begin, count = sum(sections[:-1]), sections[-1]
    cells = vector.shape[0]

    def weight_loads(k):
        slot = lax.rem(k, 3)
        size = weights[0].shape[0]
        return [
            pltpu.make_async_copy(
                weight.at[:, chunk_of(k)],
                weight_buf.at[slot, pl.ds(part * size, size)],
                weight_sem.at[slot, part],
            )
            for part, weight in enumerate(weights)
        ]

    def product_store(k):
        slot = lax.rem(k, 2)
        return pltpu.make_async_copy(product_buf.at[slot], product.at[chunk_of(k)], product_sem.at[slot])

    def prefetch(section, k):
        if section == len(sections) - 1:
            for copy in weight_loads(k):
                copy.start()

    def multiply(k, right):
        for copy in weight_loads(k):
            copy.wait()
        weight = weight_buf[lax.rem(k, 3)]

        @pl.when(k >= 2)
        def _():
            product_store(k - 2).wait()

        value = jnp.dot(vector[...], weight, preferred_element_type=jnp.float32)
        product_buf[lax.rem(k, 2)] = value.T.astype(product_buf.dtype)
        product_store(k).start()
        if with_sum:
            term = jnp.dot(weight, right[:, :cells], preferred_element_type=jnp.float32)

            @pl.when(k == 0)
            def _():
                total_out[...] = term

            @pl.when(k > 0)
            def _():
                total_out[...] += term

    def beside(i, right, odd):
        if begin == 0:
            multiply(i, right)
        else:

            @pl.when(i >= begin)
            def _():
                multiply(i - begin, right)

    scatter_kernel(
        n_h, sections, periods, left_starts, lefts, rights, tail, out, scratch, [], prefetch, beside, lambda p: None
    )
    if with_sum:
        rounded[...] = total_out[...].astype(rounded.dtype)
    for k in range(max(count - 2, 0), count):
        product_store(k).wait()


def order_columns(target, chunks, first, n_h):
    columns, rows = target.shape[1], chunks.shape[1]
    block = columns // (8 * n_h)
    for run in range(target.shape[0] // rows):
        for k in range(8 * n_h):
            at, h = k // n_h, k % n_h
            place = (h * 8 + at // 2 % 2 * 4 + at % 2 * 2 + at // 4) * block
            chunk, start = k * block // CHUNK, k * block % CHUNK
            target[run * rows : (run + 1) * rows, place : place + block] = chunks[
                first + run * columns // CHUNK + chunk, :, start : start + block
            ]


def attention_kernel(n_h, sections, periods, left_starts, scale, *refs):
    lefts, query, pairs, d_out, log_total, seg_keys, seg_mine, h0, dh1, vectors, left_one = refs[:11]
    n_rights = 2 * len(sections)
    rights, weight = refs[11 : 11 + n_rights], refs[11 + n_rights]
    (out, turned_own, turned_other, lefts_next, dh0b, grad_up, grad_down, grad_out, d_qkv, d_pairs, by_core, by_y, d_query, weight_buf, turned,
     da1, vector_rows, send_left, got_left, send, recv, local, *scratch) = refs[12 + n_rights :]
    y, c = lax.axis_index("y"), lax.axis_index("c")
    f32, b16 = jnp.float32, jnp.bfloat16
    cells, width = query.shape
    slots = 4 * cells
    n_pairs, head = width // 128, 64
    into = (((1,), (1,)), ((), ()))

    def backward(j, half):
        lanes = pl.ds(pl.multiple_of(j * 128, 128), 128)
        value_lanes = pl.ds(pl.multiple_of(width + j * 128, 128), 128)
        side = slice(half * head, (half + 1) * head)
        keys = pairs[:, :, :, lanes].reshape(slots, 128)[:, side]
        values = pairs[:, :, :, value_lanes].reshape(slots, 128)[:, side]
        mine, above = query[:, lanes][:, side], d_out[:, lanes][:, side]
        scores = lax.dot_general(keys, mine, into, preferred_element_type=f32) * scale
        scores = jnp.where(seg_keys[...] == seg_mine[...], scores, -1000000000.0)
        probs = jnp.exp(scores - log_total[pl.ds(2 * j + half, 1), :])
        d_probs = lax.dot_general(values, above, into, preferred_element_type=f32)
        inner = jnp.sum(probs * d_probs, axis=0, keepdims=True)
        d_scores = (probs * (d_probs - inner)).astype(b16)
        d_keys = jnp.dot(d_scores, mine, preferred_element_type=f32) * scale
        d_values = jnp.dot(probs.astype(b16), above, preferred_element_type=f32)
        d_pairs[0, j, :, side] = d_keys.astype(b16)
        d_pairs[1, j, :, side] = d_values.astype(b16)
        turned = keys.astype(f32).T.astype(b16)
        d_query[side] = jnp.dot(turned, d_scores, preferred_element_type=f32) * scale
        if half:
            d_qkv[:, lanes] = d_query[...].T.astype(b16)

    def to_core():
        return pltpu.make_async_remote_copy(
            src_ref=d_pairs.at[:, :, pl.ds(2 * cells, 2 * cells)], dst_ref=by_core,
            send_sem=send.at[0], recv_sem=recv.at[0], device_id={"c": 1 - c}, device_id_type=MESH,
        )

    def to_y():
        return pltpu.make_async_remote_copy(
            src_ref=d_pairs.at[:, :, pl.ds(cells, cells)], dst_ref=by_y,
            send_sem=send.at[1], recv_sem=recv.at[1], device_id={"y": 1 - y}, device_id_type=MESH,
        )

    def beside(i, right, odd):
        @pl.when(i < 2 * n_pairs)
        def _():
            backward(i // 2, odd)

    def fetch_weight():
        return pltpu.make_async_copy(weight, weight_buf, local.at[0])

    def keep_turned():
        return pltpu.make_async_copy(turned, turned_own, local.at[1])

    def send_turned():
        return pltpu.make_async_remote_copy(
            src_ref=turned, dst_ref=turned_other,
            send_sem=send.at[2], recv_sem=recv.at[2], device_id={"c": 1 - c}, device_id_type=MESH,
        )

    def to_other_left():
        return pltpu.make_async_remote_copy(
            src_ref=send_left, dst_ref=got_left,
            send_sem=send.at[3], recv_sem=recv.at[3], device_id={"c": 1 - c}, device_id_type=MESH,
        )

    def share():
        to_core().wait_recv()

        def add(j, carry):
            for kind in (0, 1):
                total = d_pairs[kind, j, : 2 * cells].astype(f32) + by_core[kind, j].astype(f32)
                d_pairs[kind, j, : 2 * cells] = total.astype(b16)
            return carry

        lax.fori_loop(0, n_pairs, add, 0)
        to_y().start()

    def collect():
        to_y().wait_recv()

        def add(j, carry):
            for kind in (0, 1):
                lanes = pl.ds(pl.multiple_of((kind + 1) * width + j * 128, 128), 128)
                total = d_pairs[kind, j, :cells].astype(f32) + by_y[kind, j].astype(f32)
                d_qkv[:, lanes] = total.astype(b16)
            return carry

        lax.fori_loop(0, n_pairs, add, 0)

    def turn():
        def tile(k, carry):
            turned[chunk_of(k)] = d_qkv[:, chunk_of(k)].astype(f32).T.astype(b16)
            return carry

        lax.fori_loop(0, 3 * width // CHUNK, tile, 0)
        keep_turned().start()
        send_turned().start()

    def project():
        fetch_weight().wait()
        for k in range(4):
            rows = weight_buf[k // 2, k % 2].reshape(width // 4, -1)[:, : 3 * width]
            da1[:, k * width // 4 : (k + 1) * width // 4] = lax.dot_general(
                d_qkv[...], rows, into, preferred_element_type=f32
            )

    def norm():
        value, above = h0[...], da1[...]
        centred = value - jnp.mean(value, axis=1, keepdims=True)
        inverse = lax.rsqrt(jnp.mean(centred * centred, axis=1, keepdims=True) + eps)
        normed = centred * inverse
        vector_rows[...] = jnp.zeros_like(vector_rows)
        vector_rows[0:1] = jnp.sum(above * normed, axis=0, keepdims=True)
        vector_rows[1:2] = jnp.sum(above, axis=0, keepdims=True)
        vector_rows[2:4] = vectors[1:3]
        above = above * vectors[0:1]
        inner = jnp.mean(above * normed, axis=1, keepdims=True)
        below = inverse * (above - jnp.mean(above, axis=1, keepdims=True) - normed * inner)
        dh0b[...] = (dh1[...] + below).astype(b16)

    def halves():
        for kind, source in enumerate((vector_rows, dh0b)):
            for part in range(8):
                lanes = pl.ds(pl.multiple_of(eighth_of(part) * (width // 8), width // 8), width // 8)
                block = source[:, lanes].astype(f32).T.astype(b16)
                rows = slice(part % 4 * (width // 8), (part % 4 + 1) * (width // 8))
                if part < 4:
                    lefts_next[1 + kind, rows, :cells] = block
                else:
                    send_left[kind, rows] = block
        to_other_left().start()

    def after(p):
        plan = {0: lambda: fetch_weight().start(), n_pairs: lambda: to_core().start(), n_pairs + 2: share}
        plan.update(zip(range(n_chunk_pairs - 2, n_chunk_pairs + 3), (collect, turn, project, norm, halves)))
        for when, action in plan.items():

            @pl.when(p == when)
            def _(action=action):
                action()

    n_chunk_pairs = (sum(sections) + 1) // 2
    scatter_kernel(
        n_h, sections, periods, left_starts, lefts, rights, None, out, scratch, [{"c": 1 - c}],
        lambda section, k: None, beside, after,
    )
    lefts_next[0] = left_one[...]
    to_other_left().wait_recv()
    for kind in (0, 1):
        lefts_next[1 + kind, :, cells:] = got_left[kind]
    if n_h > 1:
        order_columns(grad_up, out, 0, n_h)
        order_columns(grad_down, out, 4 * width // CHUNK, n_h)
        order_columns(grad_out, out, 8 * width // CHUNK, n_h)
    keep_turned().wait()
    send_turned().wait()
    for copy in (to_core(), to_y(), to_other_left()):
        copy.wait_send()


def scatter_call(kernel, lefts, rights, operands, more_operands, out_shapes, out_specs, scratch, collective_id):
    periods = [other.shape[0] // CHUNK for _, other, _ in rights]
    sections = [period * times for period, (*_, times) in zip(periods, rights)]
    n, cells = sum(sections), rights[0][0].shape[1]
    w = lefts.shape[1] // 4
    n_h = lax.axis_size("h")
    rows = w // n_h
    inner_h = n_h if rows % 16 == 0 else 1
    dma, bf16, f32 = pltpu.SemaphoreType.DMA, jnp.bfloat16, jnp.float32
    vmem, hbm = pl.BlockSpec(memory_space=pltpu.VMEM), pl.BlockSpec(memory_space=pl.ANY)
    others = max(inner_h - 1, 1)
    part_shape = jax.ShapeDtypeStruct((n, rows, CHUNK), f32)
    if inner_h == 1:
        part_shape = jax.ShapeDtypeStruct((n, w, CHUNK), bf16)
    part, *more = pl.pallas_call(
        functools.partial(kernel, inner_h, sections, periods),
        out_shape=[part_shape] + out_shapes,
        in_specs=[vmem] * (1 + len(operands)) + [hbm] * (2 * len(rights) + len(more_operands)),
        out_specs=[vmem] + out_specs,
        scratch_shapes=scratch
        + [
            pltpu.VMEM((3, CHUNK, 2 * cells), bf16),
            pltpu.VMEM((RING, 2 * w, CHUNK), f32),
            pltpu.VMEM((RING, 2 * w, CHUNK), bf16),
            pltpu.VMEM((n, 2 * w, CHUNK), bf16),
            pltpu.VMEM((RING, w, CHUNK), bf16),
            pltpu.VMEM((n, w, CHUNK), bf16),
            pltpu.VMEM((RING, w, CHUNK), bf16),
            pltpu.VMEM((n, others, w // inner_h, CHUNK), bf16),
            dma((3, 2)),
            dma((RING,)),
            dma((n,)),
            dma((RING,)),
            dma((n,)),
            dma((RING, others)),
            dma((n, others)),
        ],
        compiler_params=pltpu.CompilerParams(
            collective_id=collective_id, has_side_effects=True, vmem_limit_bytes=60 * 2**20
        ),
    )(lefts, *operands, *(half for pair in rights for half in pair[:2]), *more_operands)
    if inner_h == 1:
        part = lax.psum_scatter(part, "h", scatter_dimension=1, tiled=True).astype(f32)
    return part, *more


def scatter_product(lefts, left_starts, rights, vector, weights, product_type, with_sum, collective_id):
    (cells, features), columns = vector.shape, rights[-1][1].shape[0]
    dma = pltpu.SemaphoreType.DMA
    vmem, hbm = pl.BlockSpec(memory_space=pltpu.VMEM), pl.BlockSpec(memory_space=pl.ANY)

    def kernel(n_h, sections, periods, *refs):
        product_kernel(n_h, sections, periods, left_starts, len(weights) - with_sum, with_sum, *refs)

    return scatter_call(
        kernel,
        lefts,
        rights,
        [vector],
        weights,
        [jax.ShapeDtypeStruct((columns, cells), product_type)]
        + [jax.ShapeDtypeStruct((features, cells), kind) for kind in (jnp.float32, jnp.bfloat16)] * with_sum,
        [hbm] + [vmem] * (2 * with_sum),
        [
            pltpu.VMEM((3, features, CHUNK), jnp.bfloat16),
            pltpu.VMEM((2, CHUNK, cells), product_type),
            dma((3, len(weights))),
            dma((2,)),
        ],
        collective_id,
    )


def scatter_attention(lefts, left_starts, rights, operands, weight, scale, collective_id):
    cells, width = operands[0].shape
    own_rows = width // (8 * lax.axis_size("h"))
    bf16, f32, dma = jnp.bfloat16, jnp.float32, pltpu.SemaphoreType.DMA
    vmem, hbm = pl.BlockSpec(memory_space=pltpu.VMEM), pl.BlockSpec(memory_space=pl.ANY)

    def kernel(n_h, sections, periods, *refs):
        attention_kernel(n_h, sections, periods, left_starts, scale, *refs)

    return scatter_call(
        kernel,
        lefts,
        rights,
        operands,
        [weight],
        [
            jax.ShapeDtypeStruct((3 * width, cells), bf16),
            jax.ShapeDtypeStruct((3 * width, cells), bf16),
            jax.ShapeDtypeStruct((3,) + lefts.shape[1:], bf16),
            jax.ShapeDtypeStruct((cells, width), bf16),
            jax.ShapeDtypeStruct((own_rows, 4 * width), f32),
            jax.ShapeDtypeStruct((4 * own_rows, width), f32),
            jax.ShapeDtypeStruct((own_rows, width), f32),
        ],
        [hbm, hbm, vmem, vmem, vmem, vmem, vmem],
        [
            pltpu.VMEM((cells, 3 * width), bf16),
            pltpu.VMEM((2, width // 128, 4 * cells, 128), bf16),
            pltpu.VMEM((2, width // 128, 2 * cells, 128), bf16),
            pltpu.VMEM((2, width // 128, cells, 128), bf16),
            pltpu.VMEM((128, cells), f32),
            pltpu.VMEM(weight.shape, bf16),
            pltpu.VMEM((3 * width, cells), bf16),
            pltpu.VMEM((cells, width), f32),
            pltpu.VMEM((cells, width), f32),
            pltpu.VMEM((2, width // 2, cells), bf16),
            pltpu.VMEM((2, width // 2, cells), bf16),
            dma((4,)),
            dma((4,)),
            dma((2,)),
        ],
        collective_id,
    )


def both_cores(right, times=1):
    return right, swap(right, "c"), times


def columns_of(chunks):
    return chunks.transpose(1, 0, 2).reshape(chunks.shape[1], -1)


def on_device(
    counts,
    library,
    coords,
    lengths,
    cotangent,
    w_enc,
    w_qkv,
    w_out,
    gain_one,
    shift_one,
    w_up,
    w_down,
    gain_two,
    shift_two,
    w_dec,
):
    rows = counts.shape[0]
    width = w_qkv.shape[1] // 3
    att_scale = (width // HEADS) ** (-0.5)
    group_size = 4
    slots = rows * group_size
    scale = 10000.0 / library
    genes = counts.shape[1]
    padded = -(-genes // CHUNK) * CHUNK
    counts_f = counts.astype(jnp.float32)
    pe = by_owner(positions(coords, width), 1)
    ends = jnp.cumsum(lengths[0])
    group = [
        (lax.axis_index("y") ^ by_y) * 2 + (lax.axis_index("c") ^ by_c)
        for by_c in range(2)
        for by_y in range(2)
    ]
    place = jnp.concatenate([at * rows + jnp.arange(rows, dtype=jnp.int32) for at in group])
    seg_all = jnp.sum((place[:, None] >= ends[None, :]).astype(jnp.int32), axis=1)
    vectors = jnp.stack([gain_one, shift_one, gain_two, shift_two], axis=1)
    vectors = jnp.pad(vectors, ((0, 0), (0, 124)))
    pad = ((0, 0), (0, padded - genes))
    quarter = padded // CHUNK // 4 * CHUNK
    gene_cuts = [0, quarter, 2 * quarter, 3 * quarter, padded]
    shards = [
        jnp.pad(w_enc.T, pad),
        jnp.concatenate([w_qkv, vectors], axis=1),
        by_owner(w_out, 1),
        by_owner(w_up, 1),
        by_owner(w_down, 1),
        jnp.pad(w_dec.T, pad),
    ]
    cuts = [gene_cuts, [0, width // 2 * 3, 3 * width + 128], [0, width]]
    cuts += [[0, 2 * width, 4 * width], [0, width // 2, width]]
    cuts += [gene_cuts]
    order = [(0, 0), (0, 1), (0, 2), (0, 3), (1, 0), (1, 1), (2, 0), (3, 0), (3, 1), (4, 0), (4, 1)]
    order += [(5, 0), (5, 1), (5, 2), (5, 3)]
    (gathered, xb, xb_other, cot_other, kv_pairs, lefts, left_one, left_last, h0, query, log_total, h1, slope, _,
     hb) = gather_all(
        shards, cuts, order, counts.T, cotangent.T, scale[None, :], pe.T, seg_all, att_scale, 0
    )
    enc_all, qkv_all, out_all, up_all, down_all, dec_all = (
        w.reshape(-1, w.shape[-1]) for w in gathered
    )
    vectors = qkv_all[:, 3 * width :].astype(jnp.float32).T
    g1f, b1f, g2f, b2f = vectors[0], vectors[1], vectors[2], vectors[3]
    grad_dec, logits, dh2, dfb_turned = scatter_product(
        left_last, [0], [(cotangent.T, cot_other, 1)], hb, [dec_all, gene_tail(cotangent.T)], jnp.bfloat16, True, 1
    )
    own_rows = grad_dec.shape[1]
    grad_dec = columns_of(grad_dec)[:, :genes].T
    logits = logits[:genes].T
    dh2 = dh2.T
    dfb = dfb_turned.T
    d_act = contract_cols(dfb, down_all)
    d_hidden = (d_act * slope.T).astype(jnp.bfloat16)
    da2 = contract_cols(d_hidden, up_all)
    norm_pull = jax.vjp(layer_norm, h1, g2f, b2f)[1]
    dh1_norm, grad_gain_two, grad_shift_two = norm_pull(da2)
    dh1 = dh2 + dh1_norm
    dab = dh1.astype(jnp.bfloat16)
    d_attended = contract_cols(dab, out_all).astype(jnp.bfloat16)
    d_attended = from_owner(d_attended, 1)
    pieces = (4 * width,) + (width,) * 4
    rights = [both_cores(d_hidden.T), both_cores(dfb_turned, 4), both_cores(dab.T)]
    operands = [query, kv_pairs, d_attended, log_total, seg_all[:, None], seg_all[None, :rows], h0, dh1]
    operands += [jnp.pad(jnp.stack([g1f, grad_gain_two, grad_shift_two]), ((0, 5), (0, 0))), left_one[0]]
    grads, d_qkv, d_qkv_other, lefts, dh0b, *ordered = scatter_attention(
        lefts,
        [sum(pieces[:k]) // CHUNK for k in range(len(pieces) + 1)],
        rights,
        operands,
        gathered[1],
        att_scale,
        2,
    )
    if own_rows % 16 == 0:
        grad_up, grad_down, grad_out = ordered
    else:
        ends = [0]
        for columns in (4 * width, 4 * width, width):
            ends.append(ends[-1] + columns // CHUNK)
        grad_up, grad_down, grad_out = (grads[low:high] for low, high in zip(ends, ends[1:]))
        n_h = lax.axis_size("h")
        by_half = (2, 2, 2, 2, own_rows, n_h // 2, -1)
        grad_up = grad_up.reshape(by_half).transpose(4, 3, 5, 1, 2, 0, 6).reshape(own_rows, -1)
        by_pair = (-1, 2, 2, own_rows, 2, n_h, width // (8 * n_h))
        grad_out, grad_down = (
            g.reshape(by_pair).transpose(0, 3, 5, 2, 4, 1, 6).reshape(-1, width) for g in (grad_out, grad_down)
        )
    unit = jnp.eye(rows, dtype=jnp.bfloat16)
    grads, d_xb = scatter_product(
        lefts,
        [0, 3 * width // CHUNK, (3 * width + rows) // CHUNK],
        [(d_qkv, d_qkv_other, 1), (unit, unit, 1), (xb, xb_other, 1)],
        dh0b,
        [enc_all],
        jnp.float32,
        False,
        3,
    )
    ends = [0]
    for columns in (3 * width, rows):
        ends.append(ends[-1] + columns // CHUNK)
    grad_qkv, grad_vectors, grad_enc = (
        grads[low:high] for low, high in zip(ends, ends[1:] + [grads.shape[0]])
    )
    grad_qkv, grad_enc = columns_of(grad_qkv), columns_of(grad_enc)
    grad_gain_one, grad_shift_one, grad_gain_two, grad_shift_two = (
        grad_vectors[0, :, k] for k in range(4)
    )
    grad_enc = grad_enc[:, :genes].T
    d_xb = d_xb[:genes].T
    counts_grad = d_xb * scale[:, None] / (1.0 + counts_f * scale[:, None])
    return (
        logits,
        counts_grad,
        grad_enc,
        grad_qkv,
        grad_out,
        grad_gain_one,
        grad_shift_one,
        grad_up,
        grad_down,
        grad_gain_two,
        grad_shift_two,
        grad_dec,
    )


ALL = ("h", "x", "y", "c")


def solution(mesh):
    n_dp, n_fsdp = mesh.shape["dp"], mesh.shape["fsdp"]
    mesh = Mesh(mesh.devices.reshape((n_dp // 2, 2, 2, n_fsdp // 2)), ALL)
    placed = (
        P(ALL, None),
        P(ALL),
        P(None, ALL),
        P(("h", "x"), None),
        P(ALL, None),
        P(None, ALL),
        P(ALL, None),
        P(ALL, None),
        P(ALL),
        P(ALL),
        P(ALL, None),
        P(ALL, None),
        P(ALL),
        P(ALL),
        P(None, ALL),
    )
    return jax.shard_map(
        on_device,
        mesh=mesh,
        in_specs=placed,
        out_specs=(
            P(ALL, None),
            P(ALL, None),
            P(None, ALL),
            P(ALL, None),
            P(ALL, None),
            P(ALL),
            P(ALL),
            P(ALL, None),
            P(ALL, None),
            P(ALL),
            P(ALL),
            P(None, ALL),
        ),
        check_vma=False,
    )
```
